32 devices in a mesh: dp: 8 (over y, x, core), head: 4 (over z).
Axes of the slice: x: 2, y: 2, z: 4, core: 2. Of those that a mesh axis runs over, the one named last changes fastest.
Arguments:
- stream_in: float32 [16384, 1024], P('dp', 'head'), may hold values from -60 to 60
- qkv_weight: bfloat16 [2, 3, 1024, 1024], P(None, None, 'dp', 'head'), may hold values from -0.1875 to 0.1875
- out_weight: bfloat16 [2, 1024, 1024], P(None, 'head', 'dp'), may hold values from -0.1875 to 0.1875
- up_weight: bfloat16 [2, 1024, 4096], P(None, 'dp', 'head'), may hold values from -2 to 2
- down_weight: bfloat16 [2, 4096, 1024], P(None, 'head', 'dp'), may hold values from -0.09375 to 0.09375
- norm_gains: float32 [2, 3, 1024], P(None, None, 'head'), may hold values from 0.5 to 1.5
- norm_shifts: float32 [2, 3, 1024], P(None, None, 'head'), may hold values from -1.8 to 1.8
- hidden_gains: float32 [2, 4096], P(None, 'head'), may hold values from 0.5 to 1.5
- hidden_shifts: float32 [2, 4096], P(None, 'head'), may hold values from -1.8 to 1.8
- buckets: int32 [8], P('dp'), may hold values from 0 to 1, as said below
- valid_mask: int32 [16384], P('dp'), may hold values from 0 to 1, as said below
- cotangent: float32 [16384, 1024], P('dp', 'head'), may hold values from -6 to 6
Outputs:
- stream_out: float32 [16384, 1024], P('dp', 'head')
- stream_grad: float32 [16384, 1024], P('dp', 'head')
- qkv_grad: float32 [2, 3, 1024, 1024], P(None, None, 'dp', 'head')
- out_grad: float32 [2, 1024, 1024], P(None, 'head', 'dp')
- up_grad: float32 [2, 1024, 4096], P(None, 'dp', 'head')
- down_grad: float32 [2, 4096, 1024], P(None, 'head', 'dp')
- gains_grad: float32 [2, 3, 1024], P(None, None, 'head')
- shifts_grad: float32 [2, 3, 1024], P(None, None, 'head')
- hidden_gains_grad: float32 [2, 4096], P(None, 'head')
- hidden_shifts_grad: float32 [2, 4096], P(None, 'head')
- usage_rms: float32 [2, 3], replicated
The draws below stay inside these ranges and needn't reach their ends.
Inputs may be any that keep to these rules, and one draw needn't show every extreme that they name: `buckets`: 0: the slab holds 4 sequences of 512 tokens; 1: the slab holds one sequence of 2048 tokens. `valid_mask`: the real tokens of each sequence are a prefix of it, a quarter of its length or more.
All inputs are finite; a program needn't handle non-finite values.
Results may differ from the reference program's by a relative error of at most 0.038.
Values may be sent and summed in bfloat16 or wider, within the bound.
A program may use at most 320 MiB of HBM per device.

```python
import math
import jax
import jax.numpy as jnp
from jax import lax

D = 1024
HEADS = 16
DH = 64
FF = 4096
LAYERS = 2
LONG = 2048
SHORT = 512
SLABS = 1
TOKENS = 16384
N_DP = 8
N_HEAD = 4


def slab_layout(key):
    bucket_key, short_key, long_key = jax.random.split(key, 3)
    slab_total = SLABS * N_DP
    denom = max(slab_total - 1, 1)
    slab_index = jnp.arange(slab_total, dtype=jnp.int32)
    marks = jax.random.randint(bucket_key, (slab_total,), 0, 2)
    blocks = LONG // SHORT
    short_low = SHORT // 4 + SHORT // 2 * slab_index // denom
    long_low = LONG // 4 + LONG // 2 * slab_index // denom
    short_lens = jax.random.randint(short_key, (slab_total, blocks), short_low[:, None], short_low[:, None] + SHORT // 4 + 1)
    long_lens = jax.random.randint(long_key, (slab_total,), long_low, long_low + LONG // 4 + 1)
    position = jnp.arange(LONG)
    short_rows = (position % SHORT)[None, :] < jnp.repeat(short_lens, SHORT, axis=1)
    long_rows = position[None, :] < long_lens[:, None]
    valid_rows = jnp.where(marks[:, None] == 1, long_rows, short_rows)
    return (marks.astype(jnp.int32), valid_rows.astype(jnp.int32).reshape(slab_total * LONG))


def draw_buckets(key, part):
    marks, valid_rows = slab_layout(key)
    return marks


def draw_valid_mask(key, part):
    marks, valid_rows = slab_layout(key)
    return valid_rows


def draw_stream_in(key, part):
    key = jax.random.fold_in(key, 7)
    row_total = SLABS * LONG * N_DP
    rise = jnp.arange(row_total, dtype=jnp.float32) / max(row_total - 1, 1)
    base = jnp.clip(jax.random.normal(key, (row_total, D), jnp.float32), -6.0, 6.0)
    scale = jnp.power(10.0, rise)
    return (base * scale[:, None]).astype(jnp.float32)


def draw_up_weight(key, part):
    key = jax.random.fold_in(key, 11)
    rise = jnp.arange(FF, dtype=jnp.float32) / max(FF - 1, 1)
    base = jnp.clip(jax.random.normal(key, (LAYERS, D, FF), jnp.float32), -6.0, 6.0)
    column_scale = 0.5 + rise
    return (base * column_scale[None, None, :] / jnp.sqrt(jnp.float32(D))).astype(jnp.bfloat16)


def block_scale(key, dims, cuts, least, high):
    level = 1.0
    for dim, blocks in cuts:
        heights = jax.random.uniform(jax.random.fold_in(jax.random.fold_in(key, 6), dim), (blocks,), jnp.float32, least / len(cuts), high / len(cuts))
        level = level * jnp.repeat(jnp.exp(heights), dims[dim] // blocks).reshape((-1,) + (1,) * (len(dims) - 1 - dim))
    return level


def normal_values(own_key, extent, deviation, most, shards=(), kind=jnp.bfloat16):
    array = jax.random.normal(own_key, extent, jnp.float32) * deviation
    if len(shards) > 0:
        array = block_scale(own_key, extent, shards, -0.22, 0.18) * array
    return jnp.clip(array, min=-most, max=most).astype(kind)


def setup_inputs(seed: int = 0) -> dict:
    arg_keys = jax.random.split(jax.random.key(seed), 13)
    stream_in = draw_stream_in(jax.random.fold_in(arg_keys[12], 71), 0)
    qkv_weight = normal_values(arg_keys[1], (LAYERS, 3, D, D), D ** -0.5, 0.1875, ((2, 8), (3, 4)))
    out_weight = normal_values(arg_keys[2], (LAYERS, D, D), D ** -0.5, 0.1875, ((1, 4), (2, 8)))
    up_weight = draw_up_weight(jax.random.fold_in(arg_keys[12], 71), 0)
    down_weight = normal_values(arg_keys[4], (LAYERS, FF, D), FF ** -0.5, 0.09375, ((1, 4), (2, 8)))
    norm_gains = jnp.clip(1.0 + 0.1 * jax.random.normal(arg_keys[5], (LAYERS, 3, D), jnp.float32), 0.5, 1.5)
    norm_shifts = normal_values(arg_keys[6], (LAYERS, 3, D), 0.3, 1.8, ((2, 4),), jnp.float32)
    hidden_gains = jnp.clip(1.0 + 0.1 * jax.random.normal(arg_keys[7], (LAYERS, FF), jnp.float32), 0.5, 1.5)
    hidden_shifts = normal_values(arg_keys[8], (LAYERS, FF), 0.3, 1.8, ((1, 4),), jnp.float32)
    buckets = draw_buckets(jax.random.fold_in(arg_keys[12], 71), 0)
    valid_mask = draw_valid_mask(jax.random.fold_in(arg_keys[12], 71), 0)
    cotangent = normal_values(arg_keys[11], (TOKENS, D), 1.0, 6.0, ((0, 8), (1, 4)), jnp.float32)
    return {"stream_in": stream_in, "qkv_weight": qkv_weight, "out_weight": out_weight, "up_weight": up_weight, "down_weight": down_weight, "norm_gains": norm_gains, "norm_shifts": norm_shifts, "hidden_gains": hidden_gains, "hidden_shifts": hidden_shifts, "buckets": buckets, "valid_mask": valid_mask, "cotangent": cotangent}


norm_eps = 1e-05
masked_score = -1000000000.0
highest = lax.Precision.HIGHEST

@jax.custom_vjp
def low(v):
    return lax.optimization_barrier(v.astype(jnp.bfloat16)).astype(jnp.float32)

@jax.custom_vjp
def low_back(v):
    return v

def low_keep(v):
    return (low(v), None)

def low_pass(kept, grad):
    return (grad,)

def back_keep(v):
    return (v, None)

def back_low(kept, grad):
    return (low(grad),)
low.defvjp(low_keep, low_pass)
low_back.defvjp(back_keep, back_low)

def rounded_both(value):
    return low_back(low(value))

def layer_norm(value, scale_row, shift_row):
    centred = value - lax.optimization_barrier(jnp.mean(value, axis=-1, keepdims=True))
    variance = lax.optimization_barrier(jnp.mean(centred * centred, axis=-1, keepdims=True))
    return centred * lax.rsqrt(variance + norm_eps) * scale_row + shift_row

def grouped(inputs, matrix):
    row_count = inputs.shape[0]
    span = inputs.shape[1] // N_HEAD
    pieces = jnp.einsum('lgk,gkd->gld', inputs.reshape(row_count, N_HEAD, span), matrix.reshape(N_HEAD, span, matrix.shape[1]), precision=highest)
    return lax.optimization_barrier(jnp.sum(low(pieces), axis=0))

def attention(queries, key_rows, values, allowed):
    factor = 1.0 / math.sqrt(DH)

    def split_heads(matrix):
        return matrix.reshape(matrix.shape[0], HEADS, DH).transpose(1, 0, 2)

    def one_head(inputs):
        head_q, head_k, head_v = inputs
        scores = low_back(jnp.dot(head_q, head_k.T, precision=highest) * factor)
        scores = jnp.where(allowed, scores, masked_score)
        row_top = lax.optimization_barrier(jnp.max(scores, axis=1, keepdims=True))
        raised = jnp.exp(scores - row_top)
        probs = raised / lax.optimization_barrier(jnp.sum(raised, axis=1, keepdims=True))
        return jnp.dot(low(probs), head_v, precision=highest)
    result = lax.map(jax.checkpoint(one_head), (split_heads(queries), split_heads(key_rows), split_heads(values)))
    return result.transpose(1, 0, 2).reshape(queries.shape[0], HEADS * DH)

def masked_square(values, row_weight):
    return jnp.sum(row_weight[:, None] * values * values)

def forward(stream, qkv_weight, out_weight, up_weight, down_weight, norm_gains, norm_shifts, hidden_gains, hidden_shifts, allowed, row_weight):
    usage_rows = []
    for layer_index in range(LAYERS):
        normed_in = low(layer_norm(low(stream), norm_gains[layer_index, 0], norm_shifts[layer_index, 0]))
        queries = rounded_both(jnp.dot(normed_in, qkv_weight[layer_index, 0], precision=highest))
        key_rows = rounded_both(jnp.dot(normed_in, qkv_weight[layer_index, 1], precision=highest))
        values = rounded_both(jnp.dot(normed_in, qkv_weight[layer_index, 2], precision=highest))
        attended = low_back(attention(queries, key_rows, values, allowed))
        normed_mid = low(layer_norm(attended, norm_gains[layer_index, 1], norm_shifts[layer_index, 1]))
        branch = low_back(grouped(normed_mid, out_weight[layer_index]))
        stream = stream + branch
        normed_ffn = low(layer_norm(low(stream), norm_gains[layer_index, 2], norm_shifts[layer_index, 2]))
        hidden = low_back(jnp.dot(normed_ffn, up_weight[layer_index], precision=highest))
        active = jax.nn.gelu(hidden, approximate=False)
        normed_out = low(layer_norm(active, hidden_gains[layer_index], hidden_shifts[layer_index]))
        feed = low_back(grouped(normed_out, down_weight[layer_index]))
        stream = stream + feed
        usage_rows.append(jnp.stack([masked_square(branch, row_weight), masked_square(feed, row_weight), masked_square(stream, row_weight)]))
    return (stream, jnp.stack(usage_rows))

def reference(stream_in, qkv_weight, out_weight, up_weight, down_weight, norm_gains, norm_shifts, hidden_gains, hidden_shifts, buckets, valid_mask, cotangent):
    params = tuple((tensor.astype(jnp.float32) for tensor in (qkv_weight, out_weight, up_weight, down_weight, norm_gains, norm_shifts, hidden_gains, hidden_shifts)))
    slab_count = buckets.shape[0]
    packets = (stream_in.astype(jnp.float32).reshape(slab_count, LONG, D), cotangent.astype(jnp.float32).reshape(slab_count, LONG, D), buckets.astype(jnp.int32), valid_mask.astype(jnp.int32).reshape(slab_count, LONG))
    position = jnp.arange(LONG, dtype=jnp.int32)

    def advance(running, packet):
        grad_sums, usage_sums = running
        slab_in, slab_cot, bucket_id, slab_valid = packet
        seq_len = jnp.where(bucket_id == 1, LONG, SHORT).astype(jnp.int32)
        member = (position // seq_len).astype(jnp.int32)
        allowed = (member[:, None] == member[None, :]) & (slab_valid[None, :] == 1)
        row_weight = slab_valid.astype(jnp.float32)

        def run(slab_stream, *weights):
            return forward(slab_stream, *weights, allowed, row_weight)
        slab_out, pull_back, usage_part = jax.vjp(run, slab_in, *params, has_aux=True)
        gradients = pull_back(slab_cot)
        grad_sums = tuple((earlier + addend for earlier, addend in zip(grad_sums, gradients[1:])))
        return ((grad_sums, usage_sums + usage_part), (slab_out, gradients[0]))
    initial = (tuple((jnp.zeros_like(tensor) for tensor in params)), jnp.zeros((LAYERS, 3), jnp.float32))
    (grad_sums, usage_sums), (stream_rows, input_rows) = lax.scan(advance, initial, packets)
    valid_total = jnp.sum(valid_mask.astype(jnp.float32))
    usage_rms = jnp.sqrt(usage_sums / (valid_total * D))
    return (stream_rows.reshape(TOKENS, D), input_rows.reshape(TOKENS, D), grad_sums[0], grad_sums[1], grad_sums[2], grad_sums[3], grad_sums[4], grad_sums[5], grad_sums[6], grad_sums[7], usage_rms)
```

```python
import math

import jax
import jax.numpy as jnp
from jax import lax
from jax.experimental import pallas as pl
from jax.experimental.pallas import tpu as pltpu
from jax.sharding import PartitionSpec as P

D = 1024
FF = 4096
LONG = 2048
SHORT = 512
DH = 64
LANES = 128
BLOCKS = D // LANES
GROUPS = 4
WIDE = FF // GROUPS
EPS = 1e-05
MASKED = -1000000000.0
ROWS = 128
VMEM_BYTES = 60 * 1024 * 1024

f32 = jnp.float32
bf16 = jnp.bfloat16


def dot(a, b):
    return jnp.dot(a, b, preferred_element_type=f32)


def dot_nt(a, b):
    return lax.dot_general(a, b, (((1,), (1,)), ((), ())), preferred_element_type=f32)


def flip(a):
    return jnp.transpose(a.astype(f32), (1, 0)).astype(a.dtype)


def wide_pair(ref, one, two):
    return jnp.concatenate([ref[one], ref[two]], axis=1)


def row_loop(total, step, body):
    def advance(i, carry):
        body(pl.ds(pl.multiple_of(i * step, step), step))
        return carry

    lax.fori_loop(0, total // step, advance, 0)


def row_stats(blocks, width):
    mean = sum_lanes(blocks) / width
    square = sum_lanes([(b - mean) * (b - mean) for b in blocks]) / width
    return mean, lax.rsqrt(square + EPS)


def sum_lanes(blocks):
    total = blocks[0]
    for b in blocks[1:]:
        total = total + b
    return jnp.sum(total, axis=1, keepdims=True)


def params(**kw):
    return pltpu.CompilerParams(vmem_limit_bytes=VMEM_BYTES, **kw)


def cost(flops, size, trans=0):
    return pl.CostEstimate(flops=int(flops), bytes_accessed=int(size), transcendentals=int(trans))


def whole(shape):
    zeros = (0,) * len(shape)
    return pl.BlockSpec(shape, lambda *_: zeros)


def norm_back(dy, hat, rstd, gains, width):
    dx = [a * g for a, g in zip(dy, gains)]
    first = sum_lanes(dx) / width
    cross = sum_lanes([a * h for a, h in zip(dx, hat)]) / width
    return [rstd * (a - first - h * cross) for a, h in zip(dx, hat)]


def qkv_kernel(sc, x, gain, shift, *refs):
    weights, outs, xs = refs[:8], refs[8:16], refs[16]
    step = pl.program_id(0)
    tokens = x.shape[1]

    @pl.when(step == 0)
    def _():
        def body(r):
            blocks = [x[b, r, :].astype(f32) for b in range(BLOCKS)]
            mean, rstd = row_stats(blocks, D)
            for b in range(BLOCKS):
                xs[b, r, :] = ((blocks[b] - mean) * rstd * gain[b] + shift[b]).astype(bf16)

        row_loop(tokens, ROWS, body)

    for c in range(3):
        total = None
        for q in range(4):
            left = wide_pair(xs, sc[2 * q], sc[2 * q + 1])
            right = jnp.concatenate([weights[2 * q][0, c], weights[2 * q + 1][0, c]], axis=0)
            term = dot(left, right)
            total = term if total is None else total + term
        total = total.astype(bf16)
        for k in range(GROUPS):

            @pl.when(step == k)
            def _(k=k, c=c, total=total):
                outs[2 * k][c] = total[:, :LANES]
                outs[2 * k + 1][c] = total[:, LANES:]


def qkv_call(sc, x, gain, shift, pieces):
    tokens = x.shape[1]
    out = jax.ShapeDtypeStruct((3, tokens, LANES), bf16)
    return pl.pallas_call(
        qkv_kernel,
        out_shape=[out] * 8,
        grid_spec=pltpu.PrefetchScalarGridSpec(
            num_scalar_prefetch=1,
            grid=(GROUPS,),
            in_specs=[whole(x.shape), whole(gain.shape), whole(shift.shape)]
            + [
                pl.BlockSpec((1, 3, LANES, 256), lambda k, sc: ((sc[8] + k) % GROUPS, 0, 0, 0))
            ]
            * 8,
            out_specs=[whole(out.shape)] * 8,
            scratch_shapes=[pltpu.VMEM((BLOCKS, tokens, LANES), bf16)],
        ),
        compiler_params=params(),
        cost_estimate=cost(2 * tokens * D * 3 * D, 10 * 2**20),
        name="qkv",
    )(sc, x, gain, shift, *pieces)


def head_lanes(value, head):
    lane = lax.broadcasted_iota(jnp.int32, value.shape, 1)
    keep = (lane < DH) if head == 0 else (lane >= DH)
    return jnp.where(keep, value, jnp.zeros_like(value))


def attn_kernel(need, aux, one, *refs):
    n = (len(refs) - 6) // 2
    qkv, outs = refs[:n], refs[n : 2 * n]
    lse, kx, vt, qs, top, acc = refs[2 * n :]
    tokens = aux.shape[1]
    for r in range(n):
        kx[r] = jnp.concatenate([qkv[r][1], aux[r]], axis=1)
        turned = flip(qkv[r][2])
        ones = jnp.ones((16, tokens), bf16)
        vt[r, 0] = jnp.concatenate([turned[:DH], ones], axis=0)
        vt[r, 1] = jnp.concatenate([turned[DH:], ones], axis=0)
        qs[r] = (qkv[r][0].astype(f32) * (1.0 / math.sqrt(DH))).astype(bf16)

    def each_query(i, carry):
        query = qs[i]
        extended = [jnp.concatenate([head_lanes(query, h), one[...]], axis=1) for h in range(2)]
        top[...] = jnp.full_like(top, -3e38)
        acc[...] = jnp.zeros_like(acc)

        def each_key(j, inner):
            @pl.when(need[i * n + j] == 1)
            def _():
                for h in range(2):
                    scores = dot_nt(kx[j], extended[h])
                    before = top[h : h + 1]
                    now = jnp.maximum(before, jnp.max(scores, axis=0, keepdims=True))
                    raised = jnp.exp(scores - now).astype(bf16)
                    top[h : h + 1] = now
                    acc[h] = acc[h] * jnp.exp(before - now) + dot(vt[j, h], raised)

            return inner

        lax.fori_loop(0, n, each_key, 0)
        sums = [acc[h][DH : DH + 1] for h in range(2)]
        both = jnp.concatenate([acc[h][:DH] / sums[h] for h in range(2)], axis=0)
        qs[i] = jnp.transpose(both, (1, 0)).astype(bf16)
        for h in range(2):
            lse[i, h : h + 1] = top[h : h + 1] + jnp.log(sums[h])
        return carry

    lax.fori_loop(0, n, each_query, 0)
    for r in range(n):
        outs[r][...] = qs[r]


def attn_call(need, aux, one, parts):
    n = len(parts)
    tokens = aux.shape[1]
    out = jax.ShapeDtypeStruct((tokens, LANES), bf16)
    sums = jax.ShapeDtypeStruct((n, 8, tokens), f32)
    total = n * tokens
    res = pl.pallas_call(
        attn_kernel,
        out_shape=[out] * n + [sums],
        grid_spec=pltpu.PrefetchScalarGridSpec(
            num_scalar_prefetch=1,
            grid=(),
            in_specs=[pl.BlockSpec(memory_space=pltpu.VMEM)] * (2 + n),
            out_specs=[pl.BlockSpec(memory_space=pltpu.VMEM)] * (n + 1),
            scratch_shapes=[
                pltpu.VMEM((n, tokens, 2 * LANES), bf16),
                pltpu.VMEM((n, 2, DH + 16, tokens), bf16),
                pltpu.VMEM((n, tokens, LANES), bf16),
                pltpu.VMEM((8, tokens), f32),
                pltpu.VMEM((2, DH + 16, tokens), f32),
            ],
        ),
        compiler_params=params(),
        cost_estimate=cost(2 * total * total * 512, 4 * 2**20, 2 * total * total),
        name="attention",
    )(need, aux, one, *parts)
    return res[:n], res[n]


def proj_kernel(sc, valid, stream, gain, shift, *refs):
    att, weights = refs[:8], refs[8:16]
    mid, use, xs = refs[16:]
    tokens = stream.shape[1]

    def body(r):
        blocks = [a[r, :].astype(f32) for a in att]
        mean, rstd = row_stats(blocks, D)
        for i in range(BLOCKS):
            t = sc[8 + i]
            xs[t, r, :] = ((blocks[i] - mean) * rstd * gain[t] + shift[t]).astype(bf16)

    row_loop(tokens, ROWS, body)
    use[...] = jnp.zeros_like(use)
    keep = valid[...]
    for q in range(4):
        total = None
        for j in range(GROUPS):
            right = jnp.concatenate([weights[2 * q][j], weights[2 * q + 1][j]], axis=1)
            term = dot(wide_pair(xs, 2 * j, 2 * j + 1), right)
            total = term if total is None else total + term
        for half in range(2):
            part = total[:, half * LANES : (half + 1) * LANES]
            t = sc[2 * q + half]
            mid[t] = stream[t] + part
            use[0:1] += jnp.sum(keep * part * part, axis=0, keepdims=True)


def proj_call(sc, valid, stream, gain, shift, att, pieces):
    tokens = stream.shape[1]
    return pl.pallas_call(
        proj_kernel,
        out_shape=[
            jax.ShapeDtypeStruct(stream.shape, f32),
            jax.ShapeDtypeStruct((8, LANES), f32),
        ],
        grid_spec=pltpu.PrefetchScalarGridSpec(
            num_scalar_prefetch=1,
            grid=(),
            in_specs=[pl.BlockSpec(memory_space=pltpu.VMEM)] * 20,
            out_specs=[pl.BlockSpec(memory_space=pltpu.VMEM)] * 2,
            scratch_shapes=[pltpu.VMEM((BLOCKS, tokens, LANES), bf16)],
        ),
        compiler_params=params(),
        cost_estimate=cost(2 * tokens * D * D, 7 * 2**20),
        name="projection",
    )(sc, valid, stream, gain, shift, *att, *pieces)


def gelu_parts(h):
    half = 0.5 * (1.0 + lax.erf(h * (1.0 / math.sqrt(2.0))))
    return half


def up_kernel(sc, mid, gain, shift, hgain, hshift, *refs):
    weights = refs[:8]
    hidden, normed, low, mean_out, rstd_out, xs, act, buf = refs[8:]
    step = pl.program_id(0)
    tokens = mid.shape[1]

    @pl.when(step == 0)
    def _():
        def body(r):
            raw = [mid[b, r, :].astype(bf16) for b in range(BLOCKS)]
            blocks = [v.astype(f32) for v in raw]
            mean, rstd = row_stats(blocks, D)
            for b in range(BLOCKS):
                low[b, r, :] = raw[b]
                xs[b, r, :] = ((blocks[b] - mean) * rstd * gain[b] + shift[b]).astype(bf16)

        row_loop(tokens, ROWS, body)

    total = None
    for q in range(4):
        left = wide_pair(xs, sc[2 * q], sc[2 * q + 1])
        right = jnp.concatenate([weights[2 * q][0], weights[2 * q + 1][0]], axis=0)
        term = dot(left, right)
        total = term if total is None else total + term
    buf[...] = total

    def shape_rows(r):
        h = buf[r, :]
        hidden[0, r, :] = h.astype(bf16)
        act[step, r, :] = h * gelu_parts(h)

    row_loop(tokens, 64, shape_rows)

    @pl.when(step == GROUPS - 1)
    def _():
        def body(r):
            blocks = [act[z, r, :] for z in range(GROUPS)]
            mean, rstd = row_stats(blocks, FF)
            for z in range(GROUPS):
                normed[z, r, :] = ((blocks[z] - mean) * rstd * hgain[z] + hshift[z]).astype(bf16)
            mean_out[r, :] = jnp.broadcast_to(mean, (32, LANES))
            rstd_out[r, :] = jnp.broadcast_to(rstd, (32, LANES))

        row_loop(tokens, 32, body)


def up_call(sc, mid, gain, shift, hgain, hshift, pieces):
    tokens = mid.shape[1]
    return pl.pallas_call(
        up_kernel,
        out_shape=[
            jax.ShapeDtypeStruct((GROUPS, tokens, WIDE), bf16),
            jax.ShapeDtypeStruct((GROUPS, tokens, WIDE), bf16),
            jax.ShapeDtypeStruct(mid.shape, bf16),
            jax.ShapeDtypeStruct((tokens, LANES), f32),
            jax.ShapeDtypeStruct((tokens, LANES), f32),
        ],
        grid_spec=pltpu.PrefetchScalarGridSpec(
            num_scalar_prefetch=1,
            grid=(GROUPS,),
            in_specs=[whole(v.shape) for v in (mid, gain, shift, hgain, hshift)]
            + [pl.BlockSpec((1, LANES, WIDE), lambda k, sc: (k, 0, 0))] * 8,
            out_specs=[
                pl.BlockSpec((1, tokens, WIDE), lambda k, sc: (k, 0, 0)),
                whole((GROUPS, tokens, WIDE)),
                whole(mid.shape),
                whole((tokens, LANES)),
                whole((tokens, LANES)),
            ],
            scratch_shapes=[
                pltpu.VMEM((BLOCKS, tokens, LANES), bf16),
                pltpu.VMEM((GROUPS, tokens, WIDE), f32),
                pltpu.VMEM((tokens, WIDE), f32),
            ],
        ),
        compiler_params=params(),
        cost_estimate=cost(2 * tokens * D * FF, 20 * 2**20, tokens * FF),
        name="up",
    )(sc, mid, gain, shift, hgain, hshift, *pieces)


def down_kernel(sc, valid, mid, normed, *refs):
    weights = refs[:8]
    stream, low, use = refs[8:]
    step = pl.program_id(0)
    for q in range(4):
        right = jnp.concatenate([weights[2 * q][0], weights[2 * q + 1][0]], axis=1)
        total = dot(normed[0], right)
        for half in range(2):
            part = total[:, half * LANES : (half + 1) * LANES]
            t = sc[2 * q + half]

            @pl.when(step == 0)
            def _(t=t, part=part):
                stream[t] = part

            @pl.when(step > 0)
            def _(t=t, part=part):
                stream[t] += part

    @pl.when(step == GROUPS - 1)
    def _():
        use[...] = jnp.zeros_like(use)
        keep = valid[...]
        for b in range(BLOCKS):
            feed = stream[b]
            out = mid[b] + feed
            stream[b] = out
            low[b] = out.astype(bf16)
            use[0:1] += jnp.sum(keep * feed * feed, axis=0, keepdims=True)
            use[1:2] += jnp.sum(keep * out * out, axis=0, keepdims=True)


def down_call(sc, valid, mid, normed, pieces):
    tokens = mid.shape[1]
    return pl.pallas_call(
        down_kernel,
        out_shape=[
            jax.ShapeDtypeStruct(mid.shape, f32),
            jax.ShapeDtypeStruct(mid.shape, bf16),
            jax.ShapeDtypeStruct((8, LANES), f32),
        ],
        grid_spec=pltpu.PrefetchScalarGridSpec(
            num_scalar_prefetch=1,
            grid=(GROUPS,),
            in_specs=[
                whole(valid.shape),
                whole(mid.shape),
                pl.BlockSpec((1, tokens, WIDE), lambda k, sc: (k, 0, 0)),
            ]
            + [pl.BlockSpec((1, WIDE, LANES), lambda k, sc: (k, 0, 0))] * 8,
            out_specs=[whole(mid.shape), whole(mid.shape), whole((8, LANES))],
        ),
        compiler_params=params(),
        cost_estimate=cost(2 * tokens * D * FF, 18 * 2**20),
        name="down",
    )(sc, valid, mid, normed, *pieces)


def ffn_back_kernel(sc, grad, hidden, mean_in, rstd_in, low, gain, shift, hgain, *refs):
    downs, ups = refs[:8], refs[8:16]
    (dhid, grad_turned, normed_turned, grad_out, hgain_grad, hshift_grad, gain_grad, shift_grad) = (
        refs[16:24]
    )
    gs, dxs, hats, slopes, buf, first, cross, acc = refs[24:]
    step = pl.program_id(0)
    tokens = grad.shape[1]

    @pl.when(step == 0)
    def _():
        first[...] = jnp.zeros_like(first)
        cross[...] = jnp.zeros_like(cross)
        for b in range(BLOCKS):
            gs[b] = grad[b].astype(bf16)
            grad_turned[b] = flip(gs[b])

    @pl.when(step < GROUPS)
    def _():
        total = None
        for q in range(4):
            left = wide_pair(gs, sc[2 * q], sc[2 * q + 1])
            right = jnp.concatenate([downs[2 * q][0], downs[2 * q + 1][0]], axis=1)
            term = dot_nt(left, right)
            total = term if total is None else total + term
        buf[...] = total
        hgain_grad[step] = jnp.zeros((1, WIDE), f32)
        hshift_grad[step] = jnp.zeros((1, WIDE), f32)

        def body(r):
            h = hidden[0, r, :].astype(f32)
            half = gelu_parts(h)
            slope = half + h * (jnp.exp(-0.5 * h * h) * (1.0 / math.sqrt(2.0 * math.pi)))
            hat = (h * half - mean_in[r, 0:1]) * rstd_in[r, 0:1]
            dy = buf[r, :]
            dx = dy * hgain[step]
            both = dy * hat
            hgain_grad[step] += jnp.sum(both, axis=0, keepdims=True)
            hshift_grad[step] += jnp.sum(dy, axis=0, keepdims=True)
            first[r, :] += jnp.sum(dx, axis=1, keepdims=True) * (1.0 / FF)
            cross[r, :] += jnp.sum(dx * hat, axis=1, keepdims=True) * (1.0 / FF)
            dxs[step, r, :] = dx
            hats[step, r, :] = hat
            slopes[step, r, :] = slope.astype(bf16)

        row_loop(tokens, 32, body)

    @pl.when(step >= GROUPS)
    def _():
        z = step - GROUPS

        def body(r):
            inner = dxs[z, r, :] - first[r, 0:1] - hats[z, r, :] * cross[r, 0:1]
            dact = rstd_in[r, 0:1] * inner
            dhid[0, r, :] = (slopes[z, r, :].astype(f32) * dact).astype(bf16)

        row_loop(tokens, 64, body)
        for q in range(4):
            right = jnp.concatenate([ups[2 * q][0], ups[2 * q + 1][0]], axis=0)
            total = dot_nt(dhid[0], right)
            for part in range(2):
                t = sc[2 * q + part]
                value = total[:, part * LANES : (part + 1) * LANES]

                @pl.when(z == 0)
                def _(t=t, value=value):
                    acc[t] = value

                @pl.when(z > 0)
                def _(t=t, value=value):
                    acc[t] += value

    @pl.when(step == 2 * GROUPS - 1)
    def _():
        gain_grad[...] = jnp.zeros_like(gain_grad)
        shift_grad[...] = jnp.zeros_like(shift_grad)

        def body(r):
            blocks = [low[b, r, :].astype(f32) for b in range(BLOCKS)]
            mean, rstd = row_stats(blocks, D)
            hat = [(v - mean) * rstd for v in blocks]
            dy = [acc[b, r, :] for b in range(BLOCKS)]
            dv = norm_back(dy, hat, rstd, [gain[b] for b in range(BLOCKS)], D)
            for b in range(BLOCKS):
                gain_grad[b] += jnp.sum(dy[b] * hat[b], axis=0, keepdims=True)
                shift_grad[b] += jnp.sum(dy[b], axis=0, keepdims=True)
                grad_out[b, r, :] = grad[b, r, :] + dv[b]
                gs[b, r, :] = (hat[b] * gain[b] + shift[b]).astype(bf16)

        row_loop(tokens, ROWS, body)
        for b in range(BLOCKS):
            normed_turned[b] = flip(gs[b])


def ffn_back_call(sc, grad, hidden, mean, rstd, low, gain, shift, hgain, downs, ups):
    tokens = grad.shape[1]
    turned = (BLOCKS, LANES, tokens)
    first_half = lambda k, sc: (jnp.minimum(k, GROUPS - 1), 0, 0)
    second_half = lambda k, sc: (jnp.maximum(k - GROUPS, 0), 0, 0)
    big = (GROUPS, tokens, WIDE)
    return pl.pallas_call(
        ffn_back_kernel,
        out_shape=[
            jax.ShapeDtypeStruct(big, bf16),
            jax.ShapeDtypeStruct(turned, bf16),
            jax.ShapeDtypeStruct(turned, bf16),
            jax.ShapeDtypeStruct(grad.shape, f32),
            jax.ShapeDtypeStruct((GROUPS, 1, WIDE), f32),
            jax.ShapeDtypeStruct((GROUPS, 1, WIDE), f32),
            jax.ShapeDtypeStruct((BLOCKS, 1, LANES), f32),
            jax.ShapeDtypeStruct((BLOCKS, 1, LANES), f32),
        ],
        grid_spec=pltpu.PrefetchScalarGridSpec(
            num_scalar_prefetch=1,
            grid=(2 * GROUPS,),
            in_specs=[
                whole(grad.shape),
                pl.BlockSpec((1, tokens, WIDE), first_half),
            ]
            + [whole(v.shape) for v in (mean, rstd, low, gain, shift, hgain)]
            + [pl.BlockSpec((1, WIDE, LANES), first_half)] * 8
            + [pl.BlockSpec((1, LANES, WIDE), second_half)] * 8,
            out_specs=[
                pl.BlockSpec((1, tokens, WIDE), second_half),
                whole(turned),
                whole(turned),
                whole(grad.shape),
                whole((GROUPS, 1, WIDE)),
                whole((GROUPS, 1, WIDE)),
                whole((BLOCKS, 1, LANES)),
                whole((BLOCKS, 1, LANES)),
            ],
            scratch_shapes=[
                pltpu.VMEM((BLOCKS, tokens, LANES), bf16),
                pltpu.VMEM(big, f32),
                pltpu.VMEM(big, f32),
                pltpu.VMEM(big, bf16),
                pltpu.VMEM((tokens, WIDE), f32),
                pltpu.VMEM((tokens, LANES), f32),
                pltpu.VMEM((tokens, LANES), f32),
                pltpu.VMEM((BLOCKS, tokens, LANES), f32),
            ],
        ),
        compiler_params=params(),
        cost_estimate=cost(4 * tokens * D * FF, 32 * 2**20, 2 * tokens * FF),
        name="ffn_back",
    )(sc, grad, hidden, mean, rstd, low, gain, shift, hgain, *downs, *ups)


def proj_back_kernel(sc, grad, gain, shift, *refs):
    att, weights, outs = refs[:8], refs[8:16], refs[16:24]
    grad_turned, normed, gain_grad, shift_grad, gs, dm = refs[24:]
    tokens = grad.shape[1]
    for b in range(BLOCKS):
        gs[b] = grad[b].astype(bf16)
        grad_turned[b] = flip(gs[b])
    for j in range(GROUPS):
        total = None
        for q in range(4):
            left = wide_pair(gs, sc[2 * q], sc[2 * q + 1])
            right = jnp.concatenate([weights[2 * q][j], weights[2 * q + 1][j]], axis=1)
            term = dot_nt(left, right)
            total = term if total is None else total + term
        dm[2 * j] = total[:, :LANES]
        dm[2 * j + 1] = total[:, LANES:]
    gain_grad[...] = jnp.zeros_like(gain_grad)
    shift_grad[...] = jnp.zeros_like(shift_grad)

    def body(r):
        at = [sc[8 + i] for i in range(BLOCKS)]
        blocks = [a[r, :].astype(f32) for a in att]
        mean, rstd = row_stats(blocks, D)
        hat = [(v - mean) * rstd for v in blocks]
        dy = [dm[t, r, :] for t in at]
        dv = norm_back(dy, hat, rstd, [gain[t] for t in at], D)
        for i in range(BLOCKS):
            t = at[i]
            gain_grad[t] += jnp.sum(dy[i] * hat[i], axis=0, keepdims=True)
            shift_grad[t] += jnp.sum(dy[i], axis=0, keepdims=True)
            outs[i][r, :] = dv[i].astype(bf16)
            normed[t, r, :] = (hat[i] * gain[t] + shift[t]).astype(bf16)

    row_loop(tokens, ROWS, body)


def proj_back_call(sc, grad, gain, shift, att, pieces):
    tokens = grad.shape[1]
    return pl.pallas_call(
        proj_back_kernel,
        out_shape=[jax.ShapeDtypeStruct((tokens, LANES), bf16)] * 8
        + [
            jax.ShapeDtypeStruct((BLOCKS, LANES, tokens), bf16),
            jax.ShapeDtypeStruct((BLOCKS, tokens, LANES), bf16),
            jax.ShapeDtypeStruct((BLOCKS, 1, LANES), f32),
            jax.ShapeDtypeStruct((BLOCKS, 1, LANES), f32),
        ],
        grid_spec=pltpu.PrefetchScalarGridSpec(
            num_scalar_prefetch=1,
            grid=(),
            in_specs=[pl.BlockSpec(memory_space=pltpu.VMEM)] * 19,
            out_specs=[pl.BlockSpec(memory_space=pltpu.VMEM)] * 12,
            scratch_shapes=[
                pltpu.VMEM((BLOCKS, tokens, LANES), bf16),
                pltpu.VMEM((BLOCKS, tokens, LANES), f32),
            ],
        ),
        compiler_params=params(),
        cost_estimate=cost(2 * tokens * D * D, 9 * 2**20),
        name="projection_back",
    )(sc, grad, gain, shift, *att, *pieces)


def attn_back_kernel(need, aux, one, *refs):
    n = (len(refs) - 11) // 4
    qkv, att, datt, lse = refs[:n], refs[n : 2 * n], refs[2 * n : 3 * n], refs[3 * n]
    outs = refs[3 * n + 1 : 4 * n + 1]
    kx, kt, qs, vs, ds, delta, dq, dkey, dval, dkv = refs[4 * n + 1 :]
    for r in range(n):
        kx[r] = jnp.concatenate([qkv[r][1], aux[r]], axis=1)
        kt[r] = flip(qkv[r][1])
        qs[r] = (qkv[r][0].astype(f32) * (1.0 / math.sqrt(DH))).astype(bf16)
        vs[r] = qkv[r][2]
        ds[r] = datt[r][...]
        both = jnp.transpose(att[r][...].astype(f32) * datt[r][...].astype(f32), (1, 0))
        delta[r, 0:1] = jnp.sum(both[:DH], axis=0, keepdims=True)
        delta[r, 1:2] = jnp.sum(both[DH:], axis=0, keepdims=True)
    dq[...] = jnp.zeros_like(dq)

    def each_key(j, carry):
        dkey[...] = jnp.zeros_like(dkey)
        dval[...] = jnp.zeros_like(dval)

        def each_query(i, inner):
            @pl.when(need[i * n + j] == 1)
            def _():
                for h in range(2):
                    query = head_lanes(qs[i], h)
                    out = head_lanes(ds[i], h)
                    scores = dot_nt(kx[j], jnp.concatenate([query, one[...]], axis=1))
                    probs = jnp.exp(scores - lse[i, h : h + 1])
                    dprobs = dot_nt(vs[j], out)
                    dscores = (probs * (dprobs - delta[i, h : h + 1])).astype(bf16)
                    dval[...] += dot(probs.astype(bf16), out)
                    dkey[...] += dot(dscores, query)
                    rows = slice(h * DH, (h + 1) * DH)
                    dq[i, rows] += dot(kt[j, rows], dscores)

            return inner

        lax.fori_loop(0, n, each_query, 0)
        dkv[j, 0] = dkey[...].astype(bf16)
        dkv[j, 1] = dval[...].astype(bf16)
        return carry

    lax.fori_loop(0, n, each_key, 0)
    for r in range(n):
        outs[r][0] = (jnp.transpose(dq[r], (1, 0)) * (1.0 / math.sqrt(DH))).astype(bf16)
        outs[r][1] = dkv[r, 0]
        outs[r][2] = dkv[r, 1]


def attn_back_call(need, aux, one, parts, att, datt, lse):
    n = len(parts)
    tokens = aux.shape[1]
    total = n * tokens
    block = (n, tokens, LANES)
    return pl.pallas_call(
        attn_back_kernel,
        out_shape=[jax.ShapeDtypeStruct((3, tokens, LANES), bf16)] * n,
        grid_spec=pltpu.PrefetchScalarGridSpec(
            num_scalar_prefetch=1,
            grid=(),
            in_specs=[pl.BlockSpec(memory_space=pltpu.VMEM)] * (3 + 3 * n),
            out_specs=[pl.BlockSpec(memory_space=pltpu.VMEM)] * n,
            scratch_shapes=[
                pltpu.VMEM((n, tokens, 2 * LANES), bf16),
                pltpu.VMEM((n, LANES, tokens), bf16),
                pltpu.VMEM(block, bf16),
                pltpu.VMEM(block, bf16),
                pltpu.VMEM(block, bf16),
                pltpu.VMEM((n, 8, tokens), f32),
                pltpu.VMEM((n, LANES, tokens), f32),
                pltpu.VMEM((tokens, LANES), f32),
                pltpu.VMEM((tokens, LANES), f32),
                pltpu.VMEM((n, 2, tokens, LANES), bf16),
            ],
        ),
        compiler_params=params(),
        cost_estimate=cost(5 * total * total * 512, 8 * 2**20, 2 * total * total),
        name="attention_back",
    )(need, aux, one, *parts, *att, *datt, lse)


def qkv_back_kernel(sc, grad, low, gain, shift, *refs):
    dqkv, weights = refs[:8], refs[8:16]
    grad_out, normed_turned, gain_grad, shift_grad, acc, ns = refs[16:]
    tokens = grad.shape[1]
    for q in range(4):
        total = None
        for k in range(GROUPS):
            z = lax.rem(sc[16] + k, GROUPS)
            for c in range(3):
                left = jnp.concatenate([dqkv[2 * k][c], dqkv[2 * k + 1][c]], axis=1)
                right = jnp.concatenate(
                    [weights[2 * q][z, c], weights[2 * q + 1][z, c]], axis=0
                )
                term = dot_nt(left, right)
                total = term if total is None else total + term
        acc[sc[2 * q]] = total[:, :LANES]
        acc[sc[2 * q + 1]] = total[:, LANES:]
    gain_grad[...] = jnp.zeros_like(gain_grad)
    shift_grad[...] = jnp.zeros_like(shift_grad)

    def body(r):
        blocks = [low[b, r, :].astype(f32) for b in range(BLOCKS)]
        mean, rstd = row_stats(blocks, D)
        hat = [(v - mean) * rstd for v in blocks]
        dy = [acc[b, r, :] for b in range(BLOCKS)]
        dv = norm_back(dy, hat, rstd, [gain[b] for b in range(BLOCKS)], D)
        for b in range(BLOCKS):
            gain_grad[b] += jnp.sum(dy[b] * hat[b], axis=0, keepdims=True)
            shift_grad[b] += jnp.sum(dy[b], axis=0, keepdims=True)
            grad_out[b, r, :] = grad[b, r, :] + dv[b]
            ns[b, r, :] = (hat[b] * gain[b] + shift[b]).astype(bf16)

    row_loop(tokens, ROWS, body)
    for b in range(BLOCKS):
        normed_turned[b] = flip(ns[b])


def qkv_back_call(sc, grad, low, gain, shift, dqkv, pieces):
    tokens = grad.shape[1]
    return pl.pallas_call(
        qkv_back_kernel,
        out_shape=[
            jax.ShapeDtypeStruct(grad.shape, f32),
            jax.ShapeDtypeStruct((BLOCKS, LANES, tokens), bf16),
            jax.ShapeDtypeStruct((BLOCKS, 1, LANES), f32),
            jax.ShapeDtypeStruct((BLOCKS, 1, LANES), f32),
        ],
        grid_spec=pltpu.PrefetchScalarGridSpec(
            num_scalar_prefetch=1,
            grid=(),
            in_specs=[pl.BlockSpec(memory_space=pltpu.VMEM)] * 20,
            out_specs=[pl.BlockSpec(memory_space=pltpu.VMEM)] * 4,
            scratch_shapes=[
                pltpu.VMEM((BLOCKS, tokens, LANES), f32),
                pltpu.VMEM((BLOCKS, tokens, LANES), bf16),
            ],
        ),
        compiler_params=params(),
        cost_estimate=cost(6 * tokens * D * D, 18 * 2**20),
        name="qkv_back",
    )(sc, grad, low, gain, shift, *dqkv, *pieces)


def weight_grad_kernel(kind, added, sc, turned, *refs):
    count = {"wide": 1, "pair": 1, "qkv": 8}[kind]
    right_refs, rest = refs[:count], refs[count:]
    left = jnp.concatenate([turned[sc[m]] for m in range(4)], axis=0)
    extra = rest[0] if added else None
    outs = rest[1:] if added else rest

    def put(spot, value):
        for m in range(4):
            part = value[m * LANES : (m + 1) * LANES]
            if added:
                part = part + extra[(m,) + spot].astype(f32)
                outs[m // 2][(m % 2,) + spot] = part.astype(bf16)
            else:
                outs[0][(m,) + spot] = part.astype(bf16)

    if kind == "wide":
        put((0,), dot(left, right_refs[0][0]))
    elif kind == "pair":
        for z in range(GROUPS):
            put((z,), dot(left, wide_pair(right_refs[0], 2 * z, 2 * z + 1)))
    else:
        for k in range(GROUPS):
            z = lax.rem(sc[4] + k, GROUPS)
            for c in range(3):
                right = jnp.concatenate(
                    [right_refs[2 * k][c], right_refs[2 * k + 1][c]], axis=1
                )
                put((z, c), dot(left, right))


def weight_grad_call(kind, sc, turned, rights, extra=None):
    tokens = turned.shape[2]
    inner = {
        "wide": (GROUPS, LANES, WIDE),
        "pair": (GROUPS, LANES, 256),
        "qkv": (GROUPS, 3, LANES, 256),
    }[kind]
    added = extra is not None
    if kind == "wide":
        grid = (GROUPS,)
        right_specs = [pl.BlockSpec((1, tokens, WIDE), lambda k, sc: (k, 0, 0))]
        piece = lambda m: pl.BlockSpec((m, 1, LANES, WIDE), lambda k, sc: (0, k, 0, 0))
    else:
        grid = (1,)
        right_specs = [whole(v.shape) for v in rights]
        piece = lambda m: whole((m,) + inner)
    outs = [2, 2] if added else [4]
    width = math.prod(inner) // LANES
    return pl.pallas_call(
        lambda *refs: weight_grad_kernel(kind, added, *refs),
        out_shape=[jax.ShapeDtypeStruct((m,) + inner, bf16) for m in outs],
        grid_spec=pltpu.PrefetchScalarGridSpec(
            num_scalar_prefetch=1,
            grid=grid,
            in_specs=[whole(turned.shape)] + right_specs + ([piece(4)] if added else []),
            out_specs=[piece(m) for m in outs],
        ),
        compiler_params=params(),
        cost_estimate=cost(tokens * D * width, 2 * D * width),
        name="weight_grad_" + kind,
    )(sc, turned, *rights, *([extra] if added else []))


class Net:
    def __init__(self, n_dp, n_head):
        self.n_dp, self.n = n_dp, n_head
        self.own = lax.axis_index("dp")
        self.z = lax.axis_index("head")
        self.lo = self.own % n_head
        self.fast = n_dp == 8 and n_head == 4
        core_zero = [2, 4]
        self.one_way = [(i, i ^ core_zero[i % 2]) for i in range(n_dp)]
        self.other_way = [(i, i ^ core_zero[1 - i % 2]) for i in range(n_dp)]
        self.core = [(i, i ^ 1) for i in range(n_dp)]
        if self.fast:
            core = self.own % 2
            step = jnp.where(core == 0, 2, 4).astype(jnp.int32)
            mine = [jnp.int32(0), step, 6 - step, jnp.int32(6)]
            theirs = [jnp.int32(0), 6 - step, step, jnp.int32(6)]
            self.even = jnp.stack([jnp.bitwise_xor(self.own, v) for v in mine])
            self.odd = jnp.stack([jnp.bitwise_xor(self.own, v ^ 1) for v in theirs])
            self.rel = self.lo
            units = BLOCKS // n_head
            self.features = jnp.stack(
                [units * ((self.lo + i // units) % n_head) + i % units for i in range(BLOCKS)]
            )
        else:
            self.even = jnp.arange(4, dtype=jnp.int32)
            self.odd = jnp.arange(4, 8, dtype=jnp.int32)
            self.rel = jnp.int32(0)
            self.features = jnp.arange(BLOCKS, dtype=jnp.int32)
        self.even = self.even.astype(jnp.int32)
        self.odd = self.odd.astype(jnp.int32)
        self.table = jnp.concatenate([self.even, self.odd])
        self.scalars = jnp.concatenate(
            [self.table, self.features.astype(jnp.int32), self.rel.astype(jnp.int32)[None]]
        )

    def shift(self, value, k):
        n = self.n
        if k % n == 0:
            return value
        pairs = [(i, (i // n) * n + (i + k) % n) for i in range(self.n_dp)]
        return lax.ppermute(value, "dp", pairs)

    def gather(self, shard, kind):
        if self.fast:
            start = lax.all_gather(shard, "head")
            near = lax.ppermute(start, "dp", self.one_way)
            half = [start, near] + [lax.ppermute(v, "dp", self.other_way) for v in (start, near)]
            return half + [lax.ppermute(v, "dp", self.core) for v in half]
        tall, flat = {"qkv": (1, 2), "up": (0, 1), "out": (1, 0), "down": (1, 0)}[kind]
        full = lax.all_gather(shard, "head", axis=flat, tiled=True)
        full = lax.all_gather(full, "dp", axis=tall, tiled=True)
        if kind == "qkv":
            full = full.reshape(3, BLOCKS, LANES, GROUPS, 256).transpose(1, 3, 0, 2, 4)
        elif kind == "up":
            full = full.reshape(BLOCKS, LANES, GROUPS, WIDE).transpose(0, 2, 1, 3)
        else:
            full = full.reshape(GROUPS, -1, BLOCKS, LANES).transpose(2, 0, 1, 3)
        return [full[i] for i in range(BLOCKS)]

    def reduce(self, kind, turned, rights):
        shape = "qkv" if kind == "qkv" else ("pair" if kind == "out" else "wide")
        rel = self.rel.astype(jnp.int32)[None]
        odd_table = jnp.concatenate([self.odd, rel])
        even_table = jnp.concatenate([self.even, rel])
        (odd,) = weight_grad_call(shape, odd_table, turned, rights)
        if self.fast:
            other = lax.ppermute(odd, "dp", self.core)
            keep, send = weight_grad_call(shape, even_table, turned, rights, other)
            pair = lax.ppermute(send, "dp", self.other_way)
            mine = (keep[0].astype(f32) + pair[0].astype(f32)).astype(bf16)
            sent = (keep[1].astype(f32) + pair[1].astype(f32)).astype(bf16)
            last = lax.ppermute(sent, "dp", self.one_way)
            block = (mine.astype(f32) + last.astype(f32)).astype(bf16)
            block = lax.psum_scatter(block, "head", scatter_dimension=0, tiled=False)
            block = block.astype(f32)
            return block.T if kind in ("out", "down") else block
        (even,) = weight_grad_call(shape, even_table, turned, rights)
        full = jnp.concatenate([even, odd], axis=0)
        if kind == "qkv":
            full = full.transpose(2, 0, 3, 1, 4).reshape(3, D, D)
            tall, flat = 1, 2
        elif kind == "up":
            full = full.transpose(0, 2, 1, 3).reshape(D, FF)
            tall, flat = 0, 1
        else:
            full = full.transpose(1, 3, 0, 2).reshape(-1, D)
            tall, flat = 1, 0
        full = lax.psum_scatter(full, "dp", scatter_dimension=tall, tiled=True)
        return lax.psum_scatter(full, "head", scatter_dimension=flat, tiled=True).astype(f32)

    def to_heads(self, blocks):
        n, units = self.n, BLOCKS // self.n
        if not self.fast:
            stacked = jnp.stack(blocks)
            blocks = [
                lax.dynamic_index_in_dim(stacked, units * ((self.lo + k) % n) + u, 0, False)
                for k in range(n)
                for u in range(units)
            ]
        return [[self.shift(blocks[k * units + u], k) for k in range(n)] for u in range(units)]

    def to_tokens(self, units):
        n, count = self.n, BLOCKS // self.n
        blocks = [self.shift(units[u][k], -k) for k in range(n) for u in range(count)]
        if not self.fast:
            stacked = jnp.stack(blocks)
            order = [count * ((i // count - self.lo) % n) + i % count for i in range(BLOCKS)]
            blocks = [lax.dynamic_index_in_dim(stacked, v, 0, False) for v in order]
        return blocks

    def turn(self, k):
        n = self.n
        pairs = []
        for hi in range(self.n_dp // n):
            for lo in range(n):
                for z in range(n):
                    pairs.append(((hi * n + lo) * n + z, (hi * n + (z + k) % n) * n + lo))
        return pairs

    def rows_in(self, array):
        n = self.n
        tokens = array.shape[0] // n
        low = array.astype(bf16).reshape(n, tokens, array.shape[1])
        got = []
        for k in range(n):
            piece = lax.dynamic_index_in_dim(low, (self.z + k) % n, 0, False)
            got.append(lax.ppermute(piece, ("dp", "head"), self.turn(k)))
        stacked = jnp.stack(got)
        order = (self.lo - jnp.arange(n)) % n
        stacked = jnp.take(stacked, order, axis=0)
        units = BLOCKS // n
        stacked = stacked.reshape(n, tokens, units, LANES).transpose(0, 2, 1, 3)
        return stacked.reshape(BLOCKS, tokens, LANES)

    def rows_out(self, array):
        n = self.n
        units = BLOCKS // n
        tokens = array.shape[1]
        low = array.astype(bf16).reshape(n, units, tokens, LANES)
        got = []
        for k in range(n):
            piece = lax.dynamic_index_in_dim(low, (self.lo - k) % n, 0, False)
            back = [(b, a) for a, b in self.turn(k)]
            got.append(lax.ppermute(piece, ("dp", "head"), back))
        stacked = jnp.stack(got)
        order = (jnp.arange(n) - self.z) % n
        stacked = jnp.take(stacked, order, axis=0)
        return stacked.transpose(0, 2, 1, 3).reshape(n * tokens, units * LANES).astype(f32)


def local(
    n_dp,
    n_head,
    stream_in,
    qkv_weight,
    out_weight,
    up_weight,
    down_weight,
    norm_gains,
    norm_shifts,
    hidden_gains,
    hidden_shifts,
    buckets,
    valid_mask,
    cotangent,
):
    net = Net(n_dp, n_head)
    n = n_head
    layers = qkv_weight.shape[0]
    tokens = LONG // n
    units = BLOCKS // n

    gathered = []
    stream_low = net.rows_in(stream_in)
    for l in range(layers):
        gathered.append(
            {
                "qkv": net.gather(qkv_weight[l], "qkv"),
                "out": net.gather(out_weight[l], "out"),
                "up": net.gather(up_weight[l], "up"),
                "down": net.gather(down_weight[l], "down"),
            }
        )
    vectors = [
        v.reshape(layers, -1) for v in (norm_gains, norm_shifts, hidden_gains, hidden_shifts)
    ]
    packed = lax.all_gather(jnp.concatenate(vectors, axis=1), "head")
    third = 3 * (D // n)
    wide = FF // n

    def unpack(l):
        part = packed[:, l]
        norm = lambda v: v.reshape(n, 3, -1).transpose(1, 0, 2).reshape(3, BLOCKS, 1, LANES)
        hid = lambda v: v.reshape(GROUPS, 1, WIDE)
        return (
            norm(part[:, :third]),
            norm(part[:, third : 2 * third]),
            hid(part[:, 2 * third : 2 * third + wide]),
            hid(part[:, 2 * third + wide :]),
        )

    flags = jnp.concatenate([valid_mask, buckets])
    flags = lax.ppermute(flags, ("dp", "head"), net.turn(0))
    slab_mask = flags[:LONG].reshape(n, tokens)
    bucket = flags[LONG]
    rel_blocks = (net.lo - jnp.arange(n)) % n
    rel_mask = jnp.take(slab_mask, rel_blocks, axis=0)
    lane = jnp.arange(LANES)[None, None, :] == 0
    aux = jnp.where((rel_mask[:, :, None] == 0) & lane, MASKED, 0.0).astype(bf16)
    one = jnp.broadcast_to((jnp.arange(LANES)[None, :] == 0), (tokens, LANES)).astype(bf16)
    sequence = jnp.where(bucket == 1, 0, (rel_blocks * tokens) // SHORT)
    alive = jnp.sum(rel_mask, axis=1) > 0
    need = ((sequence[:, None] == sequence[None, :]) & alive[None, :]).astype(jnp.int32)
    need = need.reshape(n * n)
    valid = lax.dynamic_index_in_dim(slab_mask, net.lo, 0, False).astype(f32)[:, None]

    stream = stream_low.astype(f32)
    low = stream_low
    kept = []
    usage = []
    for l in range(layers):
        w = gathered[l]
        gains, shifts, hgain, hshift = unpack(l)
        blocks = qkv_call(net.scalars[jnp.array([0, 1, 2, 3, 4, 5, 6, 7, 16])], low, gains[0], shifts[0], w["qkv"])
        parts = net.to_heads(blocks)
        att, sums = [], []
        for u in range(units):
            out, lse = attn_call(need, aux, one, parts[u])
            att.append(out)
            sums.append(lse)
        rows = net.to_tokens(att)
        mid, use_branch = proj_call(
            net.scalars, valid, stream, gains[1], shifts[1], rows, w["out"]
        )
        hidden, normed, low_mid, mean, rstd = up_call(
            net.scalars, mid, gains[2], shifts[2], hgain, hshift, w["up"]
        )
        stream, next_low, use_rest = down_call(net.scalars, valid, mid, normed, w["down"])
        usage += [jnp.sum(use_branch[0]), jnp.sum(use_rest[0]), jnp.sum(use_rest[1])]
        kept.append((low, parts, att, sums, rows, hidden, normed, low_mid, mean, rstd))
        low = next_low

    stream_out = net.rows_out(stream)
    grad = net.rows_in(cotangent).astype(f32)
    weight_grads = [None] * layers
    vector_grads = [None] * layers
    for l in reversed(range(layers)):
        w = gathered[l]
        gains, shifts, hgain, hshift = unpack(l)
        low, parts, att, sums, rows, hidden, normed, low_mid, mean, rstd = kept[l]
        (dhid, grad_turned, ffn_turned, grad, hg, hs, g2, s2) = ffn_back_call(
            net.scalars, grad, hidden, mean, rstd, low_mid, gains[2], shifts[2], hgain,
            w["down"], w["up"],
        )
        down_grad = net.reduce("down", grad_turned, [normed])
        up_grad = net.reduce("up", ffn_turned, [dhid])
        res = proj_back_call(net.scalars, grad, gains[1], shifts[1], rows, w["out"])
        dmid, (turned, normed_mid, g1, s1) = res[:8], res[8:]
        datt = net.to_heads(dmid)
        dparts = [
            attn_back_call(need, aux, one, parts[u], att[u], datt[u], sums[u])
            for u in range(units)
        ]
        dqkv = net.to_tokens(dparts)
        out_grad = net.reduce("out", turned, [normed_mid])
        grad, in_turned, g0, s0 = qkv_back_call(
            net.scalars, grad, low, gains[0], shifts[0], dqkv, w["qkv"]
        )
        qkv_grad = net.reduce("qkv", in_turned, dqkv)
        weight_grads[l] = (qkv_grad, out_grad, up_grad, down_grad)
        vector_grads[l] = jnp.concatenate(
            [v.reshape(-1) for v in (g0, g1, g2, s0, s1, s2, hg, hs)]
        )
    stream_grad = net.rows_out(grad)
    tail = jnp.stack(usage + [jnp.sum(valid) * D])
    summed = lax.psum(jnp.concatenate(vector_grads + [tail]), ("dp", "head"))
    usage_rms = jnp.sqrt(summed[-1 - 3 * layers : -1] / summed[-1]).reshape(layers, 3)
    rest = summed[: -1 - 3 * layers].reshape(layers, -1)
    cut = lambda v: lax.dynamic_slice_in_dim(
        v, net.z * (v.shape[-1] // n), v.shape[-1] // n, v.ndim - 1
    )
    gains_grad = cut(rest[:, : 3 * D].reshape(layers, 3, D))
    shifts_grad = cut(rest[:, 3 * D : 6 * D].reshape(layers, 3, D))
    hidden_gains_grad = cut(rest[:, 6 * D : 6 * D + FF])
    hidden_shifts_grad = cut(rest[:, 6 * D + FF :])
    stacked = [jnp.stack([weight_grads[l][k] for l in range(layers)]) for k in range(4)]
    return (
        stream_out,
        stream_grad,
        stacked[0],
        stacked[1],
        stacked[2],
        stacked[3],
        gains_grad,
        shifts_grad,
        hidden_gains_grad,
        hidden_shifts_grad,
        usage_rms,
    )


def solution(mesh):
    n_dp, n_head = mesh.shape["dp"], mesh.shape["head"]

    def run(*args):
        return local(n_dp, n_head, *args)

    return jax.shard_map(
        run,
        mesh=mesh,
        in_specs=(
            P("dp", "head"),
            P(None, None, "dp", "head"),
            P(None, "head", "dp"),
            P(None, "dp", "head"),
            P(None, "head", "dp"),
            P(None, None, "head"),
            P(None, None, "head"),
            P(None, "head"),
            P(None, "head"),
            P("dp"),
            P("dp"),
            P("dp", "head"),
        ),
        out_specs=(
            P("dp", "head"),
            P("dp", "head"),
            P(None, None, "dp", "head"),
            P(None, "head", "dp"),
            P(None, "dp", "head"),
            P(None, "head", "dp"),
            P(None, None, "head"),
            P(None, None, "head"),
            P(None, "head"),
            P(None, "head"),
            P(),
        ),
        check_vma=False,
    )
```

```python
import functools
import math

import jax
import jax.numpy as jnp
from jax import lax
from jax.experimental import pallas as pl
from jax.experimental.pallas import tpu as pltpu
from jax.sharding import PartitionSpec as P

D = 1024
FF = 4096
LONG = 2048
SHORT = 512
DH = 64
LANES = 128
BLOCKS = D // LANES
GROUPS = 4
WIDE = FF // GROUPS
HEADS = D // GROUPS
NARROW = 4 * HEADS
BROAD = 2 * WIDE
EPS = 1e-05
MASKED = -1000000000.0
ROWS = 64
VMEM_BYTES = 60 * 1024 * 1024
MESH = pl.DeviceIdType.MESH

f32 = jnp.float32
bf16 = jnp.bfloat16


def dot(a, b):
    return jnp.dot(a, b, preferred_element_type=f32)


def dot_nt(a, b):
    return lax.dot_general(a, b, (((1,), (1,)), ((), ())), preferred_element_type=f32)


def flip(a):
    return jnp.transpose(a.astype(f32), (1, 0)).astype(a.dtype)


def row_loop(total, step, body):
    def advance(i, carry):
        body(pl.ds(pl.multiple_of(i * step, step), step))
        return carry

    lax.fori_loop(0, total // step, advance, 0)


def sum_lanes(value):
    return jnp.sum(value, axis=1, keepdims=True)


def fold_lanes(value):
    total = value[:, :LANES]
    for i in range(1, value.shape[1] // LANES):
        total = total + value[:, i * LANES : (i + 1) * LANES]
    return total


def fold_rows(value):
    total = value[:8]
    for i in range(1, value.shape[0] // 8):
        total = total + value[i * 8 : (i + 1) * 8]
    return total


def row_stats(value):
    mean = sum_lanes(value) / D
    centred = value - mean
    rstd = lax.rsqrt(sum_lanes(centred * centred) / D + EPS)
    return centred * rstd, rstd


def norm_back(dy, hat, rstd, gain):
    dx = dy * gain
    first = sum_lanes(dx) / D
    cross = sum_lanes(dx * hat) / D
    return rstd * (dx - first - hat * cross)


class Vectors:
    def __init__(self, n, layer, ref):
        self.n, self.ref = n, ref
        self.few, self.many = BLOCKS // n, 4 * BLOCKS // n
        self.at = layer * (6 * self.few + 2 * self.many)

    def rows(self, z, first, count):
        return [self.ref[z, first + p : first + p + 1, :] for p in range(count)]

    def norm(self, kind, which):
        first = self.at + (3 * kind + which) * self.few
        parts = [v for z in range(self.n) for v in self.rows(z, first, self.few)]
        return jnp.concatenate(parts, axis=1)

    def hidden(self, kind, group):
        first = self.at + 6 * self.few + kind * self.many
        share = self.n // GROUPS
        parts = [v for i in range(share) for v in self.rows(group * share + i, first, self.many)]
        return jnp.concatenate(parts, axis=1)


def params(**kw):
    return pltpu.CompilerParams(vmem_limit_bytes=VMEM_BYTES, **kw)


def cost(flops, size, trans=0):
    return pl.CostEstimate(flops=int(flops), bytes_accessed=int(size), transcendentals=int(trans))


def whole(shape):
    zeros = (0,) * len(shape)
    return pl.BlockSpec(shape, lambda *_: zeros)


def shape(dims, kind):
    return jax.ShapeDtypeStruct(dims, kind)


VM = pl.BlockSpec(memory_space=pltpu.VMEM)
HB = pl.BlockSpec(memory_space=pl.ANY)
DMA = pltpu.SemaphoreType.DMA


def group_place(n):
    dp = lax.axis_index("dp")
    lo = lax.rem(dp, n)
    return dp - lo, lo


def group_send(n, k, source, target, send_sem, recv_sem):
    base, lo = group_place(n)
    return pltpu.make_async_remote_copy(
        src_ref=source,
        dst_ref=target,
        send_sem=send_sem,
        recv_sem=recv_sem,
        device_id={"dp": base + lax.rem(lo + k + n, n)},
        device_id_type=MESH,
    )


def order_of(n):
    return [k for k in (n // 2, *range(1, n // 2), *range(n // 2 + 1, n)) if k]


def head_columns(n, k):
    _, lo = group_place(n)
    unit = lax.rem(lo + k + n, n) * (BLOCKS // n)
    if n == GROUPS:
        return lax.rem(lo + k + n, n), 0
    return unit // 2, pl.multiple_of(lax.rem(unit, 2) * LANES, LANES)


class Place:
    def __init__(self):
        dp = lax.axis_index("dp")
        self.z = lax.axis_index("head")
        self.lo = lax.rem(dp, GROUPS)
        core = lax.rem(dp, 2)
        bit_x = lax.rem(dp // 2, 2)
        bit_y = lax.rem(dp // 4, 2)
        by_x = dp + 2 - 4 * bit_x
        by_y = dp + 4 - 8 * bit_y
        self.dp, self.core, self.bit_x = dp, core, bit_x
        self.by_x, self.by_y = by_x, by_y
        self.first = by_x * (1 - core) + by_y * core
        self.second = by_y * (1 - core) + by_x * core
        self.both = by_x + by_y - dp
        self.mate = dp + 1 - 2 * core

    def partner(self, way):
        return {"mate": self.mate, "first": self.first, "second": self.second}[way]

    def others(self):
        return [{"head": lax.rem(self.z + k, GROUPS)} for k in range(1, GROUPS)]


def unlike(a, b):
    return jnp.where(a == b, 0, 1)


class Hop:
    aliases = {}

    def __init__(self, array, way):
        self.arrays, self.way = [array], way
        self.outs = [jax.ShapeDtypeStruct(array.shape, array.dtype)]
        self.sems = [DMA((2,))]

    def peers(self, at):
        return [{"dp": at.partner(self.way)}], [], 1

    def copy(self, at, ins, outs, sems):
        return pltpu.make_async_remote_copy(
            src_ref=ins[0],
            dst_ref=outs[0],
            send_sem=sems[0].at[0],
            recv_sem=sems[0].at[1],
            device_id={"dp": at.partner(self.way)},
            device_id_type=MESH,
        )

    def start(self, *args):
        self.copy(*args).start()

    def middle(self, *args):
        pass

    def finish(self, *args):
        self.copy(*args).wait()


class Near:
    aliases = {}

    def __init__(self, array):
        self.arrays = [array]
        self.outs = [jax.ShapeDtypeStruct((GROUPS - 1,) + array.shape[1:], array.dtype)]
        self.sems = [DMA((2, GROUPS - 1))]

    def peers(self, at):
        return at.others(), [], GROUPS - 1

    def copies(self, at, ins, outs, sems):
        return [
            pltpu.make_async_remote_copy(
                src_ref=ins[0].at[k],
                dst_ref=outs[0].at[k - 1],
                send_sem=sems[0].at[0, k - 1],
                recv_sem=sems[0].at[1, k - 1],
                device_id={"head": lax.rem(at.z + k, GROUPS)},
                device_id_type=MESH,
            )
            for k in (2, 1, 3)
        ]

    def start(self, *args):
        for copy in self.copies(*args):
            copy.start()

    def middle(self, *args):
        pass

    def finish(self, *args):
        for copy in self.copies(*args):
            copy.wait()


class Turn:
    aliases = {}

    def __init__(self, array, back):
        self.arrays, self.back = [array], back
        if back:
            tokens, wide = array.shape[0], array.shape[1] // GROUPS
            out = (GROUPS, tokens, wide)
        else:
            tokens, wide = array.shape[1:]
            out = (tokens, GROUPS * wide)
        self.wide = wide
        self.outs = [jax.ShapeDtypeStruct(out, array.dtype)]
        self.sems = [DMA((2, GROUPS)), DMA]

    def many(self, at):
        return [(at.dp - at.lo + t, at.lo) for t in range(GROUPS)]

    def one(self, at):
        return [(at.dp - at.lo + at.z, g) for g in range(GROUPS)]

    def peers(self, at):
        from_ = self.many(at) if self.back else self.one(at)
        return [], from_, GROUPS - 1 + unlike(at.z, at.lo)

    def each(self, op, at, ins, outs, sems):
        targets = self.one(at) if self.back else self.many(at)
        for i, (dp, z) in enumerate(targets):
            if self.back:
                source = ins[0].at[:, pl.ds(i * self.wide, self.wide)]
                target, slot = outs[0].at[at.lo], at.lo
            else:
                source = ins[0].at[i]
                column = pl.multiple_of(at.z * self.wide, self.wide)
                target, slot = outs[0].at[:, pl.ds(column, self.wide)], at.z

            def remote(i=i, dp=dp, z=z, source=source, target=target, slot=slot):
                copy = pltpu.make_async_remote_copy(
                    src_ref=source,
                    dst_ref=target,
                    send_sem=sems[0].at[0, i],
                    recv_sem=sems[0].at[1, slot],
                    device_id={"dp": dp, "head": z},
                    device_id_type=MESH,
                )
                copy.start() if op == "start" else copy.wait_send()

            def inside(source=source, target=target):
                copy = pltpu.make_async_copy(source, target, sems[1])
                copy.start() if op == "start" else copy.wait()

            away = (dp != at.dp) | (z != at.z)
            pl.when(away)(remote)
            pl.when(jnp.logical_not(away))(inside)

    def start(self, *args):
        self.each("start", *args)

    def middle(self, *args):
        pass

    def finish(self, at, ins, outs, sems):
        self.each("wait", at, ins, outs, sems)
        sources = self.many(at) if self.back else self.one(at)
        for slot, (dp, z) in enumerate(sources):

            @pl.when((dp != at.dp) | (z != at.z))
            def _(slot=slot):
                if self.back:
                    spot = outs[0].at[slot]
                else:
                    spot = outs[0].at[:, pl.ds(slot * self.wide, self.wide)]
                pltpu.make_async_remote_copy(
                    src_ref=spot,
                    dst_ref=spot,
                    send_sem=sems[0].at[0, 0],
                    recv_sem=sems[0].at[1, slot],
                    device_id={"dp": at.mate},
                    device_id_type=MESH,
                ).wait_recv()


class Host:
    def __init__(self, n, parts):
        self.n, self.parts = n, parts
        self.at = Place() if parts else None

    def barrier(self, group=True):
        n = self.n
        sem = pltpu.get_barrier_semaphore()
        count = 0
        if group:
            base, lo = group_place(n)
            for k in range(1, n):
                pl.semaphore_signal(
                    sem, inc=1, device_id={"dp": base + lax.rem(lo + k, n)}, device_id_type=MESH
                )
            count = n - 1
        for job, *_ in self.parts:
            plain, pairs, more = job.peers(self.at)
            for device in plain:
                pl.semaphore_signal(sem, inc=1, device_id=device, device_id_type=MESH)
            for dp, z in pairs:

                @pl.when((dp != self.at.dp) | (z != self.at.z))
                def _(dp=dp, z=z):
                    pl.semaphore_signal(
                        sem, inc=1, device_id={"dp": dp, "head": z}, device_id_type=MESH
                    )

            count = count + more
        pl.semaphore_wait(sem, count)

    def start(self):
        for job, *refs in self.parts:
            job.start(self.at, *refs)

    def middle(self):
        for job, *refs in self.parts:
            job.middle(self.at, *refs)

    def finish(self):
        for job, *refs in self.parts:
            job.finish(self.at, *refs)


def plain_call(
    body, n, name, ident, inputs, in_specs, out_shape, out_specs, scratch, flops, jobs, grid=()
):
    return list(
        pl.pallas_call(
            lambda *refs: body(Host(n, []), *refs),
            out_shape=out_shape,
            grid=grid,
            in_specs=in_specs,
            out_specs=out_specs,
            scratch_shapes=scratch,
            compiler_params=params(),
            cost_estimate=cost(flops, 10 * 2**20),
            name=name,
        )(*inputs)
    )


def remote_call(
    body, n, name, ident, inputs, in_specs, out_shape, out_specs, scratch, flops, jobs, grid=()
):
    job_in = [v for job in jobs for v in job.arrays]
    job_out = [v for job in jobs for v in job.outs]
    job_sems = [v for job in jobs for v in job.sems]
    aliases = {}
    i, o = len(inputs), len(out_shape)
    for job in jobs:
        aliases.update({i + a: o + b for a, b in job.aliases.items()})
        i, o = i + len(job.arrays), o + len(job.outs)

    def kernel(*refs):
        refs = list(refs)

        def take(count):
            taken = refs[:count]
            del refs[:count]
            return taken

        own_in, extra_in = take(len(inputs)), take(len(job_in))
        own_out, extra_out = take(len(out_shape)), take(len(job_out))
        own_scratch, extra_sems = take(len(scratch)), take(len(job_sems))
        parts = []
        for job in jobs:
            sizes = (len(job.arrays), len(job.outs), len(job.sems))
            lists = (extra_in, extra_out, extra_sems)
            part = [job]
            for values, size in zip(lists, sizes):
                part.append(values[:size])
                del values[:size]
            parts.append(part)
        body(Host(n, parts), *own_in, *own_out, *own_scratch)

    res = pl.pallas_call(
        kernel,
        out_shape=list(out_shape) + job_out,
        grid=grid,
        in_specs=list(in_specs) + [HB] * len(job_in),
        out_specs=list(out_specs) + [HB] * len(job_out),
        scratch_shapes=list(scratch) + job_sems,
        input_output_aliases=aliases,
        compiler_params=params(collective_id=ident, has_side_effects=True),
        cost_estimate=cost(flops, 10 * 2**20),
        name=name,
    )(*inputs, *job_in)
    return list(res)


def qkv_kernel(layer, host, low, packed, weight, *refs):
    n = host.n
    vectors = Vectors(n, layer, packed)
    gain, shift = vectors.norm(0, 0), vectors.norm(1, 0)
    outs, (xs, wide, send, wsem, ssem, rsem, lsem) = refs[:-7], refs[-7:]
    tokens = low.shape[0]
    units = BLOCKS // n
    width = units * LANES
    steps = order_of(n) + [0]

    def fetch(i):
        group, offset = head_columns(n, steps[i])
        return [
            pltpu.make_async_copy(
                weight.at[:, group, :, pl.ds(c * HEADS + offset, width)],
                wide.at[i % 2, c],
                wsem.at[i % 2, c],
            )
            for c in range(3)
        ]

    for copy in fetch(0):
        copy.start()

    def body(r):
        hat, _ = row_stats(low[r, :].astype(f32))
        xs[r, :] = (hat * gain + shift).astype(bf16)

    row_loop(tokens, ROWS, body)
    host.barrier()
    host.start()
    copies = []
    for i, k in enumerate(steps):
        if i + 1 < n:
            for copy in fetch(i + 1):
                copy.start()
        for c, copy in enumerate(fetch(i)):
            copy.wait()
            value = dot(xs[...], wide[i % 2, c].reshape(D, width)).astype(bf16)
            send[k, c] = value[:, :LANES]
            for u in range(1, units):
                outs[u * n + k][c] = value[:, u * LANES : (u + 1) * LANES]
        if k:
            copy = group_send(n, k, send.at[k], outs[k], ssem.at[k], rsem.at[k])
        else:
            copy = pltpu.make_async_copy(send.at[0], outs[0], lsem)
        copy.start()
        copies.append(copy)
    host.middle()
    for copy in copies:
        copy.wait()
    host.finish()


def qkv_call(n, ident, jobs, layer, low, packed, weight):
    tokens = low.shape[0]
    units = BLOCKS // n
    block = (3, tokens, LANES)
    res = remote_call(
        functools.partial(qkv_kernel, layer), n, "qkv", ident,
        [low, packed, weight], [VM, VM, HB],
        [jax.ShapeDtypeStruct(block, bf16)] * (n * units), [HB] * n + [VM] * (n * (units - 1)),
        [
            pltpu.VMEM((tokens, D), bf16),
            pltpu.VMEM((2, 3, BLOCKS, LANES, units * LANES), bf16),
            pltpu.VMEM((n,) + block, bf16),
            DMA((2, 3)),
            DMA((n,)),
            DMA((n,)),
            DMA,
        ],
        60 * tokens * D * D, jobs,
    )
    return [res[u * n : (u + 1) * n] for u in range(units)], res[n * units :]


def head_lanes(value, head):
    lane = lax.broadcasted_iota(jnp.int32, value.shape, 1)
    keep = (lane < DH) if head == 0 else (lane >= DH)
    return jnp.where(keep, value, jnp.zeros_like(value))


def attn_kernel(n, need, aux, one, *refs):
    qkv, (outs, lse, kx, vt, qs, top, acc) = refs[:n], refs[n:]
    tokens = aux.shape[1]
    for r in range(n):
        kx[r] = jnp.concatenate([qkv[r][1], aux[r]], axis=1)
        turned = flip(qkv[r][2])
        ones = jnp.ones((16, tokens), bf16)
        vt[r, 0] = jnp.concatenate([turned[:DH], ones], axis=0)
        vt[r, 1] = jnp.concatenate([turned[DH:], ones], axis=0)
        qs[r] = (qkv[r][0].astype(f32) * (1.0 / math.sqrt(DH))).astype(bf16)

    def each_query(i, carry):
        query = qs[i]
        extended = [jnp.concatenate([head_lanes(query, h), one[...]], axis=1) for h in range(2)]
        top[...] = jnp.full_like(top, -3e38)
        acc[...] = jnp.zeros_like(acc)

        def each_key(j, inner):
            @pl.when(need[i * n + j] == 1)
            def _():
                for h in range(2):
                    scores = dot_nt(kx[j], extended[h])
                    before = top[h : h + 1]
                    now = jnp.maximum(before, jnp.max(scores, axis=0, keepdims=True))
                    raised = jnp.exp(scores - now).astype(bf16)
                    top[h : h + 1] = now
                    acc[h] = acc[h] * jnp.exp(before - now) + dot(vt[j, h], raised)

            return inner

        lax.fori_loop(0, n, each_key, 0)
        sums = [acc[h][DH : DH + 1] for h in range(2)]
        both = jnp.concatenate([acc[h][:DH] / sums[h] for h in range(2)], axis=0)
        outs[i] = jnp.transpose(both, (1, 0)).astype(bf16)
        for h in range(2):
            lse[i, h : h + 1] = top[h : h + 1] + jnp.log(sums[h])
        return carry

    lax.fori_loop(0, n, each_query, 0)


def unit_call(kernel, n, need, aux, one, arrays, out_shape, scratch, work, name):
    total = n * aux.shape[1]
    return pl.pallas_call(
        lambda *refs: kernel(n, *refs),
        out_shape=out_shape,
        grid_spec=pltpu.PrefetchScalarGridSpec(
            num_scalar_prefetch=1,
            grid=(),
            in_specs=[VM] * (2 + len(arrays)),
            out_specs=[VM] * len(out_shape),
            scratch_shapes=scratch,
        ),
        compiler_params=params(),
        cost_estimate=cost(work * total * total * 512, 8 * 2**20),
        name=name,
    )(need, aux, one, *arrays)


def attn_call(n, need, aux, one, parts):
    tokens = aux.shape[1]
    return unit_call(
        attn_kernel, n, need, aux, one, parts,
        [
            jax.ShapeDtypeStruct((n, tokens, LANES), bf16),
            jax.ShapeDtypeStruct((n, 8, tokens), f32),
        ],
        [
            pltpu.VMEM((n, tokens, 2 * LANES), bf16),
            pltpu.VMEM((n, 2, DH + 16, tokens), bf16),
            pltpu.VMEM((n, tokens, LANES), bf16),
            pltpu.VMEM((8, tokens), f32),
            pltpu.VMEM((2, DH + 16, tokens), f32),
        ],
        12, "attention",
    )


def proj_kernel(layer, host, valid, stream, packed, weight, *refs):
    n = host.n
    vectors = Vectors(n, layer, packed)
    gain, shift = vectors.norm(0, 1), vectors.norm(1, 1)
    tokens = stream.shape[0]
    units = BLOCKS // n
    att, (mid, rows, use, xs, rx, ssem, rsem, lsem) = refs[:units], refs[units:]
    host.barrier()
    copies = [
        group_send(n, -k, att[u].at[k], rx.at[k, u], ssem.at[u, k], rsem.at[u, k])
        for k in order_of(n)
        for u in range(units)
    ]
    copies += [pltpu.make_async_copy(att[u].at[0], rx.at[0, u], lsem.at[u]) for u in range(units)]
    for copy in copies:
        copy.start()
    host.start()
    for copy in copies:
        copy.wait()
    _, lo = group_place(n)
    for k in range(n):
        first = lax.rem(lo + k, n) * (units * LANES)
        for u in range(units):
            at = pl.multiple_of(first + u * LANES, LANES)
            rows[:, pl.ds(at, LANES)] = rx[k, u]

    def body(r):
        hat, _ = row_stats(rows[r, :].astype(f32))
        xs[r, :] = (hat * gain + shift).astype(bf16)

    row_loop(tokens, ROWS, body)
    branch = None
    for g in range(GROUPS):
        term = dot_nt(xs[:, g * HEADS : (g + 1) * HEADS], weight[:, g].reshape(D, HEADS))
        branch = term if branch is None else branch + term
    mid[...] = branch
    use[...] = jnp.zeros_like(use)

    def finish(r):
        part = mid[r, :]
        use[...] += fold_rows(valid[r, :] * part * part)
        mid[r, :] = stream[r, :] + part

    row_loop(tokens, ROWS, finish)
    host.middle()
    host.finish()


def proj_call(n, ident, jobs, layer, valid, stream, packed, weight, att):
    tokens = stream.shape[0]
    units = BLOCKS // n
    flat = whole(stream.shape)
    return remote_call(
        functools.partial(proj_kernel, layer), n, "projection", ident,
        [valid, stream, packed, weight, *att],
        [whole(v.shape) for v in (valid, stream, packed)]
        + [pl.BlockSpec((BLOCKS, GROUPS, LANES, HEADS), lambda i: (0, 0, 0, 3))]
        + [whole(v.shape) for v in att],
        [
            jax.ShapeDtypeStruct(stream.shape, f32),
            jax.ShapeDtypeStruct(stream.shape, bf16),
            jax.ShapeDtypeStruct((8, D), f32),
        ],
        [flat, flat, whole((8, D))],
        [
            pltpu.VMEM((tokens, D), bf16),
            pltpu.VMEM((n, units, tokens, LANES), bf16),
            DMA((units, n)),
            DMA((units, n)),
            DMA((units,)),
        ],
        30 * tokens * D * D, jobs, grid=(1,),
    )


def ffn_kernel(
    layer, host, valid, mid, packed, weight,
    slope, hat, normed, low_mid, rstd_out, stream, low, use,
    xs, act, mean, buf, acc,
):
    step = pl.program_id(0)
    tokens = mid.shape[0]
    vectors = Vectors(host.n, layer, packed)

    @pl.when(step == 0)
    def _():
        gain, shift = vectors.norm(0, 2), vectors.norm(1, 2)
        use[...] = jnp.zeros_like(use)

        def body(r):
            raw = mid[r, :].astype(bf16)
            value, _ = row_stats(raw.astype(f32))
            low_mid[r, :] = raw
            xs[r, :] = (value * gain + shift).astype(bf16)

        row_loop(tokens, ROWS, body)
        if host.parts:
            host.barrier(False)
            host.start()

    @pl.when(step < GROUPS)
    def _():
        buf[...] = dot(xs[...], weight[...].reshape(D, WIDE))

        def body(r):
            h = buf[r, :]
            half = 0.5 * (1.0 + lax.erf(h * (1.0 / math.sqrt(2.0))))
            bell = jnp.exp(-0.5 * h * h) * (1.0 / math.sqrt(2.0 * math.pi))
            act[step, r, :] = h * half
            slope[0, r, :] = (half + h * bell).astype(bf16)

        row_loop(tokens, 32, body)

    @pl.when(step == GROUPS)
    def _():
        acc[...] = jnp.zeros_like(acc)

        def body(r):
            blocks = [act[g, r, :] for g in range(GROUPS)]
            total = sum_lanes(sum(fold_lanes(b) for b in blocks)) / FF
            square = sum(fold_lanes((b - total) * (b - total)) for b in blocks)
            rstd = lax.rsqrt(sum_lanes(square) / FF + EPS)
            mean[r, :] = jnp.broadcast_to(total, (32, LANES))
            rstd_out[r, :] = jnp.broadcast_to(rstd, (32, LANES))

        row_loop(tokens, 32, body)

    @pl.when(step >= GROUPS)
    def _():
        g = step - GROUPS
        hgain, hshift = vectors.hidden(0, g), vectors.hidden(1, g)

        def body(r):
            value = (act[g, r, :] - mean[r, 0:1]) * rstd_out[r, 0:1]
            hat[0, r, :] = value.astype(bf16)
            normed[0, r, :] = (value * hgain + hshift).astype(bf16)

        row_loop(tokens, 32, body)
        acc[...] += dot_nt(normed[0], weight[...].reshape(D, WIDE))

    @pl.when(step == 2 * GROUPS - 1)
    def _():
        def body(r):
            feed = acc[r, :]
            out = mid[r, :] + feed
            keep = valid[r, :]
            stream[r, :] = out
            low[r, :] = out.astype(bf16)
            use[0] += fold_rows(keep * feed * feed)
            use[1] += fold_rows(keep * out * out)

        row_loop(tokens, ROWS, body)
        host.middle()
        host.finish()


def first_half(s):
    return jnp.minimum(s, GROUPS - 1)


def second_half(s):
    return jnp.maximum(s - GROUPS, 0)


def half_specs(tokens):
    early = pl.BlockSpec((1, tokens, WIDE), lambda s: (first_half(s), 0, 0))
    late = pl.BlockSpec((1, tokens, WIDE), lambda s: (second_half(s), 0, 0))
    return early, late


def ffn_call(n, ident, jobs, layer, valid, mid, packed, weight):
    tokens = mid.shape[0]
    big = (GROUPS, tokens, WIDE)
    early, late = half_specs(tokens)
    flat = (tokens, D)
    call = remote_call if jobs else plain_call
    return call(
        functools.partial(ffn_kernel, layer), n, "ffn", ident,
        [valid, mid, packed, weight],
        [whole(v.shape) for v in (valid, mid, packed)]
        + [
            pl.BlockSpec(
                (BLOCKS, 1, LANES, WIDE), lambda s: (0, lax.rem(s, GROUPS), 0, s // GROUPS)
            )
        ],
        [jax.ShapeDtypeStruct(big, bf16)] * 3
        + [
            jax.ShapeDtypeStruct(flat, bf16),
            jax.ShapeDtypeStruct((tokens, LANES), f32),
            jax.ShapeDtypeStruct(flat, f32),
            jax.ShapeDtypeStruct(flat, bf16),
            jax.ShapeDtypeStruct((2, 8, D), f32),
        ],
        [early, late, late]
        + [whole(flat), whole((tokens, LANES)), whole(flat), whole(flat), whole((2, 8, D))],
        [
            pltpu.VMEM(flat, bf16),
            pltpu.VMEM(big, f32),
            pltpu.VMEM((tokens, LANES), f32),
            pltpu.VMEM((tokens, WIDE), f32),
            pltpu.VMEM(flat, f32),
        ],
        16 * tokens * D * FF, jobs, grid=(2 * GROUPS,),
    )


def ffn_back_kernel(
    layer, host, grad, hat, slope, rstd_in, low_mid, packed, weight,
    dhid, grad_turned, normed_turned, grad_out, hgrads, grads,
    gs, dxs, buf, first, cross, acc,
):
    step = pl.program_id(0)
    tokens = grad.shape[0]
    vectors = Vectors(host.n, layer, packed)

    @pl.when(step == 0)
    def _():
        first[...] = jnp.zeros_like(first)
        cross[...] = jnp.zeros_like(cross)
        hgrads[...] = jnp.zeros_like(hgrads)
        grads[...] = jnp.zeros_like(grads)
        gs[...] = grad[...].astype(bf16)
        for b in range(BLOCKS):
            grad_turned[b] = flip(gs[:, b * LANES : (b + 1) * LANES])
        if host.parts:
            host.barrier(False)
            host.start()

    @pl.when(step < GROUPS)
    def _():
        buf[...] = dot(gs[...], weight[...].reshape(D, WIDE))
        hgain = vectors.hidden(0, step)

        def body(r):
            value = hat[0, r, :].astype(f32)
            dy = buf[r, :]
            dx = dy * hgain
            hgrads[0, step] += fold_rows(dy * value)
            hgrads[1, step] += fold_rows(dy)
            first[r, :] += fold_lanes(dx)
            cross[r, :] += fold_lanes(dx * value)
            dxs[step, r, :] = dx

        row_loop(tokens, 32, body)

    @pl.when(step == GROUPS)
    def _():
        acc[...] = jnp.zeros_like(acc)

        def body(r):
            first[r, :] = jnp.broadcast_to(sum_lanes(first[r, :]) / FF, (ROWS, LANES))
            cross[r, :] = jnp.broadcast_to(sum_lanes(cross[r, :]) / FF, (ROWS, LANES))

        row_loop(tokens, ROWS, body)

    @pl.when(step >= GROUPS)
    def _():
        g = step - GROUPS

        def body(r):
            inner = dxs[g, r, :] - first[r, 0:1] - hat[0, r, :].astype(f32) * cross[r, 0:1]
            dhid[0, r, :] = (slope[0, r, :].astype(f32) * (rstd_in[r, 0:1] * inner)).astype(bf16)

        row_loop(tokens, 32, body)
        acc[...] += dot_nt(dhid[0], weight[...].reshape(D, WIDE))

    @pl.when(step == 2 * GROUPS - 1)
    def _():
        gain, shift = vectors.norm(0, 2), vectors.norm(1, 2)

        def body(r):
            value, rstd = row_stats(low_mid[r, :].astype(f32))
            dy = acc[r, :]
            grads[0] += fold_rows(dy * value)
            grads[1] += fold_rows(dy)
            grad_out[r, :] = grad[r, :] + norm_back(dy, value, rstd, gain)
            gs[r, :] = (value * gain + shift).astype(bf16)

        row_loop(tokens, ROWS, body)
        for b in range(BLOCKS):
            normed_turned[b] = flip(gs[:, b * LANES : (b + 1) * LANES])
        host.middle()
        host.finish()


def ffn_back_call(n, ident, jobs, layer, grad, hat, slope, rstd, low_mid, packed, weight):
    tokens = grad.shape[0]
    turned = (BLOCKS, LANES, tokens)
    big = (GROUPS, tokens, WIDE)
    _, late = half_specs(tokens)
    flat = (tokens, D)
    call = remote_call if jobs else plain_call
    return call(
        functools.partial(ffn_back_kernel, layer), n, "ffn_back", ident,
        [grad, hat, slope, rstd, low_mid, packed, weight],
        [
            whole(flat),
            pl.BlockSpec((1, tokens, WIDE), lambda s: (lax.rem(s, GROUPS), 0, 0)),
            late,
        ]
        + [whole(v.shape) for v in (rstd, low_mid, packed)]
        + [
            pl.BlockSpec(
                (BLOCKS, 1, LANES, WIDE), lambda s: (0, lax.rem(s, GROUPS), 0, 1 - s // GROUPS)
            )
        ],
        [
            jax.ShapeDtypeStruct(big, bf16),
            jax.ShapeDtypeStruct(turned, bf16),
            jax.ShapeDtypeStruct(turned, bf16),
            jax.ShapeDtypeStruct(flat, f32),
            jax.ShapeDtypeStruct((2, GROUPS, 8, WIDE), f32),
            jax.ShapeDtypeStruct((2, 8, D), f32),
        ],
        [late, whole(turned), whole(turned), whole(flat)]
        + [whole((2, GROUPS, 8, WIDE)), whole((2, 8, D))],
        [
            pltpu.VMEM(flat, bf16),
            pltpu.VMEM(big, f32),
            pltpu.VMEM((tokens, WIDE), f32),
            pltpu.VMEM((tokens, LANES), f32),
            pltpu.VMEM((tokens, LANES), f32),
            pltpu.VMEM(flat, f32),
        ],
        16 * tokens * D * FF, jobs, grid=(2 * GROUPS,),
    )


def proj_back_kernel(
    layer, host, grad, packed, weight, rows, *refs
):
    n = host.n
    vectors = Vectors(n, layer, packed)
    gain, shift = vectors.norm(0, 1), vectors.norm(1, 1)
    tokens = grad.shape[0]
    units = BLOCKS // n
    outs, refs = refs[:units], refs[units:]
    grad_turned, normed, grads, gs, dm, send, ssem, rsem, lsem = refs
    host.barrier()
    host.start()
    gs[...] = grad[...].astype(bf16)
    for g in range(GROUPS):
        dm[:, g * HEADS : (g + 1) * HEADS] = dot(gs[...], weight[:, g].reshape(D, HEADS))
    grads[...] = jnp.zeros_like(grads)

    def body(r):
        value, rstd = row_stats(rows[r, :].astype(f32))
        dy = dm[r, :]
        grads[0] += fold_rows(dy * value)
        grads[1] += fold_rows(dy)
        dv = norm_back(dy, value, rstd, gain).astype(bf16)
        for b in range(BLOCKS):
            send[b, r, :] = dv[:, b * LANES : (b + 1) * LANES]
        normed[r, :] = (value * gain + shift).astype(bf16)

    row_loop(tokens, ROWS, body)
    _, lo = group_place(n)
    copies = []
    for k in order_of(n) + [0]:
        for u in range(units):
            source = send.at[lax.rem(lo + k, n) * units + u]
            if k:
                copy = group_send(n, k, source, outs[u].at[k], ssem.at[u, k], rsem.at[u, k])
            else:
                copy = pltpu.make_async_copy(source, outs[u].at[0], lsem.at[u])
            copy.start()
            copies.append(copy)
    for b in range(BLOCKS):
        grad_turned[b] = flip(gs[:, b * LANES : (b + 1) * LANES])
    host.middle()
    for copy in copies:
        copy.wait()
    host.finish()


def proj_back_call(n, ident, jobs, layer, grad, packed, weight, rows):
    tokens = grad.shape[0]
    units = BLOCKS // n
    turned = (BLOCKS, LANES, tokens)
    flat = (tokens, D)
    return remote_call(
        functools.partial(proj_back_kernel, layer), n, "projection_back", ident,
        [grad, packed, weight, rows],
        [whole(v.shape) for v in (grad, packed)]
        + [pl.BlockSpec((BLOCKS, GROUPS, LANES, HEADS), lambda i: (0, 0, 0, 3)), whole(flat)],
        [
            *[jax.ShapeDtypeStruct((n, tokens, LANES), bf16)] * units,
            jax.ShapeDtypeStruct(turned, bf16),
            jax.ShapeDtypeStruct(flat, bf16),
            jax.ShapeDtypeStruct((2, 8, D), f32),
        ],
        [HB] * units + [whole(turned), whole(flat), whole((2, 8, D))],
        [
            pltpu.VMEM(flat, bf16),
            pltpu.VMEM(flat, f32),
            pltpu.VMEM((BLOCKS, tokens, LANES), bf16),
            DMA((units, n)),
            DMA((units, n)),
            DMA((units,)),
        ],
        30 * tokens * D * D, jobs, grid=(1,),
    )


def attn_back_kernel(n, need, aux, one, *refs):
    qkv, (att, datt, lse) = refs[:n], refs[n : n + 3]
    outs, refs = refs[n + 3 : 2 * n + 3], refs[2 * n + 3 :]
    kx, kt, qs, vs, delta, dq, dkey, dval, dkv = refs
    for r in range(n):
        kx[r] = jnp.concatenate([qkv[r][1], aux[r]], axis=1)
        kt[r] = flip(qkv[r][1])
        vs[r] = qkv[r][2]
        qs[r] = (qkv[r][0].astype(f32) * (1.0 / math.sqrt(DH))).astype(bf16)
        both = jnp.transpose(att[r].astype(f32) * datt[r].astype(f32), (1, 0))
        delta[r, 0:1] = jnp.sum(both[:DH], axis=0, keepdims=True)
        delta[r, 1:2] = jnp.sum(both[DH:], axis=0, keepdims=True)
    dq[...] = jnp.zeros_like(dq)

    def each_key(j, carry):
        dkey[...] = jnp.zeros_like(dkey)
        dval[...] = jnp.zeros_like(dval)

        def each_query(i, inner):
            @pl.when(need[i * n + j] == 1)
            def _():
                for h in range(2):
                    query = head_lanes(qs[i], h)
                    out = head_lanes(datt[i], h)
                    scores = dot_nt(kx[j], jnp.concatenate([query, one[...]], axis=1))
                    probs = jnp.exp(scores - lse[i, h : h + 1])
                    dprobs = dot_nt(vs[j], out)
                    dscores = (probs * (dprobs - delta[i, h : h + 1])).astype(bf16)
                    dval[...] += dot(probs.astype(bf16), out)
                    dkey[...] += dot(dscores, query)
                    rows = slice(h * DH, (h + 1) * DH)
                    dq[i, rows] += dot(kt[j, rows], dscores)

            return inner

        lax.fori_loop(0, n, each_query, 0)
        dkv[j, 0] = dkey[...].astype(bf16)
        dkv[j, 1] = dval[...].astype(bf16)
        return carry

    lax.fori_loop(0, n, each_key, 0)
    for r in range(n):
        outs[r][0] = (jnp.transpose(dq[r], (1, 0)) * (1.0 / math.sqrt(DH))).astype(bf16)
        outs[r][1] = dkv[r, 0]
        outs[r][2] = dkv[r, 1]


def attn_back_call(n, need, aux, one, parts, att, datt, lse):
    tokens = aux.shape[1]
    return unit_call(
        attn_back_kernel, n, need, aux, one, [*parts, att, datt, lse],
        [jax.ShapeDtypeStruct((3, tokens, LANES), bf16)] * n,
        [
            pltpu.VMEM((n, tokens, 2 * LANES), bf16),
            pltpu.VMEM((n, LANES, tokens), bf16),
            pltpu.VMEM((n, tokens, LANES), bf16),
            pltpu.VMEM((n, tokens, LANES), bf16),
            pltpu.VMEM((n, 8, tokens), f32),
            pltpu.VMEM((n, LANES, tokens), f32),
            pltpu.VMEM((tokens, LANES), f32),
            pltpu.VMEM((tokens, LANES), f32),
            pltpu.VMEM((n, 2, tokens, LANES), bf16),
        ],
        14, "attention_back",
    )


def qkv_back_kernel(
    layer, host, grad, low, packed, wq, wk, wv, *refs
):
    n = host.n
    vectors = Vectors(n, layer, packed)
    gain, shift = vectors.norm(0, 0), vectors.norm(1, 0)
    tokens = grad.shape[0]
    units = BLOCKS // n
    early_count = n * (units - 1)
    ready, refs = refs[:early_count], refs[early_count:]
    dparts, refs = refs[:n], refs[n:]
    dlast, refs = refs[:n], refs[n:]
    grad_out, normed_turned, grads, grad_low, acc, ns, ssem, rsem, lsem = refs
    blocks = [ready[u * n : (u + 1) * n] for u in range(units - 1)] + [dlast]
    host.barrier()
    steps = [0] + order_of(n)[::-1]
    copies = {}
    for k in order_of(n):
        copies[k] = group_send(n, -k, dparts[k], dlast[k], ssem.at[k], rsem.at[k])
        copies[k].start()
    copies[0] = pltpu.make_async_copy(dparts[0], dlast[0], lsem)
    copies[0].start()
    host.start()
    grads[...] = jnp.zeros_like(grads)

    def early(r):
        value, _ = row_stats(low[r, :].astype(f32))
        ns[r, :] = (value * gain + shift).astype(bf16)

    row_loop(tokens, ROWS, early)
    for b in range(BLOCKS):
        normed_turned[b] = flip(ns[:, b * LANES : (b + 1) * LANES])
    for i, k in enumerate(steps):
        copies[k].wait()
        group, offset = head_columns(n, k)
        total = None
        for c, weight in enumerate((wq, wk, wv)):
            left = jnp.concatenate([blocks[u][k][c] for u in range(units)], axis=1)
            right = weight[:, group, :, pl.ds(offset, units * LANES)].reshape(D, units * LANES)
            term = dot_nt(left, right)
            total = term if total is None else total + term
        if i == 0:
            acc[...] = total
        else:
            acc[...] += total

    def body(r):
        value, rstd = row_stats(low[r, :].astype(f32))
        dy = acc[r, :]
        grads[0] += fold_rows(dy * value)
        grads[1] += fold_rows(dy)
        total = grad[r, :] + norm_back(dy, value, rstd, gain)
        grad_out[r, :] = total
        grad_low[r, :] = total.astype(bf16)

    row_loop(tokens, ROWS, body)
    host.middle()
    host.finish()


def qkv_back_call(n, ident, jobs, layer, grad, low, packed, weight, ready, dparts):
    tokens = grad.shape[0]
    turned = (BLOCKS, LANES, tokens)
    flat = (tokens, D)
    columns = lambda c: pl.BlockSpec((BLOCKS, GROUPS, LANES, HEADS), lambda i: (0, 0, 0, c))
    block = (3, tokens, LANES)
    res = remote_call(
        functools.partial(qkv_back_kernel, layer), n, "qkv_back", ident,
        [grad, low, packed, weight, weight, weight, *ready, *dparts],
        [whole(v.shape) for v in (grad, low, packed)]
        + [columns(0), columns(1), columns(2)]
        + [whole(block)] * (len(ready) + n),
        [jax.ShapeDtypeStruct(block, bf16)] * n
        + [
            jax.ShapeDtypeStruct(flat, f32),
            jax.ShapeDtypeStruct(turned, bf16),
            jax.ShapeDtypeStruct((2, 8, D), f32),
            jax.ShapeDtypeStruct(flat, bf16),
        ],
        [whole(block)] * n + [whole(flat), whole(turned), whole((2, 8, D)), whole(flat)],
        [
            pltpu.VMEM(flat, f32),
            pltpu.VMEM(flat, bf16),
            DMA((n,)),
            DMA((n,)),
            DMA,
        ],
        50 * tokens * D * D, jobs, grid=(1,),
    )
    return [res[:n], *res[n:]]


def pick_rows(sc, turned, count):
    return jnp.concatenate([turned[sc[m]] for m in range(count)], axis=0)


def put_rows(value, extra, outs, spot):
    rows = value.shape[0] // LANES
    for m in range(rows):
        part = value[m * LANES : (m + 1) * LANES]
        if extra is not None:
            part = part + extra[(m,) + spot].astype(f32)
            outs[m // 2][(m % 2,) + spot] = part.astype(bf16)
        else:
            outs[0][(m,) + spot] = part.astype(bf16)


def ffn_grad_kernel(count, added, sc, up_turned, down_turned, dhid, normed, *refs):
    extra, outs = (refs[0], refs[1:]) if added else (None, refs)

    @pl.when(pl.program_id(0) == 0)
    def _():
        put_rows(dot(pick_rows(sc, up_turned, count), dhid[0]), extra, outs, (0,))

    @pl.when(pl.program_id(0) == 1)
    def _():
        put_rows(dot(pick_rows(sc, down_turned, count), normed[0]), extra, outs, (0,))


def ffn_grad_call(count, sc, up_turned, down_turned, dhid, normed, extra=None):
    tokens = up_turned.shape[2]
    added = extra is not None
    at = lambda g, sc: lax.rem(g + sc[count], GROUPS)
    left = pl.BlockSpec(
        (1, tokens, WIDE), lambda j, g, sc: (at(jnp.where(j == 0, g, GROUPS - 1), sc), 0, 0)
    )
    right = pl.BlockSpec((1, tokens, WIDE), lambda j, g, sc: (at(jnp.where(j == 1, g, 0), sc), 0, 0))
    piece = lambda m: pl.BlockSpec((m, 1, LANES, WIDE), lambda j, g, sc: (0, g, 0, j))
    outs = [2, 2] if added else [count]
    return pl.pallas_call(
        lambda *refs: ffn_grad_kernel(count, added, *refs),
        out_shape=[jax.ShapeDtypeStruct((m, GROUPS, LANES, 2 * WIDE), bf16) for m in outs],
        grid_spec=pltpu.PrefetchScalarGridSpec(
            num_scalar_prefetch=1,
            grid=(2, GROUPS),
            in_specs=[whole(up_turned.shape), whole(down_turned.shape), left, right]
            + ([piece(count)] if added else []),
            out_specs=[piece(m) for m in outs],
        ),
        compiler_params=params(),
        cost_estimate=cost(16 * tokens * count * LANES * FF, 24 * 2**20),
        name="ffn_grad",
    )(sc, up_turned, down_turned, dhid, normed, *([extra] if added else []))


def head_grad_kernel(n, count, added, sc, in_turned, out_turned, normed, *refs):
    units = BLOCKS // n
    dqkv, refs = refs[: n * units], refs[n * units :]
    extra, outs = (refs[0], refs[1:]) if added else (None, refs)
    left = pick_rows(sc, in_turned, count)
    for k in range(n):
        for c in range(3):
            right = jnp.concatenate([dqkv[u * n + k][c] for u in range(units)], axis=1)
            value = dot(left, right)
            if n == GROUPS:
                slot = lax.rem(lax.rem(sc[count + 1] + k, n) + GROUPS - sc[count], GROUPS)
                put_rows(value, extra, outs, (slot, slice(None), slice(c * HEADS, (c + 1) * HEADS)))
            else:
                unit = lax.rem(sc[count + 1] + k, n) * units
                at = pl.multiple_of(c * HEADS + lax.rem(unit, 2) * LANES, LANES)
                put_rows(value, extra, outs, (unit // 2, slice(None), pl.ds(at, LANES)))
    left = pick_rows(sc, out_turned, count)
    for g in range(GROUPS):
        slot = lax.rem(g + GROUPS - sc[count], GROUPS)
        value = dot(left, normed[:, g * HEADS : (g + 1) * HEADS])
        put_rows(value, extra, outs, (slot, slice(None), slice(3 * HEADS, 4 * HEADS)))


def head_grad_call(n, count, sc, in_turned, out_turned, dqkv, normed, extra=None):
    tokens = in_turned.shape[2]
    added = extra is not None
    outs = [2, 2] if added else [count]
    inner = (GROUPS, LANES, 4 * HEADS)
    return pl.pallas_call(
        lambda *refs: head_grad_kernel(n, count, added, *refs),
        out_shape=[jax.ShapeDtypeStruct((m,) + inner, bf16) for m in outs],
        grid_spec=pltpu.PrefetchScalarGridSpec(
            num_scalar_prefetch=1,
            grid=(1,),
            in_specs=[whole(v.shape) for v in (in_turned, out_turned, normed, *dqkv)]
            + ([whole((count,) + inner)] if added else []),
            out_specs=[whole((m,) + inner) for m in outs],
        ),
        compiler_params=params(),
        cost_estimate=cost(16 * tokens * count * LANES * 4 * D, 16 * 2**20),
        name="head_grad",
    )(sc, in_turned, out_turned, normed, *dqkv, *([extra] if added else []))


def pack_kernel(qkv, out, up, down, *refs):
    layers = qkv.shape[0]
    for l in range(layers):
        narrow, broad = refs[2 * l : 2 * l + 2]
        for c in range(3):
            narrow[:, c * HEADS : (c + 1) * HEADS] = qkv[l, c]
        narrow[:, 3 * HEADS :] = flip(out[l])
        broad[:, :WIDE] = up[l]
        broad[:, WIDE:] = flip(down[l])


def pack_call(qkv, out, up, down):
    layers = qkv.shape[0]
    flat = pl.pallas_call(
        pack_kernel,
        out_shape=[
            jax.ShapeDtypeStruct((LANES, NARROW), bf16),
            jax.ShapeDtypeStruct((LANES, BROAD), bf16),
        ]
        * layers,
        in_specs=[VM] * 4,
        out_specs=[VM] * (2 * layers),
        compiler_params=params(),
        cost_estimate=cost(0, 4 * 2**20),
        name="pack",
    )(qkv, out, up, down)
    return flat[::2], flat[1::2]


def greet(sem, place, z, others, count):
    n = GROUPS
    for k in range(1, n):
        pl.semaphore_signal(
            sem, inc=1, device_id={"head": lax.rem(z + k, n)}, device_id_type=MESH
        )
    for other in (place.by_x, place.by_y, place.mate):
        pl.semaphore_signal(sem, inc=1, device_id={"dp": other}, device_id_type=MESH)
    for to_dp, to_z in others:

        @pl.when((to_dp != place.dp) | (to_z != z))
        def _(to_dp=to_dp, to_z=to_z):
            pl.semaphore_signal(
                sem, inc=1, device_id={"dp": to_dp, "head": to_z}, device_id_type=MESH
            )

    pl.semaphore_wait(sem, n + 2 + count)


class Weights:
    def __init__(self, at, chunks, shards, gathered, hsem, ssem, rsem, lsem):
        self.at, self.chunks, self.pairs = at, chunks, list(zip(shards, gathered))
        self.hsem, self.ssem, self.rsem = hsem, ssem, rsem
        self.owns = [
            pltpu.make_async_copy(shard, out.at[at.dp, at.z], lsem.at[i])
            for i, (shard, out) in enumerate(self.pairs)
        ]

    def near(self, c):
        kind, columns = self.chunks[c][0], pl.ds(*self.chunks[c][1:])
        shard, out = self.pairs[kind]
        at = self.at
        return [
            pltpu.make_async_remote_copy(
                src_ref=shard.at[:, columns],
                dst_ref=out.at[at.dp, at.z, :, columns],
                send_sem=self.hsem.at[0, k - 1, c],
                recv_sem=self.hsem.at[1, k - 1, c],
                device_id={"head": lax.rem(at.z + k, GROUPS)},
                device_id_type=MESH,
            )
            for k in (2, 1, 3)
        ]

    def far(self, slot, row, target, c):
        kind, columns = self.chunks[c][0], pl.ds(*self.chunks[c][1:])
        out = self.pairs[kind][1]
        return pltpu.make_async_remote_copy(
            src_ref=out.at[row, :, :, columns],
            dst_ref=out.at[row, :, :, columns],
            send_sem=self.ssem.at[slot, c],
            recv_sem=self.rsem.at[slot, c],
            device_id={"dp": target},
            device_id_type=MESH,
        )

    def hops(self, stage, c):
        at = self.at
        if stage == 0:
            return self.near(c)
        if stage == 1:
            return [self.far(0, at.dp, at.first, c)]
        if stage == 2:
            return [self.far(1, at.dp, at.second, c), self.far(2, at.first, at.second, c)]
        rows = (at.dp, at.first, at.second, at.both)
        return [self.far(3 + i, row, at.mate, c) for i, row in enumerate(rows)]

    def run(self, aside):
        parts = len(self.chunks)
        for c in range(min(2, parts)):
            for copy in self.near(c):
                copy.start()
        for t in range(parts + 3):
            for stage in (1, 2, 3):
                c = t + 1 - stage
                if 0 <= c < parts:
                    if stage == 1 and c == 0:
                        for copy in self.owns:
                            copy.wait()
                    for copy in self.hops(stage - 1, c):
                        copy.wait()
                    for copy in self.hops(stage, c):
                        copy.start()
            if t + 2 < parts:
                for copy in self.near(t + 2):
                    copy.start()
            aside(t)
            c = t - 3
            if 0 <= c < parts:
                for copy in self.hops(3, c):
                    copy.wait()


def weight_chunks(shards):
    step = 512
    return [(i, c, step) for i, v in enumerate(shards) for c in range(0, v.shape[1], step)]


def weight_sems(shards):
    parts = len(weight_chunks(shards))
    return [DMA((2, 3, parts)), DMA((7, parts)), DMA((7, parts)), DMA((len(shards),))]


def gather_call(shards):
    count = len(shards)

    def kernel(*refs):
        at = Place()
        weights = Weights(at, weight_chunks(shards), refs[:count], refs[count : 2 * count], *refs[2 * count :])
        for copy in weights.owns:
            copy.start()
        greet(pltpu.get_barrier_semaphore(), at, at.z, [], 0)
        weights.run(lambda t: None)

    return pl.pallas_call(
        kernel,
        out_shape=[jax.ShapeDtypeStruct((BLOCKS, GROUPS) + v.shape, bf16) for v in shards],
        in_specs=[HB] * count,
        out_specs=[HB] * count,
        scratch_shapes=weight_sems(shards),
        compiler_params=params(collective_id=7, has_side_effects=True),
        cost_estimate=cost(0, 150 * 2**20),
        name="gather",
    )(*shards)


def start_kernel(
    chunks, shards, rows, vector, flags, gathered, low, side, vectors, flags_out,
    hsem, ssem, rsem, wsem, xsem, tsem, vsem, fsem, lsem,
):
    at = Place()
    weights = Weights(at, chunks, shards, gathered, hsem, ssem, rsem, wsem)
    dp, core, bit_x, by_x = at.dp, at.core, at.bit_x, at.by_x
    z = at.z
    n = GROUPS
    lo = lax.rem(dp, n)
    wide = rows.shape[2]
    sem = pltpu.get_barrier_semaphore()

    def targets():
        return [(xs, c2, dp - core + c2, 2 * xs + core) for xs in range(2) for c2 in range(2)]

    def sources():
        return [(dp - core + lax.rem(z, 2), g) for g in range(n)]

    turn_dp, turn_z = dp - lo + z, lo
    for copy in weights.owns:
        copy.start()
    own_vector = pltpu.make_async_copy(vector, vectors.at[z], lsem.at[2])
    own_vector.start()
    turned = [(turn_dp, turn_z)]
    greet(sem, at, z, sources() + turned, n - 1 + unlike(lax.rem(z, 2), core) + unlike(z, lo))
    small = [
        pltpu.make_async_remote_copy(
            src_ref=vector,
            dst_ref=vectors.at[z],
            send_sem=vsem.at[0, k - 1],
            recv_sem=vsem.at[1, k - 1],
            device_id={"head": lax.rem(z + k, n)},
            device_id_type=MESH,
        )
        for k in range(1, n)
    ]

    def flag_copy(op):
        def remote():
            copy = pltpu.make_async_remote_copy(
                src_ref=flags,
                dst_ref=flags_out,
                send_sem=fsem.at[0],
                recv_sem=fsem.at[1],
                device_id={"dp": turn_dp, "head": turn_z},
                device_id_type=MESH,
            )
            copy.start() if op == "start" else copy.wait()

        def inside():
            copy = pltpu.make_async_copy(flags, flags_out, lsem.at[3])
            copy.start() if op == "start" else copy.wait()

        pl.when((turn_dp != dp) | (turn_z != z))(remote)
        pl.when((turn_dp == dp) & (turn_z == z))(inside)

    flag_copy("start")
    for copy in small:
        copy.start()

    cross = pltpu.make_async_remote_copy(
        src_ref=rows.at[pl.ds(2 - 2 * bit_x, 2)],
        dst_ref=side,
        send_sem=xsem.at[0],
        recv_sem=xsem.at[1],
        device_id={"dp": by_x},
        device_id_type=MESH,
    )
    place = low.at[:, pl.ds(pl.multiple_of(z * wide, wide), wide)]

    def spread(op):
        for i, (xs, c2, to_dp, to_z) in enumerate(targets()):

            def here(source, i=i, to_dp=to_dp, to_z=to_z):
                def remote():
                    copy = pltpu.make_async_remote_copy(
                        src_ref=source,
                        dst_ref=place,
                        send_sem=tsem.at[0, i],
                        recv_sem=tsem.at[1, z],
                        device_id={"dp": to_dp, "head": to_z},
                        device_id_type=MESH,
                    )
                    if op == "start":
                        copy.start()
                    else:
                        copy.wait_send()

                pl.when((to_dp != dp) | (to_z != z))(remote)

                def inside():
                    copy = pltpu.make_async_copy(source, place, lsem.at[1])
                    if op == "start":
                        copy.start()
                    else:
                        copy.wait()

                pl.when((to_dp == dp) & (to_z == z))(inside)

            pl.when(bit_x == xs)(lambda xs=xs, c2=c2, here=here: here(rows.at[2 * xs + c2]))
            pl.when(bit_x != xs)(lambda c2=c2, here=here: here(side.at[c2]))

    cross.start()

    def aside(t):
        if t == 1:
            cross.wait()
            spread("start")

    weights.run(aside)
    own_vector.wait()
    flag_copy("wait")
    for copy in small:
        copy.wait()
    spread("wait")
    for from_dp, g in sources():

        @pl.when((from_dp != dp) | (g != z))
        def _(g=g):
            spot = low.at[:, pl.ds(g * wide, wide)]
            pltpu.make_async_remote_copy(
                src_ref=spot,
                dst_ref=spot,
                send_sem=tsem.at[0, 0],
                recv_sem=tsem.at[1, g],
                device_id={"dp": by_x},
                device_id_type=MESH,
            ).wait_recv()


def start_call(shards, rows, vector, flags):
    count = len(shards)
    chunks = weight_chunks(shards)
    tokens, wide = rows.shape[1:]

    def kernel(*refs):
        taken, refs = refs[:count], refs[count:]
        start_kernel(chunks, taken, *refs[:3], refs[3 : 3 + count], *refs[3 + count :])

    res = pl.pallas_call(
        kernel,
        out_shape=[jax.ShapeDtypeStruct((BLOCKS, GROUPS) + v.shape, bf16) for v in shards]
        + [
            jax.ShapeDtypeStruct((tokens, GROUPS * wide), bf16),
            jax.ShapeDtypeStruct((2, tokens, wide), bf16),
            jax.ShapeDtypeStruct((GROUPS,) + vector.shape, f32),
            jax.ShapeDtypeStruct(flags.shape, jnp.int32),
        ],
        in_specs=[HB] * (count + 3),
        out_specs=[HB] * (count + 4),
        scratch_shapes=[
            *weight_sems(shards),
            DMA((2,)),
            DMA((2, GROUPS)),
            DMA((2, 3)),
            DMA((2,)),
            DMA((4,)),
        ],
        compiler_params=params(collective_id=5, has_side_effects=True),
        cost_estimate=cost(0, 300 * 2**20),
        name="start",
    )(*shards, rows, vector, flags)
    return [res[:count], *res[count:]]


def vector_rows(layers):
    return -(-(28 * layers + 3 * layers + 1) // 8) * 8


def end_kernel(
    layers, rows, grads, fmine, fsent, valid, tops, vecs, uses,
    rows_out, qkv_out, out_out, up_out, down_out, vectors_out,
    mine, got, pair, last, near, pieces, fm, flast, fnear, vec, vgot, vsum,
    gsem, hsem, psem, qsem, nsem, zsem, tsem, xsem, vsem, lsem, fsem, esem,
):
    at = Place()
    dp, core, bit_x = at.dp, at.core, at.bit_x
    z = at.z
    n = GROUPS
    parts = 4
    width = grads.shape[3] // parts
    step = fmine.shape[2] // parts
    wide = rows.shape[1] // n
    sem = pltpu.get_barrier_semaphore()

    def columns(c):
        return pl.ds(c * width, width)

    def broad(c):
        return pl.ds(c * step, step)

    def loads(c):
        return [
            pltpu.make_async_copy(
                grads.at[pl.ds(0, 4), :, :, columns(c)], mine.at[:, :, :, columns(c)], gsem.at[0, c]
            ),
            pltpu.make_async_copy(
                fmine.at[:, :, broad(c)], fm.at[:, :, broad(c)], gsem.at[1, c]
            ),
        ]

    for c in range(parts):
        for copy in loads(c):
            copy.start()

    vec[...] = jnp.zeros_like(vec)
    for l in range(layers):
        base = 28 * l
        norms, hidden = vecs[4 * l : 4 * l + 3], vecs[4 * l + 3]
        for kind in range(2):
            for i in range(3):
                total = jnp.sum(norms[i][kind], axis=0, keepdims=True)
                for b in range(BLOCKS):
                    row = base + (3 * kind + i) * 2 + b % 2
                    vec[b // 2, row : row + 1, :] = total[:, b * LANES : (b + 1) * LANES]
            for g in range(n):
                total = jnp.sum(hidden[kind, g], axis=0, keepdims=True)
                for b in range(BLOCKS):
                    row = base + 12 + 8 * kind + b
                    vec[g, row : row + 1, :] = total[:, b * LANES : (b + 1) * LANES]
        branch, rest = uses[2 * l : 2 * l + 2]
        for i, value in enumerate((branch[...], rest[0], rest[1])):
            row = 28 * layers + 3 * l + i
            total = fold_lanes(jnp.sum(value, axis=0, keepdims=True))
            for g in range(n):
                vec[g, row : row + 1, :] = total
    row = 31 * layers
    count = jnp.sum(valid[...], axis=0, keepdims=True) * (D / LANES)
    for g in range(n):
        vec[g, row : row + 1, :] = jnp.broadcast_to(count, (1, LANES))

    to_dp = dp - core + lax.rem(z, 2)
    sources = [(dp - core + c2, 2 * xs + core) for xs in range(2) for c2 in range(2)]
    greet(sem, at, z, sources, n - 1 + unlike(lax.rem(z, 2), core))

    def hop(stage, c):
        if stage == 0:
            return pltpu.make_async_remote_copy(
                src_ref=grads.at[pl.ds(4, 4), :, :, columns(c)],
                dst_ref=got.at[:, :, :, columns(c)],
                send_sem=hsem.at[0, c],
                recv_sem=hsem.at[1, c],
                device_id={"dp": at.mate},
                device_id_type=MESH,
            )
        if stage == 1:
            return pltpu.make_async_remote_copy(
                src_ref=mine.at[pl.ds(2, 2), :, :, columns(c)],
                dst_ref=pair.at[:, :, :, columns(c)],
                send_sem=psem.at[0, c],
                recv_sem=psem.at[1, c],
                device_id={"dp": at.second},
                device_id_type=MESH,
            )
        return pltpu.make_async_remote_copy(
            src_ref=mine.at[1, :, :, columns(c)],
            dst_ref=last.at[:, :, columns(c)],
            send_sem=qsem.at[0, c],
            recv_sem=qsem.at[1, c],
            device_id={"dp": at.first},
            device_id_type=MESH,
        )

    def ffn_hop(c):
        return pltpu.make_async_remote_copy(
            src_ref=fsent.at[:, :, broad(c)],
            dst_ref=flast.at[:, :, broad(c)],
            send_sem=fsem.at[0, c],
            recv_sem=fsem.at[1, c],
            device_id={"dp": at.first},
            device_id_type=MESH,
        )

    def around(source, target, cols, sems, c):
        return [
            pltpu.make_async_remote_copy(
                src_ref=source(k, cols),
                dst_ref=target.at[k - 1, :, cols],
                send_sem=sems.at[0, k - 1, c],
                recv_sem=sems.at[1, k - 1, c],
                device_id={"head": lax.rem(z + k, n)},
                device_id_type=MESH,
            )
            for k in (2, 1, 3)
        ]

    def head_around(c):
        return around(lambda k, cols: mine.at[0, k, :, cols], near, columns(c), nsem, c)

    def ffn_around(c):
        return around(lambda k, cols: fm.at[k, :, cols], fnear, broad(c), esem, c)

    def add(count, other, c):
        def body(i, carry):
            m, g = i // GROUPS, lax.rem(i, GROUPS)
            value = mine[m, g, :, columns(c)].astype(f32) + other(m, g).astype(f32)
            mine[m, g, :, columns(c)] = value.astype(bf16)
            return carry

        lax.fori_loop(0, count * GROUPS, body, 0)

    def row_copies(op):
        for j in range(n):
            source = rows.at[:, pl.ds(j * wide, wide)]
            target = pieces.at[z // 2, core]

            def remote(j=j, source=source, target=target):
                copy = pltpu.make_async_remote_copy(
                    src_ref=source,
                    dst_ref=target,
                    send_sem=tsem.at[0, j],
                    recv_sem=tsem.at[1, 2 * (z // 2) + core],
                    device_id={"dp": to_dp, "head": j},
                    device_id_type=MESH,
                )
                copy.start() if op == "start" else copy.wait_send()

            def inside(source=source, target=target):
                copy = pltpu.make_async_copy(source, target, lsem.at[0])
                copy.start() if op == "start" else copy.wait()

            pl.when((to_dp != dp) | (j != z))(remote)
            pl.when((to_dp == dp) & (j == z))(inside)

    def row_arrivals():
        for xs in range(2):
            for c2 in range(2):

                @pl.when((dp - core + c2 != dp) | (2 * xs + core != z))
                def _(xs=xs, c2=c2):
                    spot = pieces.at[xs, c2]
                    pltpu.make_async_remote_copy(
                        src_ref=spot,
                        dst_ref=spot,
                        send_sem=tsem.at[0, 0],
                        recv_sem=tsem.at[1, 2 * xs + c2],
                        device_id={"dp": at.by_x},
                        device_id_type=MESH,
                    ).wait_recv()

    cross = pltpu.make_async_remote_copy(
        src_ref=pieces.at[1 - bit_x],
        dst_ref=rows_out.at[pl.ds(2 * bit_x, 2)],
        send_sem=xsem.at[0],
        recv_sem=xsem.at[1],
        device_id={"dp": at.by_x},
        device_id_type=MESH,
    )
    stay = pltpu.make_async_copy(pieces.at[bit_x], rows_out.at[pl.ds(2 * bit_x, 2)], lsem.at[1])

    def vector_near(k):
        return pltpu.make_async_remote_copy(
            src_ref=vec.at[lax.rem(z + k, n)],
            dst_ref=vgot.at[k - 1],
            send_sem=vsem.at[0, k - 1],
            recv_sem=vsem.at[1, k - 1],
            device_id={"head": lax.rem(z + k, n)},
            device_id_type=MESH,
        )

    def vector_far(i, target):
        return pltpu.make_async_remote_copy(
            src_ref=vsum.at[i],
            dst_ref=vgot.at[3 + i],
            send_sem=vsem.at[0, 3 + i],
            recv_sem=vsem.at[1, 3 + i],
            device_id={"dp": target},
            device_id_type=MESH,
        )

    def put_head(l, c, value):
        if c < 3:
            qkv_out[l, c] = value
        else:
            out_out[l] = jnp.transpose(value, (1, 0))

    def total_of(own, others):
        value = own.astype(f32)
        for other in others:
            value = value + other.astype(f32)
        return value

    row_copies("start")
    for c in range(parts):
        ffn_hop(c).start()
        hop(0, c).start()
    for k in range(1, n):
        vector_near(k).start()
    partners = (at.mate, at.first, at.second)
    for t in range(parts + 4):
        c = t
        if c < parts:
            for copy in loads(c):
                copy.wait()
            hop(0, c).wait()
            add(4, lambda m, g, c=c: got[m, g, :, columns(c)], c)
            hop(1, c).start()
            ffn_hop(c).wait()

            def body(g, carry, c=c):
                value = fm[g, :, broad(c)].astype(f32) + flast[g, :, broad(c)].astype(f32)
                fm[g, :, broad(c)] = value.astype(bf16)
                return carry

            lax.fori_loop(0, GROUPS, body, 0)
            for copy in ffn_around(c):
                copy.start()
        c = t - 1
        if 0 <= c < parts:
            hop(1, c).wait()
            add(2, lambda m, g, c=c: pair[m, g, :, columns(c)], c)
            hop(2, c).start()
        c = t - 2
        if 0 <= c < parts:
            hop(2, c).wait()
            add(1, lambda m, g, c=c: last[g, :, columns(c)], c)
            for copy in head_around(c):
                copy.start()
        if t == 1:
            for k in range(1, n):
                vector_near(k).wait()
            vsum[0] = vec[z] + vgot[0] + vgot[1] + vgot[2]
            vector_far(0, partners[0]).start()
        if 2 <= t < 5:
            i = t - 2
            vector_far(i, partners[i]).wait()
            vsum[i + 1] = vsum[i] + vgot[3 + i]
            if i < 2:
                vector_far(i + 1, partners[i + 1]).start()
        if t == 2:
            row_copies("wait")
            row_arrivals()
            cross.start()
            stay.start()
        if t == 4:
            for l in range(1, layers):
                heads, hnear, ups, unear, downs, dnear = tops[6 * l - 6 : 6 * l]
                for c in range(parts):
                    cols = slice(c * width, (c + 1) * width)
                    put_head(l, c, total_of(heads[0, :, cols], [hnear[k, :, cols] for k in range(3)]))
                up_out[l] = total_of(ups[0], [unear[k] for k in range(3)])
                down_out[l] = jnp.transpose(total_of(downs[0], [dnear[k] for k in range(3)]), (1, 0))
        c = t - 4
        if 0 <= c < parts:
            for copy in ffn_around(c):
                copy.wait()
            value = total_of(fm[0, :, broad(c)], [fnear[k, :, broad(c)] for k in range(3)])
            if c < parts // 2:
                up_out[0, :, broad(c)] = value
            else:
                down_out[0, pl.ds(c * step - WIDE, step), :] = jnp.transpose(value, (1, 0))
    for c in range(parts):
        for copy in head_around(c):
            copy.wait()
        others = [near[k, :, columns(c)] for k in range(3)]
        put_head(0, c, total_of(mine[0, 0, :, columns(c)], others))
    vectors_out[...] = vsum[3]
    cross.wait()
    stay.wait()


def end_call(rows, grads, fmine, fsent, valid, tops, vecs, uses):
    parts = 4
    layers = len(vecs) // 4
    tokens = rows.shape[0]
    wide = rows.shape[1] // GROUPS
    block = grads.shape[1:]
    broad = fmine.shape
    vector = (vector_rows(layers), LANES)
    inputs = [rows, grads, fmine, fsent, valid, *tops, *vecs, *uses]

    def spec(i, v):
        if i % 2 == 0:
            return pl.BlockSpec((1,) + v.shape[1:], lambda g: (0, 0, 0))
        return whole(v.shape)

    def kernel(*refs):
        fixed, refs = refs[:5], refs[5:]
        lists = []
        for values in (tops, vecs, uses):
            lists.append(refs[: len(values)])
            refs = refs[len(values) :]
        end_kernel(layers, *fixed, *lists, *refs)

    outs = [
        jax.ShapeDtypeStruct((layers, 3, LANES, HEADS), f32),
        jax.ShapeDtypeStruct((layers, HEADS, LANES), f32),
        jax.ShapeDtypeStruct((layers, LANES, WIDE), f32),
        jax.ShapeDtypeStruct((layers, WIDE, LANES), f32),
        jax.ShapeDtypeStruct(vector, f32),
    ]
    return pl.pallas_call(
        kernel,
        out_shape=[jax.ShapeDtypeStruct((GROUPS, tokens, wide), bf16)] + outs,
        grid=(1,),
        in_specs=[HB] * 4
        + [whole(valid.shape)]
        + [spec(i, v) for i, v in enumerate(tops)]
        + [whole(v.shape) for v in (*vecs, *uses)],
        out_specs=[HB] + [whole(v.shape) for v in outs],
        scratch_shapes=[
            pltpu.VMEM((4,) + block, bf16),
            pltpu.VMEM((4,) + block, bf16),
            pltpu.VMEM((2,) + block, bf16),
            pltpu.VMEM(block, bf16),
            pltpu.VMEM((3,) + block[1:], bf16),
            pltpu.VMEM((2, 2, tokens, wide), bf16),
            pltpu.VMEM(broad, bf16),
            pltpu.VMEM(broad, bf16),
            pltpu.VMEM((3,) + broad[1:], bf16),
            pltpu.VMEM((GROUPS,) + vector, f32),
            pltpu.VMEM((6,) + vector, f32),
            pltpu.VMEM((4,) + vector, f32),
            DMA((2, parts)),
            DMA((2, parts)),
            DMA((2, parts)),
            DMA((2, parts)),
            DMA((2, 3, parts)),
            DMA((2, 3, parts)),
            DMA((2, 4)),
            DMA((2,)),
            DMA((2, 6)),
            DMA((2,)),
            DMA((2, parts)),
            DMA((2, 3, parts)),
        ],
        compiler_params=params(collective_id=6, has_side_effects=True),
        cost_estimate=cost(0, 300 * 2**20),
        name="end",
    )(*inputs)


def after(value, *tokens):
    return lax.optimization_barrier((value, tokens))[0]


class Order:
    def __init__(self):
        self.token = None
        self.wanted = []

    def __call__(self, call, *args, first=0):
        args = list(args)
        if self.token is not None:
            args[first] = after(args[first], self.token, *self.wanted)
            self.wanted = []
        out = call(*args)
        self.token = out
        while isinstance(self.token, (list, tuple)):
            self.token = self.token[0]
        return out

    def hold(self, value):
        return after(value, self.token)

    def want(self, value):
        self.wanted.append(value)
        return value


class Net:
    def __init__(self, n_dp, n_head):
        self.n_dp, self.n = n_dp, n_head
        self.own = lax.axis_index("dp").astype(jnp.int32)
        self.z = lax.axis_index("head").astype(jnp.int32)
        self.lo = self.own % n_head
        self.fast = n_dp == BLOCKS and n_head == GROUPS
        core_zero = [2, 4]
        self.one_way = [(i, i ^ core_zero[i % 2]) for i in range(n_dp)]
        self.other_way = [(i, i ^ core_zero[1 - i % 2]) for i in range(n_dp)]
        self.core = [(i, i ^ 1) for i in range(n_dp)]
        ends = [jnp.int32(0), self.lo]
        self.all_rows = jnp.stack([jnp.int32(i) for i in range(BLOCKS)] + ends)
        if self.fast:
            step = jnp.where(self.own % 2 == 0, 2, 4).astype(jnp.int32)
            mine = [jnp.int32(0), step, 6 - step, jnp.int32(6)]
            theirs = [jnp.int32(0), 6 - step, step, jnp.int32(6)]
            ends = [self.z, self.lo]
            self.even = jnp.stack([self.own ^ v for v in mine] + ends)
            self.odd = jnp.stack([self.own ^ v ^ 1 for v in theirs] + ends)
            self.pieces = jnp.concatenate([self.even[:4], self.odd])

    def shift(self, value, k):
        n = self.n
        if k % n == 0:
            return value
        pairs = [(i, (i // n) * n + (i + k) % n) for i in range(self.n_dp)]
        return lax.ppermute(value, "dp", pairs)

    def spin(self, value, k):
        n = self.n
        return lax.ppermute(value, "head", [(i, (i + k) % n) for i in range(n)])

    def gather(self, shard):
        return lax.all_gather(shard, ("dp", "head")).reshape(BLOCKS, GROUPS, LANES, -1)

    def gather_any(self, qkv, out, up, down):
        qkv = lax.all_gather(qkv, "head", axis=2, tiled=True)
        qkv = lax.all_gather(qkv, "dp", axis=1, tiled=True).transpose(1, 0, 2).reshape(D, 3 * D)
        up = lax.all_gather(up, "head", axis=1, tiled=True)
        up = lax.all_gather(up, "dp", axis=0, tiled=True)
        out, down = [
            lax.all_gather(lax.all_gather(v, "head", axis=0, tiled=True), "dp", axis=1, tiled=True)
            for v in (out, down)
        ]

        def blocks(*parts):
            cut = [v.reshape(BLOCKS, LANES, GROUPS, -1) for v in parts]
            return jnp.concatenate(cut, axis=3).transpose(0, 2, 1, 3)

        heads = [qkv[:, c * D : (c + 1) * D] for c in range(3)]
        return blocks(*heads, out.T), blocks(up, down.T)

    def scatter(self, full, widths):
        columns = full.shape[3]
        if self.fast:
            full = full.reshape(BLOCKS * GROUPS, LANES, columns)
        else:
            full = full.transpose(0, 2, 1, 3).reshape(D, GROUPS, columns)
            parts, at = [], 0
            for w in widths:
                part = full[:, :, at : at + w].reshape(D, self.n, GROUPS * w // self.n)
                parts.append(part)
                at += w
            full = jnp.concatenate(parts, axis=2)
            full = full.reshape(self.n_dp, D // self.n_dp, self.n, -1).transpose(0, 2, 1, 3)
            full = full.reshape(self.n_dp * self.n, D // self.n_dp, -1)
        mine = lax.psum_scatter(full, ("dp", "head"), scatter_dimension=0, tiled=False)
        return mine.astype(f32)


    def add_pair(self, keep, pair):
        add = lambda i: (keep[i].astype(f32) + pair[i].astype(f32)).astype(bf16)
        return add(0), add(1)

    def add_last(self, mine, last):
        return (mine.astype(f32) + last.astype(f32)).astype(bf16)

    def turn(self, k):
        n = self.n
        pairs = []
        for hi in range(self.n_dp // n):
            for lo in range(n):
                for z in range(n):
                    pairs.append(((hi * n + lo) * n + z, (hi * n + (z + k) % n) * n + lo))
        return pairs

    def rows_in(self, array):
        n = self.n
        tokens = array.shape[0] // n
        low = array.astype(bf16).reshape(n, tokens, array.shape[1])
        got = []
        for k in range(n):
            piece = lax.dynamic_index_in_dim(low, (self.z + k) % n, 0, False)
            got.append(lax.ppermute(piece, ("dp", "head"), self.turn(k)))
        return got

    def rows_in_end(self, got):
        stacked = jnp.take(jnp.stack(got), (self.lo - jnp.arange(self.n)) % self.n, axis=0)
        return stacked.transpose(1, 0, 2).reshape(got[0].shape[0], D)

    def rows_out(self, array):
        n = self.n
        width = D // n
        low = array.astype(bf16)
        got = []
        for k in range(n):
            piece = lax.dynamic_slice_in_dim(low, ((self.lo - k) % n) * width, width, 1)
            got.append(lax.ppermute(piece, ("dp", "head"), [(b, a) for a, b in self.turn(k)]))
        return got

    def rows_out_end(self, got):
        stacked = jnp.take(jnp.stack(got), (jnp.arange(self.n) - self.z) % self.n, axis=0)
        return stacked.reshape(-1, got[0].shape[1]).astype(f32)


def local(
    n_dp,
    n_head,
    stream_in,
    qkv_weight,
    out_weight,
    up_weight,
    down_weight,
    norm_gains,
    norm_shifts,
    hidden_gains,
    hidden_shifts,
    buckets,
    valid_mask,
    cotangent,
):
    net = Net(n_dp, n_head)
    n = n_head
    layers = qkv_weight.shape[0]
    tokens = LONG // n
    order = Order()

    flags = jnp.concatenate([valid_mask, buckets])
    vectors = [
        v.reshape(layers, -1) for v in (norm_gains, norm_shifts, hidden_gains, hidden_shifts)
    ]
    packed = jnp.concatenate(vectors, axis=1)
    narrow, broad = [None] * layers, [None] * layers
    if net.fast:
        small, large = pack_call(qkv_weight, out_weight, up_weight, down_weight)
        rows = stream_in.astype(bf16).reshape(n, tokens, D // n)
        flags = jnp.pad(flags, (0, -flags.shape[0] % 1024)).reshape(-1, LANES)
        vector = packed.reshape(-1, LANES)
        started = order(start_call, small[:1], rows, vector, flags, first=1)
        (narrow[0],), stream, _, packed, flags = started
        flags = flags.reshape(-1)
        broad[0] = net.gather(order.hold(large[0]))
    else:
        for l in range(layers):
            narrow[l], broad[l] = net.gather_any(
                qkv_weight[l], out_weight[l], up_weight[l], down_weight[l]
            )
        stream = net.rows_in_end(net.rows_in(stream_in))
        flags = lax.ppermute(flags, ("dp", "head"), net.turn(0))
        packed = lax.all_gather(packed.reshape(-1, LANES), "head")
    slab_mask = flags[:LONG].reshape(n, tokens)
    bucket = flags[LONG]
    rel_blocks = (net.lo - jnp.arange(n)) % n
    rel_mask = jnp.take(slab_mask, rel_blocks, axis=0)
    lane = jnp.arange(LANES)[None, None, :] == 0
    aux = jnp.where((rel_mask[:, :, None] == 0) & lane, MASKED, 0.0).astype(bf16)
    one = jnp.broadcast_to((jnp.arange(LANES)[None, :] == 0), (tokens, LANES)).astype(bf16)
    sequence = jnp.where(bucket == 1, 0, (rel_blocks * tokens) // SHORT)
    alive = jnp.sum(rel_mask, axis=1) > 0
    need = ((sequence[:, None] == sequence[None, :]) & alive[None, :]).astype(jnp.int32)
    need = need.reshape(n * n)
    valid = lax.dynamic_index_in_dim(slab_mask, net.lo, 0, False).astype(f32)[:, None]

    low = stream
    stream = stream.astype(f32)
    halves = lambda v, axis: jnp.split(v, 2, axis=axis)
    cot = cotangent.astype(bf16).reshape(n, tokens, D // n)
    kept = []
    usage = []
    idents = iter(range(10, 64))
    for l in range(layers):
        ahead = net.fast and l + 1 < layers
        parts, _ = order(qkv_call, n, next(idents), [], l, low, packed, narrow[l], first=4)
        parts = [parts[0]] + [[net.shift(v, k) for k, v in enumerate(p)] for p in parts[1:]]
        att, lse = [], []
        for p in parts:
            outs = order(attn_call, n, need, aux, one, p, first=2)
            att.append(outs[0])
            lse.append(outs[1])
        if ahead:
            broad[l + 1] = net.gather(order.hold(large[l + 1]))
        rows_job = []
        if net.fast and l + 1 == layers:
            rows_job = [Turn(half, False) for half in halves(cot, 1)]
        mid, rows, use_branch, *late = order(
            proj_call, n, next(idents), rows_job[1:], l, valid, stream, packed, narrow[l], att,
            first=5,
        )
        if ahead:
            (narrow[l + 1],) = order(gather_call, [order.hold(small[l + 1])], first=0)
        slope, hat, normed, low_mid, rstd, stream, next_low, use_rest, *early = order(
            ffn_call, n, next(idents), rows_job[:1], l, valid, mid, packed, broad[l], first=5
        )
        if rows_job:
            grad = jnp.concatenate(early + late, axis=0).astype(f32)
        usage += [use_branch, use_rest]
        kept.append((low, parts, att, lse, rows, slope, hat, normed, low_mid, rstd))
        low = next_low

    if not net.fast:
        grad = net.rows_in_end(net.rows_in(cotangent)).astype(f32)
    if not net.fast:
        grad = net.rows_in_end(net.rows_in(cotangent)).astype(f32)
    units = BLOCKS // n
    ffn_grads, head_grads = [None] * layers, [None] * layers
    vectors, tops = [None] * layers, []

    for l in reversed(range(layers)):
        low, parts, att, lse, rows, slope, hat, normed, low_mid, rstd = kept[l]
        more = net.fast and l + 1 < layers
        last = net.fast and l + 1 == layers
        jobs = []
        if last:
            jobs = [Turn(half, True) for half in halves(stream.astype(bf16), 0)]
        if more:
            ffn_mine, sent = net.add_pair(order.hold(ffn_keep), ffn_pair)
            jobs = [Hop(head_odd, "mate"), Hop(sent, "first")]
        dhid, grad_turned, ffn_turned, grad, hgrads, grads2, *extra = order(
            ffn_back_call, n, next(idents), jobs[:1] if last else jobs, l, grad, hat, slope, rstd,
            low_mid, packed, broad[l], first=4,
        )
        ffn_args = (ffn_turned, grad_turned, dhid, normed)
        if net.fast:
            moved = extra
            if more:
                ups = net.add_last(ffn_mine[..., :WIDE], extra[1][..., :WIDE])
                downs = net.add_last(ffn_mine[..., WIDE:], extra[1][..., WIDE:])
                head_keep, send = order(
                    head_grad_call, n, 4, net.even, *head_args, extra[0], first=3
                )
                head_pair = lax.ppermute(order.hold(send), "dp", net.other_way)
            (odd,) = order(ffn_grad_call, 4, net.odd, *ffn_args, first=2)
            jobs = [Hop(odd, "mate")] + ([Near(ups)] if more else jobs[1:])
        else:
            (full,) = order(ffn_grad_call, BLOCKS, net.all_rows, *ffn_args, first=2)
            ffn_grads[l] = net.scatter(full, (WIDE, WIDE))
        res = order(
            proj_back_call, n, next(idents), jobs, l, grad, packed, narrow[l], rows, first=4
        )
        datt, (out_turned, normed_mid, grads1, *extra) = res[:units], res[units:]
        if net.fast:
            if last:
                stream_out = jnp.concatenate([moved[0], extra[1]], axis=1)
                stream_out = stream_out.reshape(LONG, D // n).astype(f32)
            if more:
                unear = extra[1]
                head_mine, sent = net.add_pair(order.hold(head_keep), head_pair)
                head_last = lax.ppermute(sent, "dp", net.one_way)
                order.want(sent)
            ffn_keep, send = order(ffn_grad_call, 4, net.even, *ffn_args, extra[0], first=2)
            ffn_pair = lax.ppermute(order.hold(send), "dp", net.other_way)
        dparts, ready = [], []
        for u in range(units):
            ready += [net.shift(v, -k) for k, v in enumerate(dparts)]
            dparts = order(
                attn_back_call, n, need, aux, one, parts[u], att[u], datt[u], lse[u], first=2
            )
            if more and u == 0:
                head_sum = order.want(net.add_last(order.hold(head_mine), head_last))
        jobs = [Near(downs), Near(head_sum)] if more else []
        dlast, grad, in_turned, grads0, grad_low, *extra = order(
            qkv_back_call, n, next(idents), jobs, l, grad, low, packed, narrow[l], ready, dparts,
            first=4,
        )
        head_args = (in_turned, out_turned, ready + dlast, normed_mid)
        vectors[l] = [grads0, grads1, grads2, hgrads]
        if net.fast:
            if more:
                tops = [head_sum, extra[1], ups, unear, downs, extra[0]] + tops
            if l:
                (head_odd,) = order(head_grad_call, n, 4, net.odd, *head_args, first=3)
            else:
                (full,) = order(head_grad_call, n, BLOCKS, net.pieces, *head_args, first=3)
        else:
            (full,) = order(head_grad_call, n, BLOCKS, net.all_rows, *head_args, first=3)
            head_grads[l] = net.scatter(full, (HEADS,) * 4)
    vectors = [v for part in vectors for v in part]
    if net.fast:
        ffn_mine, sent = net.add_pair(order.hold(ffn_keep), ffn_pair)
        moved, qkv_grad, out_grad, up_grad, down_grad, summed = order(
            end_call, grad_low, full, ffn_mine, sent, valid, tops, vectors, usage
        )
        stream_grad = moved.reshape(LONG, D // n).astype(f32)
        stacked = [qkv_grad, out_grad, up_grad, down_grad]
        norms = summed[: 28 * layers].reshape(layers, 28, LANES)
        hids = norms[:, 12:].reshape(layers, 2, FF // n)
        norms = norms[:, :12].reshape(layers, 2, 3, D // n)
        totals = jnp.sum(summed[28 * layers : 31 * layers + 1], axis=1)
        usage_rms = jnp.sqrt(totals[:-1] / totals[-1]).reshape(layers, 3)
    else:
        stream_out = net.rows_out_end(net.rows_out(stream))
        stream_grad = net.rows_out_end(net.rows_out(grad))
        norms = [jnp.sum(jnp.stack(vectors[4 * l : 4 * l + 3], 1), axis=2) for l in range(layers)]
        norms = lax.psum(jnp.stack(norms), ("dp", "head"))
        hids = [jnp.sum(vectors[4 * l + 3], axis=2).reshape(2, FF) for l in range(layers)]
        hids = lax.psum(jnp.stack(hids), ("dp", "head"))
        share = lambda v: lax.dynamic_slice_in_dim(
            v, net.z * (v.shape[-1] // n), v.shape[-1] // n, v.ndim - 1
        )
        norms, hids = share(norms), share(hids)
        totals = []
        for l in range(layers):
            branch, rest = usage[2 * l : 2 * l + 2]
            totals += [jnp.sum(branch), jnp.sum(rest[0]), jnp.sum(rest[1])]
        totals = lax.psum(jnp.stack(totals + [jnp.sum(valid) * D]), ("dp", "head"))
        usage_rms = jnp.sqrt(totals[:-1] / totals[-1]).reshape(layers, 3)
        weight_grads = []
        for l in range(layers):
            heads = head_grads[l]
            width = heads.shape[1] // 4
            qkv = heads[:, : 3 * width].reshape(-1, 3, width).transpose(1, 0, 2)
            half = ffn_grads[l].shape[1] // 2
            weight_grads.append(
                (qkv, heads[:, 3 * width :].T, ffn_grads[l][:, :half], ffn_grads[l][:, half:].T)
            )
        stacked = [jnp.stack([weight_grads[l][k] for l in range(layers)]) for k in range(4)]
    gains_grad, shifts_grad = norms[:, 0], norms[:, 1]
    hidden_gains_grad, hidden_shifts_grad = hids[:, 0], hids[:, 1]
    return (
        stream_out,
        stream_grad,
        stacked[0],
        stacked[1],
        stacked[2],
        stacked[3],
        gains_grad,
        shifts_grad,
        hidden_gains_grad,
        hidden_shifts_grad,
        usage_rms,
    )


def solution(mesh):
    n_dp, n_head = mesh.shape["dp"], mesh.shape["head"]

    def run(*args):
        return local(n_dp, n_head, *args)

    return jax.shard_map(
        run,
        mesh=mesh,
        in_specs=(
            P("dp", "head"),
            P(None, None, "dp", "head"),
            P(None, "head", "dp"),
            P(None, "dp", "head"),
            P(None, "head", "dp"),
            P(None, None, "head"),
            P(None, None, "head"),
            P(None, "head"),
            P(None, "head"),
            P("dp"),
            P("dp"),
            P("dp", "head"),
        ),
        out_specs=(
            P("dp", "head"),
            P("dp", "head"),
            P(None, None, "dp", "head"),
            P(None, "head", "dp"),
            P(None, "dp", "head"),
            P(None, "head", "dp"),
            P(None, None, "head"),
            P(None, None, "head"),
            P(None, "head"),
            P(None, "head"),
            P(),
        ),
        check_vma=False,
    )
```

```python
import functools
import math

import jax
import jax.numpy as jnp
from jax import lax
from jax.experimental import pallas as pl
from jax.experimental.pallas import tpu as pltpu
from jax.sharding import PartitionSpec as P

D = 1024
FF = 4096
LONG = 2048
SHORT = 512
DH = 64
LANES = 128
BLOCKS = D // LANES
GROUPS = 4
WIDE = FF // GROUPS
HEADS = D // GROUPS
NARROW = 4 * HEADS
BROAD = 2 * WIDE
EPS = 1e-05
MASKED = -1000000000.0
ROWS = 256
CHUNK = 256
VMEM_BYTES = 60 * 1024 * 1024
MESH = pl.DeviceIdType.MESH

f32 = jnp.float32
bf16 = jnp.bfloat16


def dot(a, b):
    return jnp.dot(a, b, preferred_element_type=f32)


def dot_nt(a, b):
    return lax.dot_general(a, b, (((1,), (1,)), ((), ())), preferred_element_type=f32)


def flip(a):
    return jnp.transpose(a.astype(f32), (1, 0)).astype(a.dtype)


def row_loop(total, step, body):
    def advance(i, carry):
        body(pl.ds(pl.multiple_of(i * step, step), step))
        return carry

    lax.fori_loop(0, total // step, advance, 0)


def sum_lanes(value):
    return jnp.sum(value, axis=1, keepdims=True)


def fold_lanes(value):
    total = value[:, :LANES]
    for i in range(1, value.shape[1] // LANES):
        total = total + value[:, i * LANES : (i + 1) * LANES]
    return total


def fold_rows(value):
    total = value[:8]
    for i in range(1, value.shape[0] // 8):
        total = total + value[i * 8 : (i + 1) * 8]
    return total


def row_stats(value):
    mean = sum_lanes(value) / D
    centred = value - mean
    rstd = lax.rsqrt(sum_lanes(centred * centred) / D + EPS)
    return centred * rstd, rstd


def norm_back(dy, hat, rstd, gain):
    dx = dy * gain
    first = sum_lanes(dx) / D
    cross = sum_lanes(dx * hat) / D
    return rstd * (dx - first - hat * cross)


class Vectors:
    def __init__(self, n, layer, ref):
        self.n, self.ref = n, ref
        self.few, self.many = BLOCKS // n, 4 * BLOCKS // n
        self.at = layer * (6 * self.few + 2 * self.many)

    def rows(self, z, first, count):
        return [self.ref[z, first + p : first + p + 1, :] for p in range(count)]

    def norm(self, kind, which):
        first = self.at + (3 * kind + which) * self.few
        parts = [v for z in range(self.n) for v in self.rows(z, first, self.few)]
        return jnp.concatenate(parts, axis=1)

    def hidden(self, kind, group):
        first = self.at + 6 * self.few + kind * self.many
        share = self.n // GROUPS
        parts = [v for i in range(share) for v in self.rows(group * share + i, first, self.many)]
        return jnp.concatenate(parts, axis=1)


def params(**kw):
    return pltpu.CompilerParams(vmem_limit_bytes=VMEM_BYTES, **kw)


def cost(flops, size, trans=0):
    return pl.CostEstimate(flops=int(flops), bytes_accessed=int(size), transcendentals=int(trans))


def whole(shape):
    zeros = (0,) * len(shape)
    return pl.BlockSpec(shape, lambda *_: zeros)


def shape(dims, kind):
    return jax.ShapeDtypeStruct(dims, kind)


VM = pl.BlockSpec(memory_space=pltpu.VMEM)
HB = pl.BlockSpec(memory_space=pl.ANY)
DMA = pltpu.SemaphoreType.DMA


def group_place(n):
    dp = lax.axis_index("dp")
    lo = lax.rem(dp, n)
    return dp - lo, lo


def group_send(n, k, source, target, send_sem, recv_sem):
    base, lo = group_place(n)
    return pltpu.make_async_remote_copy(
        src_ref=source,
        dst_ref=target,
        send_sem=send_sem,
        recv_sem=recv_sem,
        device_id={"dp": base + lax.rem(lo + k + n, n)},
        device_id_type=MESH,
    )


def order_of(n):
    return [k for k in (n // 2, *range(1, n // 2), *range(n // 2 + 1, n)) if k]


def head_columns(n, k):
    _, lo = group_place(n)
    unit = lax.rem(lo + k + n, n) * (BLOCKS // n)
    if n == GROUPS:
        return lax.rem(lo + k + n, n), 0
    return unit // 2, pl.multiple_of(lax.rem(unit, 2) * LANES, LANES)


class Place:
    def __init__(self):
        dp = lax.axis_index("dp")
        self.z = lax.axis_index("head")
        self.lo = lax.rem(dp, GROUPS)
        core = lax.rem(dp, 2)
        bit_x = lax.rem(dp // 2, 2)
        bit_y = lax.rem(dp // 4, 2)
        by_x = dp + 2 - 4 * bit_x
        by_y = dp + 4 - 8 * bit_y
        self.dp, self.core, self.bit_x = dp, core, bit_x
        self.by_x, self.by_y = by_x, by_y
        self.first = by_x * (1 - core) + by_y * core
        self.second = by_y * (1 - core) + by_x * core
        self.both = by_x + by_y - dp
        self.mate = dp + 1 - 2 * core

    def partner(self, way):
        return {"mate": self.mate, "first": self.first, "second": self.second}[way]

    def group(self, p):
        one, two = 1 - 2 * lax.rem(self.z, 2), 2 - 4 * (self.z // 2)
        return self.z + (0, two, one, one + two)[p]

    def others(self):
        return [{"head": lax.rem(self.z + k, GROUPS)} for k in range(1, GROUPS)]


def unlike(a, b):
    return jnp.where(a == b, 0, 1)


class Hop:
    aliases = {}

    def __init__(self, array, way):
        self.arrays, self.way = [array], way
        self.outs = [jax.ShapeDtypeStruct(array.shape, array.dtype)]
        self.sems = [DMA((2,))]

    def device(self, at):
        if self.way == "z":
            return {"head": at.group(1)}
        return {"dp": at.partner(self.way)}

    def peers(self, at):
        return [self.device(at)], [], 1

    def copy(self, at, ins, outs, sems):
        return pltpu.make_async_remote_copy(
            src_ref=ins[0],
            dst_ref=outs[0],
            send_sem=sems[0].at[0],
            recv_sem=sems[0].at[1],
            device_id=self.device(at),
            device_id_type=MESH,
        )

    def start(self, *args):
        self.copy(*args).start()

    def middle(self, *args):
        pass

    def finish(self, *args):
        self.copy(*args).wait()


class Near:
    aliases = {}

    def __init__(self, array):
        self.arrays = [array]
        self.outs = [jax.ShapeDtypeStruct((GROUPS - 1,) + array.shape[1:], array.dtype)]
        self.sems = [DMA((2, GROUPS - 1))]

    def peers(self, at):
        return at.others(), [], GROUPS - 1

    def copies(self, at, ins, outs, sems):
        return [
            pltpu.make_async_remote_copy(
                src_ref=ins[0].at[k],
                dst_ref=outs[0].at[k - 1],
                send_sem=sems[0].at[0, k - 1],
                recv_sem=sems[0].at[1, k - 1],
                device_id={"head": at.group(k)},
                device_id_type=MESH,
            )
            for k in (1, 2, 3)
        ]

    def start(self, *args):
        for copy in self.copies(*args):
            copy.start()

    def middle(self, *args):
        pass

    def finish(self, *args):
        for copy in self.copies(*args):
            copy.wait()


class Turn:
    def __init__(self, array, back, half, into=None):
        self.arrays, self.back = [array], back
        self.aliases = {}
        if into is not None:
            self.arrays.append(into)
            self.aliases = {1: 0}
        if back:
            tokens, wide = array.shape[0], array.shape[1] // GROUPS
            out = (GROUPS, tokens, wide)
        else:
            tokens, wide = array.shape[1:]
            out = (tokens, GROUPS * wide)
        self.wide = wide
        self.rows = pl.ds(half * (tokens // 2), tokens // 2)
        self.outs = [jax.ShapeDtypeStruct(out, array.dtype)]
        self.sems = [DMA((2, GROUPS)), DMA]

    def many(self, at):
        return [(at.dp - at.lo + t, at.lo) for t in range(GROUPS)]

    def one(self, at):
        return [(at.dp - at.lo + at.z, g) for g in range(GROUPS)]

    def peers(self, at):
        from_ = self.many(at) if self.back else self.one(at)
        return [], from_, GROUPS - 1 + unlike(at.z, at.lo)

    def each(self, op, at, ins, outs, sems):
        targets = self.one(at) if self.back else self.many(at)
        for i, (dp, z) in enumerate(targets):
            if self.back:
                source = ins[0].at[self.rows, pl.ds(i * self.wide, self.wide)]
                target, slot = outs[0].at[at.lo, self.rows], at.lo
            else:
                source = ins[0].at[i, self.rows]
                column = pl.multiple_of(at.z * self.wide, self.wide)
                target, slot = outs[0].at[self.rows, pl.ds(column, self.wide)], at.z

            def remote(i=i, dp=dp, z=z, source=source, target=target, slot=slot):
                copy = pltpu.make_async_remote_copy(
                    src_ref=source,
                    dst_ref=target,
                    send_sem=sems[0].at[0, i],
                    recv_sem=sems[0].at[1, slot],
                    device_id={"dp": dp, "head": z},
                    device_id_type=MESH,
                )
                copy.start() if op == "start" else copy.wait_send()

            def inside(source=source, target=target):
                copy = pltpu.make_async_copy(source, target, sems[1])
                copy.start() if op == "start" else copy.wait()

            away = (dp != at.dp) | (z != at.z)
            pl.when(away)(remote)
            pl.when(jnp.logical_not(away))(inside)

    def start(self, *args):
        self.each("start", *args)

    def middle(self, *args):
        pass

    def finish(self, at, ins, outs, sems):
        self.each("wait", at, ins, outs, sems)
        sources = self.many(at) if self.back else self.one(at)
        for slot, (dp, z) in enumerate(sources):

            @pl.when((dp != at.dp) | (z != at.z))
            def _(slot=slot):
                if self.back:
                    spot = outs[0].at[slot, self.rows]
                else:
                    spot = outs[0].at[self.rows, pl.ds(slot * self.wide, self.wide)]
                pltpu.make_async_remote_copy(
                    src_ref=spot,
                    dst_ref=spot,
                    send_sem=sems[0].at[0, 0],
                    recv_sem=sems[0].at[1, slot],
                    device_id={"dp": at.mate},
                    device_id_type=MESH,
                ).wait_recv()


class Host:
    def __init__(self, n, parts):
        self.n, self.parts, self.turns = n, parts, 0
        self.at = Place() if parts else None

    def barrier(self, group=True):
        n = self.n
        sem = pltpu.get_barrier_semaphore()
        count = 0
        if group:
            base, lo = group_place(n)
            for k in range(1, n):
                pl.semaphore_signal(
                    sem, inc=1, device_id={"dp": base + lax.rem(lo + k, n)}, device_id_type=MESH
                )
            count = n - 1
        for job, *_ in self.parts:
            plain, pairs, more = job.peers(self.at)
            for device in plain:
                pl.semaphore_signal(sem, inc=1, device_id=device, device_id_type=MESH)
            for dp, z in pairs:

                @pl.when((dp != self.at.dp) | (z != self.at.z))
                def _(dp=dp, z=z):
                    pl.semaphore_signal(
                        sem, inc=1, device_id={"dp": dp, "head": z}, device_id_type=MESH
                    )

            count = count + more
        pl.semaphore_wait(sem, count)

    def start(self):
        for job, *refs in self.parts:
            job.start(self.at, *refs)

    def middle(self):
        for job, *refs in self.parts:
            job.middle(self.at, *refs)

    def tick(self):
        for job, *refs in self.parts:
            if isinstance(job, Everywhere) and self.turns < len(job.chunks) + 3:
                job.tick(self.turns, self.at, *refs)
        self.turns += 1

    def tick_at(self, step):
        for job, *refs in self.parts:
            if isinstance(job, Everywhere):
                for t in range(len(job.chunks) + 3):
                    pl.when(step == t)(lambda t=t, job=job, refs=refs: job.tick(t, self.at, *refs))
        self.turns = 64

    def finish(self):
        while any(isinstance(v[0], Everywhere) for v in self.parts) and self.turns < 64:
            self.tick()
        for job, *refs in self.parts:
            job.finish(self.at, *refs)


def plain_call(
    body, n, name, ident, inputs, in_specs, out_shape, out_specs, scratch, flops, jobs, grid=()
):
    return list(
        pl.pallas_call(
            lambda *refs: body(Host(n, []), *refs),
            out_shape=out_shape,
            grid=grid,
            in_specs=in_specs,
            out_specs=out_specs,
            scratch_shapes=scratch,
            compiler_params=params(),
            cost_estimate=cost(flops, 10 * 2**20),
            name=name,
        )(*inputs)
    )


def remote_call(
    body, n, name, ident, inputs, in_specs, out_shape, out_specs, scratch, flops, jobs, grid=()
):
    job_in = [v for job in jobs for v in job.arrays]
    job_out = [v for job in jobs for v in job.outs]
    job_sems = [v for job in jobs for v in job.sems]
    aliases = {}
    i, o = len(inputs), len(out_shape)
    for job in jobs:
        aliases.update({i + a: o + b for a, b in job.aliases.items()})
        i, o = i + len(job.arrays), o + len(job.outs)

    def kernel(*refs):
        refs = list(refs)

        def take(count):
            taken = refs[:count]
            del refs[:count]
            return taken

        own_in, extra_in = take(len(inputs)), take(len(job_in))
        own_out, extra_out = take(len(out_shape)), take(len(job_out))
        own_scratch, extra_sems = take(len(scratch)), take(len(job_sems))
        parts = []
        for job in jobs:
            sizes = (len(job.arrays), len(job.outs), len(job.sems))
            lists = (extra_in, extra_out, extra_sems)
            part = [job]
            for values, size in zip(lists, sizes):
                part.append(values[:size])
                del values[:size]
            parts.append(part)
        body(Host(n, parts), *own_in, *own_out, *own_scratch)

    res = pl.pallas_call(
        kernel,
        out_shape=list(out_shape) + job_out,
        grid=grid,
        in_specs=list(in_specs) + [HB] * len(job_in),
        out_specs=list(out_specs) + [HB] * len(job_out),
        scratch_shapes=list(scratch) + job_sems,
        input_output_aliases=aliases,
        compiler_params=params(collective_id=ident, has_side_effects=True),
        cost_estimate=cost(flops, 10 * 2**20),
        name=name,
    )(*inputs, *job_in)
    return list(res)


def qkv_kernel(layer, host, low, packed, weight, *refs):
    n = host.n
    vectors = Vectors(n, layer, packed)
    gain, shift = vectors.norm(0, 0), vectors.norm(1, 0)
    outs, (xs, wide, send, wsem, ssem, rsem, lsem) = refs[:-7], refs[-7:]
    tokens = low.shape[0]
    units = BLOCKS // n
    width = units * LANES
    steps = order_of(n) + [0]

    def fetch(i):
        group, offset = head_columns(n, steps[i])
        return [
            pltpu.make_async_copy(
                weight.at[:, group, :, pl.ds(c * HEADS + offset, width)],
                wide.at[i % 2, c],
                wsem.at[i % 2, c],
            )
            for c in range(3)
        ]

    for copy in fetch(0):
        copy.start()

    def body(r):
        hat, _ = row_stats(low[r, :].astype(f32))
        xs[r, :] = (hat * gain + shift).astype(bf16)

    row_loop(tokens, ROWS, body)
    host.barrier()
    host.start()
    copies = []
    for i, k in enumerate(steps):
        if i + 1 < n:
            for copy in fetch(i + 1):
                copy.start()
        for c, copy in enumerate(fetch(i)):
            copy.wait()
            value = dot(xs[...], wide[i % 2, c].reshape(D, width)).astype(bf16)
            send[k, c] = value[:, :LANES]
            for u in range(1, units):
                outs[u * n + k][c] = value[:, u * LANES : (u + 1) * LANES]
        if k:
            copy = group_send(n, k, send.at[k], outs[k], ssem.at[k], rsem.at[k])
        else:
            copy = pltpu.make_async_copy(send.at[0], outs[0], lsem)
        copy.start()
        copies.append(copy)
    host.middle()
    for copy in copies:
        copy.wait()
    host.finish()


def qkv_call(n, ident, jobs, layer, low, packed, weight):
    tokens = low.shape[0]
    units = BLOCKS // n
    block = (3, tokens, LANES)
    res = remote_call(
        functools.partial(qkv_kernel, layer), n, "qkv", ident,
        [low, packed, weight], [VM, VM, HB],
        [jax.ShapeDtypeStruct(block, bf16)] * (n * units), [HB] * n + [VM] * (n * (units - 1)),
        [
            pltpu.VMEM((tokens, D), bf16),
            pltpu.VMEM((2, 3, BLOCKS, LANES, units * LANES), bf16),
            pltpu.VMEM((n,) + block, bf16),
            DMA((2, 3)),
            DMA((n,)),
            DMA((n,)),
            DMA,
        ],
        60 * tokens * D * D, jobs,
    )
    return [res[u * n : (u + 1) * n] for u in range(units)], res[n * units :]


def masks_kernel(n, sc, flags, aux, one, valid, need):
    tokens = aux.shape[1]
    rows = tokens // LANES
    first = lax.broadcasted_iota(jnp.int32, (LANES, LANES), 1) == 0
    one[...] = jnp.where(lax.broadcasted_iota(jnp.int32, one.shape, 1) == 0, 1.0, 0.0).astype(bf16)
    long = jnp.max(flags[LONG // LANES : LONG // LANES + 1, 0:1]) == 1
    alive, sequence = [], []
    for k in range(n):
        place = lax.rem(sc[0] + n - k, n)
        some = jnp.float32(0)
        for i in range(rows):
            row = flags[pl.ds(place * rows + i, 1), :].astype(f32)
            some = jnp.maximum(some, jnp.max(row))
            column = jnp.transpose(jnp.broadcast_to(row, (LANES, LANES)), (1, 0))
            spot = slice(i * LANES, (i + 1) * LANES)
            aux[k, spot, :] = jnp.where(first & (column == 0), MASKED, 0.0).astype(bf16)
            if k == 0:
                valid[spot, :] = column[:, 0:1]
        alive.append(some > 0)
        sequence.append(place * tokens // SHORT)
    for i in range(n):
        for j in range(n):
            joined = long | (sequence[i] == sequence[j])
            need[i * n + j] = jnp.where(joined & alive[j], 1, 0).astype(jnp.int32)


def masks_call(n, lo, flags):
    tokens = LONG // n
    return pl.pallas_call(
        lambda *refs: masks_kernel(n, *refs),
        out_shape=[
            jax.ShapeDtypeStruct((n, tokens, LANES), bf16),
            jax.ShapeDtypeStruct((tokens, LANES), bf16),
            jax.ShapeDtypeStruct((tokens, 1), f32),
            jax.ShapeDtypeStruct((n * n,), jnp.int32),
        ],
        grid_spec=pltpu.PrefetchScalarGridSpec(
            num_scalar_prefetch=1,
            grid=(),
            in_specs=[VM],
            out_specs=[VM, VM, VM, pl.BlockSpec(memory_space=pltpu.SMEM)],
        ),
        compiler_params=params(),
        cost_estimate=cost(0, 2**20),
        name="masks",
    )(lo, flags)


def head_lanes(value, head):
    lane = lax.broadcasted_iota(jnp.int32, value.shape, 1)
    keep = (lane < DH) if head == 0 else (lane >= DH)
    return jnp.where(keep, value, jnp.zeros_like(value))


def attn_kernel(n, need, aux, one, *refs):
    qkv, (outs, lse, kx, vt, qs, top, acc) = refs[:n], refs[n:]
    tokens = aux.shape[1]
    for r in range(n):
        kx[r] = jnp.concatenate([qkv[r][1], aux[r]], axis=1)
        turned = flip(qkv[r][2])
        ones = jnp.ones((16, tokens), bf16)
        vt[r, 0] = jnp.concatenate([turned[:DH], ones], axis=0)
        vt[r, 1] = jnp.concatenate([turned[DH:], ones], axis=0)
        qs[r] = (qkv[r][0].astype(f32) * (1.0 / math.sqrt(DH))).astype(bf16)

    halves = jnp.where(
        lax.broadcasted_iota(jnp.int32, (LANES, LANES), 0) // DH
        == lax.broadcasted_iota(jnp.int32, (LANES, LANES), 1),
        1.0,
        0.0,
    ).astype(bf16)
    reach = jnp.zeros((1, LANES), f32)
    longest = jnp.zeros((1, LANES), f32)
    for r in range(n):
        for which, value in ((0, qs[r]), (1, qkv[r][1])):
            size = jnp.max(dot(value * value, halves), axis=0, keepdims=True)
            if which:
                longest = jnp.maximum(longest, size)
            else:
                reach = jnp.maximum(reach, size)
    bounded = jnp.max(reach * longest) < 70.0 * 70.0

    def each_query(plain, i, carry):
        query = qs[i]
        extended = [jnp.concatenate([head_lanes(query, h), one[...]], axis=1) for h in range(2)]
        top[...] = jnp.zeros_like(top) if plain else jnp.full_like(top, -3e38)
        acc[...] = jnp.zeros_like(acc)

        def each_key(j, inner):
            @pl.when(need[i * n + j] == 1)
            def _():
                if plain:
                    raised = [jnp.exp(dot_nt(kx[j], extended[h])).astype(bf16) for h in range(2)]
                    for h in range(2):
                        acc[h] += dot(vt[j, h], raised[h])
                    return
                for h in range(2):
                    scores = dot_nt(kx[j], extended[h])
                    before = top[h : h + 1]
                    now = jnp.maximum(before, jnp.max(scores, axis=0, keepdims=True))
                    raised = jnp.exp(scores - now).astype(bf16)
                    top[h : h + 1] = now
                    acc[h] = acc[h] * jnp.exp(before - now) + dot(vt[j, h], raised)

            return inner

        lax.fori_loop(0, n, each_key, 0)
        sums = [acc[h][DH : DH + 1] for h in range(2)]
        both = jnp.concatenate([acc[h][:DH] / sums[h] for h in range(2)], axis=0)
        outs[i] = jnp.transpose(both, (1, 0)).astype(bf16)
        for h in range(2):
            lse[i, h : h + 1] = top[h : h + 1] + jnp.log(sums[h])
        return carry

    @pl.when(bounded)
    def _():
        lax.fori_loop(0, n, functools.partial(each_query, True), 0)

    @pl.when(jnp.logical_not(bounded))
    def _():
        lax.fori_loop(0, n, functools.partial(each_query, False), 0)


def unit_call(kernel, n, need, aux, one, arrays, out_shape, scratch, work, name):
    total = n * aux.shape[1]
    return pl.pallas_call(
        lambda *refs: kernel(n, *refs),
        out_shape=out_shape,
        grid_spec=pltpu.PrefetchScalarGridSpec(
            num_scalar_prefetch=1,
            grid=(),
            in_specs=[VM] * (2 + len(arrays)),
            out_specs=[VM] * len(out_shape),
            scratch_shapes=scratch,
        ),
        compiler_params=params(),
        cost_estimate=cost(work * total * total * 512, 8 * 2**20),
        name=name,
    )(need, aux, one, *arrays)


def attn_call(n, need, aux, one, parts):
    tokens = aux.shape[1]
    return unit_call(
        attn_kernel, n, need, aux, one, parts,
        [
            jax.ShapeDtypeStruct((n, tokens, LANES), bf16),
            jax.ShapeDtypeStruct((n, 8, tokens), f32),
        ],
        [
            pltpu.VMEM((n, tokens, 2 * LANES), bf16),
            pltpu.VMEM((n, 2, DH + 16, tokens), bf16),
            pltpu.VMEM((n, tokens, LANES), bf16),
            pltpu.VMEM((8, tokens), f32),
            pltpu.VMEM((2, DH + 16, tokens), f32),
        ],
        12, "attention",
    )


def proj_kernel(layer, host, valid, stream, packed, weight, *refs):
    n = host.n
    vectors = Vectors(n, layer, packed)
    gain, shift = vectors.norm(0, 1), vectors.norm(1, 1)
    tokens = stream.shape[0]
    units = BLOCKS // n
    att, (mid, rows, use, xs, rx, ssem, rsem, lsem) = refs[:units], refs[units:]
    host.barrier()
    copies = [
        group_send(n, -k, att[u].at[k], rx.at[k, u], ssem.at[u, k], rsem.at[u, k])
        for k in order_of(n)
        for u in range(units)
    ]
    copies += [pltpu.make_async_copy(att[u].at[0], rx.at[0, u], lsem.at[u]) for u in range(units)]
    for copy in copies:
        copy.start()
    host.start()
    host.tick()
    for copy in copies:
        copy.wait()
    host.tick()
    _, lo = group_place(n)
    for k in range(n):
        first = lax.rem(lo + k, n) * (units * LANES)
        for u in range(units):
            at = pl.multiple_of(first + u * LANES, LANES)
            rows[:, pl.ds(at, LANES)] = rx[k, u]

    def body(r):
        hat, _ = row_stats(rows[r, :].astype(f32))
        xs[r, :] = (hat * gain + shift).astype(bf16)

    row_loop(tokens, ROWS, body)
    host.tick()
    branch = None
    for g in range(GROUPS):
        term = dot_nt(xs[:, g * HEADS : (g + 1) * HEADS], weight[:, g].reshape(D, HEADS))
        branch = term if branch is None else branch + term
    mid[...] = branch
    host.tick()
    use[...] = jnp.zeros_like(use)

    def finish(r):
        part = mid[r, :]
        use[...] += fold_rows(valid[r, :] * part * part)
        mid[r, :] = stream[r, :].astype(f32) + part

    row_loop(tokens, ROWS, finish)
    host.middle()
    host.finish()


def proj_call(n, ident, jobs, layer, valid, stream, packed, weight, att):
    tokens = stream.shape[0]
    units = BLOCKS // n
    flat = whole(stream.shape)
    return remote_call(
        functools.partial(proj_kernel, layer), n, "projection", ident,
        [valid, stream, packed, weight, *att],
        [whole(v.shape) for v in (valid, stream, packed)]
        + [pl.BlockSpec((BLOCKS, GROUPS, LANES, HEADS), lambda i: (0, 0, 0, 3))]
        + [whole(v.shape) for v in att],
        [
            jax.ShapeDtypeStruct(stream.shape, f32),
            jax.ShapeDtypeStruct(stream.shape, bf16),
            jax.ShapeDtypeStruct((8, D), f32),
        ],
        [flat, flat, whole((8, D))],
        [
            pltpu.VMEM((tokens, D), bf16),
            pltpu.VMEM((n, units, tokens, LANES), bf16),
            DMA((units, n)),
            DMA((units, n)),
            DMA((units,)),
        ],
        30 * tokens * D * D, jobs, grid=(1,),
    )


def ffn_kernel(
    layer, host, valid, mid, packed, weight,
    slope, hat, normed, low_mid, rstd_out, stream, low, use,
    xs, act, mean, buf, acc,
):
    step = pl.program_id(0)
    tokens = mid.shape[0]
    vectors = Vectors(host.n, layer, packed)

    @pl.when(step == 0)
    def _():
        gain, shift = vectors.norm(0, 2), vectors.norm(1, 2)
        use[...] = jnp.zeros_like(use)

        def body(r):
            raw = mid[r, :].astype(bf16)
            value, _ = row_stats(raw.astype(f32))
            low_mid[r, :] = raw
            xs[r, :] = (value * gain + shift).astype(bf16)

        row_loop(tokens, ROWS, body)
        if host.parts:
            host.barrier(False)
            host.start()

    @pl.when(step < GROUPS)
    def _():
        buf[...] = dot(xs[...], weight[...].reshape(D, WIDE))

        def body(r):
            h = buf[r, :]
            half = 0.5 * (1.0 + lax.erf(h * (1.0 / math.sqrt(2.0))))
            bell = jnp.exp(-0.5 * h * h) * (1.0 / math.sqrt(2.0 * math.pi))
            act[step, r, :] = h * half
            slope[0, r, :] = (half + h * bell).astype(bf16)

        row_loop(tokens, CHUNK, body)

    @pl.when(step == GROUPS)
    def _():
        acc[...] = jnp.zeros_like(acc)

        def body(r):
            blocks = [act[g, r, :] for g in range(GROUPS)]
            total = sum_lanes(sum(fold_lanes(b) for b in blocks)) / FF
            square = sum(fold_lanes((b - total) * (b - total)) for b in blocks)
            rstd = lax.rsqrt(sum_lanes(square) / FF + EPS)
            mean[r, :] = jnp.broadcast_to(total, (CHUNK, LANES))
            rstd_out[r, :] = jnp.broadcast_to(rstd, (CHUNK, LANES))

        row_loop(tokens, CHUNK, body)

    @pl.when(step >= GROUPS)
    def _():
        g = step - GROUPS
        hgain, hshift = vectors.hidden(0, g), vectors.hidden(1, g)

        def body(r):
            value = (act[g, r, :] - mean[r, 0:1]) * rstd_out[r, 0:1]
            hat[0, r, :] = value.astype(bf16)
            normed[0, r, :] = (value * hgain + hshift).astype(bf16)

        row_loop(tokens, CHUNK, body)
        acc[...] += dot_nt(normed[0], weight[...].reshape(D, WIDE))

    @pl.when(step == 2 * GROUPS - 1)
    def _():
        def body(r):
            feed = acc[r, :]
            out = mid[r, :] + feed
            keep = valid[r, :]
            stream[r, :] = out
            low[r, :] = out.astype(bf16)
            use[0] += fold_rows(keep * feed * feed)
            use[1] += fold_rows(keep * out * out)

        row_loop(tokens, ROWS, body)

    host.tick_at(step)

    @pl.when(step == 2 * GROUPS - 1)
    def _():
        host.middle()
        host.finish()


def first_half(s):
    return jnp.minimum(s, GROUPS - 1)


def second_half(s):
    return jnp.maximum(s - GROUPS, 0)


def half_specs(tokens):
    early = pl.BlockSpec((1, tokens, WIDE), lambda s: (first_half(s), 0, 0))
    late = pl.BlockSpec((1, tokens, WIDE), lambda s: (second_half(s), 0, 0))
    return early, late


def ffn_call(n, ident, jobs, layer, valid, mid, packed, weight):
    tokens = mid.shape[0]
    big = (GROUPS, tokens, WIDE)
    early, late = half_specs(tokens)
    flat = (tokens, D)
    call = remote_call if jobs else plain_call
    return call(
        functools.partial(ffn_kernel, layer), n, "ffn", ident,
        [valid, mid, packed, weight],
        [whole(v.shape) for v in (valid, mid, packed)]
        + [
            pl.BlockSpec(
                (BLOCKS, 1, LANES, WIDE), lambda s: (0, lax.rem(s, GROUPS), 0, s // GROUPS)
            )
        ],
        [jax.ShapeDtypeStruct(big, bf16)] * 3
        + [
            jax.ShapeDtypeStruct(flat, bf16),
            jax.ShapeDtypeStruct((tokens, LANES), f32),
            jax.ShapeDtypeStruct(flat, f32),
            jax.ShapeDtypeStruct(flat, bf16),
            jax.ShapeDtypeStruct((2, 8, D), f32),
        ],
        [early, late, late]
        + [whole(flat), whole((tokens, LANES)), whole(flat), whole(flat), whole((2, 8, D))],
        [
            pltpu.VMEM(flat, bf16),
            pltpu.VMEM(big, f32),
            pltpu.VMEM((tokens, LANES), f32),
            pltpu.VMEM((tokens, WIDE), f32),
            pltpu.VMEM(flat, f32),
        ],
        16 * tokens * D * FF, jobs, grid=(2 * GROUPS,),
    )


def ffn_back_kernel(
    layer, host, grad, hat, slope, rstd_in, low_mid, packed, weight,
    dhid, grad_turned, normed_turned, grad_out, hgrads, grads,
    gs, dxs, buf, first, cross, acc,
):
    step = pl.program_id(0)
    tokens = grad.shape[0]
    vectors = Vectors(host.n, layer, packed)

    @pl.when(step == 0)
    def _():
        first[...] = jnp.zeros_like(first)
        cross[...] = jnp.zeros_like(cross)
        hgrads[...] = jnp.zeros_like(hgrads)
        grads[...] = jnp.zeros_like(grads)
        gs[...] = grad[...].astype(bf16)
        for b in range(BLOCKS):
            grad_turned[b] = flip(gs[:, b * LANES : (b + 1) * LANES])
        if host.parts:
            host.barrier(False)
            host.start()

    @pl.when(step < GROUPS)
    def _():
        buf[...] = dot(gs[...], weight[...].reshape(D, WIDE))
        hgain = vectors.hidden(0, step)

        def body(r):
            value = hat[0, r, :].astype(f32)
            dy = buf[r, :]
            dx = dy * hgain
            hgrads[0, step] += fold_rows(dy * value)
            hgrads[1, step] += fold_rows(dy)
            first[r, :] += fold_lanes(dx)
            cross[r, :] += fold_lanes(dx * value)
            dxs[step, r, :] = dx

        row_loop(tokens, CHUNK, body)

    @pl.when(step == GROUPS)
    def _():
        acc[...] = jnp.zeros_like(acc)

        def body(r):
            first[r, :] = jnp.broadcast_to(sum_lanes(first[r, :]) / FF, (ROWS, LANES))
            cross[r, :] = jnp.broadcast_to(sum_lanes(cross[r, :]) / FF, (ROWS, LANES))

        row_loop(tokens, ROWS, body)

    @pl.when(step >= GROUPS)
    def _():
        g = step - GROUPS

        def body(r):
            inner = dxs[g, r, :] - first[r, 0:1] - hat[0, r, :].astype(f32) * cross[r, 0:1]
            dhid[0, r, :] = (slope[0, r, :].astype(f32) * (rstd_in[r, 0:1] * inner)).astype(bf16)

        row_loop(tokens, CHUNK, body)
        acc[...] += dot_nt(dhid[0], weight[...].reshape(D, WIDE))

    @pl.when(step == 2 * GROUPS - 1)
    def _():
        gain, shift = vectors.norm(0, 2), vectors.norm(1, 2)

        def body(r):
            value, rstd = row_stats(low_mid[r, :].astype(f32))
            dy = acc[r, :]
            grads[0] += fold_rows(dy * value)
            grads[1] += fold_rows(dy)
            grad_out[r, :] = grad[r, :].astype(f32) + norm_back(dy, value, rstd, gain)
            gs[r, :] = (value * gain + shift).astype(bf16)

        row_loop(tokens, ROWS, body)
        for b in range(BLOCKS):
            normed_turned[b] = flip(gs[:, b * LANES : (b + 1) * LANES])
        host.middle()
        host.finish()


def ffn_back_call(n, ident, jobs, layer, grad, hat, slope, rstd, low_mid, packed, weight):
    tokens = grad.shape[0]
    turned = (BLOCKS, LANES, tokens)
    big = (GROUPS, tokens, WIDE)
    _, late = half_specs(tokens)
    flat = (tokens, D)
    call = remote_call if jobs else plain_call
    return call(
        functools.partial(ffn_back_kernel, layer), n, "ffn_back", ident,
        [grad, hat, slope, rstd, low_mid, packed, weight],
        [
            whole(flat),
            pl.BlockSpec((1, tokens, WIDE), lambda s: (lax.rem(s, GROUPS), 0, 0)),
            late,
        ]
        + [whole(v.shape) for v in (rstd, low_mid, packed)]
        + [
            pl.BlockSpec(
                (BLOCKS, 1, LANES, WIDE), lambda s: (0, lax.rem(s, GROUPS), 0, 1 - s // GROUPS)
            )
        ],
        [
            jax.ShapeDtypeStruct(big, bf16),
            jax.ShapeDtypeStruct(turned, bf16),
            jax.ShapeDtypeStruct(turned, bf16),
            jax.ShapeDtypeStruct(flat, f32),
            jax.ShapeDtypeStruct((2, GROUPS, 8, WIDE), f32),
            jax.ShapeDtypeStruct((2, 8, D), f32),
        ],
        [late, whole(turned), whole(turned), whole(flat)]
        + [whole((2, GROUPS, 8, WIDE)), whole((2, 8, D))],
        [
            pltpu.VMEM(flat, bf16),
            pltpu.VMEM(big, f32),
            pltpu.VMEM((tokens, WIDE), f32),
            pltpu.VMEM((tokens, LANES), f32),
            pltpu.VMEM((tokens, LANES), f32),
            pltpu.VMEM(flat, f32),
        ],
        16 * tokens * D * FF, jobs, grid=(2 * GROUPS,),
    )


def proj_back_kernel(
    layer, host, grad, packed, weight, rows, *refs
):
    n = host.n
    vectors = Vectors(n, layer, packed)
    gain, shift = vectors.norm(0, 1), vectors.norm(1, 1)
    tokens = grad.shape[0]
    units = BLOCKS // n
    outs, refs = refs[:units], refs[units:]
    grad_turned, normed, grads, gs, dm, send, ssem, rsem, lsem = refs
    host.barrier()
    host.start()
    gs[...] = grad[...].astype(bf16)
    for g in range(GROUPS):
        dm[:, g * HEADS : (g + 1) * HEADS] = dot(gs[...], weight[:, g].reshape(D, HEADS))
    grads[...] = jnp.zeros_like(grads)

    def body(r):
        value, rstd = row_stats(rows[r, :].astype(f32))
        dy = dm[r, :]
        grads[0] += fold_rows(dy * value)
        grads[1] += fold_rows(dy)
        dv = norm_back(dy, value, rstd, gain).astype(bf16)
        for b in range(BLOCKS):
            send[b, r, :] = dv[:, b * LANES : (b + 1) * LANES]
        normed[r, :] = (value * gain + shift).astype(bf16)

    row_loop(tokens, ROWS, body)
    _, lo = group_place(n)
    copies = []
    for k in order_of(n) + [0]:
        for u in range(units):
            source = send.at[lax.rem(lo + k, n) * units + u]
            if k:
                copy = group_send(n, k, source, outs[u].at[k], ssem.at[u, k], rsem.at[u, k])
            else:
                copy = pltpu.make_async_copy(source, outs[u].at[0], lsem.at[u])
            copy.start()
            copies.append(copy)
    for b in range(BLOCKS):
        grad_turned[b] = flip(gs[:, b * LANES : (b + 1) * LANES])
    host.middle()
    for copy in copies:
        copy.wait()
    host.finish()


def proj_back_call(n, ident, jobs, layer, grad, packed, weight, rows):
    tokens = grad.shape[0]
    units = BLOCKS // n
    turned = (BLOCKS, LANES, tokens)
    flat = (tokens, D)
    return remote_call(
        functools.partial(proj_back_kernel, layer), n, "projection_back", ident,
        [grad, packed, weight, rows],
        [whole(v.shape) for v in (grad, packed)]
        + [pl.BlockSpec((BLOCKS, GROUPS, LANES, HEADS), lambda i: (0, 0, 0, 3)), whole(flat)],
        [
            *[jax.ShapeDtypeStruct((n, tokens, LANES), bf16)] * units,
            jax.ShapeDtypeStruct(turned, bf16),
            jax.ShapeDtypeStruct(flat, bf16),
            jax.ShapeDtypeStruct((2, 8, D), f32),
        ],
        [HB] * units + [whole(turned), whole(flat), whole((2, 8, D))],
        [
            pltpu.VMEM(flat, bf16),
            pltpu.VMEM(flat, f32),
            pltpu.VMEM((BLOCKS, tokens, LANES), bf16),
            DMA((units, n)),
            DMA((units, n)),
            DMA((units,)),
        ],
        30 * tokens * D * D, jobs, grid=(1,),
    )


def attn_back_kernel(n, need, aux, one, *refs):
    qkv, (att, datt, lse) = refs[:n], refs[n : n + 3]
    outs, refs = refs[n + 3 : 2 * n + 3], refs[2 * n + 3 :]
    kx, kt, qs, vs, delta, dq, dkey, dval, dkv = refs
    for r in range(n):
        kx[r] = jnp.concatenate([qkv[r][1], aux[r]], axis=1)
        kt[r] = flip(qkv[r][1])
        vs[r] = qkv[r][2]
        qs[r] = (qkv[r][0].astype(f32) * (1.0 / math.sqrt(DH))).astype(bf16)
        both = jnp.transpose(att[r].astype(f32) * datt[r].astype(f32), (1, 0))
        delta[r, 0:1] = jnp.sum(both[:DH], axis=0, keepdims=True)
        delta[r, 1:2] = jnp.sum(both[DH:], axis=0, keepdims=True)
    dq[...] = jnp.zeros_like(dq)

    def each_key(j, carry):
        dkey[...] = jnp.zeros_like(dkey)
        dval[...] = jnp.zeros_like(dval)

        def each_query(i, inner):
            @pl.when(need[i * n + j] == 1)
            def _():
                for h in range(2):
                    query = head_lanes(qs[i], h)
                    out = head_lanes(datt[i], h)
                    scores = dot_nt(kx[j], jnp.concatenate([query, one[...]], axis=1))
                    probs = jnp.exp(scores - lse[i, h : h + 1])
                    dprobs = dot_nt(vs[j], out)
                    dscores = (probs * (dprobs - delta[i, h : h + 1])).astype(bf16)
                    dval[...] += dot(probs.astype(bf16), out)
                    dkey[...] += dot(dscores, query)
                    rows = slice(h * DH, (h + 1) * DH)
                    dq[i, rows] += dot(kt[j, rows], dscores)

            return inner

        lax.fori_loop(0, n, each_query, 0)
        dkv[j, 0] = dkey[...].astype(bf16)
        dkv[j, 1] = dval[...].astype(bf16)
        return carry

    lax.fori_loop(0, n, each_key, 0)
    for r in range(n):
        outs[r][0] = (jnp.transpose(dq[r], (1, 0)) * (1.0 / math.sqrt(DH))).astype(bf16)
        outs[r][1] = dkv[r, 0]
        outs[r][2] = dkv[r, 1]


def attn_back_call(n, need, aux, one, parts, att, datt, lse):
    tokens = aux.shape[1]
    return unit_call(
        attn_back_kernel, n, need, aux, one, [*parts, att, datt, lse],
        [jax.ShapeDtypeStruct((3, tokens, LANES), bf16)] * n,
        [
            pltpu.VMEM((n, tokens, 2 * LANES), bf16),
            pltpu.VMEM((n, LANES, tokens), bf16),
            pltpu.VMEM((n, tokens, LANES), bf16),
            pltpu.VMEM((n, tokens, LANES), bf16),
            pltpu.VMEM((n, 8, tokens), f32),
            pltpu.VMEM((n, LANES, tokens), f32),
            pltpu.VMEM((tokens, LANES), f32),
            pltpu.VMEM((tokens, LANES), f32),
            pltpu.VMEM((n, 2, tokens, LANES), bf16),
        ],
        14, "attention_back",
    )


def qkv_back_kernel(
    layer, host, grad, low, packed, wq, wk, wv, *refs
):
    n = host.n
    vectors = Vectors(n, layer, packed)
    gain, shift = vectors.norm(0, 0), vectors.norm(1, 0)
    tokens = grad.shape[0]
    units = BLOCKS // n
    early_count = n * (units - 1)
    ready, refs = refs[:early_count], refs[early_count:]
    dparts, refs = refs[:n], refs[n:]
    dlast, refs = refs[:n], refs[n:]
    grad_out, normed_turned, grads, grad_low, acc, ns, ssem, rsem, lsem = refs
    blocks = [ready[u * n : (u + 1) * n] for u in range(units - 1)] + [dlast]
    host.barrier()
    steps = [0] + order_of(n)[::-1]
    copies = {}
    for k in order_of(n):
        copies[k] = group_send(n, -k, dparts[k], dlast[k], ssem.at[k], rsem.at[k])
        copies[k].start()
    copies[0] = pltpu.make_async_copy(dparts[0], dlast[0], lsem)
    copies[0].start()
    host.start()
    grads[...] = jnp.zeros_like(grads)

    def early(r):
        value, _ = row_stats(low[r, :].astype(f32))
        ns[r, :] = (value * gain + shift).astype(bf16)

    row_loop(tokens, ROWS, early)
    for b in range(BLOCKS):
        normed_turned[b] = flip(ns[:, b * LANES : (b + 1) * LANES])
    for i, k in enumerate(steps):
        copies[k].wait()
        group, offset = head_columns(n, k)
        left, right = [], []
        for c, weight in enumerate((wq, wk, wv)):
            left += [blocks[u][k][c] for u in range(units)]
            part = weight[:, group, :, pl.ds(offset, units * LANES)]
            right.append(part.reshape(D, units * LANES))
        total = dot_nt(jnp.concatenate(left, axis=1), jnp.concatenate(right, axis=1))
        if i == 0:
            acc[...] = total
        else:
            acc[...] += total

    def body(r):
        value, rstd = row_stats(low[r, :].astype(f32))
        dy = acc[r, :]
        grads[0] += fold_rows(dy * value)
        grads[1] += fold_rows(dy)
        total = grad[r, :] + norm_back(dy, value, rstd, gain)
        grad_out[r, :] = total
        grad_low[r, :] = total.astype(bf16)

    row_loop(tokens, ROWS, body)
    host.middle()
    host.finish()


def qkv_back_call(n, ident, jobs, layer, grad, low, packed, weight, ready, dparts):
    tokens = grad.shape[0]
    turned = (BLOCKS, LANES, tokens)
    flat = (tokens, D)
    columns = lambda c: pl.BlockSpec((BLOCKS, GROUPS, LANES, HEADS), lambda i: (0, 0, 0, c))
    block = (3, tokens, LANES)
    res = remote_call(
        functools.partial(qkv_back_kernel, layer), n, "qkv_back", ident,
        [grad, low, packed, weight, weight, weight, *ready, *dparts],
        [whole(v.shape) for v in (grad, low, packed)]
        + [columns(0), columns(1), columns(2)]
        + [whole(block)] * (len(ready) + n),
        [jax.ShapeDtypeStruct(block, bf16)] * n
        + [
            jax.ShapeDtypeStruct(flat, f32),
            jax.ShapeDtypeStruct(turned, bf16),
            jax.ShapeDtypeStruct((2, 8, D), f32),
            jax.ShapeDtypeStruct(flat, bf16),
        ],
        [whole(block)] * n + [whole(flat), whole(turned), whole((2, 8, D)), whole(flat)],
        [
            pltpu.VMEM(flat, f32),
            pltpu.VMEM(flat, bf16),
            DMA((n,)),
            DMA((n,)),
            DMA,
        ],
        50 * tokens * D * D, jobs, grid=(1,),
    )
    return [res[:n], *res[n:]]


def slot_group(p):
    return 2 * (p % 2) + p // 2


def pick_rows(sc, first, turned, count):
    return jnp.concatenate([turned[sc[first + m]] for m in range(count)], axis=0)


def put_rows(value, extra, outs, spot):
    rows = value.shape[0] // LANES
    for m in range(rows):
        part = value[m * LANES : (m + 1) * LANES]
        if extra is not None:
            part = part + extra[(m,) + spot].astype(f32)
            outs[m // 2][(m % 2,) + spot] = part.astype(bf16)
        else:
            outs[0][(m,) + spot] = part.astype(bf16)


def ffn_grad_kernel(first, count, added, sc, up_turned, down_turned, dhid, normed, *refs):
    extra, outs = (refs[0], refs[1:]) if added else (None, refs)

    @pl.when(pl.program_id(0) == 0)
    def _():
        put_rows(dot(pick_rows(sc, first, up_turned, count), dhid[0]), extra, outs, (0,))

    @pl.when(pl.program_id(0) == 1)
    def _():
        put_rows(dot(pick_rows(sc, first, down_turned, count), normed[0]), extra, outs, (0,))


def ffn_grad_call(first, count, sc, up_turned, down_turned, dhid, normed, extra=None):
    tokens = up_turned.shape[2]
    added = extra is not None
    at = lambda g, sc: jnp.bitwise_xor(slot_group(g), sc[BLOCKS])
    left = pl.BlockSpec(
        (1, tokens, WIDE), lambda j, g, sc: (at(jnp.where(j == 0, g, GROUPS - 1), sc), 0, 0)
    )
    right = pl.BlockSpec((1, tokens, WIDE), lambda j, g, sc: (at(jnp.where(j == 1, g, 0), sc), 0, 0))
    piece = lambda m: pl.BlockSpec((m, 1, LANES, WIDE), lambda j, g, sc: (0, g, 0, j))
    outs = [2, 2] if added else [count]
    return pl.pallas_call(
        lambda *refs: ffn_grad_kernel(first, count, added, *refs),
        out_shape=[jax.ShapeDtypeStruct((m, GROUPS, LANES, 2 * WIDE), bf16) for m in outs],
        grid_spec=pltpu.PrefetchScalarGridSpec(
            num_scalar_prefetch=1,
            grid=(2, GROUPS),
            in_specs=[whole(up_turned.shape), whole(down_turned.shape), left, right]
            + ([piece(count)] if added else []),
            out_specs=[piece(m) for m in outs],
        ),
        compiler_params=params(),
        cost_estimate=cost(16 * tokens * count * LANES * FF, 24 * 2**20),
        name="ffn_grad",
    )(sc, up_turned, down_turned, dhid, normed, *([extra] if added else []))


def head_grad_kernel(n, first, count, added, sc, in_turned, out_turned, normed, *refs):
    units = BLOCKS // n
    dqkv, refs = refs[: n * units], refs[n * units :]
    extra, outs = (refs[0], refs[1:]) if added else (None, refs)
    left = pick_rows(sc, first, in_turned, count)
    for k in range(n):
        for c in range(3):
            right = jnp.concatenate([dqkv[u * n + k][c] for u in range(units)], axis=1)
            value = dot(left, right)
            if n == GROUPS:
                slot = slot_group(jnp.bitwise_xor(lax.rem(sc[BLOCKS + 1] + k, n), sc[BLOCKS]))
                put_rows(value, extra, outs, (slot, slice(None), slice(c * HEADS, (c + 1) * HEADS)))
            else:
                unit = lax.rem(sc[BLOCKS + 1] + k, n) * units
                at = pl.multiple_of(c * HEADS + lax.rem(unit, 2) * LANES, LANES)
                slot = slot_group(unit // 2)
                put_rows(value, extra, outs, (slot, slice(None), pl.ds(at, LANES)))
    left = pick_rows(sc, first, out_turned, count)
    for g in range(GROUPS):
        slot = slot_group(jnp.bitwise_xor(g, sc[BLOCKS]))
        value = dot(left, normed[:, g * HEADS : (g + 1) * HEADS])
        put_rows(value, extra, outs, (slot, slice(None), slice(3 * HEADS, 4 * HEADS)))


def head_grad_call(n, first, count, sc, in_turned, out_turned, dqkv, normed, extra=None):
    tokens = in_turned.shape[2]
    added = extra is not None
    outs = [2, 2] if added else [count]
    inner = (GROUPS, LANES, 4 * HEADS)
    return pl.pallas_call(
        lambda *refs: head_grad_kernel(n, first, count, added, *refs),
        out_shape=[jax.ShapeDtypeStruct((m,) + inner, bf16) for m in outs],
        grid_spec=pltpu.PrefetchScalarGridSpec(
            num_scalar_prefetch=1,
            grid=(1,),
            in_specs=[whole(v.shape) for v in (in_turned, out_turned, normed, *dqkv)]
            + ([whole((count,) + inner)] if added else []),
            out_specs=[whole((m,) + inner) for m in outs],
        ),
        compiler_params=params(),
        cost_estimate=cost(16 * tokens * count * LANES * 4 * D, 16 * 2**20),
        name="head_grad",
    )(sc, in_turned, out_turned, normed, *dqkv, *([extra] if added else []))


def pack_kernel(qkv, out, up, down, *refs):
    layers = qkv.shape[0]
    for l in range(layers):
        narrow, broad = refs[2 * l : 2 * l + 2]
        for c in range(3):
            narrow[:, c * HEADS : (c + 1) * HEADS] = qkv[l, c]
        narrow[:, 3 * HEADS :] = flip(out[l])
        broad[:, :WIDE] = up[l]
        broad[:, WIDE:] = flip(down[l])


def pack_call(qkv, out, up, down):
    layers = qkv.shape[0]
    flat = pl.pallas_call(
        pack_kernel,
        out_shape=[
            jax.ShapeDtypeStruct((LANES, NARROW), bf16),
            jax.ShapeDtypeStruct((LANES, BROAD), bf16),
        ]
        * layers,
        in_specs=[VM] * 4,
        out_specs=[VM] * (2 * layers),
        compiler_params=params(),
        cost_estimate=cost(0, 4 * 2**20),
        name="pack",
    )(qkv, out, up, down)
    return flat[::2], flat[1::2]


def greet(sem, place, z, others, count):
    n = GROUPS
    for k in range(1, n):
        pl.semaphore_signal(
            sem, inc=1, device_id={"head": lax.rem(z + k, n)}, device_id_type=MESH
        )
    for other in (place.by_x, place.by_y, place.mate):
        pl.semaphore_signal(sem, inc=1, device_id={"dp": other}, device_id_type=MESH)
    for to_dp, to_z in others:

        @pl.when((to_dp != place.dp) | (to_z != z))
        def _(to_dp=to_dp, to_z=to_z):
            pl.semaphore_signal(
                sem, inc=1, device_id={"dp": to_dp, "head": to_z}, device_id_type=MESH
            )

    pl.semaphore_wait(sem, n + 2 + count)


class Weights:
    def __init__(self, at, chunks, shards, gathered, hsem, ssem, rsem, lsem, only=None):
        self.only = only
        self.at, self.chunks, self.pairs = at, chunks, list(zip(shards, gathered))
        self.hsem, self.ssem, self.rsem = hsem, ssem, rsem
        self.lsem = lsem

    def owns(self):
        at = self.at
        copies = []
        for i, (shard, out) in enumerate(self.pairs):
            source, target = shard, out.at[at.dp, at.z]
            if self.only:
                source = shard.at[:, pl.ds(*self.only)]
                target = out.at[at.dp, at.z, :, pl.ds(*self.only)]
            copies.append(pltpu.make_async_copy(source, target, self.lsem.at[i]))
        return copies

    def near(self, c):
        kind, columns = self.chunks[c][0], pl.ds(*self.chunks[c][1:])
        shard, out = self.pairs[kind]
        at = self.at
        return [
            pltpu.make_async_remote_copy(
                src_ref=shard.at[:, columns],
                dst_ref=out.at[at.dp, at.z, :, columns],
                send_sem=self.hsem.at[0, k - 1, c],
                recv_sem=self.hsem.at[1, k - 1, c],
                device_id={"head": lax.rem(at.z + k, GROUPS)},
                device_id_type=MESH,
            )
            for k in (2, 1, 3)
        ]

    def far(self, slot, row, target, c):
        kind, columns = self.chunks[c][0], pl.ds(*self.chunks[c][1:])
        out = self.pairs[kind][1]
        return pltpu.make_async_remote_copy(
            src_ref=out.at[row, :, :, columns],
            dst_ref=out.at[row, :, :, columns],
            send_sem=self.ssem.at[slot, c],
            recv_sem=self.rsem.at[slot, c],
            device_id={"dp": target},
            device_id_type=MESH,
        )

    def hops(self, stage, c):
        at = self.at
        if stage == 0:
            return self.near(c)
        if stage == 1:
            return [self.far(0, at.dp, at.first, c)]
        if stage == 2:
            return [self.far(1, at.dp, at.second, c), self.far(2, at.first, at.second, c)]
        rows = (at.dp, at.first, at.second, at.both)
        return [self.far(3 + i, row, at.mate, c) for i, row in enumerate(rows)]

    def begin(self):
        for c in range(min(2, len(self.chunks))):
            for copy in self.near(c):
                copy.start()

    def turn(self, t):
        parts = len(self.chunks)
        for stage in (1, 2, 3):
            c = t + 1 - stage
            if 0 <= c < parts:
                if stage == 1 and c == 0:
                    for copy in self.owns():
                        copy.wait()
                for copy in self.hops(stage - 1, c):
                    copy.wait()
                for copy in self.hops(stage, c):
                    copy.start()
        if t + 2 < parts:
            for copy in self.near(t + 2):
                copy.start()
        c = t - 3
        if 0 <= c < parts:
            for copy in self.hops(3, c):
                copy.wait()

    def run(self, aside):
        self.begin()
        for t in range(len(self.chunks) + 3):
            self.turn(t)
            aside(t)


def weight_chunks(shards, step=512):
    return [(i, c, step) for i, v in enumerate(shards) for c in range(0, v.shape[1], step)]


def weight_sems(shards, step=512):
    parts = len(weight_chunks(shards, step))
    return [DMA((2, 3, parts)), DMA((7, parts)), DMA((7, parts)), DMA((len(shards),))]


class Everywhere:
    def __init__(self, shard, half, into=None):
        self.arrays = [shard] if into is None else [shard, into]
        self.aliases = {} if into is None else {1: 0}
        self.outs = [jax.ShapeDtypeStruct((BLOCKS, GROUPS) + shard.shape, shard.dtype)]
        wide = shard.shape[1] // 2
        self.half = (half * wide, wide)
        self.chunks = weight_chunks([shard], wide // 2)[2 * half : 2 * half + 2]
        parts = len(self.chunks)
        self.sems = [DMA((2, 3, parts)), DMA((7, parts)), DMA((7, parts)), DMA((1,))]

    def peers(self, at):
        partners = [{"dp": v} for v in (at.first, at.second, at.mate)]
        return at.others() + partners, [], GROUPS + 2

    def weights(self, at, ins, outs, sems):
        return Weights(at, self.chunks, ins[:1], outs, *sems, only=self.half)

    def start(self, *args):
        weights = self.weights(*args)
        for copy in weights.owns():
            copy.start()
        weights.begin()

    def tick(self, t, *args):
        self.weights(*args).turn(t)

    def middle(self, *args):
        pass

    def finish(self, *args):
        pass


def start_kernel(
    chunks, shards, rows, vector, flags, gathered, low, side, vectors, flags_out,
    hsem, ssem, rsem, wsem, xsem, tsem, vsem, fsem, lsem,
):
    at = Place()
    weights = Weights(at, chunks, shards, gathered, hsem, ssem, rsem, wsem)
    dp, core, bit_x, by_x = at.dp, at.core, at.bit_x, at.by_x
    z = at.z
    n = GROUPS
    lo = lax.rem(dp, n)
    wide = rows.shape[2]
    sem = pltpu.get_barrier_semaphore()

    def targets():
        return [(xs, c2, dp - core + c2, 2 * xs + core) for xs in range(2) for c2 in range(2)]

    def sources():
        return [(dp - core + lax.rem(z, 2), g) for g in range(n)]

    turn_dp, turn_z = dp - lo + z, lo
    for copy in weights.owns():
        copy.start()
    own_vector = pltpu.make_async_copy(vector, vectors.at[z], lsem.at[2])
    own_vector.start()
    turned = [(turn_dp, turn_z)]
    greet(sem, at, z, sources() + turned, n - 1 + unlike(lax.rem(z, 2), core) + unlike(z, lo))
    small = [
        pltpu.make_async_remote_copy(
            src_ref=vector,
            dst_ref=vectors.at[z],
            send_sem=vsem.at[0, k - 1],
            recv_sem=vsem.at[1, k - 1],
            device_id={"head": lax.rem(z + k, n)},
            device_id_type=MESH,
        )
        for k in range(1, n)
    ]

    def flag_copy(op):
        def remote():
            copy = pltpu.make_async_remote_copy(
                src_ref=flags,
                dst_ref=flags_out,
                send_sem=fsem.at[0],
                recv_sem=fsem.at[1],
                device_id={"dp": turn_dp, "head": turn_z},
                device_id_type=MESH,
            )
            copy.start() if op == "start" else copy.wait()

        def inside():
            copy = pltpu.make_async_copy(flags, flags_out, lsem.at[3])
            copy.start() if op == "start" else copy.wait()

        pl.when((turn_dp != dp) | (turn_z != z))(remote)
        pl.when((turn_dp == dp) & (turn_z == z))(inside)

    flag_copy("start")
    for copy in small:
        copy.start()

    cross = pltpu.make_async_remote_copy(
        src_ref=rows.at[pl.ds(2 - 2 * bit_x, 2)],
        dst_ref=side,
        send_sem=xsem.at[0],
        recv_sem=xsem.at[1],
        device_id={"dp": by_x},
        device_id_type=MESH,
    )
    place = low.at[:, pl.ds(pl.multiple_of(z * wide, wide), wide)]

    def spread(op):
        for i, (xs, c2, to_dp, to_z) in enumerate(targets()):

            def here(source, i=i, to_dp=to_dp, to_z=to_z):
                def remote():
                    copy = pltpu.make_async_remote_copy(
                        src_ref=source,
                        dst_ref=place,
                        send_sem=tsem.at[0, i],
                        recv_sem=tsem.at[1, z],
                        device_id={"dp": to_dp, "head": to_z},
                        device_id_type=MESH,
                    )
                    if op == "start":
                        copy.start()
                    else:
                        copy.wait_send()

                pl.when((to_dp != dp) | (to_z != z))(remote)

                def inside():
                    copy = pltpu.make_async_copy(source, place, lsem.at[1])
                    if op == "start":
                        copy.start()
                    else:
                        copy.wait()

                pl.when((to_dp == dp) & (to_z == z))(inside)

            pl.when(bit_x == xs)(lambda xs=xs, c2=c2, here=here: here(rows.at[2 * xs + c2]))
            pl.when(bit_x != xs)(lambda c2=c2, here=here: here(side.at[c2]))

    cross.start()

    def aside(t):
        if t == 1:
            cross.wait()
            spread("start")

    weights.run(aside)
    own_vector.wait()
    flag_copy("wait")
    for copy in small:
        copy.wait()
    spread("wait")
    for from_dp, g in sources():

        @pl.when((from_dp != dp) | (g != z))
        def _(g=g):
            spot = low.at[:, pl.ds(g * wide, wide)]
            pltpu.make_async_remote_copy(
                src_ref=spot,
                dst_ref=spot,
                send_sem=tsem.at[0, 0],
                recv_sem=tsem.at[1, g],
                device_id={"dp": by_x},
                device_id_type=MESH,
            ).wait_recv()


def start_call(shards, rows, vector, flags):
    count = len(shards)
    chunks = weight_chunks(shards)
    tokens, wide = rows.shape[1:]

    def kernel(*refs):
        taken, refs = refs[:count], refs[count:]
        start_kernel(chunks, taken, *refs[:3], refs[3 : 3 + count], *refs[3 + count :])

    res = pl.pallas_call(
        kernel,
        out_shape=[jax.ShapeDtypeStruct((BLOCKS, GROUPS) + v.shape, bf16) for v in shards]
        + [
            jax.ShapeDtypeStruct((tokens, GROUPS * wide), bf16),
            jax.ShapeDtypeStruct((2, tokens, wide), bf16),
            jax.ShapeDtypeStruct((GROUPS,) + vector.shape, f32),
            jax.ShapeDtypeStruct(flags.shape, jnp.int32),
        ],
        in_specs=[HB] * (count + 3),
        out_specs=[HB] * (count + 4),
        scratch_shapes=[
            *weight_sems(shards),
            DMA((2,)),
            DMA((2, GROUPS)),
            DMA((2, 3)),
            DMA((2,)),
            DMA((4,)),
        ],
        compiler_params=params(collective_id=5, has_side_effects=True),
        cost_estimate=cost(0, 300 * 2**20),
        name="start",
    )(*shards, rows, vector, flags)
    return [res[:count], *res[count:]]


def vector_rows(layers):
    return -(-(28 * layers + 3 * layers + 1) // 8) * 8


def end_kernel(
    layers, rows, grads, fsum, turned, valid, tops, vecs, uses,
    stream_out, rows_out, qkv_out, out_out, up_out, down_out,
    gains_out, shifts_out, hgains_out, hshifts_out, rms_out,
    mine, got, pair, last, near, pieces, crossed, fm, fnear, vec, vgot, vsum,
    gsem, hsem, psem, qsem, nsem, tsem, xsem, vsem, lsem, esem,
):
    at = Place()
    dp, core, bit_x = at.dp, at.core, at.bit_x
    z = at.z
    n = GROUPS
    parts = 4
    width = grads.shape[3] // parts
    step = fsum.shape[2] // parts
    wide = rows.shape[1] // n
    sem = pltpu.get_barrier_semaphore()

    def columns(c):
        return pl.ds(c * width, width)

    def broad(c):
        return pl.ds(c * step, step)

    def loads(c):
        return [
            pltpu.make_async_copy(
                grads.at[pl.ds(0, 4), :, :, columns(c)], mine.at[:, :, :, columns(c)], gsem.at[0, c]
            ),
            pltpu.make_async_copy(
                fsum.at[:, :, broad(c)], fm.at[:, :, broad(c)], gsem.at[1, c]
            ),
        ]

    for c in range(parts):
        for copy in loads(c):
            copy.start()

    vec[...] = jnp.zeros_like(vec)
    for l in range(layers):
        base = 28 * l
        norms, hidden = vecs[4 * l : 4 * l + 3], vecs[4 * l + 3]
        for kind in range(2):
            for i in range(3):
                total = jnp.sum(norms[i][kind], axis=0, keepdims=True)
                for b in range(BLOCKS):
                    row = base + (3 * kind + i) * 2 + b % 2
                    vec[b // 2, row : row + 1, :] = total[:, b * LANES : (b + 1) * LANES]
            for g in range(n):
                total = jnp.sum(hidden[kind, g], axis=0, keepdims=True)
                for b in range(BLOCKS):
                    row = base + 12 + 8 * kind + b
                    vec[g, row : row + 1, :] = total[:, b * LANES : (b + 1) * LANES]
        branch, rest = uses[2 * l : 2 * l + 2]
        for i, value in enumerate((branch[...], rest[0], rest[1])):
            row = 28 * layers + 3 * l + i
            total = fold_lanes(jnp.sum(value, axis=0, keepdims=True))
            for g in range(n):
                vec[g, row : row + 1, :] = total
    row = 31 * layers
    count = jnp.sum(valid[...], axis=0, keepdims=True) * (D / LANES)
    for g in range(n):
        vec[g, row : row + 1, :] = jnp.broadcast_to(count, (1, LANES))

    to_dp = dp - core + lax.rem(z, 2)
    sources = [(dp - core + c2, 2 * xs + core) for xs in range(2) for c2 in range(2)]
    greet(sem, at, z, sources, n - 1 + unlike(lax.rem(z, 2), core))

    def hop(stage, c):
        if stage == 0:
            return pltpu.make_async_remote_copy(
                src_ref=grads.at[pl.ds(4, 4), :, :, columns(c)],
                dst_ref=got.at[:, :, :, columns(c)],
                send_sem=hsem.at[0, c],
                recv_sem=hsem.at[1, c],
                device_id={"dp": at.mate},
                device_id_type=MESH,
            )
        if stage == 1:
            return pltpu.make_async_remote_copy(
                src_ref=mine.at[pl.ds(2, 2), :, :, columns(c)],
                dst_ref=pair.at[:, :, :, columns(c)],
                send_sem=psem.at[0, c],
                recv_sem=psem.at[1, c],
                device_id={"dp": at.second},
                device_id_type=MESH,
            )
        return pltpu.make_async_remote_copy(
            src_ref=mine.at[1, :, :, columns(c)],
            dst_ref=last.at[:, :, columns(c)],
            send_sem=qsem.at[0, c],
            recv_sem=qsem.at[1, c],
            device_id={"dp": at.first},
            device_id_type=MESH,
        )

    def way(source, target, sems, i, c):
        return pltpu.make_async_remote_copy(
            src_ref=source,
            dst_ref=target,
            send_sem=sems.at[0, i, c],
            recv_sem=sems.at[1, i, c],
            device_id={"head": at.group(2 - i)},
            device_id_type=MESH,
        )

    def head_way(i, c):
        if i == 0:
            source, target = mine.at[0, pl.ds(2, 2), :, columns(c)], near.at[pl.ds(0, 2), :, columns(c)]
        else:
            source, target = mine.at[0, 1, :, columns(c)], near.at[2, :, columns(c)]
        return way(source, target, nsem, i, c)

    def ffn_way(i, c):
        if i == 0:
            source, target = fm.at[pl.ds(2, 2), :, broad(c)], fnear.at[pl.ds(0, 2), :, broad(c)]
        else:
            source, target = fm.at[1, :, broad(c)], fnear.at[2, :, broad(c)]
        return way(source, target, esem, i, c)

    def head_between(c):
        head_way(0, c).wait()
        for k in range(2):
            value = mine[0, k, :, columns(c)].astype(f32) + near[k, :, columns(c)].astype(f32)
            mine[0, k, :, columns(c)] = value.astype(bf16)
        head_way(1, c).start()

    def ffn_between(c):
        ffn_way(0, c).wait()
        for k in range(2):
            value = fm[k, :, broad(c)].astype(f32) + fnear[k, :, broad(c)].astype(f32)
            fm[k, :, broad(c)] = value.astype(bf16)
        ffn_way(1, c).start()

    def add(count, other, c):
        def body(i, carry):
            m, g = i // GROUPS, lax.rem(i, GROUPS)
            value = mine[m, g, :, columns(c)].astype(f32) + other(m, g).astype(f32)
            mine[m, g, :, columns(c)] = value.astype(bf16)
            return carry

        lax.fori_loop(0, count * GROUPS, body, 0)

    def row_copies(op):
        for j in range(n):
            source = rows.at[:, pl.ds(j * wide, wide)]
            target = pieces.at[z // 2, core]

            def remote(j=j, source=source, target=target):
                copy = pltpu.make_async_remote_copy(
                    src_ref=source,
                    dst_ref=target,
                    send_sem=tsem.at[0, j],
                    recv_sem=tsem.at[1, 2 * (z // 2) + core],
                    device_id={"dp": to_dp, "head": j},
                    device_id_type=MESH,
                )
                copy.start() if op == "start" else copy.wait_send()

            def inside(source=source, target=target):
                copy = pltpu.make_async_copy(source, target, lsem.at[0])
                copy.start() if op == "start" else copy.wait()

            pl.when((to_dp != dp) | (j != z))(remote)
            pl.when((to_dp == dp) & (j == z))(inside)

    def row_arrivals():
        for xs in range(2):
            for c2 in range(2):

                @pl.when((dp - core + c2 != dp) | (2 * xs + core != z))
                def _(xs=xs, c2=c2):
                    spot = pieces.at[xs, c2]
                    pltpu.make_async_remote_copy(
                        src_ref=spot,
                        dst_ref=spot,
                        send_sem=tsem.at[0, 0],
                        recv_sem=tsem.at[1, 2 * xs + c2],
                        device_id={"dp": at.by_x},
                        device_id_type=MESH,
                    ).wait_recv()

    cross = pltpu.make_async_remote_copy(
        src_ref=pieces.at[1 - bit_x],
        dst_ref=crossed,
        send_sem=xsem.at[0],
        recv_sem=xsem.at[1],
        device_id={"dp": at.by_x},
        device_id_type=MESH,
    )
    def vector_near(k):
        return pltpu.make_async_remote_copy(
            src_ref=vec.at[lax.rem(z + k, n)],
            dst_ref=vgot.at[k - 1],
            send_sem=vsem.at[0, k - 1],
            recv_sem=vsem.at[1, k - 1],
            device_id={"head": lax.rem(z + k, n)},
            device_id_type=MESH,
        )

    def vector_far(i, target):
        return pltpu.make_async_remote_copy(
            src_ref=vsum.at[i],
            dst_ref=vgot.at[3 + i],
            send_sem=vsem.at[0, 3 + i],
            recv_sem=vsem.at[1, 3 + i],
            device_id={"dp": target},
            device_id_type=MESH,
        )

    def put_head(l, c, value):
        if c < 3:
            qkv_out[l, c] = value
        else:
            out_out[l] = jnp.transpose(value, (1, 0))

    def total_of(own, others):
        value = own.astype(f32)
        for other in others:
            value = value + other.astype(f32)
        return value

    row_copies("start")
    for c in range(parts):
        hop(0, c).start()
    for k in range(1, n):
        vector_near(k).start()
    partners = (at.mate, at.first, at.second)
    for t in range(parts + 4):
        c = t
        if c < parts:
            for copy in loads(c):
                copy.wait()
            hop(0, c).wait()
            add(4, lambda m, g, c=c: got[m, g, :, columns(c)], c)
            hop(1, c).start()
            ffn_way(0, c).start()
        c = t - 1
        if 0 <= c < parts:
            hop(1, c).wait()
            add(2, lambda m, g, c=c: pair[m, g, :, columns(c)], c)
            hop(2, c).start()
        c = t - 2
        if 0 <= c < parts:
            hop(2, c).wait()
            add(1, lambda m, g, c=c: last[g, :, columns(c)], c)
            head_way(0, c).start()
        if t == 1:
            for k in range(1, n):
                vector_near(k).wait()
            vsum[0] = vec[z] + vgot[0] + vgot[1] + vgot[2]
            vector_far(0, partners[0]).start()
        if 2 <= t < 5:
            i = t - 2
            vector_far(i, partners[i]).wait()
            vsum[i + 1] = vsum[i] + vgot[3 + i]
            if i < 2:
                vector_far(i + 1, partners[i + 1]).start()
        if t == 2:
            row_copies("wait")
            row_arrivals()
            cross.start()
        if t == 3:
            stream_out[...] = turned[...].astype(f32)
        if t == 4:
            for l in range(1, layers):
                heads, heads_other, wide_own, wide_other = tops[4 * l - 4 : 4 * l]
                for c in range(parts):
                    cols = slice(c * width, (c + 1) * width)
                    put_head(l, c, total_of(heads[0, :, cols], [heads_other[:, cols]]))
                up_out[l] = total_of(wide_own[0, :, :WIDE], [wide_other[:, :WIDE]])
                down = total_of(wide_own[0, :, WIDE:], [wide_other[:, WIDE:]])
                down_out[l] = jnp.transpose(down, (1, 0))
        c = t - 1
        if 0 <= c < parts:
            ffn_between(c)
        c = t - 3
        if 0 <= c < parts:
            head_between(c)
        c = t - 4
        if 0 <= c < parts:
            ffn_way(1, c).wait()
            value = total_of(fm[0, :, broad(c)], [fnear[2, :, broad(c)]])
            if c < parts // 2:
                up_out[0, :, broad(c)] = value
            else:
                down_out[0, pl.ds(c * step - WIDE, step), :] = jnp.transpose(value, (1, 0))
    for c in range(parts):
        head_way(1, c).wait()
        put_head(0, c, total_of(mine[0, 0, :, columns(c)], [near[2, :, columns(c)]]))
    for l in range(layers):
        base = 28 * l
        for kind, (norm_out, hid_out) in enumerate(
            ((gains_out, hgains_out), (shifts_out, hshifts_out))
        ):
            for i in range(3):
                at_row = base + (3 * kind + i) * 2
                parts_of = [vsum[3, at_row + p : at_row + p + 1, :] for p in range(2)]
                norm_out[l, i : i + 1, :] = jnp.concatenate(parts_of, axis=1)
            at_row = base + 12 + 8 * kind
            parts_of = [vsum[3, at_row + p : at_row + p + 1, :] for p in range(BLOCKS)]
            hid_out[l : l + 1, :] = jnp.concatenate(parts_of, axis=1)
    totals = sum_lanes(vsum[3, 28 * layers : 31 * layers + 1, :])
    rms = jnp.sqrt(totals[: 3 * layers] / totals[3 * layers :])
    rms_out[0 : 3 * layers, :] = jnp.broadcast_to(rms, (3 * layers, LANES))
    cross.wait()
    for c2 in range(2):
        rows_out[2 * bit_x + c2] = pieces[bit_x, c2].astype(f32)
        rows_out[2 - 2 * bit_x + c2] = crossed[c2].astype(f32)


def end_call(rows, grads, fsum, turned, valid, tops, vecs, uses):
    parts = 4
    layers = len(vecs) // 4
    tokens = rows.shape[0]
    wide = rows.shape[1] // GROUPS
    block = grads.shape[1:]
    broad = fsum.shape
    vector = (vector_rows(layers), LANES)
    inputs = [rows, grads, fsum, turned, valid, *tops, *vecs, *uses]

    def spec(i, v):
        if i % 2 == 0:
            return pl.BlockSpec((1,) + v.shape[1:], lambda g: (0, 0, 0))
        return whole(v.shape)

    def kernel(*refs):
        fixed, refs = refs[:5], refs[5:]
        lists = []
        for values in (tops, vecs, uses):
            lists.append(refs[: len(values)])
            refs = refs[len(values) :]
        end_kernel(layers, *fixed, *lists, *refs)

    dims = [
        turned.shape,
        turned.shape,
        (layers, 3, LANES, HEADS),
        (layers, HEADS, LANES),
        (layers, LANES, WIDE),
        (layers, WIDE, LANES),
        (layers, 3, HEADS),
        (layers, 3, HEADS),
        (layers, WIDE),
        (layers, WIDE),
        (8 * (-(-3 * layers // 8)), LANES),
    ]
    outs = [jax.ShapeDtypeStruct(d, f32) for d in dims]
    return pl.pallas_call(
        kernel,
        out_shape=outs,
        grid=(1,),
        in_specs=[HB] * 3
        + [whole(turned.shape), whole(valid.shape)]
        + [spec(i, v) for i, v in enumerate(tops)]
        + [whole(v.shape) for v in (*vecs, *uses)],
        out_specs=[whole(v.shape) for v in outs],
        scratch_shapes=[
            pltpu.VMEM((4,) + block, bf16),
            pltpu.VMEM((4,) + block, bf16),
            pltpu.VMEM((2,) + block, bf16),
            pltpu.VMEM(block, bf16),
            pltpu.VMEM((3,) + block[1:], bf16),
            pltpu.VMEM((2, 2, tokens, wide), bf16),
            pltpu.VMEM((2, tokens, wide), bf16),
            pltpu.VMEM(broad, bf16),
            pltpu.VMEM((3,) + broad[1:], bf16),
            pltpu.VMEM((GROUPS,) + vector, f32),
            pltpu.VMEM((6,) + vector, f32),
            pltpu.VMEM((4,) + vector, f32),
            DMA((2, parts)),
            DMA((2, parts)),
            DMA((2, parts)),
            DMA((2, parts)),
            DMA((2, 2, parts)),
            DMA((2, 4)),
            DMA((2,)),
            DMA((2, 6)),
            DMA((2,)),
            DMA((2, 2, parts)),
        ],
        compiler_params=params(collective_id=6, has_side_effects=True),
        cost_estimate=cost(0, 300 * 2**20),
        name="end",
    )(*inputs)


def after(value, *tokens):
    return lax.optimization_barrier((value, tokens))[0]


class Order:
    def __init__(self):
        self.token = None
        self.wanted = []

    def __call__(self, call, *args, first=0):
        args = list(args)
        if self.token is not None:
            args[first] = after(args[first], self.token, *self.wanted)
            self.wanted = []
        out = call(*args)
        self.token = out
        while isinstance(self.token, (list, tuple)):
            self.token = self.token[0]
        return out

    def hold(self, value):
        return after(value, self.token)

    def want(self, value):
        self.wanted.append(value)
        return value


class Net:
    def __init__(self, n_dp, n_head):
        self.n_dp, self.n = n_dp, n_head
        self.own = lax.axis_index("dp").astype(jnp.int32)
        self.z = lax.axis_index("head").astype(jnp.int32)
        self.lo = self.own % n_head
        self.fast = n_dp == BLOCKS and n_head == GROUPS
        core_zero = [2, 4]
        self.one_way = [(i, i ^ core_zero[i % 2]) for i in range(n_dp)]
        self.other_way = [(i, i ^ core_zero[1 - i % 2]) for i in range(n_dp)]
        self.core = [(i, i ^ 1) for i in range(n_dp)]
        if self.fast:
            step = jnp.where(self.own % 2 == 0, 2, 4).astype(jnp.int32)
            mine = [jnp.int32(0), step, 6 - step, jnp.int32(6)]
            theirs = [jnp.int32(0), 6 - step, step, jnp.int32(6)]
            rows = [self.own ^ v for v in mine] + [self.own ^ v ^ 1 for v in theirs]
            self.table = jnp.stack(rows + [self.z, self.lo])
        else:
            self.table = jnp.stack([jnp.int32(i) for i in range(BLOCKS)] + [jnp.int32(0), self.lo])

    def shift(self, value, k):
        n = self.n
        if k % n == 0:
            return value
        pairs = [(i, (i // n) * n + (i + k) % n) for i in range(self.n_dp)]
        return lax.ppermute(value, "dp", pairs)

    def across(self, value, bits):
        return lax.ppermute(value, "head", [(i, i ^ bits) for i in range(self.n)])

    def spin(self, value, k):
        n = self.n
        return lax.ppermute(value, "head", [(i, (i + k) % n) for i in range(n)])

    def gather(self, shard):
        return lax.all_gather(shard, ("dp", "head")).reshape(BLOCKS, GROUPS, LANES, -1)

    def gather_any(self, qkv, out, up, down):
        qkv = lax.all_gather(qkv, "head", axis=2, tiled=True)
        qkv = lax.all_gather(qkv, "dp", axis=1, tiled=True).transpose(1, 0, 2).reshape(D, 3 * D)
        up = lax.all_gather(up, "head", axis=1, tiled=True)
        up = lax.all_gather(up, "dp", axis=0, tiled=True)
        out, down = [
            lax.all_gather(lax.all_gather(v, "head", axis=0, tiled=True), "dp", axis=1, tiled=True)
            for v in (out, down)
        ]

        def blocks(*parts):
            cut = [v.reshape(BLOCKS, LANES, GROUPS, -1) for v in parts]
            return jnp.concatenate(cut, axis=3).transpose(0, 2, 1, 3)

        heads = [qkv[:, c * D : (c + 1) * D] for c in range(3)]
        return blocks(*heads, out.T), blocks(up, down.T)

    def scatter(self, full, widths):
        columns = full.shape[3]
        full = jnp.stack([full[:, slot_group(g)] for g in range(GROUPS)], axis=1)
        if self.fast:
            full = full.reshape(BLOCKS * GROUPS, LANES, columns)
        else:
            full = full.transpose(0, 2, 1, 3).reshape(D, GROUPS, columns)
            parts, at = [], 0
            for w in widths:
                part = full[:, :, at : at + w].reshape(D, self.n, GROUPS * w // self.n)
                parts.append(part)
                at += w
            full = jnp.concatenate(parts, axis=2)
            full = full.reshape(self.n_dp, D // self.n_dp, self.n, -1).transpose(0, 2, 1, 3)
            full = full.reshape(self.n_dp * self.n, D // self.n_dp, -1)
        mine = lax.psum_scatter(full, ("dp", "head"), scatter_dimension=0, tiled=False)
        return mine.astype(f32)


    def add_pair(self, keep, pair):
        add = lambda i: (keep[i].astype(f32) + pair[i].astype(f32)).astype(bf16)
        return add(0), add(1)

    def add_last(self, mine, last):
        return (mine.astype(f32) + last.astype(f32)).astype(bf16)

    def turn(self, k):
        n = self.n
        pairs = []
        for hi in range(self.n_dp // n):
            for lo in range(n):
                for z in range(n):
                    pairs.append(((hi * n + lo) * n + z, (hi * n + (z + k) % n) * n + lo))
        return pairs

    def rows_in(self, array):
        n = self.n
        tokens = array.shape[0] // n
        low = array.astype(bf16).reshape(n, tokens, array.shape[1])
        got = []
        for k in range(n):
            piece = lax.dynamic_index_in_dim(low, (self.z + k) % n, 0, False)
            got.append(lax.ppermute(piece, ("dp", "head"), self.turn(k)))
        return got

    def rows_in_end(self, got):
        stacked = jnp.take(jnp.stack(got), (self.lo - jnp.arange(self.n)) % self.n, axis=0)
        return stacked.transpose(1, 0, 2).reshape(got[0].shape[0], D)

    def rows_out(self, array):
        n = self.n
        width = D // n
        low = array.astype(bf16)
        got = []
        for k in range(n):
            piece = lax.dynamic_slice_in_dim(low, ((self.lo - k) % n) * width, width, 1)
            got.append(lax.ppermute(piece, ("dp", "head"), [(b, a) for a, b in self.turn(k)]))
        return got

    def rows_out_end(self, got):
        stacked = jnp.take(jnp.stack(got), (jnp.arange(self.n) - self.z) % self.n, axis=0)
        return stacked.reshape(-1, got[0].shape[1]).astype(f32)


def local(
    n_dp,
    n_head,
    stream_in,
    qkv_weight,
    out_weight,
    up_weight,
    down_weight,
    norm_gains,
    norm_shifts,
    hidden_gains,
    hidden_shifts,
    buckets,
    valid_mask,
    cotangent,
):
    net = Net(n_dp, n_head)
    n = n_head
    layers = qkv_weight.shape[0]
    tokens = LONG // n
    order = Order()

    flags = jnp.concatenate([valid_mask, buckets])
    flags = jnp.pad(flags, (0, -flags.shape[0] % 1024))
    vectors = [
        v.reshape(layers, -1) for v in (norm_gains, norm_shifts, hidden_gains, hidden_shifts)
    ]
    packed = jnp.concatenate(vectors, axis=1)
    narrow, broad = [None] * layers, [None] * layers
    if net.fast:
        small, large = pack_call(qkv_weight, out_weight, up_weight, down_weight)
        rows = stream_in.astype(bf16).reshape(n, tokens, D // n)
        flags = flags.reshape(-1, LANES)
        vector = packed.reshape(-1, LANES)
        started = order(start_call, [small[0], large[0]], rows, vector, flags, first=1)
        (narrow[0], broad[0]), stream, _, packed, flags = started
        narrow[1:] = [net.gather(order.hold(v)) for v in small[1:]]
    else:
        for l in range(layers):
            narrow[l], broad[l] = net.gather_any(
                qkv_weight[l], out_weight[l], up_weight[l], down_weight[l]
            )
        stream = net.rows_in_end(net.rows_in(stream_in))
        flags = lax.ppermute(flags, ("dp", "head"), net.turn(0))
        packed = lax.all_gather(packed.reshape(-1, LANES), "head")
    aux, one, valid, need = masks_call(n, net.lo[None], flags.reshape(-1, LANES))

    low = stream
    cot = cotangent.astype(bf16).reshape(n, tokens, D // n)
    kept = []
    usage = []
    idents = iter(range(10, 64))
    for l in range(layers):
        ahead = net.fast and l + 1 < layers
        parts, _ = order(qkv_call, n, next(idents), [], l, low, packed, narrow[l], first=4)
        if ahead:
            broad[l + 1] = net.gather(order.hold(large[l + 1]))
        parts = [parts[0]] + [[net.shift(v, k) for k, v in enumerate(p)] for p in parts[1:]]
        att, lse = [], []
        for p in parts:
            outs = order(attn_call, n, need, aux, one, p, first=2)
            att.append(outs[0])
            lse.append(outs[1])
        last = net.fast and l + 1 == layers
        jobs = [Turn(cot, False, 0)] if last else []
        mid, rows, use_branch, *extra = order(
            proj_call, n, next(idents), jobs, l, valid, stream, packed, narrow[l], att, first=5
        )
        jobs = [Turn(cot, False, 1, extra[0])] if last else []
        slope, hat, normed, low_mid, rstd, stream, next_low, use_rest, *extra = order(
            ffn_call, n, next(idents), jobs, l, valid, mid, packed, broad[l], first=5
        )
        if last:
            grad = extra[0]
        usage += [use_branch, use_rest]
        kept.append((low, parts, att, lse, rows, slope, hat, normed, low_mid, rstd))
        low = next_low

    if not net.fast:
        grad = net.rows_in_end(net.rows_in(cotangent)).astype(f32)
    if not net.fast:
        grad = net.rows_in_end(net.rows_in(cotangent)).astype(f32)
    low_out = low
    units = BLOCKS // n
    ffn_grads, head_grads = [None] * layers, [None] * layers
    vectors, tops = [None] * layers, []

    for l in reversed(range(layers)):
        low, parts, att, lse, rows, slope, hat, normed, low_mid, rstd = kept[l]
        more = net.fast and l + 1 < layers
        last = net.fast and l + 1 == layers
        jobs = []
        if last:
            jobs = [Turn(low_out, True, 0)]
        if more:
            jobs = [Hop(head_odd, "mate")]
        dhid, grad_turned, ffn_turned, grad, hgrads, grads2, *extra = order(
            ffn_back_call, n, next(idents), jobs, l, grad, hat, slope, rstd,
            low_mid, packed, broad[l], first=4,
        )
        ffn_args = (ffn_turned, grad_turned, dhid, normed)
        if net.fast:
            moved = extra
            if more:
                head_keep, send = order(
                    head_grad_call, n, 0, 4, net.table, *head_args, extra[0], first=4
                )
                head_pair = lax.ppermute(order.hold(send), "dp", net.other_way)
            (odd,) = order(ffn_grad_call, 4, 4, net.table, *ffn_args, first=3)
            jobs = [Hop(odd, "mate")]
            if more:
                ffn_mine, sent = net.add_pair(order.hold(ffn_keep), ffn_pair)
                ffn_last = lax.ppermute(order.want(sent), "dp", net.one_way)
            if last:
                jobs.append(Turn(low_out, True, 1, moved[0]))
        else:
            (full,) = order(ffn_grad_call, 0, BLOCKS, net.table, *ffn_args, first=3)
            ffn_grads[l] = net.scatter(full, (WIDE, WIDE))
        res = order(
            proj_back_call, n, next(idents), jobs, l, grad, packed, narrow[l], rows, first=4
        )
        datt, (out_turned, normed_mid, grads1, *extra) = res[:units], res[units:]
        if net.fast:
            if last:
                turned = extra[1]
            if more:
                head_mine, sent = net.add_pair(order.hold(head_keep), head_pair)
                head_last = lax.ppermute(sent, "dp", net.one_way)
                order.want(sent)
            ffn_keep, send = order(ffn_grad_call, 0, 4, net.table, *ffn_args, extra[0], first=3)
            ffn_send = send
            if more:
                ffn_sum = order.want(net.add_last(order.hold(ffn_mine), ffn_last))
                ffn_near = net.across(ffn_sum[2:], 1)
            if l == 0:
                ffn_pair = lax.ppermute(order.hold(send), "dp", net.other_way)
        dparts, ready = [], []
        for u in range(units):
            ready += [net.shift(v, -k) for k, v in enumerate(dparts)]
            dparts = order(
                attn_back_call, n, need, aux, one, parts[u], att[u], datt[u], lse[u], first=2
            )
            if more and u == 0:
                head_sum = order.want(net.add_last(order.hold(head_mine), head_last))
                ffn_own = order.want(net.add_last(order.hold(ffn_sum[:2]), ffn_near))
        jobs = []
        if net.fast and l == 0:
            ffn_mine, sent = net.add_pair(order.hold(ffn_keep), ffn_pair)
            ffn_last = lax.ppermute(order.want(sent), "dp", net.one_way)
        if more:
            ffn_other = net.across(order.hold(ffn_own[1]), 2)
            head_near = net.across(order.hold(head_sum)[2:], 1)
        dlast, grad, in_turned, grads0, grad_low, *extra = order(
            qkv_back_call, n, next(idents), jobs, l, grad, low, packed, narrow[l], ready, dparts,
            first=4,
        )
        head_args = (in_turned, out_turned, ready + dlast, normed_mid)
        vectors[l] = [grads0, grads1, grads2, hgrads]
        if net.fast:
            if more:
                head_own = order.want(net.add_last(order.hold(head_sum[:2]), head_near))
                tops = [head_own, net.across(head_own[1], 2), ffn_own, ffn_other] + tops
            if l:
                ffn_pair = lax.ppermute(order.hold(ffn_send), "dp", net.other_way)
                (head_odd,) = order(head_grad_call, n, 4, 4, net.table, *head_args, first=4)
            else:
                (full,) = order(head_grad_call, n, 0, BLOCKS, net.table, *head_args, first=4)
        else:
            (full,) = order(head_grad_call, n, 0, BLOCKS, net.table, *head_args, first=4)
            head_grads[l] = net.scatter(full, (HEADS,) * 4)
    vectors = [v for part in vectors for v in part]
    if net.fast:
        ffn_sum = net.add_last(order.hold(ffn_mine), ffn_last)
        (
            stream_out, stream_grad, qkv_grad, out_grad, up_grad, down_grad,
            gains_grad, shifts_grad, hidden_gains_grad, hidden_shifts_grad, usage_rms,
        ) = order(
            end_call, grad_low, full, ffn_sum, turned, valid, tops, vectors, usage
        )
        stream_out = stream_out.reshape(LONG, D // n)
        stream_grad = stream_grad.reshape(LONG, D // n)
        stacked = [qkv_grad, out_grad, up_grad, down_grad]
        usage_rms = usage_rms[: 3 * layers, 0].reshape(layers, 3)
    else:
        stream_out = net.rows_out_end(net.rows_out(stream))
        stream_grad = net.rows_out_end(net.rows_out(grad))
        norms = [jnp.sum(jnp.stack(vectors[4 * l : 4 * l + 3], 1), axis=2) for l in range(layers)]
        norms = lax.psum(jnp.stack(norms), ("dp", "head"))
        hids = [jnp.sum(vectors[4 * l + 3], axis=2).reshape(2, FF) for l in range(layers)]
        hids = lax.psum(jnp.stack(hids), ("dp", "head"))
        share = lambda v: lax.dynamic_slice_in_dim(
            v, net.z * (v.shape[-1] // n), v.shape[-1] // n, v.ndim - 1
        )
        norms, hids = share(norms), share(hids)
        totals = []
        for l in range(layers):
            branch, rest = usage[2 * l : 2 * l + 2]
            totals += [jnp.sum(branch), jnp.sum(rest[0]), jnp.sum(rest[1])]
        totals = lax.psum(jnp.stack(totals + [jnp.sum(valid) * D]), ("dp", "head"))
        usage_rms = jnp.sqrt(totals[:-1] / totals[-1]).reshape(layers, 3)
        weight_grads = []
        for l in range(layers):
            heads = head_grads[l]
            width = heads.shape[1] // 4
            qkv = heads[:, : 3 * width].reshape(-1, 3, width).transpose(1, 0, 2)
            half = ffn_grads[l].shape[1] // 2
            weight_grads.append(
                (qkv, heads[:, 3 * width :].T, ffn_grads[l][:, :half], ffn_grads[l][:, half:].T)
            )
        stacked = [jnp.stack([weight_grads[l][k] for l in range(layers)]) for k in range(4)]
        gains_grad, shifts_grad = norms[:, 0], norms[:, 1]
        hidden_gains_grad, hidden_shifts_grad = hids[:, 0], hids[:, 1]
    return (
        stream_out,
        stream_grad,
        stacked[0],
        stacked[1],
        stacked[2],
        stacked[3],
        gains_grad,
        shifts_grad,
        hidden_gains_grad,
        hidden_shifts_grad,
        usage_rms,
    )


def solution(mesh):
    n_dp, n_head = mesh.shape["dp"], mesh.shape["head"]

    def run(*args):
        return local(n_dp, n_head, *args)

    return jax.shard_map(
        run,
        mesh=mesh,
        in_specs=(
            P("dp", "head"),
            P(None, None, "dp", "head"),
            P(None, "head", "dp"),
            P(None, "dp", "head"),
            P(None, "head", "dp"),
            P(None, None, "head"),
            P(None, None, "head"),
            P(None, "head"),
            P(None, "head"),
            P("dp"),
            P("dp"),
            P("dp", "head"),
        ),
        out_specs=(
            P("dp", "head"),
            P("dp", "head"),
            P(None, None, "dp", "head"),
            P(None, "head", "dp"),
            P(None, "dp", "head"),
            P(None, "head", "dp"),
            P(None, None, "head"),
            P(None, None, "head"),
            P(None, "head"),
            P(None, "head"),
            P(),
        ),
        check_vma=False,
    )
```

```python
import functools
import math

import jax
import jax.numpy as jnp
from jax import lax
from jax.experimental import pallas as pl
from jax.experimental.pallas import tpu as pltpu
from jax.sharding import PartitionSpec as P

D = 1024
FF = 4096
LONG = 2048
SHORT = 512
DH = 64
LANES = 128
BLOCKS = D // LANES
GROUPS = 4
WIDE = FF // GROUPS
HEADS = D // GROUPS
NARROW = 4 * HEADS
BROAD = 2 * WIDE
EPS = 1e-05
MASKED = -1000000000.0
ROWS = 256
CHUNK = 256
VMEM_BYTES = 60 * 1024 * 1024
MESH = pl.DeviceIdType.MESH

f32 = jnp.float32
bf16 = jnp.bfloat16


def dot(a, b):
    return jnp.dot(a, b, preferred_element_type=f32)


def dot_nt(a, b):
    return lax.dot_general(a, b, (((1,), (1,)), ((), ())), preferred_element_type=f32)


def flip(a):
    return jnp.transpose(a.astype(f32), (1, 0)).astype(a.dtype)


def row_loop(total, step, body):
    def advance(i, carry):
        body(pl.ds(pl.multiple_of(i * step, step), step))
        return carry

    lax.fori_loop(0, total // step, advance, 0)


def sum_lanes(value):
    return jnp.sum(value, axis=1, keepdims=True)


def fold_lanes(value):
    total = value[:, :LANES]
    for i in range(1, value.shape[1] // LANES):
        total = total + value[:, i * LANES : (i + 1) * LANES]
    return total


def fold_rows(value):
    total = value[:8]
    for i in range(1, value.shape[0] // 8):
        total = total + value[i * 8 : (i + 1) * 8]
    return total


def row_stats(value):
    mean = sum_lanes(value) / D
    centred = value - mean
    rstd = lax.rsqrt(sum_lanes(centred * centred) / D + EPS)
    return centred * rstd, rstd


def norm_back(dy, hat, rstd, gain):
    dx = dy * gain
    first = sum_lanes(dx) / D
    cross = sum_lanes(dx * hat) / D
    return rstd * (dx - first - hat * cross)


class Vectors:
    def __init__(self, n, layer, ref):
        self.n, self.ref = n, ref
        self.few, self.many = BLOCKS // n, 4 * BLOCKS // n
        self.at = layer * (6 * self.few + 2 * self.many)

    def rows(self, z, first, count):
        return [self.ref[z, first + p : first + p + 1, :] for p in range(count)]

    def norm(self, kind, which):
        first = self.at + (3 * kind + which) * self.few
        parts = [v for z in range(self.n) for v in self.rows(z, first, self.few)]
        return jnp.concatenate(parts, axis=1)

    def hidden(self, kind, group):
        first = self.at + 6 * self.few + kind * self.many
        share = self.n // GROUPS
        parts = [v for i in range(share) for v in self.rows(group * share + i, first, self.many)]
        return jnp.concatenate(parts, axis=1)


def params(**kw):
    return pltpu.CompilerParams(vmem_limit_bytes=VMEM_BYTES, **kw)


def cost(flops, size, trans=0):
    return pl.CostEstimate(flops=int(flops), bytes_accessed=int(size), transcendentals=int(trans))


def whole(shape):
    zeros = (0,) * len(shape)
    return pl.BlockSpec(shape, lambda *_: zeros)


def shape(dims, kind):
    return jax.ShapeDtypeStruct(dims, kind)


VM = pl.BlockSpec(memory_space=pltpu.VMEM)
HB = pl.BlockSpec(memory_space=pl.ANY)
DMA = pltpu.SemaphoreType.DMA


def group_place(n):
    dp = lax.axis_index("dp")
    lo = lax.rem(dp, n)
    return dp - lo, lo


def group_send(n, k, source, target, send_sem, recv_sem):
    base, lo = group_place(n)
    return pltpu.make_async_remote_copy(
        src_ref=source,
        dst_ref=target,
        send_sem=send_sem,
        recv_sem=recv_sem,
        device_id={"dp": base + lax.rem(lo + k + n, n)},
        device_id_type=MESH,
    )


def order_of(n):
    return [k for k in (n // 2, *range(1, n // 2), *range(n // 2 + 1, n)) if k]


def head_columns(n, k):
    _, lo = group_place(n)
    unit = lax.rem(lo + k + n, n) * (BLOCKS // n)
    if n == GROUPS:
        return lax.rem(lo + k + n, n), 0
    return unit // 2, pl.multiple_of(lax.rem(unit, 2) * LANES, LANES)


class Place:
    def __init__(self):
        dp = lax.axis_index("dp")
        self.z = lax.axis_index("head")
        self.lo = lax.rem(dp, GROUPS)
        core = lax.rem(dp, 2)
        bit_x = lax.rem(dp // 2, 2)
        bit_y = lax.rem(dp // 4, 2)
        by_x = dp + 2 - 4 * bit_x
        by_y = dp + 4 - 8 * bit_y
        self.dp, self.core, self.bit_x = dp, core, bit_x
        self.by_x, self.by_y = by_x, by_y
        self.first = by_x * (1 - core) + by_y * core
        self.second = by_y * (1 - core) + by_x * core
        self.both = by_x + by_y - dp
        self.mate = dp + 1 - 2 * core

    def partner(self, way):
        return {"mate": self.mate, "first": self.first, "second": self.second}[way]

    def group(self, p):
        one, two = 1 - 2 * lax.rem(self.z, 2), 2 - 4 * (self.z // 2)
        return self.z + (0, two, one, one + two)[p]

    def others(self):
        return [{"head": lax.rem(self.z + k, GROUPS)} for k in range(1, GROUPS)]


def unlike(a, b):
    return jnp.where(a == b, 0, 1)


class Hop:
    aliases = {}

    def __init__(self, array, way):
        self.arrays, self.way = [array], way
        self.outs = [jax.ShapeDtypeStruct(array.shape, array.dtype)]
        self.sems = [DMA((2,))]

    def device(self, at):
        return {"dp": at.partner(self.way)}

    def peers(self, at):
        return [self.device(at)], [], 1

    def copy(self, at, ins, outs, sems):
        return pltpu.make_async_remote_copy(
            src_ref=ins[0],
            dst_ref=outs[0],
            send_sem=sems[0].at[0],
            recv_sem=sems[0].at[1],
            device_id=self.device(at),
            device_id_type=MESH,
        )

    def start(self, *args):
        self.copy(*args).start()

    def finish(self, *args):
        self.copy(*args).wait()


class Turn:
    def __init__(self, array, back, half=None, into=None):
        self.arrays, self.back = [array], back
        self.aliases = {}
        if into is not None:
            self.arrays.append(into)
            self.aliases = {1: 0}
        if back:
            tokens, wide = array.shape[0], array.shape[1] // GROUPS
            out = (GROUPS, tokens, wide)
        else:
            tokens, wide = array.shape[1:]
            out = (tokens, GROUPS * wide)
        self.wide = wide
        self.rows = pl.ds(0, tokens) if half is None else pl.ds(half * (tokens // 2), tokens // 2)
        self.outs = [jax.ShapeDtypeStruct(out, array.dtype)]
        self.sems = [DMA((2, GROUPS)), DMA]

    def many(self, at):
        return [(at.dp - at.lo + t, at.lo) for t in range(GROUPS)]

    def one(self, at):
        return [(at.dp - at.lo + at.z, g) for g in range(GROUPS)]

    def peers(self, at):
        from_ = self.many(at) if self.back else self.one(at)
        return [], from_, GROUPS - 1 + unlike(at.z, at.lo)

    def each(self, op, at, ins, outs, sems):
        targets = self.one(at) if self.back else self.many(at)
        for i, (dp, z) in enumerate(targets):
            if self.back:
                source = ins[0].at[self.rows, pl.ds(i * self.wide, self.wide)]
                target, slot = outs[0].at[at.lo, self.rows], at.lo
            else:
                source = ins[0].at[i, self.rows]
                column = pl.multiple_of(at.z * self.wide, self.wide)
                target, slot = outs[0].at[self.rows, pl.ds(column, self.wide)], at.z

            def remote(i=i, dp=dp, z=z, source=source, target=target, slot=slot):
                copy = pltpu.make_async_remote_copy(
                    src_ref=source,
                    dst_ref=target,
                    send_sem=sems[0].at[0, i],
                    recv_sem=sems[0].at[1, slot],
                    device_id={"dp": dp, "head": z},
                    device_id_type=MESH,
                )
                copy.start() if op == "start" else copy.wait_send()

            def inside(source=source, target=target):
                copy = pltpu.make_async_copy(source, target, sems[1])
                copy.start() if op == "start" else copy.wait()

            away = (dp != at.dp) | (z != at.z)
            pl.when(away)(remote)
            pl.when(jnp.logical_not(away))(inside)

    def start(self, *args):
        self.each("start", *args)

    def finish(self, at, ins, outs, sems):
        self.each("wait", at, ins, outs, sems)
        sources = self.many(at) if self.back else self.one(at)
        for slot, (dp, z) in enumerate(sources):

            @pl.when((dp != at.dp) | (z != at.z))
            def _(slot=slot):
                if self.back:
                    spot = outs[0].at[slot, self.rows]
                else:
                    spot = outs[0].at[self.rows, pl.ds(slot * self.wide, self.wide)]
                pltpu.make_async_remote_copy(
                    src_ref=spot,
                    dst_ref=spot,
                    send_sem=sems[0].at[0, 0],
                    recv_sem=sems[0].at[1, slot],
                    device_id={"dp": at.mate},
                    device_id_type=MESH,
                ).wait_recv()


class Host:
    def __init__(self, n, parts):
        self.n, self.parts = n, parts
        self.at = Place() if parts else None

    def barrier(self, group=True):
        n = self.n
        sem = pltpu.get_barrier_semaphore()
        count = 0
        if group:
            base, lo = group_place(n)
            for k in range(1, n):
                pl.semaphore_signal(
                    sem, inc=1, device_id={"dp": base + lax.rem(lo + k, n)}, device_id_type=MESH
                )
            count = n - 1
        for job, *_ in self.parts:
            plain, pairs, more = job.peers(self.at)
            for device in plain:
                pl.semaphore_signal(sem, inc=1, device_id=device, device_id_type=MESH)
            for dp, z in pairs:

                @pl.when((dp != self.at.dp) | (z != self.at.z))
                def _(dp=dp, z=z):
                    pl.semaphore_signal(
                        sem, inc=1, device_id={"dp": dp, "head": z}, device_id_type=MESH
                    )

            count = count + more
        pl.semaphore_wait(sem, count)

    def start(self):
        for job, *refs in self.parts:
            job.start(self.at, *refs)

    def finish(self):
        for job, *refs in self.parts:
            job.finish(self.at, *refs)


def plain_call(
    body, n, name, ident, inputs, in_specs, out_shape, out_specs, scratch, flops, jobs, grid=()
):
    return list(
        pl.pallas_call(
            lambda *refs: body(Host(n, []), *refs),
            out_shape=out_shape,
            grid=grid,
            in_specs=in_specs,
            out_specs=out_specs,
            scratch_shapes=scratch,
            compiler_params=params(),
            cost_estimate=cost(flops, 10 * 2**20),
            name=name,
        )(*inputs)
    )


def remote_call(
    body, n, name, ident, inputs, in_specs, out_shape, out_specs, scratch, flops, jobs, grid=()
):
    job_in = [v for job in jobs for v in job.arrays]
    job_out = [v for job in jobs for v in job.outs]
    job_sems = [v for job in jobs for v in job.sems]
    aliases = {}
    i, o = len(inputs), len(out_shape)
    for job in jobs:
        aliases.update({i + a: o + b for a, b in job.aliases.items()})
        i, o = i + len(job.arrays), o + len(job.outs)

    def kernel(*refs):
        refs = list(refs)

        def take(count):
            taken = refs[:count]
            del refs[:count]
            return taken

        own_in, extra_in = take(len(inputs)), take(len(job_in))
        own_out, extra_out = take(len(out_shape)), take(len(job_out))
        own_scratch, extra_sems = take(len(scratch)), take(len(job_sems))
        parts = []
        for job in jobs:
            sizes = (len(job.arrays), len(job.outs), len(job.sems))
            lists = (extra_in, extra_out, extra_sems)
            part = [job]
            for values, size in zip(lists, sizes):
                part.append(values[:size])
                del values[:size]
            parts.append(part)
        body(Host(n, parts), *own_in, *own_out, *own_scratch)

    res = pl.pallas_call(
        kernel,
        out_shape=list(out_shape) + job_out,
        grid=grid,
        in_specs=list(in_specs) + [HB] * len(job_in),
        out_specs=list(out_specs) + [HB] * len(job_out),
        scratch_shapes=list(scratch) + job_sems,
        input_output_aliases=aliases,
        compiler_params=params(collective_id=ident, has_side_effects=True),
        cost_estimate=cost(flops, 10 * 2**20),
        name=name,
    )(*inputs, *job_in)
    return list(res)


class Queries:
    def __init__(self, n, weight, outs, xs, wide, send, wsem, ssem, rsem, lsem):
        self.n, self.weight, self.outs, self.xs, self.wide, self.send = n, weight, outs, xs, wide, send
        self.wsem, self.ssem, self.rsem, self.lsem = wsem, ssem, rsem, lsem
        self.units = BLOCKS // n
        self.steps = order_of(n) + [0]

    def fetch(self, i):
        group, offset = head_columns(self.n, self.steps[i])
        width = self.units * LANES
        return [
            pltpu.make_async_copy(
                self.weight.at[:, group, :, pl.ds(c * HEADS + offset, width)],
                self.wide.at[i % 2, c],
                self.wsem.at[i % 2, c],
            )
            for c in range(3)
        ]

    def begin(self):
        for copy in self.fetch(0):
            copy.start()

    def norm(self, low, gain, shift):
        def body(r):
            hat, _ = row_stats(low[r, :].astype(f32))
            self.xs[r, :] = (hat * gain + shift).astype(bf16)

        row_loop(low.shape[0], ROWS, body)

    def copy(self, k):
        if k:
            return group_send(
                self.n, k, self.send.at[k], self.outs[k], self.ssem.at[k], self.rsem.at[k]
            )
        return pltpu.make_async_copy(self.send.at[0], self.outs[0], self.lsem)

    def step(self, i):
        k = self.steps[i]
        if i + 1 < self.n:
            for copy in self.fetch(i + 1):
                copy.start()
        for c, copy in enumerate(self.fetch(i)):
            copy.wait()
            value = dot(self.xs[...], self.wide[i % 2, c].reshape(D, -1)).astype(bf16)
            self.send[k, c] = value[:, :LANES]
            for u in range(1, self.units):
                self.outs[u * self.n + k][c] = value[:, u * LANES : (u + 1) * LANES]
        self.copy(k).start()

    def finish(self):
        for k in self.steps:
            self.copy(k).wait()


def queries_scratch(n, tokens):
    return [
        pltpu.VMEM((tokens, D), bf16),
        pltpu.VMEM((2, 3, BLOCKS, LANES, BLOCKS // n * LANES), bf16),
        pltpu.VMEM((n, 3, tokens, LANES), bf16),
        DMA((2, 3)),
        DMA((n,)),
        DMA((n,)),
        DMA,
    ]


def queries_outs(n, tokens):
    count = BLOCKS // n * n
    return [jax.ShapeDtypeStruct((3, tokens, LANES), bf16)] * count, [HB] * n + [VM] * (count - n)


def qkv_kernel(layer, host, low, packed, weight, *refs):
    vectors = Vectors(host.n, layer, packed)
    queries = Queries(host.n, weight, refs[:-7], *refs[-7:])
    queries.begin()
    queries.norm(low, vectors.norm(0, 0), vectors.norm(1, 0))
    host.barrier()
    host.start()
    for i in range(host.n):
        queries.step(i)
    queries.finish()
    host.finish()


def qkv_call(n, ident, jobs, layer, low, packed, weight):
    tokens = low.shape[0]
    units = BLOCKS // n
    out_shape, out_specs = queries_outs(n, tokens)
    res = remote_call(
        functools.partial(qkv_kernel, layer), n, "qkv", ident,
        [low, packed, weight], [VM, VM, HB], out_shape, out_specs, queries_scratch(n, tokens),
        60 * tokens * D * D, jobs,
    )
    return [res[u * n : (u + 1) * n] for u in range(units)], res[n * units :]


def masks_kernel(n, sc, flags, aux, one, valid, need):
    tokens = aux.shape[1]
    rows = tokens // LANES
    first = lax.broadcasted_iota(jnp.int32, (LANES, LANES), 1) == 0
    one[...] = jnp.where(lax.broadcasted_iota(jnp.int32, one.shape, 1) == 0, 1.0, 0.0).astype(bf16)
    long = jnp.max(flags[LONG // LANES : LONG // LANES + 1, 0:1]) == 1
    alive, sequence = [], []
    for k in range(n):
        place = lax.rem(sc[0] + n - k, n)
        some = jnp.float32(0)
        for i in range(rows):
            row = flags[pl.ds(place * rows + i, 1), :].astype(f32)
            some = jnp.maximum(some, jnp.max(row))
            column = jnp.transpose(jnp.broadcast_to(row, (LANES, LANES)), (1, 0))
            spot = slice(i * LANES, (i + 1) * LANES)
            aux[k, spot, :] = jnp.where(first & (column == 0), MASKED, 0.0).astype(bf16)
            if k == 0:
                valid[spot, :] = column[:, 0:1]
        alive.append(some > 0)
        sequence.append(place * tokens // SHORT)
    for i in range(n):
        for j in range(n):
            joined = long | (sequence[i] == sequence[j])
            need[i * n + j] = jnp.where(joined & alive[j], 1, 0).astype(jnp.int32)


def masks_call(n, lo, flags):
    tokens = LONG // n
    return pl.pallas_call(
        lambda *refs: masks_kernel(n, *refs),
        out_shape=[
            jax.ShapeDtypeStruct((n, tokens, LANES), bf16),
            jax.ShapeDtypeStruct((tokens, LANES), bf16),
            jax.ShapeDtypeStruct((tokens, 1), f32),
            jax.ShapeDtypeStruct((n * n,), jnp.int32),
        ],
        grid_spec=pltpu.PrefetchScalarGridSpec(
            num_scalar_prefetch=1,
            grid=(),
            in_specs=[VM],
            out_specs=[VM, VM, VM, pl.BlockSpec(memory_space=pltpu.SMEM)],
        ),
        compiler_params=params(),
        cost_estimate=cost(0, 2**20),
        name="masks",
    )(lo, flags)


def head_lanes(value, head):
    lane = lax.broadcasted_iota(jnp.int32, value.shape, 1)
    keep = (lane < DH) if head == 0 else (lane >= DH)
    return jnp.where(keep, value, jnp.zeros_like(value))


def attn_kernel(n, need, aux, one, *refs):
    qkv, (outs, lse, kx, vt, qs, top, acc) = refs[:n], refs[n:]
    tokens = aux.shape[1]
    for r in range(n):
        kx[r] = jnp.concatenate([qkv[r][1], aux[r]], axis=1)
        turned = flip(qkv[r][2])
        ones = jnp.ones((16, tokens), bf16)
        vt[r, 0] = jnp.concatenate([turned[:DH], ones], axis=0)
        vt[r, 1] = jnp.concatenate([turned[DH:], ones], axis=0)
        qs[r] = (qkv[r][0].astype(f32) * (1.0 / math.sqrt(DH))).astype(bf16)

    halves = jnp.where(
        lax.broadcasted_iota(jnp.int32, (LANES, LANES), 0) // DH
        == lax.broadcasted_iota(jnp.int32, (LANES, LANES), 1),
        1.0,
        0.0,
    ).astype(bf16)
    reach = jnp.zeros((1, LANES), f32)
    longest = jnp.zeros((1, LANES), f32)
    for r in range(n):
        for which, value in ((0, qs[r]), (1, qkv[r][1])):
            size = jnp.max(dot(value * value, halves), axis=0, keepdims=True)
            if which:
                longest = jnp.maximum(longest, size)
            else:
                reach = jnp.maximum(reach, size)
    bounded = jnp.max(reach * longest) < 70.0 * 70.0

    def each_query(plain, i, carry):
        query = qs[i]
        extended = [jnp.concatenate([head_lanes(query, h), one[...]], axis=1) for h in range(2)]
        top[...] = jnp.zeros_like(top) if plain else jnp.full_like(top, -3e38)
        acc[...] = jnp.zeros_like(acc)

        def each_key(j, inner):
            @pl.when(need[i * n + j] == 1)
            def _():
                if plain:
                    raised = [jnp.exp(dot_nt(kx[j], extended[h])).astype(bf16) for h in range(2)]
                    for h in range(2):
                        acc[h] += dot(vt[j, h], raised[h])
                    return
                for h in range(2):
                    scores = dot_nt(kx[j], extended[h])
                    before = top[h : h + 1]
                    now = jnp.maximum(before, jnp.max(scores, axis=0, keepdims=True))
                    raised = jnp.exp(scores - now).astype(bf16)
                    top[h : h + 1] = now
                    acc[h] = acc[h] * jnp.exp(before - now) + dot(vt[j, h], raised)

            return inner

        lax.fori_loop(0, n, each_key, 0)
        sums = [acc[h][DH : DH + 1] for h in range(2)]
        both = jnp.concatenate([acc[h][:DH] / sums[h] for h in range(2)], axis=0)
        outs[i] = jnp.transpose(both, (1, 0)).astype(bf16)
        for h in range(2):
            lse[i, h : h + 1] = top[h : h + 1] + jnp.log(sums[h])
        return carry

    @pl.when(bounded)
    def _():
        lax.fori_loop(0, n, functools.partial(each_query, True), 0)

    @pl.when(jnp.logical_not(bounded))
    def _():
        lax.fori_loop(0, n, functools.partial(each_query, False), 0)


def unit_call(kernel, n, need, aux, one, arrays, out_shape, scratch, work, name):
    total = n * aux.shape[1]
    return pl.pallas_call(
        lambda *refs: kernel(n, *refs),
        out_shape=out_shape,
        grid_spec=pltpu.PrefetchScalarGridSpec(
            num_scalar_prefetch=1,
            grid=(),
            in_specs=[VM] * (2 + len(arrays)),
            out_specs=[VM] * len(out_shape),
            scratch_shapes=scratch,
        ),
        compiler_params=params(),
        cost_estimate=cost(work * total * total * 512, 8 * 2**20),
        name=name,
    )(need, aux, one, *arrays)


def attn_call(n, need, aux, one, parts):
    tokens = aux.shape[1]
    return unit_call(
        attn_kernel, n, need, aux, one, parts,
        [
            jax.ShapeDtypeStruct((n, tokens, LANES), bf16),
            jax.ShapeDtypeStruct((n, 8, tokens), f32),
        ],
        [
            pltpu.VMEM((n, tokens, 2 * LANES), bf16),
            pltpu.VMEM((n, 2, DH + 16, tokens), bf16),
            pltpu.VMEM((n, tokens, LANES), bf16),
            pltpu.VMEM((8, tokens), f32),
            pltpu.VMEM((2, DH + 16, tokens), f32),
        ],
        12, "attention",
    )


def proj_kernel(layer, host, valid, stream, packed, weight, *refs):
    n = host.n
    vectors = Vectors(n, layer, packed)
    gain, shift = vectors.norm(0, 1), vectors.norm(1, 1)
    tokens = stream.shape[0]
    units = BLOCKS // n
    att, (mid, rows, use, xs, rx, ssem, rsem, lsem) = refs[:units], refs[units:]
    host.barrier()
    copies = [
        group_send(n, -k, att[u].at[k], rx.at[k, u], ssem.at[u, k], rsem.at[u, k])
        for k in order_of(n)
        for u in range(units)
    ]
    copies += [pltpu.make_async_copy(att[u].at[0], rx.at[0, u], lsem.at[u]) for u in range(units)]
    for copy in copies:
        copy.start()
    host.start()
    for copy in copies:
        copy.wait()
    _, lo = group_place(n)
    for k in range(n):
        first = lax.rem(lo + k, n) * (units * LANES)
        for u in range(units):
            at = pl.multiple_of(first + u * LANES, LANES)
            rows[:, pl.ds(at, LANES)] = rx[k, u]

    def body(r):
        hat, _ = row_stats(rows[r, :].astype(f32))
        xs[r, :] = (hat * gain + shift).astype(bf16)

    row_loop(tokens, ROWS, body)
    branch = None
    for g in range(GROUPS):
        term = dot_nt(xs[:, g * HEADS : (g + 1) * HEADS], weight[:, g].reshape(D, HEADS))
        branch = term if branch is None else branch + term
    mid[...] = branch
    use[...] = jnp.zeros_like(use)

    def finish(r):
        part = mid[r, :]
        use[...] += fold_rows(valid[r, :] * part * part)
        mid[r, :] = stream[r, :].astype(f32) + part

    row_loop(tokens, ROWS, finish)
    host.finish()


def proj_call(n, ident, jobs, layer, valid, stream, packed, weight, att):
    tokens = stream.shape[0]
    units = BLOCKS // n
    flat = whole(stream.shape)
    return remote_call(
        functools.partial(proj_kernel, layer), n, "projection", ident,
        [valid, stream, packed, weight, *att],
        [whole(v.shape) for v in (valid, stream, packed)]
        + [pl.BlockSpec((BLOCKS, GROUPS, LANES, HEADS), lambda i: (0, 0, 0, 3))]
        + [whole(v.shape) for v in att],
        [
            jax.ShapeDtypeStruct(stream.shape, f32),
            jax.ShapeDtypeStruct(stream.shape, bf16),
            jax.ShapeDtypeStruct((8, D), f32),
        ],
        [flat, flat, whole((8, D))],
        [
            pltpu.VMEM((tokens, D), bf16),
            pltpu.VMEM((n, units, tokens, LANES), bf16),
            DMA((units, n)),
            DMA((units, n)),
            DMA((units,)),
        ],
        30 * tokens * D * D, jobs, grid=(1,),
    )


def ffn_kernel(
    layer, host, valid, mid, packed, weight,
    slope, hat, normed, low_mid, rstd_out, stream, low, use,
    xs, act, mean, buf, acc,
):
    step = pl.program_id(0)
    tokens = mid.shape[0]
    vectors = Vectors(host.n, layer, packed)

    @pl.when(step == 0)
    def _():
        gain, shift = vectors.norm(0, 2), vectors.norm(1, 2)
        use[...] = jnp.zeros_like(use)

        def body(r):
            raw = mid[r, :].astype(bf16)
            value, _ = row_stats(raw.astype(f32))
            low_mid[r, :] = raw
            xs[r, :] = (value * gain + shift).astype(bf16)

        row_loop(tokens, ROWS, body)
        if host.parts:
            host.barrier(False)
            host.start()

    @pl.when(step < GROUPS)
    def _():
        buf[...] = dot(xs[...], weight[...].reshape(D, WIDE))

        def body(r):
            h = buf[r, :]
            half = 0.5 * (1.0 + lax.erf(h * (1.0 / math.sqrt(2.0))))
            bell = jnp.exp(-0.5 * h * h) * (1.0 / math.sqrt(2.0 * math.pi))
            act[step, r, :] = h * half
            slope[0, r, :] = (half + h * bell).astype(bf16)

        row_loop(tokens, CHUNK, body)

    @pl.when(step == GROUPS)
    def _():
        acc[...] = jnp.zeros_like(acc)

        def body(r):
            blocks = [act[g, r, :] for g in range(GROUPS)]
            total = sum_lanes(sum(fold_lanes(b) for b in blocks)) / FF
            square = sum(fold_lanes((b - total) * (b - total)) for b in blocks)
            rstd = lax.rsqrt(sum_lanes(square) / FF + EPS)
            mean[r, :] = jnp.broadcast_to(total, (CHUNK, LANES))
            rstd_out[r, :] = jnp.broadcast_to(rstd, (CHUNK, LANES))

        row_loop(tokens, CHUNK, body)

    @pl.when(step >= GROUPS)
    def _():
        g = step - GROUPS
        hgain, hshift = vectors.hidden(0, g), vectors.hidden(1, g)

        def body(r):
            value = (act[g, r, :] - mean[r, 0:1]) * rstd_out[r, 0:1]
            hat[0, r, :] = value.astype(bf16)
            normed[0, r, :] = (value * hgain + hshift).astype(bf16)

        row_loop(tokens, CHUNK, body)
        acc[...] += dot_nt(normed[0], weight[...].reshape(D, WIDE))

    @pl.when(step == 2 * GROUPS - 1)
    def _():
        def body(r):
            feed = acc[r, :]
            out = mid[r, :] + feed
            keep = valid[r, :]
            stream[r, :] = out
            low[r, :] = out.astype(bf16)
            use[0] += fold_rows(keep * feed * feed)
            use[1] += fold_rows(keep * out * out)

        row_loop(tokens, ROWS, body)

        host.finish()


def first_half(s):
    return jnp.minimum(s, GROUPS - 1)


def second_half(s):
    return jnp.maximum(s - GROUPS, 0)


def half_specs(tokens):
    early = pl.BlockSpec((1, tokens, WIDE), lambda s: (first_half(s), 0, 0))
    late = pl.BlockSpec((1, tokens, WIDE), lambda s: (second_half(s), 0, 0))
    return early, late


def ffn_call(n, ident, jobs, layer, valid, mid, packed, weight):
    tokens = mid.shape[0]
    big = (GROUPS, tokens, WIDE)
    early, late = half_specs(tokens)
    flat = (tokens, D)
    call = remote_call if jobs else plain_call
    return call(
        functools.partial(ffn_kernel, layer), n, "ffn", ident,
        [valid, mid, packed, weight],
        [whole(v.shape) for v in (valid, mid, packed)]
        + [
            pl.BlockSpec(
                (BLOCKS, 1, LANES, WIDE), lambda s: (0, lax.rem(s, GROUPS), 0, s // GROUPS)
            )
        ],
        [jax.ShapeDtypeStruct(big, bf16)] * 3
        + [
            jax.ShapeDtypeStruct(flat, bf16),
            jax.ShapeDtypeStruct((tokens, LANES), f32),
            jax.ShapeDtypeStruct(flat, f32),
            jax.ShapeDtypeStruct(flat, bf16),
            jax.ShapeDtypeStruct((2, 8, D), f32),
        ],
        [early, late, late]
        + [whole(flat), whole((tokens, LANES)), whole(flat), whole(flat), whole((2, 8, D))],
        [
            pltpu.VMEM(flat, bf16),
            pltpu.VMEM(big, f32),
            pltpu.VMEM((tokens, LANES), f32),
            pltpu.VMEM((tokens, WIDE), f32),
            pltpu.VMEM(flat, f32),
        ],
        16 * tokens * D * FF, jobs, grid=(2 * GROUPS,),
    )


def ffn_back_kernel(
    layer, host, grad, hat, slope, rstd_in, low_mid, packed, weight,
    dhid, grad_turned, normed_turned, grad_out, hgrads, grads,
    gs, dxs, buf, first, cross, acc,
):
    step = pl.program_id(0)
    tokens = grad.shape[0]
    vectors = Vectors(host.n, layer, packed)

    @pl.when(step == 0)
    def _():
        first[...] = jnp.zeros_like(first)
        cross[...] = jnp.zeros_like(cross)
        hgrads[...] = jnp.zeros_like(hgrads)
        grads[...] = jnp.zeros_like(grads)
        gs[...] = grad[...].astype(bf16)
        for b in range(BLOCKS):
            grad_turned[b] = flip(gs[:, b * LANES : (b + 1) * LANES])
        if host.parts:
            host.barrier(False)
            host.start()

    @pl.when(step < GROUPS)
    def _():
        buf[...] = dot(gs[...], weight[...].reshape(D, WIDE))
        hgain = vectors.hidden(0, step)

        def body(r):
            value = hat[0, r, :].astype(f32)
            dy = buf[r, :]
            dx = dy * hgain
            hgrads[0, step] += fold_rows(dy * value)
            hgrads[1, step] += fold_rows(dy)
            first[r, :] += fold_lanes(dx)
            cross[r, :] += fold_lanes(dx * value)
            dxs[step, r, :] = dx

        row_loop(tokens, CHUNK, body)

    @pl.when(step == GROUPS)
    def _():
        acc[...] = jnp.zeros_like(acc)

        def body(r):
            first[r, :] = jnp.broadcast_to(sum_lanes(first[r, :]) / FF, (ROWS, LANES))
            cross[r, :] = jnp.broadcast_to(sum_lanes(cross[r, :]) / FF, (ROWS, LANES))

        row_loop(tokens, ROWS, body)

    @pl.when(step >= GROUPS)
    def _():
        g = step - GROUPS

        def body(r):
            inner = dxs[g, r, :] - first[r, 0:1] - hat[0, r, :].astype(f32) * cross[r, 0:1]
            dhid[0, r, :] = (slope[0, r, :].astype(f32) * (rstd_in[r, 0:1] * inner)).astype(bf16)

        row_loop(tokens, CHUNK, body)
        acc[...] += dot_nt(dhid[0], weight[...].reshape(D, WIDE))

    @pl.when(step == 2 * GROUPS - 1)
    def _():
        gain, shift = vectors.norm(0, 2), vectors.norm(1, 2)

        def body(r):
            value, rstd = row_stats(low_mid[r, :].astype(f32))
            dy = acc[r, :]
            grads[0] += fold_rows(dy * value)
            grads[1] += fold_rows(dy)
            grad_out[r, :] = grad[r, :].astype(f32) + norm_back(dy, value, rstd, gain)
            gs[r, :] = (value * gain + shift).astype(bf16)

        row_loop(tokens, ROWS, body)
        for b in range(BLOCKS):
            normed_turned[b] = flip(gs[:, b * LANES : (b + 1) * LANES])
        host.finish()


def ffn_back_call(n, ident, jobs, layer, grad, hat, slope, rstd, low_mid, packed, weight):
    tokens = grad.shape[0]
    turned = (BLOCKS, LANES, tokens)
    big = (GROUPS, tokens, WIDE)
    _, late = half_specs(tokens)
    flat = (tokens, D)
    call = remote_call if jobs else plain_call
    return call(
        functools.partial(ffn_back_kernel, layer), n, "ffn_back", ident,
        [grad, hat, slope, rstd, low_mid, packed, weight],
        [
            whole(flat),
            pl.BlockSpec((1, tokens, WIDE), lambda s: (lax.rem(s, GROUPS), 0, 0)),
            late,
        ]
        + [whole(v.shape) for v in (rstd, low_mid, packed)]
        + [
            pl.BlockSpec(
                (BLOCKS, 1, LANES, WIDE), lambda s: (0, lax.rem(s, GROUPS), 0, 1 - s // GROUPS)
            )
        ],
        [
            jax.ShapeDtypeStruct(big, bf16),
            jax.ShapeDtypeStruct(turned, bf16),
            jax.ShapeDtypeStruct(turned, bf16),
            jax.ShapeDtypeStruct(flat, f32),
            jax.ShapeDtypeStruct((2, GROUPS, 8, WIDE), f32),
            jax.ShapeDtypeStruct((2, 8, D), f32),
        ],
        [late, whole(turned), whole(turned), whole(flat)]
        + [whole((2, GROUPS, 8, WIDE)), whole((2, 8, D))],
        [
            pltpu.VMEM(flat, bf16),
            pltpu.VMEM(big, f32),
            pltpu.VMEM((tokens, WIDE), f32),
            pltpu.VMEM((tokens, LANES), f32),
            pltpu.VMEM((tokens, LANES), f32),
            pltpu.VMEM(flat, f32),
        ],
        16 * tokens * D * FF, jobs, grid=(2 * GROUPS,),
    )


def proj_back_kernel(
    layer, host, grad, packed, weight, rows, *refs
):
    n = host.n
    vectors = Vectors(n, layer, packed)
    gain, shift = vectors.norm(0, 1), vectors.norm(1, 1)
    tokens = grad.shape[0]
    units = BLOCKS // n
    outs, refs = refs[:units], refs[units:]
    grad_turned, normed, grads, gs, dm, send, ssem, rsem, lsem = refs
    host.barrier()
    host.start()
    gs[...] = grad[...].astype(bf16)
    for g in range(GROUPS):
        dm[:, g * HEADS : (g + 1) * HEADS] = dot(gs[...], weight[:, g].reshape(D, HEADS))
    grads[...] = jnp.zeros_like(grads)

    def body(r):
        value, rstd = row_stats(rows[r, :].astype(f32))
        dy = dm[r, :]
        grads[0] += fold_rows(dy * value)
        grads[1] += fold_rows(dy)
        dv = norm_back(dy, value, rstd, gain).astype(bf16)
        for b in range(BLOCKS):
            send[b, r, :] = dv[:, b * LANES : (b + 1) * LANES]
        normed[r, :] = (value * gain + shift).astype(bf16)

    row_loop(tokens, ROWS, body)
    _, lo = group_place(n)
    copies = []
    for k in order_of(n) + [0]:
        for u in range(units):
            source = send.at[lax.rem(lo + k, n) * units + u]
            if k:
                copy = group_send(n, k, source, outs[u].at[k], ssem.at[u, k], rsem.at[u, k])
            else:
                copy = pltpu.make_async_copy(source, outs[u].at[0], lsem.at[u])
            copy.start()
            copies.append(copy)
    for b in range(BLOCKS):
        grad_turned[b] = flip(gs[:, b * LANES : (b + 1) * LANES])
    for copy in copies:
        copy.wait()
    host.finish()


def proj_back_call(n, ident, jobs, layer, grad, packed, weight, rows):
    tokens = grad.shape[0]
    units = BLOCKS // n
    turned = (BLOCKS, LANES, tokens)
    flat = (tokens, D)
    return remote_call(
        functools.partial(proj_back_kernel, layer), n, "projection_back", ident,
        [grad, packed, weight, rows],
        [whole(v.shape) for v in (grad, packed)]
        + [pl.BlockSpec((BLOCKS, GROUPS, LANES, HEADS), lambda i: (0, 0, 0, 3)), whole(flat)],
        [
            *[jax.ShapeDtypeStruct((n, tokens, LANES), bf16)] * units,
            jax.ShapeDtypeStruct(turned, bf16),
            jax.ShapeDtypeStruct(flat, bf16),
            jax.ShapeDtypeStruct((2, 8, D), f32),
        ],
        [HB] * units + [whole(turned), whole(flat), whole((2, 8, D))],
        [
            pltpu.VMEM(flat, bf16),
            pltpu.VMEM(flat, f32),
            pltpu.VMEM((BLOCKS, tokens, LANES), bf16),
            DMA((units, n)),
            DMA((units, n)),
            DMA((units,)),
        ],
        30 * tokens * D * D, jobs, grid=(1,),
    )


def attn_back_kernel(n, need, aux, one, *refs):
    qkv, (att, datt, lse) = refs[:n], refs[n : n + 3]
    outs, refs = refs[n + 3 : 2 * n + 3], refs[2 * n + 3 :]
    kx, kt, qs, vs, delta, dq, dkey, dval, dkv = refs
    for r in range(n):
        kx[r] = jnp.concatenate([qkv[r][1], aux[r]], axis=1)
        kt[r] = flip(qkv[r][1])
        vs[r] = qkv[r][2]
        qs[r] = (qkv[r][0].astype(f32) * (1.0 / math.sqrt(DH))).astype(bf16)
        both = jnp.transpose(att[r].astype(f32) * datt[r].astype(f32), (1, 0))
        delta[r, 0:1] = jnp.sum(both[:DH], axis=0, keepdims=True)
        delta[r, 1:2] = jnp.sum(both[DH:], axis=0, keepdims=True)
    dq[...] = jnp.zeros_like(dq)

    def each_key(j, carry):
        dkey[...] = jnp.zeros_like(dkey)
        dval[...] = jnp.zeros_like(dval)

        def each_query(i, inner):
            @pl.when(need[i * n + j] == 1)
            def _():
                for h in range(2):
                    query = head_lanes(qs[i], h)
                    out = head_lanes(datt[i], h)
                    scores = dot_nt(kx[j], jnp.concatenate([query, one[...]], axis=1))
                    probs = jnp.exp(scores - lse[i, h : h + 1])
                    dprobs = dot_nt(vs[j], out)
                    dscores = (probs * (dprobs - delta[i, h : h + 1])).astype(bf16)
                    dval[...] += dot(probs.astype(bf16), out)
                    dkey[...] += dot(dscores, query)
                    rows = slice(h * DH, (h + 1) * DH)
                    dq[i, rows] += dot(kt[j, rows], dscores)

            return inner

        lax.fori_loop(0, n, each_query, 0)
        dkv[j, 0] = dkey[...].astype(bf16)
        dkv[j, 1] = dval[...].astype(bf16)
        return carry

    lax.fori_loop(0, n, each_key, 0)
    for r in range(n):
        outs[r][0] = (jnp.transpose(dq[r], (1, 0)) * (1.0 / math.sqrt(DH))).astype(bf16)
        outs[r][1] = dkv[r, 0]
        outs[r][2] = dkv[r, 1]


def attn_back_call(n, need, aux, one, parts, att, datt, lse):
    tokens = aux.shape[1]
    return unit_call(
        attn_back_kernel, n, need, aux, one, [*parts, att, datt, lse],
        [jax.ShapeDtypeStruct((3, tokens, LANES), bf16)] * n,
        [
            pltpu.VMEM((n, tokens, 2 * LANES), bf16),
            pltpu.VMEM((n, LANES, tokens), bf16),
            pltpu.VMEM((n, tokens, LANES), bf16),
            pltpu.VMEM((n, tokens, LANES), bf16),
            pltpu.VMEM((n, 8, tokens), f32),
            pltpu.VMEM((n, LANES, tokens), f32),
            pltpu.VMEM((tokens, LANES), f32),
            pltpu.VMEM((tokens, LANES), f32),
            pltpu.VMEM((n, 2, tokens, LANES), bf16),
        ],
        14, "attention_back",
    )


def qkv_back_kernel(
    layer, host, grad, low, packed, wq, wk, wv, *refs
):
    n = host.n
    vectors = Vectors(n, layer, packed)
    gain, shift = vectors.norm(0, 0), vectors.norm(1, 0)
    tokens = grad.shape[0]
    units = BLOCKS // n
    early_count = n * (units - 1)
    ready, refs = refs[:early_count], refs[early_count:]
    dparts, refs = refs[:n], refs[n:]
    dlast, refs = refs[:n], refs[n:]
    grad_out, normed_turned, grads, grad_low, acc, ns, ssem, rsem, lsem = refs
    blocks = [ready[u * n : (u + 1) * n] for u in range(units - 1)] + [dlast]
    host.barrier()
    steps = [0] + order_of(n)[::-1]
    copies = {}
    for k in order_of(n):
        copies[k] = group_send(n, -k, dparts[k], dlast[k], ssem.at[k], rsem.at[k])
        copies[k].start()
    copies[0] = pltpu.make_async_copy(dparts[0], dlast[0], lsem)
    copies[0].start()
    host.start()
    grads[...] = jnp.zeros_like(grads)

    def early(r):
        value, _ = row_stats(low[r, :].astype(f32))
        ns[r, :] = (value * gain + shift).astype(bf16)

    row_loop(tokens, ROWS, early)
    for b in range(BLOCKS):
        normed_turned[b] = flip(ns[:, b * LANES : (b + 1) * LANES])
    for i, k in enumerate(steps):
        copies[k].wait()
        group, offset = head_columns(n, k)
        left, right = [], []
        for c, weight in enumerate((wq, wk, wv)):
            left += [blocks[u][k][c] for u in range(units)]
            part = weight[:, group, :, pl.ds(offset, units * LANES)]
            right.append(part.reshape(D, units * LANES))
        total = dot_nt(jnp.concatenate(left, axis=1), jnp.concatenate(right, axis=1))
        if i == 0:
            acc[...] = total
        else:
            acc[...] += total

    def body(r):
        value, rstd = row_stats(low[r, :].astype(f32))
        dy = acc[r, :]
        grads[0] += fold_rows(dy * value)
        grads[1] += fold_rows(dy)
        total = grad[r, :] + norm_back(dy, value, rstd, gain)
        grad_out[r, :] = total
        grad_low[r, :] = total.astype(bf16)

    row_loop(tokens, ROWS, body)
    host.finish()


def qkv_back_call(n, ident, jobs, layer, grad, low, packed, weight, ready, dparts):
    tokens = grad.shape[0]
    turned = (BLOCKS, LANES, tokens)
    flat = (tokens, D)
    columns = lambda c: pl.BlockSpec((BLOCKS, GROUPS, LANES, HEADS), lambda i: (0, 0, 0, c))
    block = (3, tokens, LANES)
    res = remote_call(
        functools.partial(qkv_back_kernel, layer), n, "qkv_back", ident,
        [grad, low, packed, weight, weight, weight, *ready, *dparts],
        [whole(v.shape) for v in (grad, low, packed)]
        + [columns(0), columns(1), columns(2)]
        + [whole(block)] * (len(ready) + n),
        [jax.ShapeDtypeStruct(block, bf16)] * n
        + [
            jax.ShapeDtypeStruct(flat, f32),
            jax.ShapeDtypeStruct(turned, bf16),
            jax.ShapeDtypeStruct((2, 8, D), f32),
            jax.ShapeDtypeStruct(flat, bf16),
        ],
        [whole(block)] * n + [whole(flat), whole(turned), whole((2, 8, D)), whole(flat)],
        [
            pltpu.VMEM(flat, f32),
            pltpu.VMEM(flat, bf16),
            DMA((n,)),
            DMA((n,)),
            DMA,
        ],
        50 * tokens * D * D, jobs, grid=(1,),
    )
    return [res[:n], *res[n:]]


def slot_group(p):
    return 2 * (p % 2) + p // 2


def pick_rows(sc, first, turned, count):
    return jnp.concatenate([turned[sc[first + m]] for m in range(count)], axis=0)


def put_rows(value, extra, outs, spot):
    rows = value.shape[0] // LANES
    for m in range(rows):
        part = value[m * LANES : (m + 1) * LANES]
        if extra is not None:
            part = part + extra[(m,) + spot].astype(f32)
            outs[m // 2][(m % 2,) + spot] = part.astype(bf16)
        else:
            outs[0][(m,) + spot] = part.astype(bf16)


def ffn_grad_kernel(ups, first, count, added, sc, up_turned, down_turned, *refs):
    split = added and ups
    dhid, normed, refs = [v.at[0] for v in refs[:2]], [v.at[0] for v in refs[2:4]], refs[4:]
    extra, outs = (refs[0], refs[1:]) if added else (None, refs)

    @pl.when(pl.program_id(0) == 0)
    def _():
        left = pick_rows(sc, first + ups, up_turned, count)
        for i in range(2):
            put_rows(dot(left, dhid[i][...]), extra, outs[:2] if split else outs, (i,))

    @pl.when(pl.program_id(0) == 1)
    def _():
        left = pick_rows(sc, first, down_turned, count)
        for i in range(2):
            put_rows(dot(left, normed[i][...]), extra, outs[2:] if split else outs, (i,))


def ffn_grad_call(ups, first, count, sc, up_turned, down_turned, dhid, normed, extra=None):
    tokens = up_turned.shape[2]
    added = extra is not None
    def block(i, kind, idle):
        def at(j, p, sc):
            p = jnp.where(j == kind, p, idle)
            return (jnp.bitwise_xor(p + 2 * i, sc[BLOCKS]), 0, 0)

        return pl.BlockSpec((1, tokens, WIDE), at)

    lefts = [block(i, 0, 1) for i in range(2)]
    rights = [block(i, 1, 0) for i in range(2)]
    piece = lambda m: pl.BlockSpec((m, 2, LANES, WIDE), lambda j, p, sc: (0, p, 0, j))
    outs = [2, 2] if added else [count]
    specs = [piece(m) for m in outs]
    wide = 2 * WIDE
    if added and ups:

        def half(kind, idle):
            at = lambda j, p, sc: (0, jnp.where(j == kind, p, idle), 0, 0)
            return pl.BlockSpec((2, 2, LANES, WIDE), at)

        outs, specs, wide = [2] * 4, [half(0, 1)] * 2 + [half(1, 0)] * 2, WIDE
    return pl.pallas_call(
        lambda *refs: ffn_grad_kernel(ups, first, count, added, *refs),
        out_shape=[jax.ShapeDtypeStruct((m, GROUPS, LANES, wide), bf16) for m in outs],
        grid_spec=pltpu.PrefetchScalarGridSpec(
            num_scalar_prefetch=1,
            grid=(2, GROUPS // 2),
            in_specs=[whole(up_turned.shape), whole(down_turned.shape), *lefts, *rights]
            + ([piece(count)] if added else []),
            out_specs=specs,
        ),
        compiler_params=params(),
        cost_estimate=cost(16 * tokens * count * LANES * FF, 24 * 2**20),
        name="ffn_grad",
    )(sc, up_turned, down_turned, dhid, dhid, normed, normed, *([extra] if added else []))


def head_grad_kernel(n, first, count, added, sc, in_turned, out_turned, normed, *refs):
    units = BLOCKS // n
    dqkv, refs = refs[: n * units], refs[n * units :]
    extra, outs = (refs[0], refs[1:]) if added else (None, refs)
    left = pick_rows(sc, first, in_turned, count)
    for k in range(n):
        for c in range(3):
            right = jnp.concatenate([dqkv[u * n + k][c] for u in range(units)], axis=1)
            value = dot(left, right)
            if n == GROUPS:
                slot = slot_group(jnp.bitwise_xor(lax.rem(sc[BLOCKS + 1] + k, n), sc[BLOCKS]))
                put_rows(value, extra, outs, (slot, slice(None), slice(c * HEADS, (c + 1) * HEADS)))
            else:
                unit = lax.rem(sc[BLOCKS + 1] + k, n) * units
                at = pl.multiple_of(c * HEADS + lax.rem(unit, 2) * LANES, LANES)
                slot = slot_group(unit // 2)
                put_rows(value, extra, outs, (slot, slice(None), pl.ds(at, LANES)))
    left = pick_rows(sc, first, out_turned, count)
    for g in range(GROUPS):
        slot = slot_group(jnp.bitwise_xor(g, sc[BLOCKS]))
        value = dot(left, normed[:, g * HEADS : (g + 1) * HEADS])
        put_rows(value, extra, outs, (slot, slice(None), slice(3 * HEADS, 4 * HEADS)))


def head_grad_call(n, first, count, sc, in_turned, out_turned, dqkv, normed, extra=None):
    tokens = in_turned.shape[2]
    added = extra is not None
    outs = [2, 2] if added else [count]
    inner = (GROUPS, LANES, 4 * HEADS)
    return pl.pallas_call(
        lambda *refs: head_grad_kernel(n, first, count, added, *refs),
        out_shape=[jax.ShapeDtypeStruct((m,) + inner, bf16) for m in outs],
        grid_spec=pltpu.PrefetchScalarGridSpec(
            num_scalar_prefetch=1,
            grid=(1,),
            in_specs=[whole(v.shape) for v in (in_turned, out_turned, normed, *dqkv)]
            + ([whole((count,) + inner)] if added else []),
            out_specs=[whole((m,) + inner) for m in outs],
        ),
        compiler_params=params(),
        cost_estimate=cost(16 * tokens * count * LANES * 4 * D, 16 * 2**20),
        name="head_grad",
    )(sc, in_turned, out_turned, normed, *dqkv, *([extra] if added else []))


def pack_kernel(qkv, out, up, down, *refs):
    layers = qkv.shape[0]
    for l in range(layers):
        narrow, broad = refs[2 * l : 2 * l + 2]
        for c in range(3):
            narrow[:, c * HEADS : (c + 1) * HEADS] = qkv[l, c]
        narrow[:, 3 * HEADS :] = flip(out[l])
        broad[:, :WIDE] = up[l]
        broad[:, WIDE:] = flip(down[l])


def pack_call(qkv, out, up, down):
    layers = qkv.shape[0]
    flat = pl.pallas_call(
        pack_kernel,
        out_shape=[
            jax.ShapeDtypeStruct((LANES, NARROW), bf16),
            jax.ShapeDtypeStruct((LANES, BROAD), bf16),
        ]
        * layers,
        in_specs=[VM] * 4,
        out_specs=[VM] * (2 * layers),
        compiler_params=params(),
        cost_estimate=cost(0, 4 * 2**20),
        name="pack",
    )(qkv, out, up, down)
    return flat[::2], flat[1::2]


def greet(sem, place, z, others, count):
    n = GROUPS
    for k in range(1, n):
        pl.semaphore_signal(
            sem, inc=1, device_id={"head": lax.rem(z + k, n)}, device_id_type=MESH
        )
    for other in (place.by_x, place.by_y, place.mate):
        pl.semaphore_signal(sem, inc=1, device_id={"dp": other}, device_id_type=MESH)
    for to_dp, to_z in others:

        @pl.when((to_dp != place.dp) | (to_z != z))
        def _(to_dp=to_dp, to_z=to_z):
            pl.semaphore_signal(
                sem, inc=1, device_id={"dp": to_dp, "head": to_z}, device_id_type=MESH
            )

    pl.semaphore_wait(sem, n + 2 + count)


class Weights:
    def __init__(self, at, chunks, shards, gathered, hsem, ssem, rsem, lsem):
        self.at, self.chunks, self.pairs = at, chunks, list(zip(shards, gathered))
        self.hsem, self.ssem, self.rsem = hsem, ssem, rsem
        self.lsem = lsem

    def owns(self):
        at = self.at
        return [
            pltpu.make_async_copy(shard, out.at[at.dp, at.z], self.lsem.at[i])
            for i, (shard, out) in enumerate(self.pairs)
        ]

    def near(self, c):
        kind, columns = self.chunks[c][0], pl.ds(*self.chunks[c][1:])
        shard, out = self.pairs[kind]
        at = self.at
        return [
            pltpu.make_async_remote_copy(
                src_ref=shard.at[:, columns],
                dst_ref=out.at[at.dp, at.z, :, columns],
                send_sem=self.hsem.at[0, k - 1, c],
                recv_sem=self.hsem.at[1, k - 1, c],
                device_id={"head": lax.rem(at.z + k, GROUPS)},
                device_id_type=MESH,
            )
            for k in (2, 1, 3)
        ]

    def far(self, slot, row, target, c):
        kind, columns = self.chunks[c][0], pl.ds(*self.chunks[c][1:])
        out = self.pairs[kind][1]
        return pltpu.make_async_remote_copy(
            src_ref=out.at[row, :, :, columns],
            dst_ref=out.at[row, :, :, columns],
            send_sem=self.ssem.at[slot, c],
            recv_sem=self.rsem.at[slot, c],
            device_id={"dp": target},
            device_id_type=MESH,
        )

    def hops(self, stage, c):
        at = self.at
        if stage == 0:
            return self.near(c)
        if stage == 1:
            return [self.far(0, at.dp, at.first, c)]
        if stage == 2:
            return [self.far(1, at.dp, at.second, c), self.far(2, at.first, at.second, c)]
        rows = (at.dp, at.first, at.second, at.both)
        return [self.far(3 + i, row, at.mate, c) for i, row in enumerate(rows)]

    def begin(self):
        for c in range(min(2, len(self.chunks))):
            for copy in self.near(c):
                copy.start()

    def turn(self, t):
        parts = len(self.chunks)
        for stage in (1, 2, 3):
            c = t + 1 - stage
            if 0 <= c < parts:
                if stage == 1 and c == 0:
                    for copy in self.owns():
                        copy.wait()
                for copy in self.hops(stage - 1, c):
                    copy.wait()
                for copy in self.hops(stage, c):
                    copy.start()
        if t + 2 < parts:
            for copy in self.near(t + 2):
                copy.start()
        c = t - 3
        if 0 <= c < parts:
            for copy in self.hops(3, c):
                copy.wait()

    def run(self, aside):
        self.begin()
        for t in range(len(self.chunks) + 3):
            self.turn(t)
            aside(t)


def weight_chunks(shards, step=512):
    return [(i, c, step) for i, v in enumerate(shards) for c in range(0, v.shape[1], step)]


def weight_sems(shards, step=512):
    parts = len(weight_chunks(shards, step))
    return [DMA((2, 3, parts)), DMA((7, parts)), DMA((7, parts)), DMA((len(shards),))]


def start_kernel(
    chunks, shards, rows, vector, flags, gathered, low, side, vectors, flags_out, blocks,
    hsem, ssem, rsem, wsem, xsem, tsem, vsem, fsem, lsem, low_here, vectors_here, *scratch,
):
    queries = Queries(GROUPS, gathered[0], blocks, *scratch)
    at = Place()
    weights = Weights(at, chunks, shards, gathered, hsem, ssem, rsem, wsem)
    dp, core, bit_x, by_x = at.dp, at.core, at.bit_x, at.by_x
    z = at.z
    n = GROUPS
    lo = lax.rem(dp, n)
    wide = rows.shape[2]
    sem = pltpu.get_barrier_semaphore()

    def targets():
        return [(xs, c2, dp - core + c2, 2 * xs + core) for xs in range(2) for c2 in range(2)]

    def sources():
        return [(dp - core + lax.rem(z, 2), g) for g in range(n)]

    turn_dp, turn_z = dp - lo + z, lo
    for copy in weights.owns():
        copy.start()
    own_vector = pltpu.make_async_copy(vector, vectors.at[z], lsem.at[2])
    own_vector.start()
    turned = [(turn_dp, turn_z)]
    across = at.by_x + 1 - 2 * core
    greet(
        sem, at, z, sources() + turned + [(across, z)],
        n + unlike(lax.rem(z, 2), core) + unlike(z, lo),
    )
    small = [
        pltpu.make_async_remote_copy(
            src_ref=vector,
            dst_ref=vectors.at[z],
            send_sem=vsem.at[0, k - 1],
            recv_sem=vsem.at[1, k - 1],
            device_id={"head": lax.rem(z + k, n)},
            device_id_type=MESH,
        )
        for k in range(1, n)
    ]

    def flag_copy(op):
        def remote():
            copy = pltpu.make_async_remote_copy(
                src_ref=flags,
                dst_ref=flags_out,
                send_sem=fsem.at[0],
                recv_sem=fsem.at[1],
                device_id={"dp": turn_dp, "head": turn_z},
                device_id_type=MESH,
            )
            copy.start() if op == "start" else copy.wait()

        def inside():
            copy = pltpu.make_async_copy(flags, flags_out, lsem.at[3])
            copy.start() if op == "start" else copy.wait()

        pl.when((turn_dp != dp) | (turn_z != z))(remote)
        pl.when((turn_dp == dp) & (turn_z == z))(inside)

    flag_copy("start")
    for copy in small:
        copy.start()

    cross = pltpu.make_async_remote_copy(
        src_ref=rows.at[pl.ds(2 - 2 * bit_x, 2)],
        dst_ref=side,
        send_sem=xsem.at[0],
        recv_sem=xsem.at[1],
        device_id={"dp": by_x},
        device_id_type=MESH,
    )
    place = low.at[:, pl.ds(pl.multiple_of(z * wide, wide), wide)]

    def spread(op):
        for i, (xs, c2, to_dp, to_z) in enumerate(targets()):

            def here(source, i=i, to_dp=to_dp, to_z=to_z):
                def remote():
                    copy = pltpu.make_async_remote_copy(
                        src_ref=source,
                        dst_ref=place,
                        send_sem=tsem.at[0, i],
                        recv_sem=tsem.at[1, z],
                        device_id={"dp": to_dp, "head": to_z},
                        device_id_type=MESH,
                    )
                    if op == "start":
                        copy.start()
                    else:
                        copy.wait_send()

                pl.when((to_dp != dp) | (to_z != z))(remote)

                def inside():
                    copy = pltpu.make_async_copy(source, place, lsem.at[1])
                    if op == "start":
                        copy.start()
                    else:
                        copy.wait()

                pl.when((to_dp == dp) & (to_z == z))(inside)

            pl.when(bit_x == xs)(lambda xs=xs, c2=c2, here=here: here(rows.at[2 * xs + c2]))
            pl.when(bit_x != xs)(lambda c2=c2, here=here: here(side.at[c2]))

    cross.start()

    def arrivals():
        spread("wait")
        for from_dp, g in sources():

            @pl.when((from_dp != dp) | (g != z))
            def _(g=g):
                spot = low.at[:, pl.ds(g * wide, wide)]
                pltpu.make_async_remote_copy(
                    src_ref=spot,
                    dst_ref=spot,
                    send_sem=tsem.at[0, 0],
                    recv_sem=tsem.at[1, g],
                    device_id={"dp": by_x},
                    device_id_type=MESH,
                ).wait_recv()

    ready = sum(kind == 0 for kind, *_ in chunks) + 2
    loads = [
        pltpu.make_async_copy(low, low_here, lsem.at[0]),
        pltpu.make_async_copy(vectors, vectors_here, lsem.at[2]),
    ]

    def aside(t):
        if t == 1:
            cross.wait()
            spread("start")
        if t == ready:
            queries.begin()
            own_vector.wait()
            for copy in small:
                copy.wait()
            arrivals()
            for copy in loads:
                copy.start()
            for copy in loads:
                copy.wait()
            norms = Vectors(n, 0, vectors_here)
            queries.norm(low_here, norms.norm(0, 0), norms.norm(1, 0))
        if ready < t <= ready + n:
            queries.step(t - ready - 1)

    weights.run(aside)
    flag_copy("wait")
    queries.finish()


def start_call(shards, rows, vector, flags):
    count = len(shards)
    chunks = weight_chunks(shards)
    tokens, wide = rows.shape[1:]

    out_shape, out_specs = queries_outs(GROUPS, tokens)

    def kernel(*refs):
        taken, refs = refs[:count], refs[count:]
        given, refs = refs[:3], refs[3:]
        gathered, refs = refs[:count], refs[count:]
        others, refs = refs[:4], refs[4:]
        blocks, refs = refs[: len(out_shape)], refs[len(out_shape) :]
        start_kernel(chunks, taken, *given, gathered, *others, blocks, *refs)

    res = pl.pallas_call(
        kernel,
        out_shape=[jax.ShapeDtypeStruct((BLOCKS, GROUPS) + v.shape, bf16) for v in shards]
        + [
            jax.ShapeDtypeStruct((tokens, GROUPS * wide), bf16),
            jax.ShapeDtypeStruct((2, tokens, wide), bf16),
            jax.ShapeDtypeStruct((GROUPS,) + vector.shape, f32),
            jax.ShapeDtypeStruct(flags.shape, jnp.int32),
        ]
        + out_shape,
        in_specs=[HB] * (count + 3),
        out_specs=[HB] * (count + 4) + out_specs,
        scratch_shapes=[
            *weight_sems(shards),
            DMA((2,)),
            DMA((2, GROUPS)),
            DMA((2, 3)),
            DMA((2,)),
            DMA((4,)),
            pltpu.VMEM((tokens, GROUPS * wide), bf16),
            pltpu.VMEM((GROUPS,) + vector.shape, f32),
            *queries_scratch(GROUPS, tokens),
        ],
        compiler_params=params(collective_id=5, has_side_effects=True),
        cost_estimate=cost(0, 300 * 2**20),
        name="start",
    )(*shards, rows, vector, flags)
    blocks = res[count + 4 :]
    parts = [blocks[u * GROUPS : (u + 1) * GROUPS] for u in range(len(blocks) // GROUPS)]
    return [res[:count], *res[count : count + 4], parts]


def vector_rows(layers):
    return -(-(28 * layers + 3 * layers + 1) // 8) * 8


def end_kernel(
    layers, rows, grads, fsum, turned, valid, tops, vecs, uses,
    stream_out, rows_out, qkv_out, out_out, up_out, down_out,
    gains_out, shifts_out, hgains_out, hshifts_out, rms_out,
    mine, got, pair, last, near, pieces, crossed, fm, fnear, vec, vgot, vsum,
    gsem, hsem, psem, qsem, nsem, tsem, xsem, vsem, lsem, esem,
):
    at = Place()
    dp, core, bit_x = at.dp, at.core, at.bit_x
    z = at.z
    n = GROUPS
    parts = 4
    width = grads.shape[3] // parts
    step = fsum.shape[2] // parts
    wide = rows.shape[1] // n
    sem = pltpu.get_barrier_semaphore()

    def columns(c):
        return pl.ds(c * width, width)

    def broad(c):
        return pl.ds(c * step, step)

    def loads(c):
        return [
            pltpu.make_async_copy(
                grads.at[pl.ds(0, 4), :, :, columns(c)], mine.at[:, :, :, columns(c)], gsem.at[0, c]
            ),
            pltpu.make_async_copy(
                fsum.at[:, :, broad(c)], fm.at[:, :, broad(c)], gsem.at[1, c]
            ),
        ]

    for c in range(parts):
        for copy in loads(c):
            copy.start()

    vec[...] = jnp.zeros_like(vec)
    for l in range(layers):
        base = 28 * l
        norms, hidden = vecs[4 * l : 4 * l + 3], vecs[4 * l + 3]
        for kind in range(2):
            for i in range(3):
                total = jnp.sum(norms[i][kind], axis=0, keepdims=True)
                for b in range(BLOCKS):
                    row = base + (3 * kind + i) * 2 + b % 2
                    vec[b // 2, row : row + 1, :] = total[:, b * LANES : (b + 1) * LANES]
            for g in range(n):
                total = jnp.sum(hidden[kind, g], axis=0, keepdims=True)
                for b in range(BLOCKS):
                    row = base + 12 + 8 * kind + b
                    vec[g, row : row + 1, :] = total[:, b * LANES : (b + 1) * LANES]
        branch, rest = uses[2 * l : 2 * l + 2]
        for i, value in enumerate((branch[...], rest[0], rest[1])):
            row = 28 * layers + 3 * l + i
            total = fold_lanes(jnp.sum(value, axis=0, keepdims=True))
            for g in range(n):
                vec[g, row : row + 1, :] = total
    row = 31 * layers
    count = jnp.sum(valid[...], axis=0, keepdims=True) * (D / LANES)
    for g in range(n):
        vec[g, row : row + 1, :] = jnp.broadcast_to(count, (1, LANES))

    to_dp = dp - core + lax.rem(z, 2)
    sources = [(dp - core + c2, 2 * xs + core) for xs in range(2) for c2 in range(2)]
    greet(sem, at, z, sources, n - 1 + unlike(lax.rem(z, 2), core))

    def hop(stage, c):
        if stage == 0:
            return pltpu.make_async_remote_copy(
                src_ref=grads.at[pl.ds(4, 4), :, :, columns(c)],
                dst_ref=got.at[:, :, :, columns(c)],
                send_sem=hsem.at[0, c],
                recv_sem=hsem.at[1, c],
                device_id={"dp": at.mate},
                device_id_type=MESH,
            )
        if stage == 1:
            return pltpu.make_async_remote_copy(
                src_ref=mine.at[pl.ds(2, 2), :, :, columns(c)],
                dst_ref=pair.at[:, :, :, columns(c)],
                send_sem=psem.at[0, c],
                recv_sem=psem.at[1, c],
                device_id={"dp": at.second},
                device_id_type=MESH,
            )
        return pltpu.make_async_remote_copy(
            src_ref=mine.at[1, :, :, columns(c)],
            dst_ref=last.at[:, :, columns(c)],
            send_sem=qsem.at[0, c],
            recv_sem=qsem.at[1, c],
            device_id={"dp": at.first},
            device_id_type=MESH,
        )

    def way(source, target, sems, i, c):
        return pltpu.make_async_remote_copy(
            src_ref=source,
            dst_ref=target,
            send_sem=sems.at[0, i, c],
            recv_sem=sems.at[1, i, c],
            device_id={"head": at.group(2 - i)},
            device_id_type=MESH,
        )

    def head_way(i, c):
        if i == 0:
            source, target = mine.at[0, pl.ds(2, 2), :, columns(c)], near.at[pl.ds(0, 2), :, columns(c)]
        else:
            source, target = mine.at[0, 1, :, columns(c)], near.at[2, :, columns(c)]
        return way(source, target, nsem, i, c)

    def ffn_way(i, c):
        if i == 0:
            source, target = fm.at[pl.ds(2, 2), :, broad(c)], fnear.at[pl.ds(0, 2), :, broad(c)]
        else:
            source, target = fm.at[1, :, broad(c)], fnear.at[2, :, broad(c)]
        return way(source, target, esem, i, c)

    def head_between(c):
        head_way(0, c).wait()
        for k in range(2):
            value = mine[0, k, :, columns(c)].astype(f32) + near[k, :, columns(c)].astype(f32)
            mine[0, k, :, columns(c)] = value.astype(bf16)
        head_way(1, c).start()

    def ffn_between(c):
        ffn_way(0, c).wait()
        for k in range(2):
            value = fm[k, :, broad(c)].astype(f32) + fnear[k, :, broad(c)].astype(f32)
            fm[k, :, broad(c)] = value.astype(bf16)
        ffn_way(1, c).start()

    def add(count, other, c):
        def body(i, carry):
            m, g = i // GROUPS, lax.rem(i, GROUPS)
            value = mine[m, g, :, columns(c)].astype(f32) + other(m, g).astype(f32)
            mine[m, g, :, columns(c)] = value.astype(bf16)
            return carry

        lax.fori_loop(0, count * GROUPS, body, 0)

    def row_copies(op):
        for j in range(n):
            source = rows.at[:, pl.ds(j * wide, wide)]
            target = pieces.at[z // 2, core]

            def remote(j=j, source=source, target=target):
                copy = pltpu.make_async_remote_copy(
                    src_ref=source,
                    dst_ref=target,
                    send_sem=tsem.at[0, j],
                    recv_sem=tsem.at[1, 2 * (z // 2) + core],
                    device_id={"dp": to_dp, "head": j},
                    device_id_type=MESH,
                )
                copy.start() if op == "start" else copy.wait_send()

            def inside(source=source, target=target):
                copy = pltpu.make_async_copy(source, target, lsem.at[0])
                copy.start() if op == "start" else copy.wait()

            pl.when((to_dp != dp) | (j != z))(remote)
            pl.when((to_dp == dp) & (j == z))(inside)

    def row_arrivals():
        for xs in range(2):
            for c2 in range(2):

                @pl.when((dp - core + c2 != dp) | (2 * xs + core != z))
                def _(xs=xs, c2=c2):
                    spot = pieces.at[xs, c2]
                    pltpu.make_async_remote_copy(
                        src_ref=spot,
                        dst_ref=spot,
                        send_sem=tsem.at[0, 0],
                        recv_sem=tsem.at[1, 2 * xs + c2],
                        device_id={"dp": at.by_x},
                        device_id_type=MESH,
                    ).wait_recv()

    cross = pltpu.make_async_remote_copy(
        src_ref=pieces.at[1 - bit_x],
        dst_ref=crossed,
        send_sem=xsem.at[0],
        recv_sem=xsem.at[1],
        device_id={"dp": at.by_x},
        device_id_type=MESH,
    )
    def vector_near(k):
        return pltpu.make_async_remote_copy(
            src_ref=vec.at[lax.rem(z + k, n)],
            dst_ref=vgot.at[k - 1],
            send_sem=vsem.at[0, k - 1],
            recv_sem=vsem.at[1, k - 1],
            device_id={"head": lax.rem(z + k, n)},
            device_id_type=MESH,
        )

    def vector_far(i, target):
        return pltpu.make_async_remote_copy(
            src_ref=vsum.at[i],
            dst_ref=vgot.at[3 + i],
            send_sem=vsem.at[0, 3 + i],
            recv_sem=vsem.at[1, 3 + i],
            device_id={"dp": target},
            device_id_type=MESH,
        )

    def put_head(l, c, value):
        if c < 3:
            qkv_out[l, c] = value
        else:
            out_out[l] = jnp.transpose(value, (1, 0))

    def total_of(own, others):
        value = own.astype(f32)
        for other in others:
            value = value + other.astype(f32)
        return value

    row_copies("start")
    for c in range(parts):
        hop(0, c).start()
    for k in range(1, n):
        vector_near(k).start()
    partners = (at.mate, at.first, at.second)
    for t in range(parts + 4):
        c = t
        if c < parts:
            for copy in loads(c):
                copy.wait()
            hop(0, c).wait()
            add(4, lambda m, g, c=c: got[m, g, :, columns(c)], c)
            hop(1, c).start()
            ffn_way(0, c).start()
        c = t - 1
        if 0 <= c < parts:
            hop(1, c).wait()
            add(2, lambda m, g, c=c: pair[m, g, :, columns(c)], c)
            hop(2, c).start()
        c = t - 2
        if 0 <= c < parts:
            hop(2, c).wait()
            add(1, lambda m, g, c=c: last[g, :, columns(c)], c)
            head_way(0, c).start()
        if t == 1:
            for k in range(1, n):
                vector_near(k).wait()
            vsum[0] = vec[z] + vgot[0] + vgot[1] + vgot[2]
            vector_far(0, partners[0]).start()
        if 2 <= t < 5:
            i = t - 2
            vector_far(i, partners[i]).wait()
            vsum[i + 1] = vsum[i] + vgot[3 + i]
            if i < 2:
                vector_far(i + 1, partners[i + 1]).start()
        if t == 2:
            row_copies("wait")
            row_arrivals()
            cross.start()
        if t == 3:
            stream_out[...] = turned[...].astype(f32)
        if t == 4:
            for l in range(1, layers):
                heads, heads_other, ups, ups_other, downs, downs_other = tops[6 * l - 6 : 6 * l]
                for c in range(parts):
                    cols = slice(c * width, (c + 1) * width)
                    put_head(l, c, total_of(heads[0, :, cols], [heads_other[:, cols]]))
                up_out[l] = total_of(ups[0], [ups_other[...]])
                down_out[l] = jnp.transpose(total_of(downs[0], [downs_other[...]]), (1, 0))
        c = t - 1
        if 0 <= c < parts:
            ffn_between(c)
        c = t - 3
        if 0 <= c < parts:
            head_between(c)
        c = t - 4
        if 0 <= c < parts:
            ffn_way(1, c).wait()
            value = total_of(fm[0, :, broad(c)], [fnear[2, :, broad(c)]])
            if c < parts // 2:
                up_out[0, :, broad(c)] = value
            else:
                down_out[0, pl.ds(c * step - WIDE, step), :] = jnp.transpose(value, (1, 0))
    for c in range(parts):
        head_way(1, c).wait()
        put_head(0, c, total_of(mine[0, 0, :, columns(c)], [near[2, :, columns(c)]]))
    for l in range(layers):
        base = 28 * l
        for kind, (norm_out, hid_out) in enumerate(
            ((gains_out, hgains_out), (shifts_out, hshifts_out))
        ):
            for i in range(3):
                at_row = base + (3 * kind + i) * 2
                parts_of = [vsum[3, at_row + p : at_row + p + 1, :] for p in range(2)]
                norm_out[l, i : i + 1, :] = jnp.concatenate(parts_of, axis=1)
            at_row = base + 12 + 8 * kind
            parts_of = [vsum[3, at_row + p : at_row + p + 1, :] for p in range(BLOCKS)]
            hid_out[l : l + 1, :] = jnp.concatenate(parts_of, axis=1)
    totals = sum_lanes(vsum[3, 28 * layers : 31 * layers + 1, :])
    rms = jnp.sqrt(totals[: 3 * layers] / totals[3 * layers :])
    rms_out[0 : 3 * layers, :] = jnp.broadcast_to(rms, (3 * layers, LANES))
    cross.wait()
    for c2 in range(2):
        rows_out[2 * bit_x + c2] = pieces[bit_x, c2].astype(f32)
        rows_out[2 - 2 * bit_x + c2] = crossed[c2].astype(f32)


def end_call(rows, grads, fsum, turned, valid, tops, vecs, uses):
    parts = 4
    layers = len(vecs) // 4
    tokens = rows.shape[0]
    wide = rows.shape[1] // GROUPS
    block = grads.shape[1:]
    broad = fsum.shape
    vector = (vector_rows(layers), LANES)
    inputs = [rows, grads, fsum, turned, valid, *tops, *vecs, *uses]

    def spec(i, v):
        if i % 2 == 0:
            return pl.BlockSpec((1,) + v.shape[1:], lambda g: (0, 0, 0))
        return whole(v.shape)

    def kernel(*refs):
        fixed, refs = refs[:5], refs[5:]
        lists = []
        for values in (tops, vecs, uses):
            lists.append(refs[: len(values)])
            refs = refs[len(values) :]
        end_kernel(layers, *fixed, *lists, *refs)

    dims = [
        turned.shape,
        turned.shape,
        (layers, 3, LANES, HEADS),
        (layers, HEADS, LANES),
        (layers, LANES, WIDE),
        (layers, WIDE, LANES),
        (layers, 3, HEADS),
        (layers, 3, HEADS),
        (layers, WIDE),
        (layers, WIDE),
        (8 * (-(-3 * layers // 8)), LANES),
    ]
    outs = [jax.ShapeDtypeStruct(d, f32) for d in dims]
    return pl.pallas_call(
        kernel,
        out_shape=outs,
        grid=(1,),
        in_specs=[HB] * 3
        + [whole(turned.shape), whole(valid.shape)]
        + [spec(i, v) for i, v in enumerate(tops)]
        + [whole(v.shape) for v in (*vecs, *uses)],
        out_specs=[whole(v.shape) for v in outs],
        scratch_shapes=[
            pltpu.VMEM((4,) + block, bf16),
            pltpu.VMEM((4,) + block, bf16),
            pltpu.VMEM((2,) + block, bf16),
            pltpu.VMEM(block, bf16),
            pltpu.VMEM((3,) + block[1:], bf16),
            pltpu.VMEM((2, 2, tokens, wide), bf16),
            pltpu.VMEM((2, tokens, wide), bf16),
            pltpu.VMEM(broad, bf16),
            pltpu.VMEM((3,) + broad[1:], bf16),
            pltpu.VMEM((GROUPS,) + vector, f32),
            pltpu.VMEM((6,) + vector, f32),
            pltpu.VMEM((4,) + vector, f32),
            DMA((2, parts)),
            DMA((2, parts)),
            DMA((2, parts)),
            DMA((2, parts)),
            DMA((2, 2, parts)),
            DMA((2, 4)),
            DMA((2,)),
            DMA((2, 6)),
            DMA((2,)),
            DMA((2, 2, parts)),
        ],
        compiler_params=params(collective_id=6, has_side_effects=True),
        cost_estimate=cost(0, 300 * 2**20),
        name="end",
    )(*inputs)


def after(value, *tokens):
    return lax.optimization_barrier((value, tokens))[0]


class Order:
    def __init__(self):
        self.token = None
        self.wanted = []

    def __call__(self, call, *args, first=0):
        args = list(args)
        if self.token is not None:
            args[first] = after(args[first], self.token, *self.wanted)
            self.wanted = []
        out = call(*args)
        self.token = out
        while isinstance(self.token, (list, tuple)):
            self.token = self.token[0]
        return out

    def hold(self, value):
        return after(value, self.token)

    def want(self, value):
        self.wanted.append(value)
        return value


class Net:
    def __init__(self, n_dp, n_head):
        self.n_dp, self.n = n_dp, n_head
        self.own = lax.axis_index("dp").astype(jnp.int32)
        self.z = lax.axis_index("head").astype(jnp.int32)
        self.lo = self.own % n_head
        self.fast = n_dp == BLOCKS and n_head == GROUPS
        core_zero = [2, 4]
        self.one_way = [(i, i ^ core_zero[i % 2]) for i in range(n_dp)]
        self.other_way = [(i, i ^ core_zero[1 - i % 2]) for i in range(n_dp)]
        self.by_x = [(i, i ^ 2) for i in range(n_dp)]
        self.by_y = [(i, i ^ 4) for i in range(n_dp)]
        self.core = [(i, i ^ 1) for i in range(n_dp)]
        if self.fast:
            step = jnp.where(self.own % 2 == 0, 2, 4).astype(jnp.int32)
            mine = [jnp.int32(0), step, 6 - step, jnp.int32(6)]
            theirs = [jnp.int32(0), 6 - step, step, jnp.int32(6)]
            rows = [self.own ^ v for v in mine] + [self.own ^ v ^ 1 for v in theirs]
            straight = [self.own ^ v for v in (0, 2, 4, 6, 1, 3, 5, 7)]
            self.table = jnp.stack(rows + [self.z, self.lo] + straight)
        else:
            self.table = jnp.stack([jnp.int32(i) for i in range(BLOCKS)] + [jnp.int32(0), self.lo])

    def shift(self, value, k):
        n = self.n
        if k % n == 0:
            return value
        pairs = [(i, (i // n) * n + (i + k) % n) for i in range(self.n_dp)]
        return lax.ppermute(value, "dp", pairs)

    def across(self, value, bits):
        return lax.ppermute(value, "head", [(i, i ^ bits) for i in range(self.n)])

    def spin(self, value, k):
        n = self.n
        return lax.ppermute(value, "head", [(i, (i + k) % n) for i in range(n)])

    def gather(self, shard):
        return lax.all_gather(shard, ("dp", "head")).reshape(BLOCKS, GROUPS, LANES, -1)

    def gather_any(self, qkv, out, up, down):
        qkv = lax.all_gather(qkv, "head", axis=2, tiled=True)
        qkv = lax.all_gather(qkv, "dp", axis=1, tiled=True).transpose(1, 0, 2).reshape(D, 3 * D)
        up = lax.all_gather(up, "head", axis=1, tiled=True)
        up = lax.all_gather(up, "dp", axis=0, tiled=True)
        out, down = [
            lax.all_gather(lax.all_gather(v, "head", axis=0, tiled=True), "dp", axis=1, tiled=True)
            for v in (out, down)
        ]

        def blocks(*parts):
            cut = [v.reshape(BLOCKS, LANES, GROUPS, -1) for v in parts]
            return jnp.concatenate(cut, axis=3).transpose(0, 2, 1, 3)

        heads = [qkv[:, c * D : (c + 1) * D] for c in range(3)]
        return blocks(*heads, out.T), blocks(up, down.T)

    def scatter(self, full, widths):
        columns = full.shape[3]
        full = jnp.stack([full[:, slot_group(g)] for g in range(GROUPS)], axis=1)
        if self.fast:
            full = full.reshape(BLOCKS * GROUPS, LANES, columns)
        else:
            full = full.transpose(0, 2, 1, 3).reshape(D, GROUPS, columns)
            parts, at = [], 0
            for w in widths:
                part = full[:, :, at : at + w].reshape(D, self.n, GROUPS * w // self.n)
                parts.append(part)
                at += w
            full = jnp.concatenate(parts, axis=2)
            full = full.reshape(self.n_dp, D // self.n_dp, self.n, -1).transpose(0, 2, 1, 3)
            full = full.reshape(self.n_dp * self.n, D // self.n_dp, -1)
        mine = lax.psum_scatter(full, ("dp", "head"), scatter_dimension=0, tiled=False)
        return mine.astype(f32)


    def add_pair(self, keep, pair):
        add = lambda i: (keep[i].astype(f32) + pair[i].astype(f32)).astype(bf16)
        return add(0), add(1)

    def add_last(self, mine, last):
        return (mine.astype(f32) + last.astype(f32)).astype(bf16)

    def turn(self, k):
        n = self.n
        pairs = []
        for hi in range(self.n_dp // n):
            for lo in range(n):
                for z in range(n):
                    pairs.append(((hi * n + lo) * n + z, (hi * n + (z + k) % n) * n + lo))
        return pairs

    def rows_in(self, array):
        n = self.n
        tokens = array.shape[0] // n
        low = array.astype(bf16).reshape(n, tokens, array.shape[1])
        got = []
        for k in range(n):
            piece = lax.dynamic_index_in_dim(low, (self.z + k) % n, 0, False)
            got.append(lax.ppermute(piece, ("dp", "head"), self.turn(k)))
        return got

    def rows_in_end(self, got):
        stacked = jnp.take(jnp.stack(got), (self.lo - jnp.arange(self.n)) % self.n, axis=0)
        return stacked.transpose(1, 0, 2).reshape(got[0].shape[0], D)

    def rows_out(self, array):
        n = self.n
        width = D // n
        low = array.astype(bf16)
        got = []
        for k in range(n):
            piece = lax.dynamic_slice_in_dim(low, ((self.lo - k) % n) * width, width, 1)
            got.append(lax.ppermute(piece, ("dp", "head"), [(b, a) for a, b in self.turn(k)]))
        return got

    def rows_out_end(self, got):
        stacked = jnp.take(jnp.stack(got), (jnp.arange(self.n) - self.z) % self.n, axis=0)
        return stacked.reshape(-1, got[0].shape[1]).astype(f32)


def local(
    n_dp,
    n_head,
    stream_in,
    qkv_weight,
    out_weight,
    up_weight,
    down_weight,
    norm_gains,
    norm_shifts,
    hidden_gains,
    hidden_shifts,
    buckets,
    valid_mask,
    cotangent,
):
    net = Net(n_dp, n_head)
    n = n_head
    layers = qkv_weight.shape[0]
    tokens = LONG // n
    order = Order()

    flags = jnp.concatenate([valid_mask, buckets])
    flags = jnp.pad(flags, (0, -flags.shape[0] % 1024))
    vectors = [
        v.reshape(layers, -1) for v in (norm_gains, norm_shifts, hidden_gains, hidden_shifts)
    ]
    packed = jnp.concatenate(vectors, axis=1)
    narrow, broad = [None] * layers, [None] * layers
    if net.fast:
        small, large = pack_call(qkv_weight, out_weight, up_weight, down_weight)
        rows = stream_in.astype(bf16).reshape(n, tokens, D // n)
        flags = flags.reshape(-1, LANES)
        vector = packed.reshape(-1, LANES)
        started = order(start_call, [small[0], large[0]], rows, vector, flags, first=1)
        (narrow[0], broad[0]), stream, _, packed, flags, first_parts = started
        narrow[1:] = [net.gather(order.hold(v)) for v in small[1:]]
    else:
        for l in range(layers):
            narrow[l], broad[l] = net.gather_any(
                qkv_weight[l], out_weight[l], up_weight[l], down_weight[l]
            )
        stream = net.rows_in_end(net.rows_in(stream_in))
        flags = lax.ppermute(flags, ("dp", "head"), net.turn(0))
        packed = lax.all_gather(packed.reshape(-1, LANES), "head")
    aux, one, valid, need = masks_call(n, net.lo[None], flags.reshape(-1, LANES))

    low = stream
    cot = cotangent.astype(bf16).reshape(n, tokens, D // n)
    kept = []
    usage = []
    idents = iter(range(10, 64))
    for l in range(layers):
        ahead = net.fast and l + 1 < layers
        if net.fast and l == 0:
            parts = first_parts
        else:
            parts, _ = order(qkv_call, n, next(idents), [], l, low, packed, narrow[l], first=4)
        if ahead:
            broad[l + 1] = net.gather(order.hold(large[l + 1]))
        parts = [parts[0]] + [[net.shift(v, k) for k, v in enumerate(p)] for p in parts[1:]]
        att, lse = [], []
        for p in parts:
            outs = order(attn_call, n, need, aux, one, p, first=2)
            att.append(outs[0])
            lse.append(outs[1])
        last = net.fast and l + 1 == layers
        jobs = [Turn(cot, False, 0)] if last else []
        mid, rows, use_branch, *extra = order(
            proj_call, n, next(idents), jobs, l, valid, stream, packed, narrow[l], att, first=5
        )
        jobs = [Turn(cot, False, 1, extra[0])] if last else []
        slope, hat, normed, low_mid, rstd, stream, next_low, use_rest, *extra = order(
            ffn_call, n, next(idents), jobs, l, valid, mid, packed, broad[l], first=5
        )
        if last:
            grad = extra[0]
        usage += [use_branch, use_rest]
        kept.append((low, parts, att, lse, rows, slope, hat, normed, low_mid, rstd))
        low = next_low

    if not net.fast:
        grad = net.rows_in_end(net.rows_in(cotangent)).astype(f32)
    if not net.fast:
        grad = net.rows_in_end(net.rows_in(cotangent)).astype(f32)
    low_out = low
    units = BLOCKS // n
    ffn_grads, head_grads = [None] * layers, [None] * layers
    vectors, tops = [None] * layers, []

    for l in reversed(range(layers)):
        low, parts, att, lse, rows, slope, hat, normed, low_mid, rstd = kept[l]
        more = net.fast and l + 1 < layers
        last = net.fast and l + 1 == layers
        jobs = []
        if last:
            jobs = [Turn(low_out, True, 0)]
        if more:
            jobs = [Hop(head_odd, "mate")]
        dhid, grad_turned, ffn_turned, grad, hgrads, grads2, *extra = order(
            ffn_back_call, n, next(idents), jobs, l, grad, hat, slope, rstd,
            low_mid, packed, broad[l], first=4,
        )
        ffn_args = (ffn_turned, grad_turned, dhid, normed)
        if net.fast:
            moved = extra
            if more:
                head_keep, send = order(
                    head_grad_call, n, 0, 4, net.table, *head_args, extra[0], first=4
                )
                head_pair = lax.ppermute(order.hold(send), "dp", net.other_way)
            ups = BLOCKS + 2 if l else 0
            (odd,) = order(ffn_grad_call, ups, 4, 4, net.table, *ffn_args, first=4)
            jobs = [Hop(odd, "mate")]
            if more:
                wide_sums = [
                    net.add_last(order.hold(ups_mine), ups_last),
                    net.add_last(order.hold(downs_mine), downs_last),
                ]
                wide_near = [net.across(order.want(v)[2:], 1) for v in wide_sums]
            if last:
                jobs.append(Turn(low_out, True, 1, moved[0]))
        else:
            (full,) = order(ffn_grad_call, 0, 0, BLOCKS, net.table, *ffn_args, first=4)
            ffn_grads[l] = net.scatter(full, (WIDE, WIDE))
        res = order(
            proj_back_call, n, next(idents), jobs, l, grad, packed, narrow[l], rows, first=4
        )
        datt, (out_turned, normed_mid, grads1, *extra) = res[:units], res[units:]
        if net.fast:
            if last:
                turned = extra[1]
            if more:
                head_mine, sent = net.add_pair(order.hold(head_keep), head_pair)
                head_last = lax.ppermute(sent, "dp", net.one_way)
                order.want(sent)
            sums = order(ffn_grad_call, ups, 0, 4, net.table, *ffn_args, extra[0], first=4)
            if l:
                up_pair = lax.ppermute(order.hold(sums[1]), "dp", net.by_y)
                down_pair = lax.ppermute(order.hold(sums[3]), "dp", net.other_way)
            if more:
                wide_own = [
                    order.want(net.add_last(order.hold(v[:2]), other))
                    for v, other in zip(wide_sums, wide_near)
                ]
            if l == 0:
                ffn_pair = lax.ppermute(order.hold(sums[1]), "dp", net.other_way)
        dparts, ready = [], []
        for u in range(units):
            ready += [net.shift(v, -k) for k, v in enumerate(dparts)]
            dparts = order(
                attn_back_call, n, need, aux, one, parts[u], att[u], datt[u], lse[u], first=2
            )
            if more and u == 0:
                head_sum = order.want(net.add_last(order.hold(head_mine), head_last))
                wide_other = [net.across(order.hold(v[1]), 2) for v in wide_own]
            if net.fast and l and u == 0:
                order.want(down_pair)
        jobs = []
        if net.fast and l == 0:
            ffn_mine, sent = net.add_pair(order.hold(sums[0]), ffn_pair)
            ffn_last = lax.ppermute(order.want(sent), "dp", net.one_way)
        if more:
            head_near = net.across(order.hold(head_sum)[2:], 1)
        dlast, grad, in_turned, grads0, grad_low, *extra = order(
            qkv_back_call, n, next(idents), jobs, l, grad, low, packed, narrow[l], ready, dparts,
            first=4,
        )
        head_args = (in_turned, out_turned, ready + dlast, normed_mid)
        vectors[l] = [grads0, grads1, grads2, hgrads]
        if net.fast:
            if more:
                head_own = order.want(net.add_last(order.hold(head_sum[:2]), head_near))
                pairs = [v for pair in zip(wide_own, wide_other) for v in pair]
                tops = [head_own, net.across(head_own[1], 2), *pairs] + tops
            if l:
                (head_odd,) = order(head_grad_call, n, 4, 4, net.table, *head_args, first=4)
                ups_mine, ups_sent = net.add_pair(order.hold(sums[0]), up_pair)
                downs_mine, downs_sent = net.add_pair(order.hold(sums[2]), down_pair)
                order.want(ups_sent)
                order.want(downs_sent)
                ups_last = lax.ppermute(ups_sent, "dp", net.by_x)
                downs_last = lax.ppermute(downs_sent, "dp", net.one_way)
            else:
                (full,) = order(head_grad_call, n, 0, BLOCKS, net.table, *head_args, first=4)
        else:
            (full,) = order(head_grad_call, n, 0, BLOCKS, net.table, *head_args, first=4)
            head_grads[l] = net.scatter(full, (HEADS,) * 4)
    vectors = [v for part in vectors for v in part]
    if net.fast:
        ffn_sum = net.add_last(order.hold(ffn_mine), ffn_last)
        (
            stream_out, stream_grad, qkv_grad, out_grad, up_grad, down_grad,
            gains_grad, shifts_grad, hidden_gains_grad, hidden_shifts_grad, usage_rms,
        ) = order(
            end_call, grad_low, full, ffn_sum, turned, valid, tops, vectors, usage
        )
        stream_out = stream_out.reshape(LONG, D // n)
        stream_grad = stream_grad.reshape(LONG, D // n)
        stacked = [qkv_grad, out_grad, up_grad, down_grad]
        usage_rms = usage_rms[: 3 * layers, 0].reshape(layers, 3)
    else:
        stream_out = net.rows_out_end(net.rows_out(stream))
        stream_grad = net.rows_out_end(net.rows_out(grad))
        norms = [jnp.sum(jnp.stack(vectors[4 * l : 4 * l + 3], 1), axis=2) for l in range(layers)]
        norms = lax.psum(jnp.stack(norms), ("dp", "head"))
        hids = [jnp.sum(vectors[4 * l + 3], axis=2).reshape(2, FF) for l in range(layers)]
        hids = lax.psum(jnp.stack(hids), ("dp", "head"))
        share = lambda v: lax.dynamic_slice_in_dim(
            v, net.z * (v.shape[-1] // n), v.shape[-1] // n, v.ndim - 1
        )
        norms, hids = share(norms), share(hids)
        totals = []
        for l in range(layers):
            branch, rest = usage[2 * l : 2 * l + 2]
            totals += [jnp.sum(branch), jnp.sum(rest[0]), jnp.sum(rest[1])]
        totals = lax.psum(jnp.stack(totals + [jnp.sum(valid) * D]), ("dp", "head"))
        usage_rms = jnp.sqrt(totals[:-1] / totals[-1]).reshape(layers, 3)
        weight_grads = []
        for l in range(layers):
            heads = head_grads[l]
            width = heads.shape[1] // 4
            qkv = heads[:, : 3 * width].reshape(-1, 3, width).transpose(1, 0, 2)
            half = ffn_grads[l].shape[1] // 2
            weight_grads.append(
                (qkv, heads[:, 3 * width :].T, ffn_grads[l][:, :half], ffn_grads[l][:, half:].T)
            )
        stacked = [jnp.stack([weight_grads[l][k] for l in range(layers)]) for k in range(4)]
        gains_grad, shifts_grad = norms[:, 0], norms[:, 1]
        hidden_gains_grad, hidden_shifts_grad = hids[:, 0], hids[:, 1]
    return (
        stream_out,
        stream_grad,
        stacked[0],
        stacked[1],
        stacked[2],
        stacked[3],
        gains_grad,
        shifts_grad,
        hidden_gains_grad,
        hidden_shifts_grad,
        usage_rms,
    )


def solution(mesh):
    n_dp, n_head = mesh.shape["dp"], mesh.shape["head"]

    def run(*args):
        return local(n_dp, n_head, *args)

    return jax.shard_map(
        run,
        mesh=mesh,
        in_specs=(
            P("dp", "head"),
            P(None, None, "dp", "head"),
            P(None, "head", "dp"),
            P(None, "dp", "head"),
            P(None, "head", "dp"),
            P(None, None, "head"),
            P(None, None, "head"),
            P(None, "head"),
            P(None, "head"),
            P("dp"),
            P("dp"),
            P("dp", "head"),
        ),
        out_specs=(
            P("dp", "head"),
            P("dp", "head"),
            P(None, None, "dp", "head"),
            P(None, "head", "dp"),
            P(None, "dp", "head"),
            P(None, "head", "dp"),
            P(None, None, "head"),
            P(None, None, "head"),
            P(None, "head"),
            P(None, "head"),
            P(),
        ),
        check_vma=False,
    )
```

```python
import functools
import math

import jax
import jax.numpy as jnp
from jax import lax
from jax.experimental import pallas as pl
from jax.experimental.pallas import tpu as pltpu
from jax.sharding import PartitionSpec as P

D = 1024
FF = 4096
LONG = 2048
SHORT = 512
DH = 64
LANES = 128
BLOCKS = D // LANES
GROUPS = 4
WIDE = FF // GROUPS
HEADS = D // GROUPS
NARROW = 4 * HEADS
BROAD = 2 * WIDE
EPS = 1e-05
MASKED = -1000000000.0
ROWS = 512
CHUNK = 256
VMEM_BYTES = 60 * 1024 * 1024
MESH = pl.DeviceIdType.MESH

f32 = jnp.float32
bf16 = jnp.bfloat16


def dot(a, b):
    return jnp.dot(a, b, preferred_element_type=f32)


def dot_nt(a, b):
    return lax.dot_general(a, b, (((1,), (1,)), ((), ())), preferred_element_type=f32)


def flip(a):
    return jnp.transpose(a.astype(f32), (1, 0)).astype(a.dtype)


def row_loop(total, step, body):
    step = min(step, total)

    def advance(i, carry):
        body(pl.ds(pl.multiple_of(i * step, step), step))
        return carry

    lax.fori_loop(0, total // step, advance, 0)


def sum_lanes(value):
    return jnp.sum(value, axis=1, keepdims=True)


def fold_lanes(value):
    total = value[:, :LANES]
    for i in range(1, value.shape[1] // LANES):
        total = total + value[:, i * LANES : (i + 1) * LANES]
    return total


def fold_rows(value):
    total = value[:8]
    for i in range(1, value.shape[0] // 8):
        total = total + value[i * 8 : (i + 1) * 8]
    return total


def row_stats(value):
    mean = sum_lanes(value) / D
    centred = value - mean
    rstd = lax.rsqrt(sum_lanes(centred * centred) / D + EPS)
    return centred * rstd, rstd


def norm_back(dy, hat, rstd, gain):
    dx = dy * gain
    first = sum_lanes(dx) / D
    cross = sum_lanes(dx * hat) / D
    return rstd * (dx - first - hat * cross)


class Vectors:
    def __init__(self, n, layer, ref):
        self.n, self.ref = n, ref
        self.few, self.many = BLOCKS // n, 4 * BLOCKS // n
        self.at = layer * (6 * self.few + 2 * self.many)

    def rows(self, z, first, count):
        return [self.ref[z, first + p : first + p + 1, :] for p in range(count)]

    def norm(self, kind, which):
        first = self.at + (3 * kind + which) * self.few
        parts = [v for z in range(self.n) for v in self.rows(z, first, self.few)]
        return jnp.concatenate(parts, axis=1)

    def hidden(self, kind, group):
        first = self.at + 6 * self.few + kind * self.many
        share = self.n // GROUPS
        parts = [v for i in range(share) for v in self.rows(group * share + i, first, self.many)]
        return jnp.concatenate(parts, axis=1)


def params(**kw):
    return pltpu.CompilerParams(vmem_limit_bytes=VMEM_BYTES, **kw)


def cost(flops, size, trans=0):
    return pl.CostEstimate(flops=int(flops), bytes_accessed=int(size), transcendentals=int(trans))


def whole(shape):
    zeros = (0,) * len(shape)
    return pl.BlockSpec(shape, lambda *_: zeros)


def shape(dims, kind):
    return jax.ShapeDtypeStruct(dims, kind)


VM = pl.BlockSpec(memory_space=pltpu.VMEM)
HB = pl.BlockSpec(memory_space=pl.ANY)
DMA = pltpu.SemaphoreType.DMA


def group_place(n):
    dp = lax.axis_index("dp")
    lo = lax.rem(dp, n)
    return dp - lo, lo


def group_send(n, k, source, target, send_sem, recv_sem):
    base, lo = group_place(n)
    return pltpu.make_async_remote_copy(
        src_ref=source,
        dst_ref=target,
        send_sem=send_sem,
        recv_sem=recv_sem,
        device_id={"dp": base + lax.rem(lo + k + n, n)},
        device_id_type=MESH,
    )


def order_of(n):
    return [k for k in (n // 2, *range(1, n // 2), *range(n // 2 + 1, n)) if k]


def head_columns(n, k):
    _, lo = group_place(n)
    unit = lax.rem(lo + k + n, n) * (BLOCKS // n)
    if n == GROUPS:
        return lax.rem(lo + k + n, n), 0
    return unit // 2, pl.multiple_of(lax.rem(unit, 2) * LANES, LANES)


class Place:
    def __init__(self):
        dp = lax.axis_index("dp")
        self.z = lax.axis_index("head")
        self.lo = lax.rem(dp, GROUPS)
        core = lax.rem(dp, 2)
        bit_x = lax.rem(dp // 2, 2)
        bit_y = lax.rem(dp // 4, 2)
        by_x = dp + 2 - 4 * bit_x
        by_y = dp + 4 - 8 * bit_y
        self.dp, self.core, self.bit_x = dp, core, bit_x
        self.by_x, self.by_y = by_x, by_y
        self.first = by_x * (1 - core) + by_y * core
        self.second = by_y * (1 - core) + by_x * core
        self.both = by_x + by_y - dp
        self.mate = dp + 1 - 2 * core

    def partner(self, way):
        return {"mate": self.mate, "first": self.first, "second": self.second}[way]

    def group(self, p):
        one, two = 1 - 2 * lax.rem(self.z, 2), 2 - 4 * (self.z // 2)
        return self.z + (0, two, one, one + two)[p]

    def others(self):
        return [{"head": lax.rem(self.z + k, GROUPS)} for k in range(1, GROUPS)]


def unlike(a, b):
    return jnp.where(a == b, 0, 1)


class Hop:
    aliases = {}

    def __init__(self, array, way):
        self.arrays, self.way = [array], way
        self.outs = [jax.ShapeDtypeStruct(array.shape, array.dtype)]
        self.sems = [DMA((2,))]

    def device(self, at):
        return {"dp": at.partner(self.way)}

    def peers(self, at):
        return [self.device(at)], [], 1

    def copy(self, at, ins, outs, sems):
        return pltpu.make_async_remote_copy(
            src_ref=ins[0],
            dst_ref=outs[0],
            send_sem=sems[0].at[0],
            recv_sem=sems[0].at[1],
            device_id=self.device(at),
            device_id_type=MESH,
        )

    def start(self, *args):
        self.copy(*args).start()

    def finish(self, *args):
        self.copy(*args).wait()


class Turn:
    def __init__(self, array, back, half=None, into=None):
        self.arrays, self.back = [array], back
        self.aliases = {}
        if into is not None:
            self.arrays.append(into)
            self.aliases = {1: 0}
        if back:
            tokens, wide = array.shape[0], array.shape[1] // GROUPS
            out = (GROUPS, tokens, wide)
        else:
            tokens, wide = array.shape[1:]
            out = (tokens, GROUPS * wide)
        self.wide = wide
        self.rows = pl.ds(0, tokens) if half is None else pl.ds(half * (tokens // 2), tokens // 2)
        self.outs = [jax.ShapeDtypeStruct(out, array.dtype)]
        self.sems = [DMA((2, GROUPS)), DMA]

    def many(self, at):
        return [(at.dp - at.lo + t, at.lo) for t in range(GROUPS)]

    def one(self, at):
        return [(at.dp - at.lo + at.z, g) for g in range(GROUPS)]

    def peers(self, at):
        from_ = self.many(at) if self.back else self.one(at)
        return [], from_, GROUPS - 1 + unlike(at.z, at.lo)

    def each(self, op, at, ins, outs, sems):
        targets = self.one(at) if self.back else self.many(at)
        for i, (dp, z) in enumerate(targets):
            if self.back:
                source = ins[0].at[self.rows, pl.ds(i * self.wide, self.wide)]
                target, slot = outs[0].at[at.lo, self.rows], at.lo
            else:
                source = ins[0].at[i, self.rows]
                column = pl.multiple_of(at.z * self.wide, self.wide)
                target, slot = outs[0].at[self.rows, pl.ds(column, self.wide)], at.z

            def remote(i=i, dp=dp, z=z, source=source, target=target, slot=slot):
                copy = pltpu.make_async_remote_copy(
                    src_ref=source,
                    dst_ref=target,
                    send_sem=sems[0].at[0, i],
                    recv_sem=sems[0].at[1, slot],
                    device_id={"dp": dp, "head": z},
                    device_id_type=MESH,
                )
                copy.start() if op == "start" else copy.wait_send()

            def inside(source=source, target=target):
                copy = pltpu.make_async_copy(source, target, sems[1])
                copy.start() if op == "start" else copy.wait()

            away = (dp != at.dp) | (z != at.z)
            pl.when(away)(remote)
            pl.when(jnp.logical_not(away))(inside)

    def start(self, *args):
        self.each("start", *args)

    def finish(self, at, ins, outs, sems):
        self.each("wait", at, ins, outs, sems)
        sources = self.many(at) if self.back else self.one(at)
        for slot, (dp, z) in enumerate(sources):

            @pl.when((dp != at.dp) | (z != at.z))
            def _(slot=slot):
                if self.back:
                    spot = outs[0].at[slot, self.rows]
                else:
                    spot = outs[0].at[self.rows, pl.ds(slot * self.wide, self.wide)]
                pltpu.make_async_remote_copy(
                    src_ref=spot,
                    dst_ref=spot,
                    send_sem=sems[0].at[0, 0],
                    recv_sem=sems[0].at[1, slot],
                    device_id={"dp": at.mate},
                    device_id_type=MESH,
                ).wait_recv()


class Host:
    def __init__(self, n, parts):
        self.n, self.parts = n, parts
        self.at = Place() if parts else None

    def barrier(self, group=True):
        n = self.n
        sem = pltpu.get_barrier_semaphore()
        count = 0
        if group:
            base, lo = group_place(n)
            for k in range(1, n):
                pl.semaphore_signal(
                    sem, inc=1, device_id={"dp": base + lax.rem(lo + k, n)}, device_id_type=MESH
                )
            count = n - 1
        for job, *_ in self.parts:
            plain, pairs, more = job.peers(self.at)
            for device in plain:
                pl.semaphore_signal(sem, inc=1, device_id=device, device_id_type=MESH)
            for dp, z in pairs:

                @pl.when((dp != self.at.dp) | (z != self.at.z))
                def _(dp=dp, z=z):
                    pl.semaphore_signal(
                        sem, inc=1, device_id={"dp": dp, "head": z}, device_id_type=MESH
                    )

            count = count + more
        pl.semaphore_wait(sem, count)

    def start(self):
        for job, *refs in self.parts:
            job.start(self.at, *refs)

    def finish(self):
        for job, *refs in self.parts:
            job.finish(self.at, *refs)


def plain_call(
    body, n, name, ident, inputs, in_specs, out_shape, out_specs, scratch, flops, jobs, grid=()
):
    return list(
        pl.pallas_call(
            lambda *refs: body(Host(n, []), *refs),
            out_shape=out_shape,
            grid=grid,
            in_specs=in_specs,
            out_specs=out_specs,
            scratch_shapes=scratch,
            compiler_params=params(),
            cost_estimate=cost(flops, 10 * 2**20),
            name=name,
        )(*inputs)
    )


def remote_call(
    body, n, name, ident, inputs, in_specs, out_shape, out_specs, scratch, flops, jobs, grid=()
):
    job_in = [v for job in jobs for v in job.arrays]
    job_out = [v for job in jobs for v in job.outs]
    job_sems = [v for job in jobs for v in job.sems]
    aliases = {}
    i, o = len(inputs), len(out_shape)
    for job in jobs:
        aliases.update({i + a: o + b for a, b in job.aliases.items()})
        i, o = i + len(job.arrays), o + len(job.outs)

    def kernel(*refs):
        refs = list(refs)

        def take(count):
            taken = refs[:count]
            del refs[:count]
            return taken

        own_in, extra_in = take(len(inputs)), take(len(job_in))
        own_out, extra_out = take(len(out_shape)), take(len(job_out))
        own_scratch, extra_sems = take(len(scratch)), take(len(job_sems))
        parts = []
        for job in jobs:
            sizes = (len(job.arrays), len(job.outs), len(job.sems))
            lists = (extra_in, extra_out, extra_sems)
            part = [job]
            for values, size in zip(lists, sizes):
                part.append(values[:size])
                del values[:size]
            parts.append(part)
        body(Host(n, parts), *own_in, *own_out, *own_scratch)

    res = pl.pallas_call(
        kernel,
        out_shape=list(out_shape) + job_out,
        grid=grid,
        in_specs=list(in_specs) + [HB] * len(job_in),
        out_specs=list(out_specs) + [HB] * len(job_out),
        scratch_shapes=list(scratch) + job_sems,
        input_output_aliases=aliases,
        compiler_params=params(collective_id=ident, has_side_effects=True),
        cost_estimate=cost(flops, 10 * 2**20),
        name=name,
    )(*inputs, *job_in)
    return list(res)


class Queries:
    def __init__(self, n, weight, outs, xs, wide, send, wsem, ssem, rsem, lsem):
        self.n, self.weight, self.outs, self.xs, self.wide, self.send = n, weight, outs, xs, wide, send
        self.wsem, self.ssem, self.rsem, self.lsem = wsem, ssem, rsem, lsem
        self.units = BLOCKS // n
        self.steps = order_of(n) + [0]

    def fetch(self, i):
        group, offset = head_columns(self.n, self.steps[i])
        width = self.units * LANES
        return [
            pltpu.make_async_copy(
                self.weight.at[:, group, :, pl.ds(c * HEADS + offset, width)],
                self.wide.at[i % 2, c],
                self.wsem.at[i % 2, c],
            )
            for c in range(3)
        ]

    def begin(self):
        for copy in self.fetch(0):
            copy.start()

    def norm(self, low, gain, shift):
        def body(r):
            hat, _ = row_stats(low[r, :].astype(f32))
            self.xs[r, :] = (hat * gain + shift).astype(bf16)

        row_loop(low.shape[0], ROWS, body)

    def copy(self, k):
        if k:
            return group_send(
                self.n, k, self.send.at[k], self.outs[k], self.ssem.at[k], self.rsem.at[k]
            )
        return pltpu.make_async_copy(self.send.at[0], self.outs[0], self.lsem)

    def step(self, i):
        k = self.steps[i]
        if i + 1 < self.n:
            for copy in self.fetch(i + 1):
                copy.start()
        for c, copy in enumerate(self.fetch(i)):
            copy.wait()
            value = dot(self.xs[...], self.wide[i % 2, c].reshape(D, -1)).astype(bf16)
            self.send[k, c] = value[:, :LANES]
            for u in range(1, self.units):
                self.outs[u * self.n + k][c] = value[:, u * LANES : (u + 1) * LANES]
        self.copy(k).start()

    def finish(self):
        for k in self.steps:
            self.copy(k).wait()


def queries_scratch(n, tokens):
    return [
        pltpu.VMEM((tokens, D), bf16),
        pltpu.VMEM((2, 3, BLOCKS, LANES, BLOCKS // n * LANES), bf16),
        pltpu.VMEM((n, 3, tokens, LANES), bf16),
        DMA((2, 3)),
        DMA((n,)),
        DMA((n,)),
        DMA,
    ]


def queries_outs(n, tokens):
    count = BLOCKS // n * n
    return [jax.ShapeDtypeStruct((3, tokens, LANES), bf16)] * count, [HB] * n + [VM] * (count - n)


def qkv_kernel(layer, host, low, packed, weight, *refs):
    vectors = Vectors(host.n, layer, packed)
    queries = Queries(host.n, weight, refs[:-7], *refs[-7:])
    queries.begin()
    queries.norm(low, vectors.norm(0, 0), vectors.norm(1, 0))
    host.barrier()
    host.start()
    for i in range(host.n):
        queries.step(i)
    queries.finish()
    host.finish()


def qkv_call(n, ident, jobs, layer, low, packed, weight):
    tokens = low.shape[0]
    units = BLOCKS // n
    out_shape, out_specs = queries_outs(n, tokens)
    res = remote_call(
        functools.partial(qkv_kernel, layer), n, "qkv", ident,
        [low, packed, weight], [VM, VM, HB], out_shape, out_specs, queries_scratch(n, tokens),
        60 * tokens * D * D, jobs,
    )
    return [res[u * n : (u + 1) * n] for u in range(units)], res[n * units :]


def masks_kernel(n, sc, flags, aux, one, valid, need):
    tokens = aux.shape[1]
    rows = tokens // LANES
    first = lax.broadcasted_iota(jnp.int32, (LANES, LANES), 1) == 0
    one[...] = jnp.where(lax.broadcasted_iota(jnp.int32, one.shape, 1) == 0, 1.0, 0.0).astype(bf16)
    long = jnp.max(flags[LONG // LANES : LONG // LANES + 1, 0:1]) == 1
    alive, sequence = [], []
    for k in range(n):
        place = lax.rem(sc[0] + n - k, n)
        some = jnp.float32(0)
        for i in range(rows):
            row = flags[pl.ds(place * rows + i, 1), :].astype(f32)
            some = jnp.maximum(some, jnp.max(row))
            column = jnp.transpose(jnp.broadcast_to(row, (LANES, LANES)), (1, 0))
            spot = slice(i * LANES, (i + 1) * LANES)
            aux[k, spot, :] = jnp.where(first & (column == 0), MASKED, 0.0).astype(bf16)
            if k == 0:
                valid[spot, :] = column[:, 0:1]
        alive.append(some > 0)
        sequence.append(place * tokens // SHORT)
    for i in range(n):
        for j in range(n):
            joined = long | (sequence[i] == sequence[j])
            need[i * n + j] = jnp.where(joined & alive[j], 1, 0).astype(jnp.int32)


def masks_call(n, lo, flags):
    tokens = LONG // n
    return pl.pallas_call(
        lambda *refs: masks_kernel(n, *refs),
        out_shape=[
            jax.ShapeDtypeStruct((n, tokens, LANES), bf16),
            jax.ShapeDtypeStruct((tokens, LANES), bf16),
            jax.ShapeDtypeStruct((tokens, 1), f32),
            jax.ShapeDtypeStruct((n * n,), jnp.int32),
        ],
        grid_spec=pltpu.PrefetchScalarGridSpec(
            num_scalar_prefetch=1,
            grid=(),
            in_specs=[VM],
            out_specs=[VM, VM, VM, pl.BlockSpec(memory_space=pltpu.SMEM)],
        ),
        compiler_params=params(),
        cost_estimate=cost(0, 2**20),
        name="masks",
    )(lo, flags)


def head_lanes(value, head):
    lane = lax.broadcasted_iota(jnp.int32, value.shape, 1)
    keep = (lane < DH) if head == 0 else (lane >= DH)
    return jnp.where(keep, value, jnp.zeros_like(value))


def attn_kernel(n, need, aux, one, *refs):
    qkv, (outs, lse, kx, vt, qs, top, acc) = refs[:n], refs[n:]
    tokens = aux.shape[1]
    for r in range(n):
        kx[r] = jnp.concatenate([qkv[r][1], aux[r]], axis=1)
        turned = flip(qkv[r][2])
        ones = jnp.ones((16, tokens), bf16)
        vt[r, 0] = jnp.concatenate([turned[:DH], ones], axis=0)
        vt[r, 1] = jnp.concatenate([turned[DH:], ones], axis=0)
        qs[r] = (qkv[r][0].astype(f32) * (1.0 / math.sqrt(DH))).astype(bf16)

    halves = jnp.where(
        lax.broadcasted_iota(jnp.int32, (LANES, LANES), 0) // DH
        == lax.broadcasted_iota(jnp.int32, (LANES, LANES), 1),
        1.0,
        0.0,
    ).astype(bf16)
    reach = jnp.zeros((1, LANES), f32)
    longest = jnp.zeros((1, LANES), f32)
    for r in range(n):
        for which, value in ((0, qs[r]), (1, qkv[r][1])):
            size = jnp.max(dot(value * value, halves), axis=0, keepdims=True)
            if which:
                longest = jnp.maximum(longest, size)
            else:
                reach = jnp.maximum(reach, size)
    bounded = jnp.max(reach * longest) < 70.0 * 70.0

    def each_query(plain, i, carry):
        query = qs[i]
        extended = [jnp.concatenate([head_lanes(query, h), one[...]], axis=1) for h in range(2)]
        top[...] = jnp.zeros_like(top) if plain else jnp.full_like(top, -3e38)
        acc[...] = jnp.zeros_like(acc)

        def each_key(j, inner):
            @pl.when(need[i * n + j] == 1)
            def _():
                if plain:
                    raised = [jnp.exp(dot_nt(kx[j], extended[h])).astype(bf16) for h in range(2)]
                    for h in range(2):
                        acc[h] += dot(vt[j, h], raised[h])
                    return
                for h in range(2):
                    scores = dot_nt(kx[j], extended[h])
                    before = top[h : h + 1]
                    now = jnp.maximum(before, jnp.max(scores, axis=0, keepdims=True))
                    raised = jnp.exp(scores - now).astype(bf16)
                    top[h : h + 1] = now
                    acc[h] = acc[h] * jnp.exp(before - now) + dot(vt[j, h], raised)

            return inner

        lax.fori_loop(0, n, each_key, 0)
        sums = [acc[h][DH : DH + 1] for h in range(2)]
        both = jnp.concatenate([acc[h][:DH] / sums[h] for h in range(2)], axis=0)
        outs[i] = jnp.transpose(both, (1, 0)).astype(bf16)
        for h in range(2):
            lse[i, h : h + 1] = top[h : h + 1] + jnp.log(sums[h])
        return carry

    @pl.when(bounded)
    def _():
        lax.fori_loop(0, n, functools.partial(each_query, True), 0)

    @pl.when(jnp.logical_not(bounded))
    def _():
        lax.fori_loop(0, n, functools.partial(each_query, False), 0)


def unit_call(kernel, n, need, aux, one, arrays, out_shape, scratch, work, name):
    total = n * aux.shape[1]
    return pl.pallas_call(
        lambda *refs: kernel(n, *refs),
        out_shape=out_shape,
        grid_spec=pltpu.PrefetchScalarGridSpec(
            num_scalar_prefetch=1,
            grid=(),
            in_specs=[VM] * (2 + len(arrays)),
            out_specs=[VM] * len(out_shape),
            scratch_shapes=scratch,
        ),
        compiler_params=params(),
        cost_estimate=cost(work * total * total * 512, 8 * 2**20),
        name=name,
    )(need, aux, one, *arrays)


def attn_call(n, need, aux, one, parts):
    tokens = aux.shape[1]
    return unit_call(
        attn_kernel, n, need, aux, one, parts,
        [
            jax.ShapeDtypeStruct((n, tokens, LANES), bf16),
            jax.ShapeDtypeStruct((n, 8, tokens), f32),
        ],
        [
            pltpu.VMEM((n, tokens, 2 * LANES), bf16),
            pltpu.VMEM((n, 2, DH + 16, tokens), bf16),
            pltpu.VMEM((n, tokens, LANES), bf16),
            pltpu.VMEM((8, tokens), f32),
            pltpu.VMEM((2, DH + 16, tokens), f32),
        ],
        12, "attention",
    )


def proj_kernel(layer, host, valid, stream, packed, weight, *refs):
    n = host.n
    vectors = Vectors(n, layer, packed)
    gain, shift = vectors.norm(0, 1), vectors.norm(1, 1)
    tokens = stream.shape[0]
    units = BLOCKS // n
    att, (mid, rows, use, xs, rx, ssem, rsem, lsem) = refs[:units], refs[units:]
    host.barrier()
    copies = [
        group_send(n, -k, att[u].at[k], rx.at[k, u], ssem.at[u, k], rsem.at[u, k])
        for k in order_of(n)
        for u in range(units)
    ]
    copies += [pltpu.make_async_copy(att[u].at[0], rx.at[0, u], lsem.at[u]) for u in range(units)]
    for copy in copies:
        copy.start()
    host.start()
    for copy in copies:
        copy.wait()
    _, lo = group_place(n)
    for k in range(n):
        first = lax.rem(lo + k, n) * (units * LANES)
        for u in range(units):
            at = pl.multiple_of(first + u * LANES, LANES)
            rows[:, pl.ds(at, LANES)] = rx[k, u]

    def body(r):
        hat, _ = row_stats(rows[r, :].astype(f32))
        xs[r, :] = (hat * gain + shift).astype(bf16)

    row_loop(tokens, ROWS, body)
    branch = None
    for g in range(GROUPS):
        term = dot_nt(xs[:, g * HEADS : (g + 1) * HEADS], weight[:, g].reshape(D, HEADS))
        branch = term if branch is None else branch + term
    mid[...] = branch
    use[...] = jnp.zeros_like(use)

    def finish(r):
        part = mid[r, :]
        use[...] += fold_rows(valid[r, :] * part * part)
        mid[r, :] = stream[r, :].astype(f32) + part

    row_loop(tokens, ROWS, finish)
    host.finish()


def proj_call(n, ident, jobs, layer, valid, stream, packed, weight, att):
    tokens = stream.shape[0]
    units = BLOCKS // n
    flat = whole(stream.shape)
    return remote_call(
        functools.partial(proj_kernel, layer), n, "projection", ident,
        [valid, stream, packed, weight, *att],
        [whole(v.shape) for v in (valid, stream, packed)]
        + [pl.BlockSpec((BLOCKS, GROUPS, LANES, HEADS), lambda i: (0, 0, 0, 3))]
        + [whole(v.shape) for v in att],
        [
            jax.ShapeDtypeStruct(stream.shape, f32),
            jax.ShapeDtypeStruct(stream.shape, bf16),
            jax.ShapeDtypeStruct((8, D), f32),
        ],
        [flat, flat, whole((8, D))],
        [
            pltpu.VMEM((tokens, D), bf16),
            pltpu.VMEM((n, units, tokens, LANES), bf16),
            DMA((units, n)),
            DMA((units, n)),
            DMA((units,)),
        ],
        30 * tokens * D * D, jobs, grid=(1,),
    )


def ffn_kernel(
    layer, host, valid, mid, packed, weight,
    slope, hat, normed, low_mid, rstd_out, stream, low, use,
    xs, act, mean, buf, acc,
):
    step = pl.program_id(0)
    tokens = mid.shape[0]
    vectors = Vectors(host.n, layer, packed)

    @pl.when(step == 0)
    def _():
        gain, shift = vectors.norm(0, 2), vectors.norm(1, 2)
        use[...] = jnp.zeros_like(use)

        def body(r):
            raw = mid[r, :].astype(bf16)
            value, _ = row_stats(raw.astype(f32))
            low_mid[r, :] = raw
            xs[r, :] = (value * gain + shift).astype(bf16)

        row_loop(tokens, ROWS, body)
        if host.parts:
            host.barrier(False)
            host.start()

    @pl.when(step < GROUPS)
    def _():
        buf[...] = dot(xs[...], weight[...].reshape(D, WIDE))

        def body(r):
            h = buf[r, :]
            half = 0.5 * (1.0 + lax.erf(h * (1.0 / math.sqrt(2.0))))
            bell = jnp.exp(-0.5 * h * h) * (1.0 / math.sqrt(2.0 * math.pi))
            act[step, r, :] = h * half
            slope[0, r, :] = (half + h * bell).astype(bf16)

        row_loop(tokens, CHUNK, body)

    @pl.when(step == GROUPS)
    def _():
        acc[...] = jnp.zeros_like(acc)

        def body(r):
            blocks = [act[g, r, :] for g in range(GROUPS)]
            total = sum_lanes(sum(fold_lanes(b) for b in blocks)) / FF
            square = sum(fold_lanes((b - total) * (b - total)) for b in blocks)
            rstd = lax.rsqrt(sum_lanes(square) / FF + EPS)
            mean[r, :] = jnp.broadcast_to(total, (CHUNK, LANES))
            rstd_out[r, :] = jnp.broadcast_to(rstd, (CHUNK, LANES))

        row_loop(tokens, CHUNK, body)

    @pl.when(step >= GROUPS)
    def _():
        g = step - GROUPS
        hgain, hshift = vectors.hidden(0, g), vectors.hidden(1, g)

        def body(r):
            value = (act[g, r, :] - mean[r, 0:1]) * rstd_out[r, 0:1]
            hat[0, r, :] = value.astype(bf16)
            normed[0, r, :] = (value * hgain + hshift).astype(bf16)

        row_loop(tokens, CHUNK, body)
        acc[...] += dot_nt(normed[0], weight[...].reshape(D, WIDE))

    @pl.when(step == 2 * GROUPS - 1)
    def _():
        def body(r):
            feed = acc[r, :]
            out = mid[r, :] + feed
            keep = valid[r, :]
            stream[r, :] = out
            low[r, :] = out.astype(bf16)
            use[0] += fold_rows(keep * feed * feed)
            use[1] += fold_rows(keep * out * out)

        row_loop(tokens, ROWS, body)

        host.finish()


def first_half(s):
    return jnp.minimum(s, GROUPS - 1)


def second_half(s):
    return jnp.maximum(s - GROUPS, 0)


def half_specs(tokens):
    early = pl.BlockSpec((1, tokens, WIDE), lambda s: (first_half(s), 0, 0))
    late = pl.BlockSpec((1, tokens, WIDE), lambda s: (second_half(s), 0, 0))
    return early, late


def ffn_call(n, ident, jobs, layer, valid, mid, packed, weight):
    tokens = mid.shape[0]
    big = (GROUPS, tokens, WIDE)
    early, late = half_specs(tokens)
    flat = (tokens, D)
    call = remote_call if jobs else plain_call
    return call(
        functools.partial(ffn_kernel, layer), n, "ffn", ident,
        [valid, mid, packed, weight],
        [whole(v.shape) for v in (valid, mid, packed)]
        + [
            pl.BlockSpec(
                (BLOCKS, 1, LANES, WIDE), lambda s: (0, lax.rem(s, GROUPS), 0, s // GROUPS)
            )
        ],
        [jax.ShapeDtypeStruct(big, bf16)] * 3
        + [
            jax.ShapeDtypeStruct(flat, bf16),
            jax.ShapeDtypeStruct((tokens, LANES), f32),
            jax.ShapeDtypeStruct(flat, f32),
            jax.ShapeDtypeStruct(flat, bf16),
            jax.ShapeDtypeStruct((2, 8, D), f32),
        ],
        [early, late, late]
        + [whole(flat), whole((tokens, LANES)), whole(flat), whole(flat), whole((2, 8, D))],
        [
            pltpu.VMEM(flat, bf16),
            pltpu.VMEM(big, f32),
            pltpu.VMEM((tokens, LANES), f32),
            pltpu.VMEM((tokens, WIDE), f32),
            pltpu.VMEM(flat, f32),
        ],
        16 * tokens * D * FF, jobs, grid=(2 * GROUPS,),
    )


def ffn_back_kernel(
    layer, host, grad, hat, slope, rstd_in, low_mid, packed, weight,
    dhid, grad_turned, normed_turned, grad_out, hgrads, grads,
    gs, dxs, buf, first, cross, acc,
):
    step = pl.program_id(0)
    tokens = grad.shape[0]
    vectors = Vectors(host.n, layer, packed)

    @pl.when(step == 0)
    def _():
        first[...] = jnp.zeros_like(first)
        cross[...] = jnp.zeros_like(cross)
        hgrads[...] = jnp.zeros_like(hgrads)
        grads[...] = jnp.zeros_like(grads)
        gs[...] = grad[...].astype(bf16)
        for b in range(BLOCKS):
            grad_turned[b] = flip(gs[:, b * LANES : (b + 1) * LANES])
        if host.parts:
            host.barrier(False)
            host.start()

    @pl.when(step < GROUPS)
    def _():
        buf[...] = dot(gs[...], weight[...].reshape(D, WIDE))
        hgain = vectors.hidden(0, step)

        def body(r):
            value = hat[0, r, :].astype(f32)
            dy = buf[r, :]
            dx = dy * hgain
            hgrads[0, step] += fold_rows(dy * value)
            hgrads[1, step] += fold_rows(dy)
            first[r, :] += fold_lanes(dx)
            cross[r, :] += fold_lanes(dx * value)
            dxs[step, r, :] = dx

        row_loop(tokens, CHUNK, body)

    @pl.when(step == GROUPS)
    def _():
        acc[...] = jnp.zeros_like(acc)

        def body(r):
            for ref in (first, cross):
                ref[r, :] = jnp.broadcast_to(sum_lanes(ref[r, :]) / FF, ref[r, :].shape)

        row_loop(tokens, ROWS, body)

    @pl.when(step >= GROUPS)
    def _():
        g = step - GROUPS

        def body(r):
            inner = dxs[g, r, :] - first[r, 0:1] - hat[0, r, :].astype(f32) * cross[r, 0:1]
            dhid[0, r, :] = (slope[0, r, :].astype(f32) * (rstd_in[r, 0:1] * inner)).astype(bf16)

        row_loop(tokens, CHUNK, body)
        acc[...] += dot_nt(dhid[0], weight[...].reshape(D, WIDE))

    @pl.when(step == 2 * GROUPS - 1)
    def _():
        gain, shift = vectors.norm(0, 2), vectors.norm(1, 2)

        def body(r):
            value, rstd = row_stats(low_mid[r, :].astype(f32))
            dy = acc[r, :]
            grads[0] += fold_rows(dy * value)
            grads[1] += fold_rows(dy)
            grad_out[r, :] = grad[r, :].astype(f32) + norm_back(dy, value, rstd, gain)
            gs[r, :] = (value * gain + shift).astype(bf16)

        row_loop(tokens, ROWS, body)
        for b in range(BLOCKS):
            normed_turned[b] = flip(gs[:, b * LANES : (b + 1) * LANES])
        host.finish()


def ffn_back_call(n, ident, jobs, layer, grad, hat, slope, rstd, low_mid, packed, weight):
    tokens = grad.shape[0]
    turned = (BLOCKS, LANES, tokens)
    big = (GROUPS, tokens, WIDE)
    _, late = half_specs(tokens)
    flat = (tokens, D)
    call = remote_call if jobs else plain_call
    return call(
        functools.partial(ffn_back_kernel, layer), n, "ffn_back", ident,
        [grad, hat, slope, rstd, low_mid, packed, weight],
        [
            whole(flat),
            pl.BlockSpec((1, tokens, WIDE), lambda s: (lax.rem(s, GROUPS), 0, 0)),
            late,
        ]
        + [whole(v.shape) for v in (rstd, low_mid, packed)]
        + [
            pl.BlockSpec(
                (BLOCKS, 1, LANES, WIDE), lambda s: (0, lax.rem(s, GROUPS), 0, 1 - s // GROUPS)
            )
        ],
        [
            jax.ShapeDtypeStruct(big, bf16),
            jax.ShapeDtypeStruct(turned, bf16),
            jax.ShapeDtypeStruct(turned, bf16),
            jax.ShapeDtypeStruct(flat, f32),
            jax.ShapeDtypeStruct((2, GROUPS, 8, WIDE), f32),
            jax.ShapeDtypeStruct((2, 8, D), f32),
        ],
        [late, whole(turned), whole(turned), whole(flat)]
        + [whole((2, GROUPS, 8, WIDE)), whole((2, 8, D))],
        [
            pltpu.VMEM(flat, bf16),
            pltpu.VMEM(big, f32),
            pltpu.VMEM((tokens, WIDE), f32),
            pltpu.VMEM((tokens, LANES), f32),
            pltpu.VMEM((tokens, LANES), f32),
            pltpu.VMEM(flat, f32),
        ],
        16 * tokens * D * FF, jobs, grid=(2 * GROUPS,),
    )


def proj_back_kernel(
    layer, host, grad, packed, weight, rows, *refs
):
    n = host.n
    vectors = Vectors(n, layer, packed)
    gain, shift = vectors.norm(0, 1), vectors.norm(1, 1)
    tokens = grad.shape[0]
    units = BLOCKS // n
    outs, refs = refs[:units], refs[units:]
    grad_turned, normed, grads, gs, dm, send, ssem, rsem, lsem = refs
    host.barrier()
    host.start()
    gs[...] = grad[...].astype(bf16)
    for g in range(GROUPS):
        dm[:, g * HEADS : (g + 1) * HEADS] = dot(gs[...], weight[:, g].reshape(D, HEADS))
    grads[...] = jnp.zeros_like(grads)

    def body(r):
        value, rstd = row_stats(rows[r, :].astype(f32))
        dy = dm[r, :]
        grads[0] += fold_rows(dy * value)
        grads[1] += fold_rows(dy)
        dv = norm_back(dy, value, rstd, gain).astype(bf16)
        for b in range(BLOCKS):
            send[b, r, :] = dv[:, b * LANES : (b + 1) * LANES]
        normed[r, :] = (value * gain + shift).astype(bf16)

    row_loop(tokens, ROWS, body)
    _, lo = group_place(n)
    copies = []
    for k in order_of(n) + [0]:
        for u in range(units):
            source = send.at[lax.rem(lo + k, n) * units + u]
            if k:
                copy = group_send(n, k, source, outs[u].at[k], ssem.at[u, k], rsem.at[u, k])
            else:
                copy = pltpu.make_async_copy(source, outs[u].at[0], lsem.at[u])
            copy.start()
            copies.append(copy)
    for b in range(BLOCKS):
        grad_turned[b] = flip(gs[:, b * LANES : (b + 1) * LANES])
    for copy in copies:
        copy.wait()
    host.finish()


def proj_back_call(n, ident, jobs, layer, grad, packed, weight, rows):
    tokens = grad.shape[0]
    units = BLOCKS // n
    turned = (BLOCKS, LANES, tokens)
    flat = (tokens, D)
    return remote_call(
        functools.partial(proj_back_kernel, layer), n, "projection_back", ident,
        [grad, packed, weight, rows],
        [whole(v.shape) for v in (grad, packed)]
        + [pl.BlockSpec((BLOCKS, GROUPS, LANES, HEADS), lambda i: (0, 0, 0, 3)), whole(flat)],
        [
            *[jax.ShapeDtypeStruct((n, tokens, LANES), bf16)] * units,
            jax.ShapeDtypeStruct(turned, bf16),
            jax.ShapeDtypeStruct(flat, bf16),
            jax.ShapeDtypeStruct((2, 8, D), f32),
        ],
        [HB] * units + [whole(turned), whole(flat), whole((2, 8, D))],
        [
            pltpu.VMEM(flat, bf16),
            pltpu.VMEM(flat, f32),
            pltpu.VMEM((BLOCKS, tokens, LANES), bf16),
            DMA((units, n)),
            DMA((units, n)),
            DMA((units,)),
        ],
        30 * tokens * D * D, jobs, grid=(1,),
    )


def attn_back_kernel(n, need, aux, one, *refs):
    qkv, (att, datt, lse) = refs[:n], refs[n : n + 3]
    outs, refs = refs[n + 3 : 2 * n + 3], refs[2 * n + 3 :]
    kx, kt, qs, vs, delta, dq, dkey, dval, dkv = refs
    for r in range(n):
        kx[r] = jnp.concatenate([qkv[r][1], aux[r]], axis=1)
        kt[r] = flip(qkv[r][1])
        vs[r] = qkv[r][2]
        qs[r] = (qkv[r][0].astype(f32) * (1.0 / math.sqrt(DH))).astype(bf16)
        both = jnp.transpose(att[r].astype(f32) * datt[r].astype(f32), (1, 0))
        delta[r, 0:1] = jnp.sum(both[:DH], axis=0, keepdims=True)
        delta[r, 1:2] = jnp.sum(both[DH:], axis=0, keepdims=True)
    dq[...] = jnp.zeros_like(dq)

    def each_key(j, carry):
        dkey[...] = jnp.zeros_like(dkey)
        dval[...] = jnp.zeros_like(dval)

        def each_query(i, inner):
            @pl.when(need[i * n + j] == 1)
            def _():
                for h in range(2):
                    query = head_lanes(qs[i], h)
                    out = head_lanes(datt[i], h)
                    scores = dot_nt(kx[j], jnp.concatenate([query, one[...]], axis=1))
                    probs = jnp.exp(scores - lse[i, h : h + 1])
                    dprobs = dot_nt(vs[j], out)
                    dscores = (probs * (dprobs - delta[i, h : h + 1])).astype(bf16)
                    dval[...] += dot(probs.astype(bf16), out)
                    dkey[...] += dot(dscores, query)
                    rows = slice(h * DH, (h + 1) * DH)
                    dq[i, rows] += dot(kt[j, rows], dscores)

            return inner

        lax.fori_loop(0, n, each_query, 0)
        dkv[j, 0] = dkey[...].astype(bf16)
        dkv[j, 1] = dval[...].astype(bf16)
        return carry

    lax.fori_loop(0, n, each_key, 0)
    for r in range(n):
        outs[r][0] = (jnp.transpose(dq[r], (1, 0)) * (1.0 / math.sqrt(DH))).astype(bf16)
        outs[r][1] = dkv[r, 0]
        outs[r][2] = dkv[r, 1]


def attn_back_call(n, need, aux, one, parts, att, datt, lse):
    tokens = aux.shape[1]
    return unit_call(
        attn_back_kernel, n, need, aux, one, [*parts, att, datt, lse],
        [jax.ShapeDtypeStruct((3, tokens, LANES), bf16)] * n,
        [
            pltpu.VMEM((n, tokens, 2 * LANES), bf16),
            pltpu.VMEM((n, LANES, tokens), bf16),
            pltpu.VMEM((n, tokens, LANES), bf16),
            pltpu.VMEM((n, tokens, LANES), bf16),
            pltpu.VMEM((n, 8, tokens), f32),
            pltpu.VMEM((n, LANES, tokens), f32),
            pltpu.VMEM((tokens, LANES), f32),
            pltpu.VMEM((tokens, LANES), f32),
            pltpu.VMEM((n, 2, tokens, LANES), bf16),
        ],
        14, "attention_back",
    )


def qkv_back_kernel(
    layer, host, grad, low, packed, wq, wk, wv, *refs
):
    n = host.n
    vectors = Vectors(n, layer, packed)
    gain, shift = vectors.norm(0, 0), vectors.norm(1, 0)
    tokens = grad.shape[0]
    units = BLOCKS // n
    early_count = n * (units - 1)
    ready, refs = refs[:early_count], refs[early_count:]
    dparts, refs = refs[:n], refs[n:]
    dlast, refs = refs[:n], refs[n:]
    grad_out, normed_turned, grads, grad_low, acc, ns, hats, scales, ssem, rsem, lsem = refs
    blocks = [ready[u * n : (u + 1) * n] for u in range(units - 1)] + [dlast]
    host.barrier()
    steps = [0] + order_of(n)[::-1]
    copies = {}
    for k in order_of(n):
        copies[k] = group_send(n, -k, dparts[k], dlast[k], ssem.at[k], rsem.at[k])
        copies[k].start()
    copies[0] = pltpu.make_async_copy(dparts[0], dlast[0], lsem)
    copies[0].start()
    host.start()
    grads[...] = jnp.zeros_like(grads)

    def early(r):
        value, rstd = row_stats(low[r, :].astype(f32))
        hats[r, :] = value
        scales[r, :] = jnp.broadcast_to(rstd, scales[r, :].shape)
        ns[r, :] = (value * gain + shift).astype(bf16)

    row_loop(tokens, ROWS, early)
    for b in range(BLOCKS):
        normed_turned[b] = flip(ns[:, b * LANES : (b + 1) * LANES])
    for i, k in enumerate(steps):
        copies[k].wait()
        group, offset = head_columns(n, k)
        left, right = [], []
        for c, weight in enumerate((wq, wk, wv)):
            left += [blocks[u][k][c] for u in range(units)]
            part = weight[:, group, :, pl.ds(offset, units * LANES)]
            right.append(part.reshape(D, units * LANES))
        total = dot_nt(jnp.concatenate(left, axis=1), jnp.concatenate(right, axis=1))
        if i == 0:
            acc[...] = total
        else:
            acc[...] += total

    def body(r):
        value, rstd = hats[r, :], scales[r, 0:1]
        dy = acc[r, :]
        grads[0] += fold_rows(dy * value)
        grads[1] += fold_rows(dy)
        total = grad[r, :] + norm_back(dy, value, rstd, gain)
        grad_out[r, :] = total
        grad_low[r, :] = total.astype(bf16)

    row_loop(tokens, ROWS, body)
    host.finish()


def qkv_back_call(n, ident, jobs, layer, grad, low, packed, weight, ready, dparts):
    tokens = grad.shape[0]
    turned = (BLOCKS, LANES, tokens)
    flat = (tokens, D)
    columns = lambda c: pl.BlockSpec((BLOCKS, GROUPS, LANES, HEADS), lambda i: (0, 0, 0, c))
    block = (3, tokens, LANES)
    res = remote_call(
        functools.partial(qkv_back_kernel, layer), n, "qkv_back", ident,
        [grad, low, packed, weight, weight, weight, *ready, *dparts],
        [whole(v.shape) for v in (grad, low, packed)]
        + [columns(0), columns(1), columns(2)]
        + [whole(block)] * (len(ready) + n),
        [jax.ShapeDtypeStruct(block, bf16)] * n
        + [
            jax.ShapeDtypeStruct(flat, f32),
            jax.ShapeDtypeStruct(turned, bf16),
            jax.ShapeDtypeStruct((2, 8, D), f32),
            jax.ShapeDtypeStruct(flat, bf16),
        ],
        [whole(block)] * n + [whole(flat), whole(turned), whole((2, 8, D)), whole(flat)],
        [
            pltpu.VMEM(flat, f32),
            pltpu.VMEM(flat, bf16),
            pltpu.VMEM(flat, f32),
            pltpu.VMEM((tokens, LANES), f32),
            DMA((n,)),
            DMA((n,)),
            DMA,
        ],
        50 * tokens * D * D, jobs, grid=(1,),
    )
    return [res[:n], *res[n:]]


def slot_group(p):
    return 2 * (p % 2) + p // 2


def pick_rows(sc, first, turned, count):
    return jnp.concatenate([turned[sc[first + m]] for m in range(count)], axis=0)


def put_rows(value, extra, outs, spot):
    rows = value.shape[0] // LANES
    for m in range(rows):
        part = value[m * LANES : (m + 1) * LANES]
        if extra is not None:
            part = part + extra[(m,) + spot].astype(f32)
            outs[m // 2][(m % 2,) + spot] = part.astype(bf16)
        else:
            outs[0][(m,) + spot] = part.astype(bf16)


def ffn_grad_kernel(ups, first, count, added, sc, up_turned, down_turned, *refs):
    split = added and ups
    dhid, normed, refs = [v.at[0] for v in refs[:2]], [v.at[0] for v in refs[2:4]], refs[4:]
    extra, outs = (refs[0], refs[1:]) if added else (None, refs)

    @pl.when(pl.program_id(0) == 0)
    def _():
        left = pick_rows(sc, first + ups, up_turned, count)
        for i in range(2):
            put_rows(dot(left, dhid[i][...]), extra, outs[:2] if split else outs, (i,))

    @pl.when(pl.program_id(0) == 1)
    def _():
        left = pick_rows(sc, first, down_turned, count)
        for i in range(2):
            put_rows(dot(left, normed[i][...]), extra, outs[2:] if split else outs, (i,))


def ffn_grad_call(ups, first, count, sc, up_turned, down_turned, dhid, normed, extra=None):
    tokens = up_turned.shape[2]
    added = extra is not None
    def block(i, kind, idle):
        def at(j, p, sc):
            p = jnp.where(j == kind, p, idle)
            return (jnp.bitwise_xor(p + 2 * i, sc[BLOCKS]), 0, 0)

        return pl.BlockSpec((1, tokens, WIDE), at)

    lefts = [block(i, 0, 1) for i in range(2)]
    rights = [block(i, 1, 0) for i in range(2)]
    piece = lambda m: pl.BlockSpec((m, 2, LANES, WIDE), lambda j, p, sc: (0, p, 0, j))
    outs = [2, 2] if added else [count]
    specs = [piece(m) for m in outs]
    wide = 2 * WIDE
    if added and ups:

        def half(kind, idle):
            at = lambda j, p, sc: (0, jnp.where(j == kind, p, idle), 0, 0)
            return pl.BlockSpec((2, 2, LANES, WIDE), at)

        outs, specs, wide = [2] * 4, [half(0, 1)] * 2 + [half(1, 0)] * 2, WIDE
    return pl.pallas_call(
        lambda *refs: ffn_grad_kernel(ups, first, count, added, *refs),
        out_shape=[jax.ShapeDtypeStruct((m, GROUPS, LANES, wide), bf16) for m in outs],
        grid_spec=pltpu.PrefetchScalarGridSpec(
            num_scalar_prefetch=1,
            grid=(2, GROUPS // 2),
            in_specs=[whole(up_turned.shape), whole(down_turned.shape), *lefts, *rights]
            + ([piece(count)] if added else []),
            out_specs=specs,
        ),
        compiler_params=params(),
        cost_estimate=cost(16 * tokens * count * LANES * FF, 24 * 2**20),
        name="ffn_grad",
    )(sc, up_turned, down_turned, dhid, dhid, normed, normed, *([extra] if added else []))


def head_grad_kernel(n, first, count, added, sc, in_turned, out_turned, normed, *refs):
    units = BLOCKS // n
    dqkv, refs = refs[: n * units], refs[n * units :]
    extra, outs = (refs[0], refs[1:]) if added else (None, refs)
    left = pick_rows(sc, first, in_turned, count)
    for k in range(n):
        for c in range(3):
            right = jnp.concatenate([dqkv[u * n + k][c] for u in range(units)], axis=1)
            value = dot(left, right)
            if n == GROUPS:
                slot = slot_group(jnp.bitwise_xor(lax.rem(sc[BLOCKS + 1] + k, n), sc[BLOCKS]))
                put_rows(value, extra, outs, (slot, slice(None), slice(c * HEADS, (c + 1) * HEADS)))
            else:
                unit = lax.rem(sc[BLOCKS + 1] + k, n) * units
                at = pl.multiple_of(c * HEADS + lax.rem(unit, 2) * LANES, LANES)
                slot = slot_group(unit // 2)
                put_rows(value, extra, outs, (slot, slice(None), pl.ds(at, LANES)))
    left = pick_rows(sc, first, out_turned, count)
    for g in range(GROUPS):
        slot = slot_group(jnp.bitwise_xor(g, sc[BLOCKS]))
        value = dot(left, normed[:, g * HEADS : (g + 1) * HEADS])
        put_rows(value, extra, outs, (slot, slice(None), slice(3 * HEADS, 4 * HEADS)))


def head_grad_call(n, first, count, sc, in_turned, out_turned, dqkv, normed, extra=None):
    tokens = in_turned.shape[2]
    added = extra is not None
    outs = [2, 2] if added else [count]
    inner = (GROUPS, LANES, 4 * HEADS)
    return pl.pallas_call(
        lambda *refs: head_grad_kernel(n, first, count, added, *refs),
        out_shape=[jax.ShapeDtypeStruct((m,) + inner, bf16) for m in outs],
        grid_spec=pltpu.PrefetchScalarGridSpec(
            num_scalar_prefetch=1,
            grid=(1,),
            in_specs=[whole(v.shape) for v in (in_turned, out_turned, normed, *dqkv)]
            + ([whole((count,) + inner)] if added else []),
            out_specs=[whole((m,) + inner) for m in outs],
        ),
        compiler_params=params(),
        cost_estimate=cost(16 * tokens * count * LANES * 4 * D, 16 * 2**20),
        name="head_grad",
    )(sc, in_turned, out_turned, normed, *dqkv, *([extra] if added else []))


def pack_kernel(qkv, out, up, down, *refs):
    layers = qkv.shape[0]
    for l in range(layers):
        narrow, broad = refs[2 * l : 2 * l + 2]
        for c in range(3):
            narrow[:, c * HEADS : (c + 1) * HEADS] = qkv[l, c]
        narrow[:, 3 * HEADS :] = flip(out[l])
        broad[:, :WIDE] = up[l]
        broad[:, WIDE:] = flip(down[l])


def pack_call(qkv, out, up, down):
    layers = qkv.shape[0]
    flat = pl.pallas_call(
        pack_kernel,
        out_shape=[
            jax.ShapeDtypeStruct((LANES, NARROW), bf16),
            jax.ShapeDtypeStruct((LANES, BROAD), bf16),
        ]
        * layers,
        in_specs=[VM] * 4,
        out_specs=[VM] * (2 * layers),
        compiler_params=params(),
        cost_estimate=cost(0, 4 * 2**20),
        name="pack",
    )(qkv, out, up, down)
    return flat[::2], flat[1::2]


def greet(sem, place, z, others, count):
    n = GROUPS
    for k in range(1, n):
        pl.semaphore_signal(
            sem, inc=1, device_id={"head": lax.rem(z + k, n)}, device_id_type=MESH
        )
    for other in (place.by_x, place.by_y, place.mate):
        pl.semaphore_signal(sem, inc=1, device_id={"dp": other}, device_id_type=MESH)
    for to_dp, to_z in others:

        @pl.when((to_dp != place.dp) | (to_z != z))
        def _(to_dp=to_dp, to_z=to_z):
            pl.semaphore_signal(
                sem, inc=1, device_id={"dp": to_dp, "head": to_z}, device_id_type=MESH
            )

    pl.semaphore_wait(sem, n + 2 + count)


class Weights:
    def __init__(self, at, chunks, shards, gathered, hsem, ssem, rsem, lsem):
        self.at, self.chunks, self.pairs = at, chunks, list(zip(shards, gathered))
        self.hsem, self.ssem, self.rsem = hsem, ssem, rsem
        self.lsem = lsem

    def owns(self):
        at = self.at
        return [
            pltpu.make_async_copy(shard, out.at[at.dp, at.z], self.lsem.at[i])
            for i, (shard, out) in enumerate(self.pairs)
        ]

    def near(self, c):
        kind, columns = self.chunks[c][0], pl.ds(*self.chunks[c][1:])
        shard, out = self.pairs[kind]
        at = self.at
        return [
            pltpu.make_async_remote_copy(
                src_ref=shard.at[:, columns],
                dst_ref=out.at[at.dp, at.z, :, columns],
                send_sem=self.hsem.at[0, k - 1, c],
                recv_sem=self.hsem.at[1, k - 1, c],
                device_id={"head": lax.rem(at.z + k, GROUPS)},
                device_id_type=MESH,
            )
            for k in (2, 1, 3)
        ]

    def far(self, slot, row, target, c):
        kind, columns = self.chunks[c][0], pl.ds(*self.chunks[c][1:])
        out = self.pairs[kind][1]
        return pltpu.make_async_remote_copy(
            src_ref=out.at[row, :, :, columns],
            dst_ref=out.at[row, :, :, columns],
            send_sem=self.ssem.at[slot, c],
            recv_sem=self.rsem.at[slot, c],
            device_id={"dp": target},
            device_id_type=MESH,
        )

    def hops(self, stage, c):
        at = self.at
        if stage == 0:
            return self.near(c)
        if stage == 1:
            return [self.far(0, at.dp, at.first, c)]
        if stage == 2:
            return [self.far(1, at.dp, at.second, c), self.far(2, at.first, at.second, c)]
        rows = (at.dp, at.first, at.second, at.both)
        return [self.far(3 + i, row, at.mate, c) for i, row in enumerate(rows)]

    def begin(self):
        for c in range(min(2, len(self.chunks))):
            for copy in self.near(c):
                copy.start()

    def turn(self, t):
        parts = len(self.chunks)
        for stage in (1, 2, 3):
            c = t + 1 - stage
            if 0 <= c < parts:
                if stage == 1 and c == 0:
                    for copy in self.owns():
                        copy.wait()
                for copy in self.hops(stage - 1, c):
                    copy.wait()
                for copy in self.hops(stage, c):
                    copy.start()
        if t + 2 < parts:
            for copy in self.near(t + 2):
                copy.start()
        c = t - 3
        if 0 <= c < parts:
            for copy in self.hops(3, c):
                copy.wait()

    def run(self, aside):
        self.begin()
        for t in range(len(self.chunks) + 3):
            self.turn(t)
            aside(t)


def weight_chunks(shards, step=512):
    return [(i, c, step) for i, v in enumerate(shards) for c in range(0, v.shape[1], step)]


def weight_sems(shards, step=512):
    parts = len(weight_chunks(shards, step))
    return [DMA((2, 3, parts)), DMA((7, parts)), DMA((7, parts)), DMA((len(shards),))]


def start_kernel(
    chunks, shards, rows, vector, flags, gathered, low, side, vectors, flags_out, blocks,
    hsem, ssem, rsem, wsem, xsem, tsem, vsem, fsem, lsem, low_here, vectors_here, *scratch,
):
    queries = Queries(GROUPS, gathered[0], blocks, *scratch)
    at = Place()
    weights = Weights(at, chunks, shards, gathered, hsem, ssem, rsem, wsem)
    dp, core, bit_x, by_x = at.dp, at.core, at.bit_x, at.by_x
    z = at.z
    n = GROUPS
    lo = lax.rem(dp, n)
    wide = rows.shape[2]
    sem = pltpu.get_barrier_semaphore()

    def targets():
        return [(xs, c2, dp - core + c2, 2 * xs + core) for xs in range(2) for c2 in range(2)]

    def sources():
        return [(dp - core + lax.rem(z, 2), g) for g in range(n)]

    turn_dp, turn_z = dp - lo + z, lo
    for copy in weights.owns():
        copy.start()
    own_vector = pltpu.make_async_copy(vector, vectors.at[z], lsem.at[2])
    own_vector.start()
    turned = [(turn_dp, turn_z)]
    across = at.by_x + 1 - 2 * core
    greet(
        sem, at, z, sources() + turned + [(across, z)],
        n + unlike(lax.rem(z, 2), core) + unlike(z, lo),
    )
    small = [
        pltpu.make_async_remote_copy(
            src_ref=vector,
            dst_ref=vectors.at[z],
            send_sem=vsem.at[0, k - 1],
            recv_sem=vsem.at[1, k - 1],
            device_id={"head": lax.rem(z + k, n)},
            device_id_type=MESH,
        )
        for k in range(1, n)
    ]

    def flag_copy(op):
        def remote():
            copy = pltpu.make_async_remote_copy(
                src_ref=flags,
                dst_ref=flags_out,
                send_sem=fsem.at[0],
                recv_sem=fsem.at[1],
                device_id={"dp": turn_dp, "head": turn_z},
                device_id_type=MESH,
            )
            copy.start() if op == "start" else copy.wait()

        def inside():
            copy = pltpu.make_async_copy(flags, flags_out, lsem.at[3])
            copy.start() if op == "start" else copy.wait()

        pl.when((turn_dp != dp) | (turn_z != z))(remote)
        pl.when((turn_dp == dp) & (turn_z == z))(inside)

    flag_copy("start")
    for copy in small:
        copy.start()

    cross = pltpu.make_async_remote_copy(
        src_ref=rows.at[pl.ds(2 - 2 * bit_x, 2)],
        dst_ref=side,
        send_sem=xsem.at[0],
        recv_sem=xsem.at[1],
        device_id={"dp": by_x},
        device_id_type=MESH,
    )
    place = low.at[:, pl.ds(pl.multiple_of(z * wide, wide), wide)]

    def spread(op):
        for i, (xs, c2, to_dp, to_z) in enumerate(targets()):

            def here(source, i=i, to_dp=to_dp, to_z=to_z):
                def remote():
                    copy = pltpu.make_async_remote_copy(
                        src_ref=source,
                        dst_ref=place,
                        send_sem=tsem.at[0, i],
                        recv_sem=tsem.at[1, z],
                        device_id={"dp": to_dp, "head": to_z},
                        device_id_type=MESH,
                    )
                    if op == "start":
                        copy.start()
                    else:
                        copy.wait_send()

                pl.when((to_dp != dp) | (to_z != z))(remote)

                def inside():
                    copy = pltpu.make_async_copy(source, place, lsem.at[1])
                    if op == "start":
                        copy.start()
                    else:
                        copy.wait()

                pl.when((to_dp == dp) & (to_z == z))(inside)

            pl.when(bit_x == xs)(lambda xs=xs, c2=c2, here=here: here(rows.at[2 * xs + c2]))
            pl.when(bit_x != xs)(lambda c2=c2, here=here: here(side.at[c2]))

    cross.start()

    def arrivals():
        spread("wait")
        for from_dp, g in sources():

            @pl.when((from_dp != dp) | (g != z))
            def _(g=g):
                spot = low.at[:, pl.ds(g * wide, wide)]
                pltpu.make_async_remote_copy(
                    src_ref=spot,
                    dst_ref=spot,
                    send_sem=tsem.at[0, 0],
                    recv_sem=tsem.at[1, g],
                    device_id={"dp": by_x},
                    device_id_type=MESH,
                ).wait_recv()

    ready = sum(kind == 0 for kind, *_ in chunks) + 2
    loads = [
        pltpu.make_async_copy(low, low_here, lsem.at[0]),
        pltpu.make_async_copy(vectors, vectors_here, lsem.at[2]),
    ]

    def aside(t):
        if t == 1:
            cross.wait()
            spread("start")
        if t == ready:
            queries.begin()
            own_vector.wait()
            for copy in small:
                copy.wait()
            arrivals()
            for copy in loads:
                copy.start()
            for copy in loads:
                copy.wait()
            norms = Vectors(n, 0, vectors_here)
            queries.norm(low_here, norms.norm(0, 0), norms.norm(1, 0))
        if ready < t <= ready + n:
            queries.step(t - ready - 1)

    weights.run(aside)
    flag_copy("wait")
    queries.finish()


def start_call(shards, rows, vector, flags):
    count = len(shards)
    chunks = weight_chunks(shards)
    tokens, wide = rows.shape[1:]

    out_shape, out_specs = queries_outs(GROUPS, tokens)

    def kernel(*refs):
        taken, refs = refs[:count], refs[count:]
        given, refs = refs[:3], refs[3:]
        gathered, refs = refs[:count], refs[count:]
        others, refs = refs[:4], refs[4:]
        blocks, refs = refs[: len(out_shape)], refs[len(out_shape) :]
        start_kernel(chunks, taken, *given, gathered, *others, blocks, *refs)

    res = pl.pallas_call(
        kernel,
        out_shape=[jax.ShapeDtypeStruct((BLOCKS, GROUPS) + v.shape, bf16) for v in shards]
        + [
            jax.ShapeDtypeStruct((tokens, GROUPS * wide), bf16),
            jax.ShapeDtypeStruct((2, tokens, wide), bf16),
            jax.ShapeDtypeStruct((GROUPS,) + vector.shape, f32),
            jax.ShapeDtypeStruct(flags.shape, jnp.int32),
        ]
        + out_shape,
        in_specs=[HB] * (count + 3),
        out_specs=[HB] * (count + 4) + out_specs,
        scratch_shapes=[
            *weight_sems(shards),
            DMA((2,)),
            DMA((2, GROUPS)),
            DMA((2, 3)),
            DMA((2,)),
            DMA((4,)),
            pltpu.VMEM((tokens, GROUPS * wide), bf16),
            pltpu.VMEM((GROUPS,) + vector.shape, f32),
            *queries_scratch(GROUPS, tokens),
        ],
        compiler_params=params(collective_id=5, has_side_effects=True),
        cost_estimate=cost(0, 300 * 2**20),
        name="start",
    )(*shards, rows, vector, flags)
    blocks = res[count + 4 :]
    parts = [blocks[u * GROUPS : (u + 1) * GROUPS] for u in range(len(blocks) // GROUPS)]
    return [res[:count], *res[count : count + 4], parts]


def vector_rows(layers):
    return -(-(28 * layers + 3 * layers + 1) // 8) * 8


def end_kernel(
    layers, rows, grads, fsum, turned, valid, tops, vecs, uses,
    stream_out, rows_out, qkv_out, out_out, up_out, down_out,
    gains_out, shifts_out, hgains_out, hshifts_out, rms_out,
    mine, got, pair, last, near, pieces, crossed, fm, fnear, vec, vgot, vsum,
    gsem, hsem, psem, qsem, nsem, tsem, xsem, vsem, lsem, esem,
):
    at = Place()
    dp, core, bit_x = at.dp, at.core, at.bit_x
    z = at.z
    n = GROUPS
    parts = 4
    width = grads.shape[3] // parts
    step = fsum.shape[2] // parts
    wide = rows.shape[1] // n
    sem = pltpu.get_barrier_semaphore()

    def columns(c):
        return pl.ds(c * width, width)

    def broad(c):
        return pl.ds(c * step, step)

    def loads(c):
        return [
            pltpu.make_async_copy(
                grads.at[pl.ds(0, 4), :, :, columns(c)], mine.at[:, :, :, columns(c)], gsem.at[0, c]
            ),
            pltpu.make_async_copy(
                fsum.at[:, :, broad(c)], fm.at[:, :, broad(c)], gsem.at[1, c]
            ),
        ]

    for c in range(parts):
        for copy in loads(c):
            copy.start()

    vec[...] = jnp.zeros_like(vec)
    for l in range(layers):
        base = 28 * l
        norms, hidden = vecs[4 * l : 4 * l + 3], vecs[4 * l + 3]
        for kind in range(2):
            for i in range(3):
                total = jnp.sum(norms[i][kind], axis=0, keepdims=True)
                for b in range(BLOCKS):
                    row = base + (3 * kind + i) * 2 + b % 2
                    vec[b // 2, row : row + 1, :] = total[:, b * LANES : (b + 1) * LANES]
            for g in range(n):
                total = jnp.sum(hidden[kind, g], axis=0, keepdims=True)
                for b in range(BLOCKS):
                    row = base + 12 + 8 * kind + b
                    vec[g, row : row + 1, :] = total[:, b * LANES : (b + 1) * LANES]
        branch, rest = uses[2 * l : 2 * l + 2]
        for i, value in enumerate((branch[...], rest[0], rest[1])):
            row = 28 * layers + 3 * l + i
            total = fold_lanes(jnp.sum(value, axis=0, keepdims=True))
            for g in range(n):
                vec[g, row : row + 1, :] = total
    row = 31 * layers
    count = jnp.sum(valid[...], axis=0, keepdims=True) * (D / LANES)
    for g in range(n):
        vec[g, row : row + 1, :] = jnp.broadcast_to(count, (1, LANES))

    to_dp = dp - core + lax.rem(z, 2)
    sources = [(dp - core + c2, 2 * xs + core) for xs in range(2) for c2 in range(2)]
    greet(sem, at, z, sources, n - 1 + unlike(lax.rem(z, 2), core))

    def hop(stage, c):
        if stage == 0:
            return pltpu.make_async_remote_copy(
                src_ref=grads.at[pl.ds(4, 4), :, :, columns(c)],
                dst_ref=got.at[:, :, :, columns(c)],
                send_sem=hsem.at[0, c],
                recv_sem=hsem.at[1, c],
                device_id={"dp": at.mate},
                device_id_type=MESH,
            )
        if stage == 1:
            return pltpu.make_async_remote_copy(
                src_ref=mine.at[pl.ds(2, 2), :, :, columns(c)],
                dst_ref=pair.at[:, :, :, columns(c)],
                send_sem=psem.at[0, c],
                recv_sem=psem.at[1, c],
                device_id={"dp": at.second},
                device_id_type=MESH,
            )
        return pltpu.make_async_remote_copy(
            src_ref=mine.at[1, :, :, columns(c)],
            dst_ref=last.at[:, :, columns(c)],
            send_sem=qsem.at[0, c],
            recv_sem=qsem.at[1, c],
            device_id={"dp": at.first},
            device_id_type=MESH,
        )

    def way(source, target, sems, i, c):
        return pltpu.make_async_remote_copy(
            src_ref=source,
            dst_ref=target,
            send_sem=sems.at[0, i, c],
            recv_sem=sems.at[1, i, c],
            device_id={"head": at.group(2 - i)},
            device_id_type=MESH,
        )

    def head_way(i, c):
        if i == 0:
            source, target = mine.at[0, pl.ds(2, 2), :, columns(c)], near.at[pl.ds(0, 2), :, columns(c)]
        else:
            source, target = mine.at[0, 1, :, columns(c)], near.at[2, :, columns(c)]
        return way(source, target, nsem, i, c)

    def ffn_way(i, c):
        if i == 0:
            source, target = fm.at[pl.ds(2, 2), :, broad(c)], fnear.at[pl.ds(0, 2), :, broad(c)]
        else:
            source, target = fm.at[1, :, broad(c)], fnear.at[2, :, broad(c)]
        return way(source, target, esem, i, c)

    def head_between(c):
        head_way(0, c).wait()
        for k in range(2):
            value = mine[0, k, :, columns(c)].astype(f32) + near[k, :, columns(c)].astype(f32)
            mine[0, k, :, columns(c)] = value.astype(bf16)
        head_way(1, c).start()

    def ffn_between(c):
        ffn_way(0, c).wait()
        for k in range(2):
            value = fm[k, :, broad(c)].astype(f32) + fnear[k, :, broad(c)].astype(f32)
            fm[k, :, broad(c)] = value.astype(bf16)
        ffn_way(1, c).start()

    def add(count, other, c):
        def body(i, carry):
            m, g = i // GROUPS, lax.rem(i, GROUPS)
            value = mine[m, g, :, columns(c)].astype(f32) + other(m, g).astype(f32)
            mine[m, g, :, columns(c)] = value.astype(bf16)
            return carry

        lax.fori_loop(0, count * GROUPS, body, 0)

    def row_copies(op):
        for j in range(n):
            source = rows.at[:, pl.ds(j * wide, wide)]
            target = pieces.at[z // 2, core]

            def remote(j=j, source=source, target=target):
                copy = pltpu.make_async_remote_copy(
                    src_ref=source,
                    dst_ref=target,
                    send_sem=tsem.at[0, j],
                    recv_sem=tsem.at[1, 2 * (z // 2) + core],
                    device_id={"dp": to_dp, "head": j},
                    device_id_type=MESH,
                )
                copy.start() if op == "start" else copy.wait_send()

            def inside(source=source, target=target):
                copy = pltpu.make_async_copy(source, target, lsem.at[0])
                copy.start() if op == "start" else copy.wait()

            pl.when((to_dp != dp) | (j != z))(remote)
            pl.when((to_dp == dp) & (j == z))(inside)

    def row_arrivals():
        for xs in range(2):
            for c2 in range(2):

                @pl.when((dp - core + c2 != dp) | (2 * xs + core != z))
                def _(xs=xs, c2=c2):
                    spot = pieces.at[xs, c2]
                    pltpu.make_async_remote_copy(
                        src_ref=spot,
                        dst_ref=spot,
                        send_sem=tsem.at[0, 0],
                        recv_sem=tsem.at[1, 2 * xs + c2],
                        device_id={"dp": at.by_x},
                        device_id_type=MESH,
                    ).wait_recv()

    cross = pltpu.make_async_remote_copy(
        src_ref=pieces.at[1 - bit_x],
        dst_ref=crossed,
        send_sem=xsem.at[0],
        recv_sem=xsem.at[1],
        device_id={"dp": at.by_x},
        device_id_type=MESH,
    )
    def vector_near(k):
        return pltpu.make_async_remote_copy(
            src_ref=vec.at[lax.rem(z + k, n)],
            dst_ref=vgot.at[k - 1],
            send_sem=vsem.at[0, k - 1],
            recv_sem=vsem.at[1, k - 1],
            device_id={"head": lax.rem(z + k, n)},
            device_id_type=MESH,
        )

    def vector_far(i, target):
        return pltpu.make_async_remote_copy(
            src_ref=vsum.at[i],
            dst_ref=vgot.at[3 + i],
            send_sem=vsem.at[0, 3 + i],
            recv_sem=vsem.at[1, 3 + i],
            device_id={"dp": target},
            device_id_type=MESH,
        )

    def put_head(l, c, value):
        if c < 3:
            qkv_out[l, c] = value
        else:
            out_out[l] = jnp.transpose(value, (1, 0))

    def total_of(own, others):
        value = own.astype(f32)
        for other in others:
            value = value + other.astype(f32)
        return value

    row_copies("start")
    for c in range(parts):
        hop(0, c).start()
    for k in range(1, n):
        vector_near(k).start()
    partners = (at.mate, at.first, at.second)
    for t in range(parts + 4):
        c = t
        if c < parts:
            for copy in loads(c):
                copy.wait()
            hop(0, c).wait()
            add(4, lambda m, g, c=c: got[m, g, :, columns(c)], c)
            hop(1, c).start()
            ffn_way(0, c).start()
        c = t - 1
        if 0 <= c < parts:
            hop(1, c).wait()
            add(2, lambda m, g, c=c: pair[m, g, :, columns(c)], c)
            hop(2, c).start()
        c = t - 2
        if 0 <= c < parts:
            hop(2, c).wait()
            add(1, lambda m, g, c=c: last[g, :, columns(c)], c)
            head_way(0, c).start()
        if t == 1:
            for k in range(1, n):
                vector_near(k).wait()
            vsum[0] = vec[z] + vgot[0] + vgot[1] + vgot[2]
            vector_far(0, partners[0]).start()
        if 2 <= t < 5:
            i = t - 2
            vector_far(i, partners[i]).wait()
            vsum[i + 1] = vsum[i] + vgot[3 + i]
            if i < 2:
                vector_far(i + 1, partners[i + 1]).start()
        if t == 2:
            row_copies("wait")
            row_arrivals()
            cross.start()
        if t == 3:
            stream_out[...] = turned[...].astype(f32)
        if t == 4:
            for l in range(1, layers):
                heads, heads_other, ups, ups_other, downs, downs_other = tops[6 * l - 6 : 6 * l]
                for c in range(parts):
                    cols = slice(c * width, (c + 1) * width)
                    put_head(l, c, total_of(heads[0, :, cols], [heads_other[:, cols]]))
                up_out[l] = total_of(ups[0], [ups_other[...]])
                down_out[l] = jnp.transpose(total_of(downs[0], [downs_other[...]]), (1, 0))
        c = t - 1
        if 0 <= c < parts:
            ffn_between(c)
        c = t - 3
        if 0 <= c < parts:
            head_between(c)
        c = t - 4
        if 0 <= c < parts:
            ffn_way(1, c).wait()
            value = total_of(fm[0, :, broad(c)], [fnear[2, :, broad(c)]])
            if c < parts // 2:
                up_out[0, :, broad(c)] = value
            else:
                down_out[0, pl.ds(c * step - WIDE, step), :] = jnp.transpose(value, (1, 0))
    for c in range(parts):
        head_way(1, c).wait()
        put_head(0, c, total_of(mine[0, 0, :, columns(c)], [near[2, :, columns(c)]]))
    for l in range(layers):
        base = 28 * l
        for kind, (norm_out, hid_out) in enumerate(
            ((gains_out, hgains_out), (shifts_out, hshifts_out))
        ):
            for i in range(3):
                at_row = base + (3 * kind + i) * 2
                parts_of = [vsum[3, at_row + p : at_row + p + 1, :] for p in range(2)]
                norm_out[l, i : i + 1, :] = jnp.concatenate(parts_of, axis=1)
            at_row = base + 12 + 8 * kind
            parts_of = [vsum[3, at_row + p : at_row + p + 1, :] for p in range(BLOCKS)]
            hid_out[l : l + 1, :] = jnp.concatenate(parts_of, axis=1)
    totals = sum_lanes(vsum[3, 28 * layers : 31 * layers + 1, :])
    rms = jnp.sqrt(totals[: 3 * layers] / totals[3 * layers :])
    rms_out[0 : 3 * layers, :] = jnp.broadcast_to(rms, (3 * layers, LANES))
    cross.wait()
    for c2 in range(2):
        rows_out[2 * bit_x + c2] = pieces[bit_x, c2].astype(f32)
        rows_out[2 - 2 * bit_x + c2] = crossed[c2].astype(f32)


def end_call(rows, grads, fsum, turned, valid, tops, vecs, uses):
    parts = 4
    layers = len(vecs) // 4
    tokens = rows.shape[0]
    wide = rows.shape[1] // GROUPS
    block = grads.shape[1:]
    broad = fsum.shape
    vector = (vector_rows(layers), LANES)
    inputs = [rows, grads, fsum, turned, valid, *tops, *vecs, *uses]

    def spec(i, v):
        if i % 2 == 0:
            return pl.BlockSpec((1,) + v.shape[1:], lambda g: (0, 0, 0))
        return whole(v.shape)

    def kernel(*refs):
        fixed, refs = refs[:5], refs[5:]
        lists = []
        for values in (tops, vecs, uses):
            lists.append(refs[: len(values)])
            refs = refs[len(values) :]
        end_kernel(layers, *fixed, *lists, *refs)

    dims = [
        turned.shape,
        turned.shape,
        (layers, 3, LANES, HEADS),
        (layers, HEADS, LANES),
        (layers, LANES, WIDE),
        (layers, WIDE, LANES),
        (layers, 3, HEADS),
        (layers, 3, HEADS),
        (layers, WIDE),
        (layers, WIDE),
        (8 * (-(-3 * layers // 8)), LANES),
    ]
    outs = [jax.ShapeDtypeStruct(d, f32) for d in dims]
    return pl.pallas_call(
        kernel,
        out_shape=outs,
        grid=(1,),
        in_specs=[HB] * 3
        + [whole(turned.shape), whole(valid.shape)]
        + [spec(i, v) for i, v in enumerate(tops)]
        + [whole(v.shape) for v in (*vecs, *uses)],
        out_specs=[whole(v.shape) for v in outs],
        scratch_shapes=[
            pltpu.VMEM((4,) + block, bf16),
            pltpu.VMEM((4,) + block, bf16),
            pltpu.VMEM((2,) + block, bf16),
            pltpu.VMEM(block, bf16),
            pltpu.VMEM((3,) + block[1:], bf16),
            pltpu.VMEM((2, 2, tokens, wide), bf16),
            pltpu.VMEM((2, tokens, wide), bf16),
            pltpu.VMEM(broad, bf16),
            pltpu.VMEM((3,) + broad[1:], bf16),
            pltpu.VMEM((GROUPS,) + vector, f32),
            pltpu.VMEM((6,) + vector, f32),
            pltpu.VMEM((4,) + vector, f32),
            DMA((2, parts)),
            DMA((2, parts)),
            DMA((2, parts)),
            DMA((2, parts)),
            DMA((2, 2, parts)),
            DMA((2, 4)),
            DMA((2,)),
            DMA((2, 6)),
            DMA((2,)),
            DMA((2, 2, parts)),
        ],
        compiler_params=params(collective_id=6, has_side_effects=True),
        cost_estimate=cost(0, 300 * 2**20),
        name="end",
    )(*inputs)


def after(value, *tokens):
    return lax.optimization_barrier((value, tokens))[0]


class Order:
    def __init__(self):
        self.token = None
        self.wanted = []

    def __call__(self, call, *args, first=0):
        args = list(args)
        if self.token is not None:
            args[first] = after(args[first], self.token, *self.wanted)
            self.wanted = []
        out = call(*args)
        self.token = out
        while isinstance(self.token, (list, tuple)):
            self.token = self.token[0]
        return out

    def hold(self, value):
        return after(value, self.token)

    def want(self, value):
        self.wanted.append(value)
        return value


class Net:
    def __init__(self, n_dp, n_head):
        self.n_dp, self.n = n_dp, n_head
        self.own = lax.axis_index("dp").astype(jnp.int32)
        self.z = lax.axis_index("head").astype(jnp.int32)
        self.lo = self.own % n_head
        self.fast = n_dp == BLOCKS and n_head == GROUPS
        core_zero = [2, 4]
        self.one_way = [(i, i ^ core_zero[i % 2]) for i in range(n_dp)]
        self.other_way = [(i, i ^ core_zero[1 - i % 2]) for i in range(n_dp)]
        self.by_x = [(i, i ^ 2) for i in range(n_dp)]
        self.by_y = [(i, i ^ 4) for i in range(n_dp)]
        self.core = [(i, i ^ 1) for i in range(n_dp)]
        if self.fast:
            step = jnp.where(self.own % 2 == 0, 2, 4).astype(jnp.int32)
            mine = [jnp.int32(0), step, 6 - step, jnp.int32(6)]
            theirs = [jnp.int32(0), 6 - step, step, jnp.int32(6)]
            rows = [self.own ^ v for v in mine] + [self.own ^ v ^ 1 for v in theirs]
            straight = [self.own ^ v for v in (0, 2, 4, 6, 1, 3, 5, 7)]
            self.table = jnp.stack(rows + [self.z, self.lo] + straight)
        else:
            self.table = jnp.stack([jnp.int32(i) for i in range(BLOCKS)] + [jnp.int32(0), self.lo])

    def shift(self, value, k):
        n = self.n
        if k % n == 0:
            return value
        pairs = [(i, (i // n) * n + (i + k) % n) for i in range(self.n_dp)]
        return lax.ppermute(value, "dp", pairs)

    def across(self, value, bits):
        return lax.ppermute(value, "head", [(i, i ^ bits) for i in range(self.n)])

    def spin(self, value, k):
        n = self.n
        return lax.ppermute(value, "head", [(i, (i + k) % n) for i in range(n)])

    def gather(self, shard):
        return lax.all_gather(shard, ("dp", "head")).reshape(BLOCKS, GROUPS, LANES, -1)

    def gather_any(self, qkv, out, up, down):
        qkv = lax.all_gather(qkv, "head", axis=2, tiled=True)
        qkv = lax.all_gather(qkv, "dp", axis=1, tiled=True).transpose(1, 0, 2).reshape(D, 3 * D)
        up = lax.all_gather(up, "head", axis=1, tiled=True)
        up = lax.all_gather(up, "dp", axis=0, tiled=True)
        out, down = [
            lax.all_gather(lax.all_gather(v, "head", axis=0, tiled=True), "dp", axis=1, tiled=True)
            for v in (out, down)
        ]

        def blocks(*parts):
            cut = [v.reshape(BLOCKS, LANES, GROUPS, -1) for v in parts]
            return jnp.concatenate(cut, axis=3).transpose(0, 2, 1, 3)

        heads = [qkv[:, c * D : (c + 1) * D] for c in range(3)]
        return blocks(*heads, out.T), blocks(up, down.T)

    def scatter(self, full, widths):
        columns = full.shape[3]
        full = jnp.stack([full[:, slot_group(g)] for g in range(GROUPS)], axis=1)
        if self.fast:
            full = full.reshape(BLOCKS * GROUPS, LANES, columns)
        else:
            full = full.transpose(0, 2, 1, 3).reshape(D, GROUPS, columns)
            parts, at = [], 0
            for w in widths:
                part = full[:, :, at : at + w].reshape(D, self.n, GROUPS * w // self.n)
                parts.append(part)
                at += w
            full = jnp.concatenate(parts, axis=2)
            full = full.reshape(self.n_dp, D // self.n_dp, self.n, -1).transpose(0, 2, 1, 3)
            full = full.reshape(self.n_dp * self.n, D // self.n_dp, -1)
        mine = lax.psum_scatter(full, ("dp", "head"), scatter_dimension=0, tiled=False)
        return mine.astype(f32)


    def add_pair(self, keep, pair):
        add = lambda i: (keep[i].astype(f32) + pair[i].astype(f32)).astype(bf16)
        return add(0), add(1)

    def add_last(self, mine, last):
        return (mine.astype(f32) + last.astype(f32)).astype(bf16)

    def turn(self, k):
        n = self.n
        pairs = []
        for hi in range(self.n_dp // n):
            for lo in range(n):
                for z in range(n):
                    pairs.append(((hi * n + lo) * n + z, (hi * n + (z + k) % n) * n + lo))
        return pairs

    def rows_in(self, array):
        n = self.n
        tokens = array.shape[0] // n
        low = array.astype(bf16).reshape(n, tokens, array.shape[1])
        got = []
        for k in range(n):
            piece = lax.dynamic_index_in_dim(low, (self.z + k) % n, 0, False)
            got.append(lax.ppermute(piece, ("dp", "head"), self.turn(k)))
        return got

    def rows_in_end(self, got):
        stacked = jnp.take(jnp.stack(got), (self.lo - jnp.arange(self.n)) % self.n, axis=0)
        return stacked.transpose(1, 0, 2).reshape(got[0].shape[0], D)

    def rows_out(self, array):
        n = self.n
        width = D // n
        low = array.astype(bf16)
        got = []
        for k in range(n):
            piece = lax.dynamic_slice_in_dim(low, ((self.lo - k) % n) * width, width, 1)
            got.append(lax.ppermute(piece, ("dp", "head"), [(b, a) for a, b in self.turn(k)]))
        return got

    def rows_out_end(self, got):
        stacked = jnp.take(jnp.stack(got), (jnp.arange(self.n) - self.z) % self.n, axis=0)
        return stacked.reshape(-1, got[0].shape[1]).astype(f32)


def local(
    n_dp,
    n_head,
    stream_in,
    qkv_weight,
    out_weight,
    up_weight,
    down_weight,
    norm_gains,
    norm_shifts,
    hidden_gains,
    hidden_shifts,
    buckets,
    valid_mask,
    cotangent,
):
    net = Net(n_dp, n_head)
    n = n_head
    layers = qkv_weight.shape[0]
    tokens = LONG // n
    order = Order()

    flags = jnp.concatenate([valid_mask, buckets])
    flags = jnp.pad(flags, (0, -flags.shape[0] % 1024))
    vectors = [
        v.reshape(layers, -1) for v in (norm_gains, norm_shifts, hidden_gains, hidden_shifts)
    ]
    packed = jnp.concatenate(vectors, axis=1)
    narrow, broad = [None] * layers, [None] * layers
    if net.fast:
        small, large = pack_call(qkv_weight, out_weight, up_weight, down_weight)
        rows = stream_in.astype(bf16).reshape(n, tokens, D // n)
        flags = flags.reshape(-1, LANES)
        vector = packed.reshape(-1, LANES)
        started = order(start_call, [small[0], large[0]], rows, vector, flags, first=1)
        (narrow[0], broad[0]), stream, _, packed, flags, first_parts = started
        narrow[1:] = [net.gather(order.hold(v)) for v in small[1:]]
    else:
        for l in range(layers):
            narrow[l], broad[l] = net.gather_any(
                qkv_weight[l], out_weight[l], up_weight[l], down_weight[l]
            )
        stream = net.rows_in_end(net.rows_in(stream_in))
        flags = lax.ppermute(flags, ("dp", "head"), net.turn(0))
        packed = lax.all_gather(packed.reshape(-1, LANES), "head")
    aux, one, valid, need = masks_call(n, net.lo[None], flags.reshape(-1, LANES))

    low = stream
    cot = cotangent.astype(bf16).reshape(n, tokens, D // n)
    kept = []
    usage = []
    idents = iter(range(10, 64))
    for l in range(layers):
        ahead = net.fast and l + 1 < layers
        if net.fast and l == 0:
            parts = first_parts
        else:
            parts, _ = order(qkv_call, n, next(idents), [], l, low, packed, narrow[l], first=4)
        if ahead:
            broad[l + 1] = net.gather(order.hold(large[l + 1]))
        parts = [parts[0]] + [[net.shift(v, k) for k, v in enumerate(p)] for p in parts[1:]]
        att, lse = [], []
        for p in parts:
            outs = order(attn_call, n, need, aux, one, p, first=2)
            att.append(outs[0])
            lse.append(outs[1])
        last = net.fast and l + 1 == layers
        jobs = [Turn(cot, False, 0)] if last else []
        mid, rows, use_branch, *extra = order(
            proj_call, n, next(idents), jobs, l, valid, stream, packed, narrow[l], att, first=5
        )
        jobs = [Turn(cot, False, 1, extra[0])] if last else []
        slope, hat, normed, low_mid, rstd, stream, next_low, use_rest, *extra = order(
            ffn_call, n, next(idents), jobs, l, valid, mid, packed, broad[l], first=5
        )
        if last:
            grad = extra[0]
        usage += [use_branch, use_rest]
        kept.append((low, parts, att, lse, rows, slope, hat, normed, low_mid, rstd))
        low = next_low

    if not net.fast:
        grad = net.rows_in_end(net.rows_in(cotangent)).astype(f32)
    if not net.fast:
        grad = net.rows_in_end(net.rows_in(cotangent)).astype(f32)
    low_out = low
    units = BLOCKS // n
    ffn_grads, head_grads = [None] * layers, [None] * layers
    vectors, tops = [None] * layers, []

    for l in reversed(range(layers)):
        low, parts, att, lse, rows, slope, hat, normed, low_mid, rstd = kept[l]
        more = net.fast and l + 1 < layers
        last = net.fast and l + 1 == layers
        jobs = []
        if last:
            jobs = [Turn(low_out, True, 0)]
        if more:
            jobs = [Hop(head_odd, "mate")]
        dhid, grad_turned, ffn_turned, grad, hgrads, grads2, *extra = order(
            ffn_back_call, n, next(idents), jobs, l, grad, hat, slope, rstd,
            low_mid, packed, broad[l], first=4,
        )
        ffn_args = (ffn_turned, grad_turned, dhid, normed)
        if net.fast:
            moved = extra
            if more:
                head_keep, send = order(
                    head_grad_call, n, 0, 4, net.table, *head_args, extra[0], first=4
                )
                head_pair = lax.ppermute(order.hold(send), "dp", net.other_way)
            ups = BLOCKS + 2 if l else 0
            (odd,) = order(ffn_grad_call, ups, 4, 4, net.table, *ffn_args, first=4)
            jobs = [Hop(odd, "mate")]
            if more:
                wide_sums = [
                    net.add_last(order.hold(ups_mine), ups_last),
                    net.add_last(order.hold(downs_mine), downs_last),
                ]
                wide_near = [net.across(order.want(v)[2:], 1) for v in wide_sums]
            if last:
                jobs.append(Turn(low_out, True, 1, moved[0]))
        else:
            (full,) = order(ffn_grad_call, 0, 0, BLOCKS, net.table, *ffn_args, first=4)
            ffn_grads[l] = net.scatter(full, (WIDE, WIDE))
        res = order(
            proj_back_call, n, next(idents), jobs, l, grad, packed, narrow[l], rows, first=4
        )
        datt, (out_turned, normed_mid, grads1, *extra) = res[:units], res[units:]
        if net.fast:
            if last:
                turned = extra[1]
            if more:
                head_mine, sent = net.add_pair(order.hold(head_keep), head_pair)
                head_last = lax.ppermute(sent, "dp", net.one_way)
                order.want(sent)
            sums = order(ffn_grad_call, ups, 0, 4, net.table, *ffn_args, extra[0], first=4)
            if l:
                up_pair = lax.ppermute(order.hold(sums[1]), "dp", net.by_y)
                down_pair = lax.ppermute(order.hold(sums[3]), "dp", net.other_way)
            if more:
                wide_own = [
                    order.want(net.add_last(order.hold(v[:2]), other))
                    for v, other in zip(wide_sums, wide_near)
                ]
            if l == 0:
                ffn_pair = lax.ppermute(order.hold(sums[1]), "dp", net.other_way)
        dparts, ready = [], []
        for u in range(units):
            ready += [net.shift(v, -k) for k, v in enumerate(dparts)]
            dparts = order(
                attn_back_call, n, need, aux, one, parts[u], att[u], datt[u], lse[u], first=2
            )
            if more and u == 0:
                head_sum = order.want(net.add_last(order.hold(head_mine), head_last))
                wide_other = [net.across(order.hold(v[1]), 2) for v in wide_own]
            if net.fast and l and u == 0:
                order.want(down_pair)
        jobs = []
        if net.fast and l == 0:
            ffn_mine, sent = net.add_pair(order.hold(sums[0]), ffn_pair)
            ffn_last = lax.ppermute(order.want(sent), "dp", net.one_way)
        if more:
            head_near = net.across(order.hold(head_sum)[2:], 1)
        dlast, grad, in_turned, grads0, grad_low, *extra = order(
            qkv_back_call, n, next(idents), jobs, l, grad, low, packed, narrow[l], ready, dparts,
            first=4,
        )
        head_args = (in_turned, out_turned, ready + dlast, normed_mid)
        vectors[l] = [grads0, grads1, grads2, hgrads]
        if net.fast:
            if more:
                head_own = order.want(net.add_last(order.hold(head_sum[:2]), head_near))
                pairs = [v for pair in zip(wide_own, wide_other) for v in pair]
                tops = [head_own, net.across(head_own[1], 2), *pairs] + tops
            if l:
                (head_odd,) = order(head_grad_call, n, 4, 4, net.table, *head_args, first=4)
                ups_mine, ups_sent = net.add_pair(order.hold(sums[0]), up_pair)
                downs_mine, downs_sent = net.add_pair(order.hold(sums[2]), down_pair)
                order.want(ups_sent)
                order.want(downs_sent)
                ups_last = lax.ppermute(ups_sent, "dp", net.by_x)
                downs_last = lax.ppermute(downs_sent, "dp", net.one_way)
            else:
                (full,) = order(head_grad_call, n, 0, BLOCKS, net.table, *head_args, first=4)
        else:
            (full,) = order(head_grad_call, n, 0, BLOCKS, net.table, *head_args, first=4)
            head_grads[l] = net.scatter(full, (HEADS,) * 4)
    vectors = [v for part in vectors for v in part]
    if net.fast:
        ffn_sum = net.add_last(order.hold(ffn_mine), ffn_last)
        (
            stream_out, stream_grad, qkv_grad, out_grad, up_grad, down_grad,
            gains_grad, shifts_grad, hidden_gains_grad, hidden_shifts_grad, usage_rms,
        ) = order(
            end_call, grad_low, full, ffn_sum, turned, valid, tops, vectors, usage
        )
        stream_out = stream_out.reshape(LONG, D // n)
        stream_grad = stream_grad.reshape(LONG, D // n)
        stacked = [qkv_grad, out_grad, up_grad, down_grad]
        usage_rms = usage_rms[: 3 * layers, 0].reshape(layers, 3)
    else:
        stream_out = net.rows_out_end(net.rows_out(stream))
        stream_grad = net.rows_out_end(net.rows_out(grad))
        norms = [jnp.sum(jnp.stack(vectors[4 * l : 4 * l + 3], 1), axis=2) for l in range(layers)]
        norms = lax.psum(jnp.stack(norms), ("dp", "head"))
        hids = [jnp.sum(vectors[4 * l + 3], axis=2).reshape(2, FF) for l in range(layers)]
        hids = lax.psum(jnp.stack(hids), ("dp", "head"))
        share = lambda v: lax.dynamic_slice_in_dim(
            v, net.z * (v.shape[-1] // n), v.shape[-1] // n, v.ndim - 1
        )
        norms, hids = share(norms), share(hids)
        totals = []
        for l in range(layers):
            branch, rest = usage[2 * l : 2 * l + 2]
            totals += [jnp.sum(branch), jnp.sum(rest[0]), jnp.sum(rest[1])]
        totals = lax.psum(jnp.stack(totals + [jnp.sum(valid) * D]), ("dp", "head"))
        usage_rms = jnp.sqrt(totals[:-1] / totals[-1]).reshape(layers, 3)
        weight_grads = []
        for l in range(layers):
            heads = head_grads[l]
            width = heads.shape[1] // 4
            qkv = heads[:, : 3 * width].reshape(-1, 3, width).transpose(1, 0, 2)
            half = ffn_grads[l].shape[1] // 2
            weight_grads.append(
                (qkv, heads[:, 3 * width :].T, ffn_grads[l][:, :half], ffn_grads[l][:, half:].T)
            )
        stacked = [jnp.stack([weight_grads[l][k] for l in range(layers)]) for k in range(4)]
        gains_grad, shifts_grad = norms[:, 0], norms[:, 1]
        hidden_gains_grad, hidden_shifts_grad = hids[:, 0], hids[:, 1]
    return (
        stream_out,
        stream_grad,
        stacked[0],
        stacked[1],
        stacked[2],
        stacked[3],
        gains_grad,
        shifts_grad,
        hidden_gains_grad,
        hidden_shifts_grad,
        usage_rms,
    )


def solution(mesh):
    n_dp, n_head = mesh.shape["dp"], mesh.shape["head"]

    def run(*args):
        return local(n_dp, n_head, *args)

    return jax.shard_map(
        run,
        mesh=mesh,
        in_specs=(
            P("dp", "head"),
            P(None, None, "dp", "head"),
            P(None, "head", "dp"),
            P(None, "dp", "head"),
            P(None, "head", "dp"),
            P(None, None, "head"),
            P(None, None, "head"),
            P(None, "head"),
            P(None, "head"),
            P("dp"),
            P("dp"),
            P("dp", "head"),
        ),
        out_specs=(
            P("dp", "head"),
            P("dp", "head"),
            P(None, None, "dp", "head"),
            P(None, "head", "dp"),
            P(None, "dp", "head"),
            P(None, "head", "dp"),
            P(None, None, "head"),
            P(None, None, "head"),
            P(None, "head"),
            P(None, "head"),
            P(),
        ),
        check_vma=False,
    )
```

```python
import functools
import math

import jax
import jax.numpy as jnp
from jax import lax
from jax.experimental import pallas as pl
from jax.experimental.pallas import tpu as pltpu
from jax.sharding import PartitionSpec as P

D = 1024
FF = 4096
LONG = 2048
SHORT = 512
DH = 64
LANES = 128
BLOCKS = D // LANES
GROUPS = 4
WIDE = FF // GROUPS
HEADS = D // GROUPS
NARROW = 4 * HEADS
BROAD = 2 * WIDE
EPS = 1e-05
MASKED = -1000000000.0
ROWS = 512
CHUNK = 256
VMEM_BYTES = 60 * 1024 * 1024
MESH = pl.DeviceIdType.MESH

f32 = jnp.float32
bf16 = jnp.bfloat16


def dot(a, b):
    return jnp.dot(a, b, preferred_element_type=f32)


def dot_nt(a, b):
    return lax.dot_general(a, b, (((1,), (1,)), ((), ())), preferred_element_type=f32)


def flip(a):
    return jnp.transpose(a.astype(f32), (1, 0)).astype(a.dtype)


def row_loop(total, step, body):
    step = min(step, total)

    def advance(i, carry):
        body(pl.ds(pl.multiple_of(i * step, step), step))
        return carry

    lax.fori_loop(0, total // step, advance, 0)


def sum_lanes(value):
    return jnp.sum(value, axis=1, keepdims=True)


def fold_lanes(value):
    total = value[:, :LANES]
    for i in range(1, value.shape[1] // LANES):
        total = total + value[:, i * LANES : (i + 1) * LANES]
    return total


def fold_rows(value):
    total = value[:8]
    for i in range(1, value.shape[0] // 8):
        total = total + value[i * 8 : (i + 1) * 8]
    return total


def row_stats(value):
    mean = sum_lanes(value) / D
    centred = value - mean
    rstd = lax.rsqrt(sum_lanes(centred * centred) / D + EPS)
    return centred * rstd, rstd


def norm_back(dy, hat, rstd, gain):
    dx = dy * gain
    first = sum_lanes(dx) / D
    cross = sum_lanes(dx * hat) / D
    return rstd * (dx - first - hat * cross)


class Vectors:
    def __init__(self, n, layer, ref):
        self.n, self.ref = n, ref
        self.few, self.many = BLOCKS // n, 4 * BLOCKS // n
        self.at = layer * (6 * self.few + 2 * self.many)

    def rows(self, z, first, count):
        return [self.ref[z, first + p : first + p + 1, :] for p in range(count)]

    def norm(self, kind, which):
        first = self.at + (3 * kind + which) * self.few
        parts = [v for z in range(self.n) for v in self.rows(z, first, self.few)]
        return jnp.concatenate(parts, axis=1)

    def hidden(self, kind, group):
        first = self.at + 6 * self.few + kind * self.many
        share = self.n // GROUPS
        parts = [v for i in range(share) for v in self.rows(group * share + i, first, self.many)]
        return jnp.concatenate(parts, axis=1)


def params(**kw):
    return pltpu.CompilerParams(vmem_limit_bytes=VMEM_BYTES, **kw)


def cost(flops, size, trans=0):
    return pl.CostEstimate(flops=int(flops), bytes_accessed=int(size), transcendentals=int(trans))


def whole(shape):
    zeros = (0,) * len(shape)
    return pl.BlockSpec(shape, lambda *_: zeros)


def shape(dims, kind):
    return jax.ShapeDtypeStruct(dims, kind)


VM = pl.BlockSpec(memory_space=pltpu.VMEM)
HB = pl.BlockSpec(memory_space=pl.ANY)
DMA = pltpu.SemaphoreType.DMA


def group_place(n):
    dp = lax.axis_index("dp")
    lo = lax.rem(dp, n)
    return dp - lo, lo


def group_send(n, k, source, target, send_sem, recv_sem):
    base, lo = group_place(n)
    return pltpu.make_async_remote_copy(
        src_ref=source,
        dst_ref=target,
        send_sem=send_sem,
        recv_sem=recv_sem,
        device_id={"dp": base + lax.rem(lo + k + n, n)},
        device_id_type=MESH,
    )


def order_of(n):
    return [k for k in (n // 2, *range(1, n // 2), *range(n // 2 + 1, n)) if k]


def head_columns(n, k):
    _, lo = group_place(n)
    unit = lax.rem(lo + k + n, n) * (BLOCKS // n)
    if n == GROUPS:
        return lax.rem(lo + k + n, n), 0
    return unit // 2, pl.multiple_of(lax.rem(unit, 2) * LANES, LANES)


class Place:
    def __init__(self):
        dp = lax.axis_index("dp")
        self.z = lax.axis_index("head")
        self.lo = lax.rem(dp, GROUPS)
        core = lax.rem(dp, 2)
        bit_x = lax.rem(dp // 2, 2)
        bit_y = lax.rem(dp // 4, 2)
        by_x = dp + 2 - 4 * bit_x
        by_y = dp + 4 - 8 * bit_y
        self.dp, self.core, self.bit_x = dp, core, bit_x
        self.by_x, self.by_y = by_x, by_y
        self.first = by_x * (1 - core) + by_y * core
        self.second = by_y * (1 - core) + by_x * core
        self.both = by_x + by_y - dp
        self.mate = dp + 1 - 2 * core

    def partner(self, way):
        return {"mate": self.mate, "first": self.first, "second": self.second}[way]

    def group(self, p):
        one, two = 1 - 2 * lax.rem(self.z, 2), 2 - 4 * (self.z // 2)
        return self.z + (0, two, one, one + two)[p]

    def others(self):
        return [{"head": lax.rem(self.z + k, GROUPS)} for k in range(1, GROUPS)]


def unlike(a, b):
    return jnp.where(a == b, 0, 1)


class Hop:
    aliases = {}

    def __init__(self, array, way):
        self.arrays, self.way = [array], way
        self.outs = [jax.ShapeDtypeStruct(array.shape, array.dtype)]
        self.sems = [DMA((2,))]

    def device(self, at):
        return {"dp": at.partner(self.way)}

    def peers(self, at):
        return [self.device(at)], [], 1

    def copy(self, at, ins, outs, sems):
        return pltpu.make_async_remote_copy(
            src_ref=ins[0],
            dst_ref=outs[0],
            send_sem=sems[0].at[0],
            recv_sem=sems[0].at[1],
            device_id=self.device(at),
            device_id_type=MESH,
        )

    def start(self, *args):
        self.copy(*args).start()

    def finish(self, *args):
        self.copy(*args).wait()


class Turn:
    def __init__(self, array, back, half=None, into=None):
        self.arrays, self.back = [array], back
        self.aliases = {}
        if into is not None:
            self.arrays.append(into)
            self.aliases = {1: 0}
        if back:
            tokens, wide = array.shape[0], array.shape[1] // GROUPS
            out = (GROUPS, tokens, wide)
        else:
            tokens, wide = array.shape[1:]
            out = (tokens, GROUPS * wide)
        self.wide = wide
        self.rows = pl.ds(0, tokens) if half is None else pl.ds(half * (tokens // 2), tokens // 2)
        self.outs = [jax.ShapeDtypeStruct(out, array.dtype)]
        self.sems = [DMA((2, GROUPS)), DMA]

    def many(self, at):
        return [(at.dp - at.lo + t, at.lo) for t in range(GROUPS)]

    def one(self, at):
        return [(at.dp - at.lo + at.z, g) for g in range(GROUPS)]

    def peers(self, at):
        from_ = self.many(at) if self.back else self.one(at)
        return [], from_, GROUPS - 1 + unlike(at.z, at.lo)

    def each(self, op, at, ins, outs, sems):
        targets = self.one(at) if self.back else self.many(at)
        for i, (dp, z) in enumerate(targets):
            if self.back:
                source = ins[0].at[self.rows, pl.ds(i * self.wide, self.wide)]
                target, slot = outs[0].at[at.lo, self.rows], at.lo
            else:
                source = ins[0].at[i, self.rows]
                column = pl.multiple_of(at.z * self.wide, self.wide)
                target, slot = outs[0].at[self.rows, pl.ds(column, self.wide)], at.z

            def remote(i=i, dp=dp, z=z, source=source, target=target, slot=slot):
                copy = pltpu.make_async_remote_copy(
                    src_ref=source,
                    dst_ref=target,
                    send_sem=sems[0].at[0, i],
                    recv_sem=sems[0].at[1, slot],
                    device_id={"dp": dp, "head": z},
                    device_id_type=MESH,
                )
                copy.start() if op == "start" else copy.wait_send()

            def inside(source=source, target=target):
                copy = pltpu.make_async_copy(source, target, sems[1])
                copy.start() if op == "start" else copy.wait()

            away = (dp != at.dp) | (z != at.z)
            pl.when(away)(remote)
            pl.when(jnp.logical_not(away))(inside)

    def start(self, *args):
        self.each("start", *args)

    def finish(self, at, ins, outs, sems):
        self.each("wait", at, ins, outs, sems)
        sources = self.many(at) if self.back else self.one(at)
        for slot, (dp, z) in enumerate(sources):

            @pl.when((dp != at.dp) | (z != at.z))
            def _(slot=slot):
                if self.back:
                    spot = outs[0].at[slot, self.rows]
                else:
                    spot = outs[0].at[self.rows, pl.ds(slot * self.wide, self.wide)]
                pltpu.make_async_remote_copy(
                    src_ref=spot,
                    dst_ref=spot,
                    send_sem=sems[0].at[0, 0],
                    recv_sem=sems[0].at[1, slot],
                    device_id={"dp": at.mate},
                    device_id_type=MESH,
                ).wait_recv()


class Host:
    def __init__(self, n, parts):
        self.n, self.parts = n, parts
        self.at = Place() if parts else None

    def barrier(self, group=True):
        n = self.n
        sem = pltpu.get_barrier_semaphore()
        count = 0
        if group:
            base, lo = group_place(n)
            for k in range(1, n):
                pl.semaphore_signal(
                    sem, inc=1, device_id={"dp": base + lax.rem(lo + k, n)}, device_id_type=MESH
                )
            count = n - 1
        for job, *_ in self.parts:
            plain, pairs, more = job.peers(self.at)
            for device in plain:
                pl.semaphore_signal(sem, inc=1, device_id=device, device_id_type=MESH)
            for dp, z in pairs:

                @pl.when((dp != self.at.dp) | (z != self.at.z))
                def _(dp=dp, z=z):
                    pl.semaphore_signal(
                        sem, inc=1, device_id={"dp": dp, "head": z}, device_id_type=MESH
                    )

            count = count + more
        pl.semaphore_wait(sem, count)

    def start(self):
        for job, *refs in self.parts:
            job.start(self.at, *refs)

    def finish(self):
        for job, *refs in self.parts:
            job.finish(self.at, *refs)


def plain_call(
    body, n, name, ident, inputs, in_specs, out_shape, out_specs, scratch, flops, jobs, grid=()
):
    return list(
        pl.pallas_call(
            lambda *refs: body(Host(n, []), *refs),
            out_shape=out_shape,
            grid=grid,
            in_specs=in_specs,
            out_specs=out_specs,
            scratch_shapes=scratch,
            compiler_params=params(),
            cost_estimate=cost(flops, 10 * 2**20),
            name=name,
        )(*inputs)
    )


def remote_call(
    body, n, name, ident, inputs, in_specs, out_shape, out_specs, scratch, flops, jobs, grid=()
):
    job_in = [v for job in jobs for v in job.arrays]
    job_out = [v for job in jobs for v in job.outs]
    job_sems = [v for job in jobs for v in job.sems]
    aliases = {}
    i, o = len(inputs), len(out_shape)
    for job in jobs:
        aliases.update({i + a: o + b for a, b in job.aliases.items()})
        i, o = i + len(job.arrays), o + len(job.outs)

    def kernel(*refs):
        refs = list(refs)

        def take(count):
            taken = refs[:count]
            del refs[:count]
            return taken

        own_in, extra_in = take(len(inputs)), take(len(job_in))
        own_out, extra_out = take(len(out_shape)), take(len(job_out))
        own_scratch, extra_sems = take(len(scratch)), take(len(job_sems))
        parts = []
        for job in jobs:
            sizes = (len(job.arrays), len(job.outs), len(job.sems))
            lists = (extra_in, extra_out, extra_sems)
            part = [job]
            for values, size in zip(lists, sizes):
                part.append(values[:size])
                del values[:size]
            parts.append(part)
        body(Host(n, parts), *own_in, *own_out, *own_scratch)

    res = pl.pallas_call(
        kernel,
        out_shape=list(out_shape) + job_out,
        grid=grid,
        in_specs=list(in_specs) + [HB] * len(job_in),
        out_specs=list(out_specs) + [HB] * len(job_out),
        scratch_shapes=list(scratch) + job_sems,
        input_output_aliases=aliases,
        compiler_params=params(collective_id=ident, has_side_effects=True),
        cost_estimate=cost(flops, 10 * 2**20),
        name=name,
    )(*inputs, *job_in)
    return list(res)


class Queries:
    def __init__(self, n, weight, outs, xs, wide, send, wsem, ssem, rsem, lsem):
        self.n, self.weight, self.outs, self.xs, self.wide, self.send = n, weight, outs, xs, wide, send
        self.wsem, self.ssem, self.rsem, self.lsem = wsem, ssem, rsem, lsem
        self.units = BLOCKS // n
        self.steps = order_of(n) + [0]

    def fetch(self, i):
        group, offset = head_columns(self.n, self.steps[i])
        width = self.units * LANES
        return [
            pltpu.make_async_copy(
                self.weight.at[:, group, :, pl.ds(c * HEADS + offset, width)],
                self.wide.at[i % 2, c],
                self.wsem.at[i % 2, c],
            )
            for c in range(3)
        ]

    def begin(self):
        for copy in self.fetch(0):
            copy.start()

    def norm(self, low, gain, shift):
        def body(r):
            hat, _ = row_stats(low[r, :].astype(f32))
            self.xs[r, :] = (hat * gain + shift).astype(bf16)

        row_loop(low.shape[0], ROWS, body)

    def copy(self, k):
        if k:
            return group_send(
                self.n, k, self.send.at[k], self.outs[k], self.ssem.at[k], self.rsem.at[k]
            )
        return pltpu.make_async_copy(self.send.at[0], self.outs[0], self.lsem)

    def step(self, i):
        k = self.steps[i]
        if i + 1 < self.n:
            for copy in self.fetch(i + 1):
                copy.start()
        for c, copy in enumerate(self.fetch(i)):
            copy.wait()
            value = dot(self.xs[...], self.wide[i % 2, c].reshape(D, -1)).astype(bf16)
            self.send[k, c] = value[:, :LANES]
            for u in range(1, self.units):
                self.outs[u * self.n + k][c] = value[:, u * LANES : (u + 1) * LANES]
        self.copy(k).start()

    def finish(self):
        for k in self.steps:
            self.copy(k).wait()


def queries_scratch(n, tokens):
    return [
        pltpu.VMEM((tokens, D), bf16),
        pltpu.VMEM((2, 3, BLOCKS, LANES, BLOCKS // n * LANES), bf16),
        pltpu.VMEM((n, 3, tokens, LANES), bf16),
        DMA((2, 3)),
        DMA((n,)),
        DMA((n,)),
        DMA,
    ]


def queries_outs(n, tokens):
    count = BLOCKS // n * n
    return [jax.ShapeDtypeStruct((3, tokens, LANES), bf16)] * count, [HB] * n + [VM] * (count - n)


def qkv_kernel(layer, host, low, packed, weight, *refs):
    vectors = Vectors(host.n, layer, packed)
    queries = Queries(host.n, weight, refs[:-7], *refs[-7:])
    queries.begin()
    queries.norm(low, vectors.norm(0, 0), vectors.norm(1, 0))
    host.barrier()
    host.start()
    for i in range(host.n):
        queries.step(i)
    queries.finish()
    host.finish()


def qkv_call(n, ident, jobs, layer, low, packed, weight):
    tokens = low.shape[0]
    units = BLOCKS // n
    out_shape, out_specs = queries_outs(n, tokens)
    res = remote_call(
        functools.partial(qkv_kernel, layer), n, "qkv", ident,
        [low, packed, weight], [VM, VM, HB], out_shape, out_specs, queries_scratch(n, tokens),
        60 * tokens * D * D, jobs,
    )
    return [res[u * n : (u + 1) * n] for u in range(units)], res[n * units :]


def masks_kernel(n, sc, flags, aux, one, valid, need):
    tokens = aux.shape[1]
    rows = tokens // LANES
    first = lax.broadcasted_iota(jnp.int32, (LANES, LANES), 1) == 0
    one[...] = jnp.where(lax.broadcasted_iota(jnp.int32, one.shape, 1) == 0, 1.0, 0.0).astype(bf16)
    long = jnp.max(flags[LONG // LANES : LONG // LANES + 1, 0:1]) == 1
    alive, sequence = [], []
    for k in range(n):
        place = lax.rem(sc[0] + n - k, n)
        some = jnp.float32(0)
        for i in range(rows):
            row = flags[pl.ds(place * rows + i, 1), :].astype(f32)
            some = jnp.maximum(some, jnp.max(row))
            column = jnp.transpose(jnp.broadcast_to(row, (LANES, LANES)), (1, 0))
            spot = slice(i * LANES, (i + 1) * LANES)
            aux[k, spot, :] = jnp.where(first & (column == 0), MASKED, 0.0).astype(bf16)
            if k == 0:
                valid[spot, :] = column[:, 0:1]
        alive.append(some > 0)
        sequence.append(place * tokens // SHORT)
    for i in range(n):
        for j in range(n):
            joined = long | (sequence[i] == sequence[j])
            need[i * n + j] = jnp.where(joined & alive[j], 1, 0).astype(jnp.int32)


def masks_call(n, lo, flags):
    tokens = LONG // n
    return pl.pallas_call(
        lambda *refs: masks_kernel(n, *refs),
        out_shape=[
            jax.ShapeDtypeStruct((n, tokens, LANES), bf16),
            jax.ShapeDtypeStruct((tokens, LANES), bf16),
            jax.ShapeDtypeStruct((tokens, 1), f32),
            jax.ShapeDtypeStruct((n * n,), jnp.int32),
        ],
        grid_spec=pltpu.PrefetchScalarGridSpec(
            num_scalar_prefetch=1,
            grid=(),
            in_specs=[VM],
            out_specs=[VM, VM, VM, pl.BlockSpec(memory_space=pltpu.SMEM)],
        ),
        compiler_params=params(),
        cost_estimate=cost(0, 2**20),
        name="masks",
    )(lo, flags)


def head_lanes(value, head):
    lane = lax.broadcasted_iota(jnp.int32, value.shape, 1)
    keep = (lane < DH) if head == 0 else (lane >= DH)
    return jnp.where(keep, value, jnp.zeros_like(value))


def attn_kernel(n, need, aux, one, *refs):
    qkv, (outs, lse, kx, vt, qs, top, acc) = refs[:n], refs[n:]
    tokens = aux.shape[1]
    for r in range(n):
        kx[r] = jnp.concatenate([qkv[r][1], aux[r]], axis=1)
        turned = flip(qkv[r][2])
        ones = jnp.ones((16, tokens), bf16)
        vt[r, 0] = jnp.concatenate([turned[:DH], ones], axis=0)
        vt[r, 1] = jnp.concatenate([turned[DH:], ones], axis=0)
        qs[r] = (qkv[r][0].astype(f32) * (1.0 / math.sqrt(DH))).astype(bf16)

    halves = jnp.where(
        lax.broadcasted_iota(jnp.int32, (LANES, LANES), 0) // DH
        == lax.broadcasted_iota(jnp.int32, (LANES, LANES), 1),
        1.0,
        0.0,
    ).astype(bf16)
    reach = jnp.zeros((1, LANES), f32)
    longest = jnp.zeros((1, LANES), f32)
    for r in range(n):
        for which, value in ((0, qs[r]), (1, qkv[r][1])):
            size = jnp.max(dot(value * value, halves), axis=0, keepdims=True)
            if which:
                longest = jnp.maximum(longest, size)
            else:
                reach = jnp.maximum(reach, size)
    bounded = jnp.max(reach * longest) < 70.0 * 70.0

    def each_query(plain, i, carry):
        query = qs[i]
        extended = [jnp.concatenate([head_lanes(query, h), one[...]], axis=1) for h in range(2)]
        top[...] = jnp.zeros_like(top) if plain else jnp.full_like(top, -3e38)
        acc[...] = jnp.zeros_like(acc)

        def each_key(j, inner):
            @pl.when(need[i * n + j] == 1)
            def _():
                if plain:
                    raised = [jnp.exp(dot_nt(kx[j], extended[h])).astype(bf16) for h in range(2)]
                    for h in range(2):
                        acc[h] += dot(vt[j, h], raised[h])
                    return
                for h in range(2):
                    scores = dot_nt(kx[j], extended[h])
                    before = top[h : h + 1]
                    now = jnp.maximum(before, jnp.max(scores, axis=0, keepdims=True))
                    raised = jnp.exp(scores - now).astype(bf16)
                    top[h : h + 1] = now
                    acc[h] = acc[h] * jnp.exp(before - now) + dot(vt[j, h], raised)

            return inner

        lax.fori_loop(0, n, each_key, 0)
        sums = [acc[h][DH : DH + 1] for h in range(2)]
        both = jnp.concatenate([acc[h][:DH] / sums[h] for h in range(2)], axis=0)
        outs[i] = jnp.transpose(both, (1, 0)).astype(bf16)
        for h in range(2):
            lse[i, h : h + 1] = top[h : h + 1] + jnp.log(sums[h])
        return carry

    @pl.when(bounded)
    def _():
        lax.fori_loop(0, n, functools.partial(each_query, True), 0)

    @pl.when(jnp.logical_not(bounded))
    def _():
        lax.fori_loop(0, n, functools.partial(each_query, False), 0)


def unit_call(kernel, n, need, aux, one, arrays, out_shape, scratch, work, name):
    total = n * aux.shape[1]
    return pl.pallas_call(
        lambda *refs: kernel(n, *refs),
        out_shape=out_shape,
        grid_spec=pltpu.PrefetchScalarGridSpec(
            num_scalar_prefetch=1,
            grid=(),
            in_specs=[VM] * (2 + len(arrays)),
            out_specs=[VM] * len(out_shape),
            scratch_shapes=scratch,
        ),
        compiler_params=params(),
        cost_estimate=cost(work * total * total * 512, 8 * 2**20),
        name=name,
    )(need, aux, one, *arrays)


def attn_call(n, need, aux, one, parts):
    tokens = aux.shape[1]
    return unit_call(
        attn_kernel, n, need, aux, one, parts,
        [
            jax.ShapeDtypeStruct((n, tokens, LANES), bf16),
            jax.ShapeDtypeStruct((n, 8, tokens), f32),
        ],
        [
            pltpu.VMEM((n, tokens, 2 * LANES), bf16),
            pltpu.VMEM((n, 2, DH + 16, tokens), bf16),
            pltpu.VMEM((n, tokens, LANES), bf16),
            pltpu.VMEM((8, tokens), f32),
            pltpu.VMEM((2, DH + 16, tokens), f32),
        ],
        12, "attention",
    )


def proj_kernel(layer, host, valid, stream, packed, weight, *refs):
    n = host.n
    vectors = Vectors(n, layer, packed)
    gain, shift = vectors.norm(0, 1), vectors.norm(1, 1)
    tokens = stream.shape[0]
    units = BLOCKS // n
    att, (mid, rows, use, xs, rx, ssem, rsem, lsem) = refs[:units], refs[units:]
    host.barrier()
    copies = [
        group_send(n, -k, att[u].at[k], rx.at[k, u], ssem.at[u, k], rsem.at[u, k])
        for k in order_of(n)
        for u in range(units)
    ]
    copies += [pltpu.make_async_copy(att[u].at[0], rx.at[0, u], lsem.at[u]) for u in range(units)]
    for copy in copies:
        copy.start()
    host.start()
    for copy in copies:
        copy.wait()
    _, lo = group_place(n)
    for k in range(n):
        first = lax.rem(lo + k, n) * (units * LANES)
        for u in range(units):
            at = pl.multiple_of(first + u * LANES, LANES)
            rows[:, pl.ds(at, LANES)] = rx[k, u]

    def body(r):
        hat, _ = row_stats(rows[r, :].astype(f32))
        xs[r, :] = (hat * gain + shift).astype(bf16)

    row_loop(tokens, ROWS, body)
    branch = None
    for g in range(GROUPS):
        term = dot_nt(xs[:, g * HEADS : (g + 1) * HEADS], weight[:, g].reshape(D, HEADS))
        branch = term if branch is None else branch + term
    mid[...] = branch
    use[...] = jnp.zeros_like(use)

    def finish(r):
        part = mid[r, :]
        use[...] += fold_rows(valid[r, :] * part * part)
        mid[r, :] = stream[r, :].astype(f32) + part

    row_loop(tokens, ROWS, finish)
    host.finish()


def proj_call(n, ident, jobs, layer, valid, stream, packed, weight, att):
    tokens = stream.shape[0]
    units = BLOCKS // n
    flat = whole(stream.shape)
    return remote_call(
        functools.partial(proj_kernel, layer), n, "projection", ident,
        [valid, stream, packed, weight, *att],
        [whole(v.shape) for v in (valid, stream, packed)]
        + [pl.BlockSpec((BLOCKS, GROUPS, LANES, HEADS), lambda i: (0, 0, 0, 3))]
        + [whole(v.shape) for v in att],
        [
            jax.ShapeDtypeStruct(stream.shape, f32),
            jax.ShapeDtypeStruct(stream.shape, bf16),
            jax.ShapeDtypeStruct((8, D), f32),
        ],
        [flat, flat, whole((8, D))],
        [
            pltpu.VMEM((tokens, D), bf16),
            pltpu.VMEM((n, units, tokens, LANES), bf16),
            DMA((units, n)),
            DMA((units, n)),
            DMA((units,)),
        ],
        30 * tokens * D * D, jobs, grid=(1,),
    )


def ffn_kernel(
    layer, host, valid, mid, packed, weight,
    slope, hat, normed, low_mid, rstd_out, stream, low, use,
    xs, act, mean, buf, acc,
):
    step = pl.program_id(0)
    tokens = mid.shape[0]
    vectors = Vectors(host.n, layer, packed)

    @pl.when(step == 0)
    def _():
        gain, shift = vectors.norm(0, 2), vectors.norm(1, 2)
        use[...] = jnp.zeros_like(use)

        def body(r):
            raw = mid[r, :].astype(bf16)
            value, _ = row_stats(raw.astype(f32))
            low_mid[r, :] = raw
            xs[r, :] = (value * gain + shift).astype(bf16)

        row_loop(tokens, ROWS, body)
        if host.parts:
            host.barrier(False)
            host.start()

    @pl.when(step < GROUPS)
    def _():
        buf[...] = dot(xs[...], weight[...].reshape(D, WIDE))

        def body(r):
            h = buf[r, :]
            half = 0.5 * (1.0 + lax.erf(h * (1.0 / math.sqrt(2.0))))
            bell = jnp.exp(-0.5 * h * h) * (1.0 / math.sqrt(2.0 * math.pi))
            act[step, r, :] = h * half
            slope[0, r, :] = (half + h * bell).astype(bf16)

        row_loop(tokens, CHUNK, body)

    @pl.when(step == GROUPS)
    def _():
        acc[...] = jnp.zeros_like(acc)

        def body(r):
            blocks = [act[g, r, :] for g in range(GROUPS)]
            total = sum_lanes(sum(fold_lanes(b) for b in blocks)) / FF
            square = sum(fold_lanes((b - total) * (b - total)) for b in blocks)
            rstd = lax.rsqrt(sum_lanes(square) / FF + EPS)
            mean[r, :] = jnp.broadcast_to(total, (CHUNK, LANES))
            rstd_out[r, :] = jnp.broadcast_to(rstd, (CHUNK, LANES))

        row_loop(tokens, CHUNK, body)

    @pl.when(step >= GROUPS)
    def _():
        g = step - GROUPS
        hgain, hshift = vectors.hidden(0, g), vectors.hidden(1, g)

        def body(r):
            value = (act[g, r, :] - mean[r, 0:1]) * rstd_out[r, 0:1]
            hat[0, r, :] = value.astype(bf16)
            normed[0, r, :] = (value * hgain + hshift).astype(bf16)

        row_loop(tokens, CHUNK, body)
        acc[...] += dot_nt(normed[0], weight[...].reshape(D, WIDE))

    @pl.when(step == 2 * GROUPS - 1)
    def _():
        def body(r):
            feed = acc[r, :]
            out = mid[r, :] + feed
            keep = valid[r, :]
            stream[r, :] = out
            low[r, :] = out.astype(bf16)
            use[0] += fold_rows(keep * feed * feed)
            use[1] += fold_rows(keep * out * out)

        row_loop(tokens, ROWS, body)

        host.finish()


def first_half(s):
    return jnp.minimum(s, GROUPS - 1)


def second_half(s):
    return jnp.maximum(s - GROUPS, 0)


def half_specs(tokens):
    early = pl.BlockSpec((1, tokens, WIDE), lambda s: (first_half(s), 0, 0))
    late = pl.BlockSpec((1, tokens, WIDE), lambda s: (second_half(s), 0, 0))
    return early, late


def ffn_call(n, ident, jobs, layer, valid, mid, packed, weight):
    tokens = mid.shape[0]
    big = (GROUPS, tokens, WIDE)
    early, late = half_specs(tokens)
    flat = (tokens, D)
    call = remote_call if jobs else plain_call
    return call(
        functools.partial(ffn_kernel, layer), n, "ffn", ident,
        [valid, mid, packed, weight],
        [whole(v.shape) for v in (valid, mid, packed)]
        + [
            pl.BlockSpec(
                (BLOCKS, 1, LANES, WIDE), lambda s: (0, lax.rem(s, GROUPS), 0, s // GROUPS)
            )
        ],
        [jax.ShapeDtypeStruct(big, bf16)] * 3
        + [
            jax.ShapeDtypeStruct(flat, bf16),
            jax.ShapeDtypeStruct((tokens, LANES), f32),
            jax.ShapeDtypeStruct(flat, f32),
            jax.ShapeDtypeStruct(flat, bf16),
            jax.ShapeDtypeStruct((2, 8, D), f32),
        ],
        [early, late, late]
        + [whole(flat), whole((tokens, LANES)), whole(flat), whole(flat), whole((2, 8, D))],
        [
            pltpu.VMEM(flat, bf16),
            pltpu.VMEM(big, f32),
            pltpu.VMEM((tokens, LANES), f32),
            pltpu.VMEM((tokens, WIDE), f32),
            pltpu.VMEM(flat, f32),
        ],
        16 * tokens * D * FF, jobs, grid=(2 * GROUPS,),
    )


def ffn_back_kernel(
    layer, host, grad, hat, slope, rstd_in, low_mid, packed, weight,
    dhid, grad_turned, normed_turned, grad_out, hgrads, grads,
    gs, dxs, buf, first, cross, acc,
):
    step = pl.program_id(0)
    tokens = grad.shape[0]
    vectors = Vectors(host.n, layer, packed)

    @pl.when(step == 0)
    def _():
        first[...] = jnp.zeros_like(first)
        cross[...] = jnp.zeros_like(cross)
        hgrads[...] = jnp.zeros_like(hgrads)
        grads[...] = jnp.zeros_like(grads)
        gs[...] = grad[...].astype(bf16)
        for b in range(BLOCKS):
            grad_turned[b] = flip(gs[:, b * LANES : (b + 1) * LANES])
        if host.parts:
            host.barrier(False)
            host.start()

    @pl.when(step < GROUPS)
    def _():
        buf[...] = dot(gs[...], weight[...].reshape(D, WIDE))
        hgain = vectors.hidden(0, step)

        def body(r):
            value = hat[0, r, :].astype(f32)
            dy = buf[r, :]
            dx = dy * hgain
            hgrads[0, step] += fold_rows(dy * value)
            hgrads[1, step] += fold_rows(dy)
            first[r, :] += fold_lanes(dx)
            cross[r, :] += fold_lanes(dx * value)
            dxs[step, r, :] = dx

        row_loop(tokens, CHUNK, body)

    @pl.when(step == GROUPS)
    def _():
        acc[...] = jnp.zeros_like(acc)

        def body(r):
            for ref in (first, cross):
                ref[r, :] = jnp.broadcast_to(sum_lanes(ref[r, :]) / FF, ref[r, :].shape)

        row_loop(tokens, ROWS, body)

    @pl.when(step >= GROUPS)
    def _():
        g = step - GROUPS

        def body(r):
            inner = dxs[g, r, :] - first[r, 0:1] - hat[0, r, :].astype(f32) * cross[r, 0:1]
            dhid[0, r, :] = (slope[0, r, :].astype(f32) * (rstd_in[r, 0:1] * inner)).astype(bf16)

        row_loop(tokens, CHUNK, body)
        acc[...] += dot_nt(dhid[0], weight[...].reshape(D, WIDE))

    @pl.when(step == 2 * GROUPS - 1)
    def _():
        gain, shift = vectors.norm(0, 2), vectors.norm(1, 2)

        def body(r):
            value, rstd = row_stats(low_mid[r, :].astype(f32))
            dy = acc[r, :]
            grads[0] += fold_rows(dy * value)
            grads[1] += fold_rows(dy)
            grad_out[r, :] = grad[r, :].astype(f32) + norm_back(dy, value, rstd, gain)
            gs[r, :] = (value * gain + shift).astype(bf16)

        row_loop(tokens, ROWS, body)
        for b in range(BLOCKS):
            normed_turned[b] = flip(gs[:, b * LANES : (b + 1) * LANES])
        host.finish()


def ffn_back_call(n, ident, jobs, layer, grad, hat, slope, rstd, low_mid, packed, weight):
    tokens = grad.shape[0]
    turned = (BLOCKS, LANES, tokens)
    big = (GROUPS, tokens, WIDE)
    _, late = half_specs(tokens)
    flat = (tokens, D)
    call = remote_call if jobs else plain_call
    return call(
        functools.partial(ffn_back_kernel, layer), n, "ffn_back", ident,
        [grad, hat, slope, rstd, low_mid, packed, weight],
        [
            whole(flat),
            pl.BlockSpec((1, tokens, WIDE), lambda s: (lax.rem(s, GROUPS), 0, 0)),
            late,
        ]
        + [whole(v.shape) for v in (rstd, low_mid, packed)]
        + [
            pl.BlockSpec(
                (BLOCKS, 1, LANES, WIDE), lambda s: (0, lax.rem(s, GROUPS), 0, 1 - s // GROUPS)
            )
        ],
        [
            jax.ShapeDtypeStruct(big, bf16),
            jax.ShapeDtypeStruct(turned, bf16),
            jax.ShapeDtypeStruct(turned, bf16),
            jax.ShapeDtypeStruct(flat, f32),
            jax.ShapeDtypeStruct((2, GROUPS, 8, WIDE), f32),
            jax.ShapeDtypeStruct((2, 8, D), f32),
        ],
        [late, whole(turned), whole(turned), whole(flat)]
        + [whole((2, GROUPS, 8, WIDE)), whole((2, 8, D))],
        [
            pltpu.VMEM(flat, bf16),
            pltpu.VMEM(big, f32),
            pltpu.VMEM((tokens, WIDE), f32),
            pltpu.VMEM((tokens, LANES), f32),
            pltpu.VMEM((tokens, LANES), f32),
            pltpu.VMEM(flat, f32),
        ],
        16 * tokens * D * FF, jobs, grid=(2 * GROUPS,),
    )


def proj_back_kernel(
    layer, host, grad, packed, weight, rows, *refs
):
    n = host.n
    vectors = Vectors(n, layer, packed)
    gain, shift = vectors.norm(0, 1), vectors.norm(1, 1)
    tokens = grad.shape[0]
    units = BLOCKS // n
    outs, refs = refs[:units], refs[units:]
    grad_turned, normed, grads, gs, dm, send, ssem, rsem, lsem = refs
    host.barrier()
    host.start()
    gs[...] = grad[...].astype(bf16)
    for g in range(GROUPS):
        dm[:, g * HEADS : (g + 1) * HEADS] = dot(gs[...], weight[:, g].reshape(D, HEADS))
    grads[...] = jnp.zeros_like(grads)

    def body(r):
        value, rstd = row_stats(rows[r, :].astype(f32))
        dy = dm[r, :]
        grads[0] += fold_rows(dy * value)
        grads[1] += fold_rows(dy)
        dv = norm_back(dy, value, rstd, gain).astype(bf16)
        for b in range(BLOCKS):
            send[b, r, :] = dv[:, b * LANES : (b + 1) * LANES]
        normed[r, :] = (value * gain + shift).astype(bf16)

    row_loop(tokens, ROWS, body)
    _, lo = group_place(n)
    copies = []
    for k in order_of(n) + [0]:
        for u in range(units):
            source = send.at[lax.rem(lo + k, n) * units + u]
            if k:
                copy = group_send(n, k, source, outs[u].at[k], ssem.at[u, k], rsem.at[u, k])
            else:
                copy = pltpu.make_async_copy(source, outs[u].at[0], lsem.at[u])
            copy.start()
            copies.append(copy)
    for b in range(BLOCKS):
        grad_turned[b] = flip(gs[:, b * LANES : (b + 1) * LANES])
    for copy in copies:
        copy.wait()
    host.finish()


def proj_back_call(n, ident, jobs, layer, grad, packed, weight, rows):
    tokens = grad.shape[0]
    units = BLOCKS // n
    turned = (BLOCKS, LANES, tokens)
    flat = (tokens, D)
    return remote_call(
        functools.partial(proj_back_kernel, layer), n, "projection_back", ident,
        [grad, packed, weight, rows],
        [whole(v.shape) for v in (grad, packed)]
        + [pl.BlockSpec((BLOCKS, GROUPS, LANES, HEADS), lambda i: (0, 0, 0, 3)), whole(flat)],
        [
            *[jax.ShapeDtypeStruct((n, tokens, LANES), bf16)] * units,
            jax.ShapeDtypeStruct(turned, bf16),
            jax.ShapeDtypeStruct(flat, bf16),
            jax.ShapeDtypeStruct((2, 8, D), f32),
        ],
        [HB] * units + [whole(turned), whole(flat), whole((2, 8, D))],
        [
            pltpu.VMEM(flat, bf16),
            pltpu.VMEM(flat, f32),
            pltpu.VMEM((BLOCKS, tokens, LANES), bf16),
            DMA((units, n)),
            DMA((units, n)),
            DMA((units,)),
        ],
        30 * tokens * D * D, jobs, grid=(1,),
    )


def attn_back_kernel(n, need, aux, one, *refs):
    qkv, (att, datt, lse) = refs[:n], refs[n : n + 3]
    outs, refs = refs[n + 3 : 2 * n + 3], refs[2 * n + 3 :]
    kx, kt, qs, vs, delta, dq, dkey, dval, dkv = refs
    for r in range(n):
        kx[r] = jnp.concatenate([qkv[r][1], aux[r]], axis=1)
        kt[r] = flip(qkv[r][1])
        vs[r] = qkv[r][2]
        qs[r] = (qkv[r][0].astype(f32) * (1.0 / math.sqrt(DH))).astype(bf16)
        both = jnp.transpose(att[r].astype(f32) * datt[r].astype(f32), (1, 0))
        delta[r, 0:1] = jnp.sum(both[:DH], axis=0, keepdims=True)
        delta[r, 1:2] = jnp.sum(both[DH:], axis=0, keepdims=True)
    dq[...] = jnp.zeros_like(dq)

    def each_key(j, carry):
        dkey[...] = jnp.zeros_like(dkey)
        dval[...] = jnp.zeros_like(dval)

        def each_query(i, inner):
            @pl.when(need[i * n + j] == 1)
            def _():
                for h in range(2):
                    query = head_lanes(qs[i], h)
                    out = head_lanes(datt[i], h)
                    scores = dot_nt(kx[j], jnp.concatenate([query, one[...]], axis=1))
                    probs = jnp.exp(scores - lse[i, h : h + 1])
                    dprobs = dot_nt(vs[j], out)
                    dscores = (probs * (dprobs - delta[i, h : h + 1])).astype(bf16)
                    dval[...] += dot(probs.astype(bf16), out)
                    dkey[...] += dot(dscores, query)
                    rows = slice(h * DH, (h + 1) * DH)
                    dq[i, rows] += dot(kt[j, rows], dscores)

            return inner

        lax.fori_loop(0, n, each_query, 0)
        dkv[j, 0] = dkey[...].astype(bf16)
        dkv[j, 1] = dval[...].astype(bf16)
        return carry

    lax.fori_loop(0, n, each_key, 0)
    for r in range(n):
        outs[r][0] = (jnp.transpose(dq[r], (1, 0)) * (1.0 / math.sqrt(DH))).astype(bf16)
        outs[r][1] = dkv[r, 0]
        outs[r][2] = dkv[r, 1]


def attn_back_call(n, need, aux, one, parts, att, datt, lse):
    tokens = aux.shape[1]
    return unit_call(
        attn_back_kernel, n, need, aux, one, [*parts, att, datt, lse],
        [jax.ShapeDtypeStruct((3, tokens, LANES), bf16)] * n,
        [
            pltpu.VMEM((n, tokens, 2 * LANES), bf16),
            pltpu.VMEM((n, LANES, tokens), bf16),
            pltpu.VMEM((n, tokens, LANES), bf16),
            pltpu.VMEM((n, tokens, LANES), bf16),
            pltpu.VMEM((n, 8, tokens), f32),
            pltpu.VMEM((n, LANES, tokens), f32),
            pltpu.VMEM((tokens, LANES), f32),
            pltpu.VMEM((tokens, LANES), f32),
            pltpu.VMEM((n, 2, tokens, LANES), bf16),
        ],
        14, "attention_back",
    )


def qkv_back_kernel(
    layer, host, grad, low, packed, wq, wk, wv, *refs
):
    n = host.n
    vectors = Vectors(n, layer, packed)
    gain, shift = vectors.norm(0, 0), vectors.norm(1, 0)
    tokens = grad.shape[0]
    units = BLOCKS // n
    early_count = n * (units - 1)
    ready, refs = refs[:early_count], refs[early_count:]
    dparts, refs = refs[:n], refs[n:]
    dlast, refs = refs[:n], refs[n:]
    grad_out, normed_turned, grads, grad_low, acc, ns, hats, scales, ssem, rsem, lsem = refs
    blocks = [ready[u * n : (u + 1) * n] for u in range(units - 1)] + [dlast]
    host.barrier()
    steps = [0] + order_of(n)[::-1]
    copies = {}
    for k in order_of(n):
        copies[k] = group_send(n, -k, dparts[k], dlast[k], ssem.at[k], rsem.at[k])
        copies[k].start()
    copies[0] = pltpu.make_async_copy(dparts[0], dlast[0], lsem)
    copies[0].start()
    host.start()
    grads[...] = jnp.zeros_like(grads)

    def early(r):
        value, rstd = row_stats(low[r, :].astype(f32))
        hats[r, :] = value
        scales[r, :] = jnp.broadcast_to(rstd, scales[r, :].shape)
        ns[r, :] = (value * gain + shift).astype(bf16)

    row_loop(tokens, ROWS, early)
    for b in range(BLOCKS):
        normed_turned[b] = flip(ns[:, b * LANES : (b + 1) * LANES])
    for i, k in enumerate(steps):
        copies[k].wait()
        group, offset = head_columns(n, k)
        left, right = [], []
        for c, weight in enumerate((wq, wk, wv)):
            left += [blocks[u][k][c] for u in range(units)]
            part = weight[:, group, :, pl.ds(offset, units * LANES)]
            right.append(part.reshape(D, units * LANES))
        total = dot_nt(jnp.concatenate(left, axis=1), jnp.concatenate(right, axis=1))
        if i == 0:
            acc[...] = total
        else:
            acc[...] += total

    def body(r):
        value, rstd = hats[r, :], scales[r, 0:1]
        dy = acc[r, :]
        grads[0] += fold_rows(dy * value)
        grads[1] += fold_rows(dy)
        total = grad[r, :] + norm_back(dy, value, rstd, gain)
        grad_out[r, :] = total
        grad_low[r, :] = total.astype(bf16)

    row_loop(tokens, ROWS, body)
    host.finish()


def qkv_back_call(n, ident, jobs, layer, grad, low, packed, weight, ready, dparts):
    tokens = grad.shape[0]
    turned = (BLOCKS, LANES, tokens)
    flat = (tokens, D)
    columns = lambda c: pl.BlockSpec((BLOCKS, GROUPS, LANES, HEADS), lambda i: (0, 0, 0, c))
    block = (3, tokens, LANES)
    res = remote_call(
        functools.partial(qkv_back_kernel, layer), n, "qkv_back", ident,
        [grad, low, packed, weight, weight, weight, *ready, *dparts],
        [whole(v.shape) for v in (grad, low, packed)]
        + [columns(0), columns(1), columns(2)]
        + [whole(block)] * (len(ready) + n),
        [jax.ShapeDtypeStruct(block, bf16)] * n
        + [
            jax.ShapeDtypeStruct(flat, f32),
            jax.ShapeDtypeStruct(turned, bf16),
            jax.ShapeDtypeStruct((2, 8, D), f32),
            jax.ShapeDtypeStruct(flat, bf16),
        ],
        [whole(block)] * n + [whole(flat), whole(turned), whole((2, 8, D)), whole(flat)],
        [
            pltpu.VMEM(flat, f32),
            pltpu.VMEM(flat, bf16),
            pltpu.VMEM(flat, f32),
            pltpu.VMEM((tokens, LANES), f32),
            DMA((n,)),
            DMA((n,)),
            DMA,
        ],
        50 * tokens * D * D, jobs, grid=(1,),
    )
    return [res[:n], *res[n:]]


def slot_group(p):
    return 2 * (p % 2) + p // 2


def pick_rows(sc, first, turned, count):
    return jnp.concatenate([turned[sc[first + m]] for m in range(count)], axis=0)


def put_rows(value, extra, outs, spot):
    rows = value.shape[0] // LANES
    for m in range(rows):
        part = value[m * LANES : (m + 1) * LANES]
        if extra is not None:
            part = part + extra[(m,) + spot].astype(f32)
            outs[m // 2][(m % 2,) + spot] = part.astype(bf16)
        else:
            outs[0][(m,) + spot] = part.astype(bf16)


def ffn_grad_kernel(ups, first, count, added, sc, up_turned, down_turned, *refs):
    split = added and ups
    dhid, normed, refs = [v.at[0] for v in refs[:2]], [v.at[0] for v in refs[2:4]], refs[4:]
    extra, outs = (refs[0], refs[1:]) if added else (None, refs)

    @pl.when(pl.program_id(0) == 0)
    def _():
        left = pick_rows(sc, first + ups, up_turned, count)
        for i in range(2):
            put_rows(dot(left, dhid[i][...]), extra, outs[:2] if split else outs, (i,))

    @pl.when(pl.program_id(0) == 1)
    def _():
        left = pick_rows(sc, first, down_turned, count)
        for i in range(2):
            put_rows(dot(left, normed[i][...]), extra, outs[2:] if split else outs, (i,))


def ffn_grad_call(ups, first, count, sc, up_turned, down_turned, dhid, normed, extra=None):
    tokens = up_turned.shape[2]
    added = extra is not None
    def block(i, kind, idle):
        def at(j, p, sc):
            p = jnp.where(j == kind, p, idle)
            return (jnp.bitwise_xor(p + 2 * i, sc[BLOCKS]), 0, 0)

        return pl.BlockSpec((1, tokens, WIDE), at)

    lefts = [block(i, 0, 1) for i in range(2)]
    rights = [block(i, 1, 0) for i in range(2)]
    piece = lambda m: pl.BlockSpec((m, 2, LANES, WIDE), lambda j, p, sc: (0, p, 0, j))
    outs = [2, 2] if added else [count]
    specs = [piece(m) for m in outs]
    wide = 2 * WIDE
    if added and ups:

        def half(kind, idle):
            at = lambda j, p, sc: (0, jnp.where(j == kind, p, idle), 0, 0)
            return pl.BlockSpec((2, 2, LANES, WIDE), at)

        outs, specs, wide = [2] * 4, [half(0, 1)] * 2 + [half(1, 0)] * 2, WIDE
    return pl.pallas_call(
        lambda *refs: ffn_grad_kernel(ups, first, count, added, *refs),
        out_shape=[jax.ShapeDtypeStruct((m, GROUPS, LANES, wide), bf16) for m in outs],
        grid_spec=pltpu.PrefetchScalarGridSpec(
            num_scalar_prefetch=1,
            grid=(2, GROUPS // 2),
            in_specs=[whole(up_turned.shape), whole(down_turned.shape), *lefts, *rights]
            + ([piece(count)] if added else []),
            out_specs=specs,
        ),
        compiler_params=params(),
        cost_estimate=cost(16 * tokens * count * LANES * FF, 24 * 2**20),
        name="ffn_grad",
    )(sc, up_turned, down_turned, dhid, dhid, normed, normed, *([extra] if added else []))


def head_grad_kernel(n, first, count, added, sc, in_turned, out_turned, normed, *refs):
    units = BLOCKS // n
    dqkv, refs = refs[: n * units], refs[n * units :]
    extra, outs = (refs[0], refs[1:]) if added else (None, refs)
    left = pick_rows(sc, first, in_turned, count)
    for k in range(n):
        for c in range(3):
            right = jnp.concatenate([dqkv[u * n + k][c] for u in range(units)], axis=1)
            value = dot(left, right)
            if n == GROUPS:
                slot = slot_group(jnp.bitwise_xor(lax.rem(sc[BLOCKS + 1] + k, n), sc[BLOCKS]))
                put_rows(value, extra, outs, (slot, slice(None), slice(c * HEADS, (c + 1) * HEADS)))
            else:
                unit = lax.rem(sc[BLOCKS + 1] + k, n) * units
                at = pl.multiple_of(c * HEADS + lax.rem(unit, 2) * LANES, LANES)
                slot = slot_group(unit // 2)
                put_rows(value, extra, outs, (slot, slice(None), pl.ds(at, LANES)))
    left = pick_rows(sc, first, out_turned, count)
    for g in range(GROUPS):
        slot = slot_group(jnp.bitwise_xor(g, sc[BLOCKS]))
        value = dot(left, normed[:, g * HEADS : (g + 1) * HEADS])
        put_rows(value, extra, outs, (slot, slice(None), slice(3 * HEADS, 4 * HEADS)))


def head_grad_call(n, first, count, sc, in_turned, out_turned, dqkv, normed, extra=None):
    tokens = in_turned.shape[2]
    added = extra is not None
    outs = [2, 2] if added else [count]
    inner = (GROUPS, LANES, 4 * HEADS)
    return pl.pallas_call(
        lambda *refs: head_grad_kernel(n, first, count, added, *refs),
        out_shape=[jax.ShapeDtypeStruct((m,) + inner, bf16) for m in outs],
        grid_spec=pltpu.PrefetchScalarGridSpec(
            num_scalar_prefetch=1,
            grid=(1,),
            in_specs=[whole(v.shape) for v in (in_turned, out_turned, normed, *dqkv)]
            + ([whole((count,) + inner)] if added else []),
            out_specs=[whole((m,) + inner) for m in outs],
        ),
        compiler_params=params(),
        cost_estimate=cost(16 * tokens * count * LANES * 4 * D, 16 * 2**20),
        name="head_grad",
    )(sc, in_turned, out_turned, normed, *dqkv, *([extra] if added else []))


def pack_kernel(qkv, out, up, down, *refs):
    layers = qkv.shape[0]
    for l in range(layers):
        narrow, broad = refs[2 * l : 2 * l + 2]
        for c in range(3):
            narrow[:, c * HEADS : (c + 1) * HEADS] = qkv[l, c]
        narrow[:, 3 * HEADS :] = flip(out[l])
        broad[:, :WIDE] = up[l]
        broad[:, WIDE:] = flip(down[l])


def pack_call(qkv, out, up, down):
    layers = qkv.shape[0]
    flat = pl.pallas_call(
        pack_kernel,
        out_shape=[
            jax.ShapeDtypeStruct((LANES, NARROW), bf16),
            jax.ShapeDtypeStruct((LANES, BROAD), bf16),
        ]
        * layers,
        in_specs=[VM] * 4,
        out_specs=[VM] * (2 * layers),
        compiler_params=params(),
        cost_estimate=cost(0, 4 * 2**20),
        name="pack",
    )(qkv, out, up, down)
    return flat[::2], flat[1::2]


def greet(sem, place, z, others, count):
    n = GROUPS
    for k in range(1, n):
        pl.semaphore_signal(
            sem, inc=1, device_id={"head": lax.rem(z + k, n)}, device_id_type=MESH
        )
    for other in (place.by_x, place.by_y, place.mate):
        pl.semaphore_signal(sem, inc=1, device_id={"dp": other}, device_id_type=MESH)
    for to_dp, to_z in others:

        @pl.when((to_dp != place.dp) | (to_z != z))
        def _(to_dp=to_dp, to_z=to_z):
            pl.semaphore_signal(
                sem, inc=1, device_id={"dp": to_dp, "head": to_z}, device_id_type=MESH
            )

    pl.semaphore_wait(sem, n + 2 + count)


class Weights:
    def __init__(self, at, chunks, shards, gathered, hsem, ssem, rsem, lsem):
        self.at, self.chunks, self.pairs = at, chunks, list(zip(shards, gathered))
        self.hsem, self.ssem, self.rsem = hsem, ssem, rsem
        self.lsem = lsem

    def owns(self):
        at = self.at
        return [
            pltpu.make_async_copy(shard, out.at[at.dp, at.z], self.lsem.at[i])
            for i, (shard, out) in enumerate(self.pairs)
        ]

    def near(self, c):
        kind, columns = self.chunks[c][0], pl.ds(*self.chunks[c][1:])
        shard, out = self.pairs[kind]
        at = self.at
        return [
            pltpu.make_async_remote_copy(
                src_ref=shard.at[:, columns],
                dst_ref=out.at[at.dp, at.z, :, columns],
                send_sem=self.hsem.at[0, k - 1, c],
                recv_sem=self.hsem.at[1, k - 1, c],
                device_id={"head": lax.rem(at.z + k, GROUPS)},
                device_id_type=MESH,
            )
            for k in (2, 1, 3)
        ]

    def far(self, slot, row, target, c):
        kind, columns = self.chunks[c][0], pl.ds(*self.chunks[c][1:])
        out = self.pairs[kind][1]
        return pltpu.make_async_remote_copy(
            src_ref=out.at[row, :, :, columns],
            dst_ref=out.at[row, :, :, columns],
            send_sem=self.ssem.at[slot, c],
            recv_sem=self.rsem.at[slot, c],
            device_id={"dp": target},
            device_id_type=MESH,
        )

    def hops(self, stage, c):
        at = self.at
        if stage == 0:
            return self.near(c)
        if stage == 1:
            return [self.far(0, at.dp, at.first, c)]
        if stage == 2:
            return [self.far(1, at.dp, at.second, c), self.far(2, at.first, at.second, c)]
        rows = (at.dp, at.first, at.second, at.both)
        return [self.far(3 + i, row, at.mate, c) for i, row in enumerate(rows)]

    def begin(self):
        for c in range(min(2, len(self.chunks))):
            for copy in self.near(c):
                copy.start()

    def turn(self, t):
        parts = len(self.chunks)
        for stage in (1, 2, 3):
            c = t + 1 - stage
            if 0 <= c < parts:
                if stage == 1 and c == 0:
                    for copy in self.owns():
                        copy.wait()
                for copy in self.hops(stage - 1, c):
                    copy.wait()
                for copy in self.hops(stage, c):
                    copy.start()
        if t + 2 < parts:
            for copy in self.near(t + 2):
                copy.start()
        c = t - 3
        if 0 <= c < parts:
            for copy in self.hops(3, c):
                copy.wait()

    def run(self, aside):
        self.begin()
        for t in range(len(self.chunks) + 3):
            self.turn(t)
            aside(t)


def weight_chunks(shards, step=512):
    return [(i, c, step) for i, v in enumerate(shards) for c in range(0, v.shape[1], step)]


def weight_sems(shards, step=512):
    parts = len(weight_chunks(shards, step))
    return [DMA((2, 3, parts)), DMA((7, parts)), DMA((7, parts)), DMA((len(shards),))]


def start_kernel(
    chunks, shards, rows, vector, flags, gathered, low, side, vectors, flags_out, blocks,
    hsem, ssem, rsem, wsem, xsem, tsem, vsem, fsem, lsem, low_here, vectors_here, *scratch,
):
    queries = Queries(GROUPS, gathered[0], blocks, *scratch)
    at = Place()
    weights = Weights(at, chunks, shards, gathered, hsem, ssem, rsem, wsem)
    dp, core, bit_x, by_x = at.dp, at.core, at.bit_x, at.by_x
    z = at.z
    n = GROUPS
    lo = lax.rem(dp, n)
    wide = rows.shape[2]
    sem = pltpu.get_barrier_semaphore()

    def targets():
        return [(xs, c2, dp - core + c2, 2 * xs + core) for xs in range(2) for c2 in range(2)]

    def sources():
        return [(dp - core + lax.rem(z, 2), g) for g in range(n)]

    turn_dp, turn_z = dp - lo + z, lo
    for copy in weights.owns():
        copy.start()
    own_vector = pltpu.make_async_copy(vector, vectors.at[z], lsem.at[2])
    own_vector.start()
    turned = [(turn_dp, turn_z)]
    across = at.by_x + 1 - 2 * core
    greet(
        sem, at, z, sources() + turned + [(across, z)],
        n + unlike(lax.rem(z, 2), core) + unlike(z, lo),
    )
    small = [
        pltpu.make_async_remote_copy(
            src_ref=vector,
            dst_ref=vectors.at[z],
            send_sem=vsem.at[0, k - 1],
            recv_sem=vsem.at[1, k - 1],
            device_id={"head": lax.rem(z + k, n)},
            device_id_type=MESH,
        )
        for k in range(1, n)
    ]

    def flag_copy(op):
        def remote():
            copy = pltpu.make_async_remote_copy(
                src_ref=flags,
                dst_ref=flags_out,
                send_sem=fsem.at[0],
                recv_sem=fsem.at[1],
                device_id={"dp": turn_dp, "head": turn_z},
                device_id_type=MESH,
            )
            copy.start() if op == "start" else copy.wait()

        def inside():
            copy = pltpu.make_async_copy(flags, flags_out, lsem.at[3])
            copy.start() if op == "start" else copy.wait()

        pl.when((turn_dp != dp) | (turn_z != z))(remote)
        pl.when((turn_dp == dp) & (turn_z == z))(inside)

    flag_copy("start")
    for copy in small:
        copy.start()

    cross = pltpu.make_async_remote_copy(
        src_ref=rows.at[pl.ds(2 - 2 * bit_x, 2)],
        dst_ref=side,
        send_sem=xsem.at[0],
        recv_sem=xsem.at[1],
        device_id={"dp": by_x},
        device_id_type=MESH,
    )
    place = low.at[:, pl.ds(pl.multiple_of(z * wide, wide), wide)]

    def spread(op):
        for i, (xs, c2, to_dp, to_z) in enumerate(targets()):

            def here(source, i=i, to_dp=to_dp, to_z=to_z):
                def remote():
                    copy = pltpu.make_async_remote_copy(
                        src_ref=source,
                        dst_ref=place,
                        send_sem=tsem.at[0, i],
                        recv_sem=tsem.at[1, z],
                        device_id={"dp": to_dp, "head": to_z},
                        device_id_type=MESH,
                    )
                    if op == "start":
                        copy.start()
                    else:
                        copy.wait_send()

                pl.when((to_dp != dp) | (to_z != z))(remote)

                def inside():
                    copy = pltpu.make_async_copy(source, place, lsem.at[1])
                    if op == "start":
                        copy.start()
                    else:
                        copy.wait()

                pl.when((to_dp == dp) & (to_z == z))(inside)

            pl.when(bit_x == xs)(lambda xs=xs, c2=c2, here=here: here(rows.at[2 * xs + c2]))
            pl.when(bit_x != xs)(lambda c2=c2, here=here: here(side.at[c2]))

    cross.start()

    def arrivals():
        spread("wait")
        for from_dp, g in sources():

            @pl.when((from_dp != dp) | (g != z))
            def _(g=g):
                spot = low.at[:, pl.ds(g * wide, wide)]
                pltpu.make_async_remote_copy(
                    src_ref=spot,
                    dst_ref=spot,
                    send_sem=tsem.at[0, 0],
                    recv_sem=tsem.at[1, g],
                    device_id={"dp": by_x},
                    device_id_type=MESH,
                ).wait_recv()

    ready = sum(kind == 0 for kind, *_ in chunks) + 2
    loads = [
        pltpu.make_async_copy(low, low_here, lsem.at[0]),
        pltpu.make_async_copy(vectors, vectors_here, lsem.at[2]),
    ]

    def aside(t):
        if t == 1:
            cross.wait()
            spread("start")
        if t == ready:
            queries.begin()
            own_vector.wait()
            for copy in small:
                copy.wait()
            arrivals()
            for copy in loads:
                copy.start()
            for copy in loads:
                copy.wait()
            norms = Vectors(n, 0, vectors_here)
            queries.norm(low_here, norms.norm(0, 0), norms.norm(1, 0))
        if ready < t <= ready + n:
            queries.step(t - ready - 1)

    weights.run(aside)
    flag_copy("wait")
    queries.finish()


def start_call(shards, rows, vector, flags):
    count = len(shards)
    chunks = weight_chunks(shards)
    tokens, wide = rows.shape[1:]

    out_shape, out_specs = queries_outs(GROUPS, tokens)

    def kernel(*refs):
        taken, refs = refs[:count], refs[count:]
        given, refs = refs[:3], refs[3:]
        gathered, refs = refs[:count], refs[count:]
        others, refs = refs[:4], refs[4:]
        blocks, refs = refs[: len(out_shape)], refs[len(out_shape) :]
        start_kernel(chunks, taken, *given, gathered, *others, blocks, *refs)

    res = pl.pallas_call(
        kernel,
        out_shape=[jax.ShapeDtypeStruct((BLOCKS, GROUPS) + v.shape, bf16) for v in shards]
        + [
            jax.ShapeDtypeStruct((tokens, GROUPS * wide), bf16),
            jax.ShapeDtypeStruct((2, tokens, wide), bf16),
            jax.ShapeDtypeStruct((GROUPS,) + vector.shape, f32),
            jax.ShapeDtypeStruct(flags.shape, jnp.int32),
        ]
        + out_shape,
        in_specs=[HB] * (count + 3),
        out_specs=[HB] * (count + 4) + out_specs,
        scratch_shapes=[
            *weight_sems(shards),
            DMA((2,)),
            DMA((2, GROUPS)),
            DMA((2, 3)),
            DMA((2,)),
            DMA((4,)),
            pltpu.VMEM((tokens, GROUPS * wide), bf16),
            pltpu.VMEM((GROUPS,) + vector.shape, f32),
            *queries_scratch(GROUPS, tokens),
        ],
        compiler_params=params(collective_id=5, has_side_effects=True),
        cost_estimate=cost(0, 300 * 2**20),
        name="start",
    )(*shards, rows, vector, flags)
    blocks = res[count + 4 :]
    parts = [blocks[u * GROUPS : (u + 1) * GROUPS] for u in range(len(blocks) // GROUPS)]
    return [res[:count], *res[count : count + 4], parts]


def vector_rows(layers):
    return -(-(28 * layers + 3 * layers + 1) // 8) * 8


def end_kernel(
    layers, rows, grads, fsum, valid, tops, vecs, uses,
    rows_out, qkv_out, out_out, up_out, down_out,
    gains_out, shifts_out, hgains_out, hshifts_out, rms_out,
    mine, got, pair, last, near, pieces, crossed, fm, fnear, vec, vgot, vsum,
    gsem, hsem, psem, qsem, nsem, tsem, xsem, vsem, lsem, esem,
):
    at = Place()
    dp, core, bit_x = at.dp, at.core, at.bit_x
    z = at.z
    n = GROUPS
    parts = 4
    width = grads.shape[3] // parts
    step = fsum.shape[2] // parts
    wide = rows.shape[1] // n
    sem = pltpu.get_barrier_semaphore()

    def columns(c):
        return pl.ds(c * width, width)

    def broad(c):
        return pl.ds(c * step, step)

    def loads(c):
        return [
            pltpu.make_async_copy(
                grads.at[pl.ds(0, 4), :, :, columns(c)], mine.at[:, :, :, columns(c)], gsem.at[0, c]
            ),
            pltpu.make_async_copy(
                fsum.at[:, :, broad(c)], fm.at[:, :, broad(c)], gsem.at[1, c]
            ),
        ]

    for c in range(parts):
        for copy in loads(c):
            copy.start()

    vec[...] = jnp.zeros_like(vec)
    for l in range(layers):
        base = 28 * l
        norms, hidden = vecs[4 * l : 4 * l + 3], vecs[4 * l + 3]
        for kind in range(2):
            for i in range(3):
                total = jnp.sum(norms[i][kind], axis=0, keepdims=True)
                for b in range(BLOCKS):
                    row = base + (3 * kind + i) * 2 + b % 2
                    vec[b // 2, row : row + 1, :] = total[:, b * LANES : (b + 1) * LANES]
            for g in range(n):
                total = jnp.sum(hidden[kind, g], axis=0, keepdims=True)
                for b in range(BLOCKS):
                    row = base + 12 + 8 * kind + b
                    vec[g, row : row + 1, :] = total[:, b * LANES : (b + 1) * LANES]
        branch, rest = uses[2 * l : 2 * l + 2]
        for i, value in enumerate((branch[...], rest[0], rest[1])):
            row = 28 * layers + 3 * l + i
            total = fold_lanes(jnp.sum(value, axis=0, keepdims=True))
            for g in range(n):
                vec[g, row : row + 1, :] = total
    row = 31 * layers
    count = jnp.sum(valid[...], axis=0, keepdims=True) * (D / LANES)
    for g in range(n):
        vec[g, row : row + 1, :] = jnp.broadcast_to(count, (1, LANES))

    to_dp = dp - core + lax.rem(z, 2)
    sources = [(dp - core + c2, 2 * xs + core) for xs in range(2) for c2 in range(2)]
    greet(sem, at, z, sources, n - 1 + unlike(lax.rem(z, 2), core))

    def hop(stage, c):
        if stage == 0:
            return pltpu.make_async_remote_copy(
                src_ref=grads.at[pl.ds(4, 4), :, :, columns(c)],
                dst_ref=got.at[:, :, :, columns(c)],
                send_sem=hsem.at[0, c],
                recv_sem=hsem.at[1, c],
                device_id={"dp": at.mate},
                device_id_type=MESH,
            )
        if stage == 1:
            return pltpu.make_async_remote_copy(
                src_ref=mine.at[pl.ds(2, 2), :, :, columns(c)],
                dst_ref=pair.at[:, :, :, columns(c)],
                send_sem=psem.at[0, c],
                recv_sem=psem.at[1, c],
                device_id={"dp": at.second},
                device_id_type=MESH,
            )
        return pltpu.make_async_remote_copy(
            src_ref=mine.at[1, :, :, columns(c)],
            dst_ref=last.at[:, :, columns(c)],
            send_sem=qsem.at[0, c],
            recv_sem=qsem.at[1, c],
            device_id={"dp": at.first},
            device_id_type=MESH,
        )

    def way(source, target, sems, i, c):
        return pltpu.make_async_remote_copy(
            src_ref=source,
            dst_ref=target,
            send_sem=sems.at[0, i, c],
            recv_sem=sems.at[1, i, c],
            device_id={"head": at.group(2 - i)},
            device_id_type=MESH,
        )

    def head_way(i, c):
        if i == 0:
            source, target = mine.at[0, pl.ds(2, 2), :, columns(c)], near.at[pl.ds(0, 2), :, columns(c)]
        else:
            source, target = mine.at[0, 1, :, columns(c)], near.at[2, :, columns(c)]
        return way(source, target, nsem, i, c)

    def ffn_way(i, c):
        if i == 0:
            source, target = fm.at[pl.ds(2, 2), :, broad(c)], fnear.at[pl.ds(0, 2), :, broad(c)]
        else:
            source, target = fm.at[1, :, broad(c)], fnear.at[2, :, broad(c)]
        return way(source, target, esem, i, c)

    def head_between(c):
        head_way(0, c).wait()
        for k in range(2):
            value = mine[0, k, :, columns(c)].astype(f32) + near[k, :, columns(c)].astype(f32)
            mine[0, k, :, columns(c)] = value.astype(bf16)
        head_way(1, c).start()

    def ffn_between(c):
        ffn_way(0, c).wait()
        for k in range(2):
            value = fm[k, :, broad(c)].astype(f32) + fnear[k, :, broad(c)].astype(f32)
            fm[k, :, broad(c)] = value.astype(bf16)
        ffn_way(1, c).start()

    def add(count, other, c):
        def body(i, carry):
            m, g = i // GROUPS, lax.rem(i, GROUPS)
            value = mine[m, g, :, columns(c)].astype(f32) + other(m, g).astype(f32)
            mine[m, g, :, columns(c)] = value.astype(bf16)
            return carry

        lax.fori_loop(0, count * GROUPS, body, 0)

    def row_copies(op):
        for j in range(n):
            source = rows.at[:, pl.ds(j * wide, wide)]
            target = pieces.at[z // 2, core]

            def remote(j=j, source=source, target=target):
                copy = pltpu.make_async_remote_copy(
                    src_ref=source,
                    dst_ref=target,
                    send_sem=tsem.at[0, j],
                    recv_sem=tsem.at[1, 2 * (z // 2) + core],
                    device_id={"dp": to_dp, "head": j},
                    device_id_type=MESH,
                )
                copy.start() if op == "start" else copy.wait_send()

            def inside(source=source, target=target):
                copy = pltpu.make_async_copy(source, target, lsem.at[0])
                copy.start() if op == "start" else copy.wait()

            pl.when((to_dp != dp) | (j != z))(remote)
            pl.when((to_dp == dp) & (j == z))(inside)

    def row_arrivals():
        for xs in range(2):
            for c2 in range(2):

                @pl.when((dp - core + c2 != dp) | (2 * xs + core != z))
                def _(xs=xs, c2=c2):
                    spot = pieces.at[xs, c2]
                    pltpu.make_async_remote_copy(
                        src_ref=spot,
                        dst_ref=spot,
                        send_sem=tsem.at[0, 0],
                        recv_sem=tsem.at[1, 2 * xs + c2],
                        device_id={"dp": at.by_x},
                        device_id_type=MESH,
                    ).wait_recv()

    cross = pltpu.make_async_remote_copy(
        src_ref=pieces.at[1 - bit_x],
        dst_ref=crossed,
        send_sem=xsem.at[0],
        recv_sem=xsem.at[1],
        device_id={"dp": at.by_x},
        device_id_type=MESH,
    )
    def vector_near(k):
        return pltpu.make_async_remote_copy(
            src_ref=vec.at[lax.rem(z + k, n)],
            dst_ref=vgot.at[k - 1],
            send_sem=vsem.at[0, k - 1],
            recv_sem=vsem.at[1, k - 1],
            device_id={"head": lax.rem(z + k, n)},
            device_id_type=MESH,
        )

    def vector_far(i, target):
        return pltpu.make_async_remote_copy(
            src_ref=vsum.at[i],
            dst_ref=vgot.at[3 + i],
            send_sem=vsem.at[0, 3 + i],
            recv_sem=vsem.at[1, 3 + i],
            device_id={"dp": target},
            device_id_type=MESH,
        )

    def put_head(l, c, value):
        if c < 3:
            qkv_out[l, c] = value
        else:
            out_out[l] = jnp.transpose(value, (1, 0))

    def total_of(own, others):
        value = own.astype(f32)
        for other in others:
            value = value + other.astype(f32)
        return value

    row_copies("start")
    for c in range(parts):
        hop(0, c).start()
    for k in range(1, n):
        vector_near(k).start()
    partners = (at.mate, at.first, at.second)
    for t in range(parts + 4):
        c = t
        if c < parts:
            for copy in loads(c):
                copy.wait()
            hop(0, c).wait()
            add(4, lambda m, g, c=c: got[m, g, :, columns(c)], c)
            hop(1, c).start()
            ffn_way(0, c).start()
        c = t - 1
        if 0 <= c < parts:
            hop(1, c).wait()
            add(2, lambda m, g, c=c: pair[m, g, :, columns(c)], c)
            hop(2, c).start()
        c = t - 2
        if 0 <= c < parts:
            hop(2, c).wait()
            add(1, lambda m, g, c=c: last[g, :, columns(c)], c)
            head_way(0, c).start()
        if t == 1:
            for k in range(1, n):
                vector_near(k).wait()
            vsum[0] = vec[z] + vgot[0] + vgot[1] + vgot[2]
            vector_far(0, partners[0]).start()
        if 2 <= t < 5:
            i = t - 2
            vector_far(i, partners[i]).wait()
            vsum[i + 1] = vsum[i] + vgot[3 + i]
            if i < 2:
                vector_far(i + 1, partners[i + 1]).start()
        if t == 2:
            row_copies("wait")
            row_arrivals()
            cross.start()
        if t == 4:
            for l in range(1, layers):
                heads, heads_other, ups, ups_other, downs, downs_other = tops[6 * l - 6 : 6 * l]
                for c in range(parts):
                    cols = slice(c * width, (c + 1) * width)
                    put_head(l, c, total_of(heads[0, :, cols], [heads_other[:, cols]]))
                up_out[l] = total_of(ups[0], [ups_other[...]])
                down_out[l] = jnp.transpose(total_of(downs[0], [downs_other[...]]), (1, 0))
        c = t - 1
        if 0 <= c < parts:
            ffn_between(c)
        c = t - 3
        if 0 <= c < parts:
            head_between(c)
        c = t - 4
        if 0 <= c < parts:
            ffn_way(1, c).wait()
            value = total_of(fm[0, :, broad(c)], [fnear[2, :, broad(c)]])
            if c < parts // 2:
                up_out[0, :, broad(c)] = value
            else:
                down_out[0, pl.ds(c * step - WIDE, step), :] = jnp.transpose(value, (1, 0))
    for c in range(parts):
        head_way(1, c).wait()
        put_head(0, c, total_of(mine[0, 0, :, columns(c)], [near[2, :, columns(c)]]))
    for l in range(layers):
        base = 28 * l
        for kind, (norm_out, hid_out) in enumerate(
            ((gains_out, hgains_out), (shifts_out, hshifts_out))
        ):
            for i in range(3):
                at_row = base + (3 * kind + i) * 2
                parts_of = [vsum[3, at_row + p : at_row + p + 1, :] for p in range(2)]
                norm_out[l, i : i + 1, :] = jnp.concatenate(parts_of, axis=1)
            at_row = base + 12 + 8 * kind
            parts_of = [vsum[3, at_row + p : at_row + p + 1, :] for p in range(BLOCKS)]
            hid_out[l : l + 1, :] = jnp.concatenate(parts_of, axis=1)
    totals = sum_lanes(vsum[3, 28 * layers : 31 * layers + 1, :])
    rms = jnp.sqrt(totals[: 3 * layers] / totals[3 * layers :])
    rms_out[0 : 3 * layers, :] = jnp.broadcast_to(rms, (3 * layers, LANES))
    cross.wait()
    for c2 in range(2):
        rows_out[2 * bit_x + c2] = pieces[bit_x, c2]
        rows_out[2 - 2 * bit_x + c2] = crossed[c2]


def end_call(rows, grads, fsum, valid, tops, vecs, uses):
    parts = 4
    layers = len(vecs) // 4
    tokens = rows.shape[0]
    wide = rows.shape[1] // GROUPS
    block = grads.shape[1:]
    broad = fsum.shape
    vector = (vector_rows(layers), LANES)
    inputs = [rows, grads, fsum, valid, *tops, *vecs, *uses]

    def spec(i, v):
        if i % 2 == 0:
            return pl.BlockSpec((1,) + v.shape[1:], lambda g: (0, 0, 0))
        return whole(v.shape)

    def kernel(*refs):
        fixed, refs = refs[:4], refs[4:]
        lists = []
        for values in (tops, vecs, uses):
            lists.append(refs[: len(values)])
            refs = refs[len(values) :]
        end_kernel(layers, *fixed, *lists, *refs)

    dims = [
        (GROUPS, tokens, wide),
        (layers, 3, LANES, HEADS),
        (layers, HEADS, LANES),
        (layers, LANES, WIDE),
        (layers, WIDE, LANES),
        (layers, 3, HEADS),
        (layers, 3, HEADS),
        (layers, WIDE),
        (layers, WIDE),
        (8 * (-(-3 * layers // 8)), LANES),
    ]
    outs = [jax.ShapeDtypeStruct(d, f32 if i else bf16) for i, d in enumerate(dims)]
    return pl.pallas_call(
        kernel,
        out_shape=outs,
        grid=(1,),
        in_specs=[HB] * 3
        + [whole(valid.shape)]
        + [spec(i, v) for i, v in enumerate(tops)]
        + [whole(v.shape) for v in (*vecs, *uses)],
        out_specs=[whole(v.shape) for v in outs],
        scratch_shapes=[
            pltpu.VMEM((4,) + block, bf16),
            pltpu.VMEM((4,) + block, bf16),
            pltpu.VMEM((2,) + block, bf16),
            pltpu.VMEM(block, bf16),
            pltpu.VMEM((3,) + block[1:], bf16),
            pltpu.VMEM((2, 2, tokens, wide), bf16),
            pltpu.VMEM((2, tokens, wide), bf16),
            pltpu.VMEM(broad, bf16),
            pltpu.VMEM((3,) + broad[1:], bf16),
            pltpu.VMEM((GROUPS,) + vector, f32),
            pltpu.VMEM((6,) + vector, f32),
            pltpu.VMEM((4,) + vector, f32),
            DMA((2, parts)),
            DMA((2, parts)),
            DMA((2, parts)),
            DMA((2, parts)),
            DMA((2, 2, parts)),
            DMA((2, 4)),
            DMA((2,)),
            DMA((2, 6)),
            DMA((2,)),
            DMA((2, 2, parts)),
        ],
        compiler_params=params(collective_id=6, has_side_effects=True),
        cost_estimate=cost(0, 300 * 2**20),
        name="end",
    )(*inputs)


def after(value, *tokens):
    return lax.optimization_barrier((value, tokens))[0]


class Order:
    def __init__(self):
        self.token = None
        self.wanted = []

    def __call__(self, call, *args, first=0):
        args = list(args)
        if self.token is not None:
            args[first] = after(args[first], self.token, *self.wanted)
            self.wanted = []
        out = call(*args)
        self.token = out
        while isinstance(self.token, (list, tuple)):
            self.token = self.token[0]
        return out

    def hold(self, value):
        return after(value, self.token)

    def want(self, value):
        self.wanted.append(value)
        return value


class Net:
    def __init__(self, n_dp, n_head):
        self.n_dp, self.n = n_dp, n_head
        self.own = lax.axis_index("dp").astype(jnp.int32)
        self.z = lax.axis_index("head").astype(jnp.int32)
        self.lo = self.own % n_head
        self.fast = n_dp == BLOCKS and n_head == GROUPS
        core_zero = [2, 4]
        self.one_way = [(i, i ^ core_zero[i % 2]) for i in range(n_dp)]
        self.other_way = [(i, i ^ core_zero[1 - i % 2]) for i in range(n_dp)]
        self.by_x = [(i, i ^ 2) for i in range(n_dp)]
        self.by_y = [(i, i ^ 4) for i in range(n_dp)]
        self.core = [(i, i ^ 1) for i in range(n_dp)]
        if self.fast:
            step = jnp.where(self.own % 2 == 0, 2, 4).astype(jnp.int32)
            mine = [jnp.int32(0), step, 6 - step, jnp.int32(6)]
            theirs = [jnp.int32(0), 6 - step, step, jnp.int32(6)]
            rows = [self.own ^ v for v in mine] + [self.own ^ v ^ 1 for v in theirs]
            straight = [self.own ^ v for v in (0, 2, 4, 6, 1, 3, 5, 7)]
            self.table = jnp.stack(rows + [self.z, self.lo] + straight)
        else:
            self.table = jnp.stack([jnp.int32(i) for i in range(BLOCKS)] + [jnp.int32(0), self.lo])

    def shift(self, value, k):
        n = self.n
        if k % n == 0:
            return value
        pairs = [(i, (i // n) * n + (i + k) % n) for i in range(self.n_dp)]
        return lax.ppermute(value, "dp", pairs)

    def across(self, value, bits):
        return lax.ppermute(value, "head", [(i, i ^ bits) for i in range(self.n)])

    def spin(self, value, k):
        n = self.n
        return lax.ppermute(value, "head", [(i, (i + k) % n) for i in range(n)])

    def gather(self, shard):
        return lax.all_gather(shard, ("dp", "head")).reshape(BLOCKS, GROUPS, LANES, -1)

    def gather_any(self, qkv, out, up, down):
        qkv = lax.all_gather(qkv, "head", axis=2, tiled=True)
        qkv = lax.all_gather(qkv, "dp", axis=1, tiled=True).transpose(1, 0, 2).reshape(D, 3 * D)
        up = lax.all_gather(up, "head", axis=1, tiled=True)
        up = lax.all_gather(up, "dp", axis=0, tiled=True)
        out, down = [
            lax.all_gather(lax.all_gather(v, "head", axis=0, tiled=True), "dp", axis=1, tiled=True)
            for v in (out, down)
        ]

        def blocks(*parts):
            cut = [v.reshape(BLOCKS, LANES, GROUPS, -1) for v in parts]
            return jnp.concatenate(cut, axis=3).transpose(0, 2, 1, 3)

        heads = [qkv[:, c * D : (c + 1) * D] for c in range(3)]
        return blocks(*heads, out.T), blocks(up, down.T)

    def scatter(self, full, widths):
        columns = full.shape[3]
        full = jnp.stack([full[:, slot_group(g)] for g in range(GROUPS)], axis=1)
        if self.fast:
            full = full.reshape(BLOCKS * GROUPS, LANES, columns)
        else:
            full = full.transpose(0, 2, 1, 3).reshape(D, GROUPS, columns)
            parts, at = [], 0
            for w in widths:
                part = full[:, :, at : at + w].reshape(D, self.n, GROUPS * w // self.n)
                parts.append(part)
                at += w
            full = jnp.concatenate(parts, axis=2)
            full = full.reshape(self.n_dp, D // self.n_dp, self.n, -1).transpose(0, 2, 1, 3)
            full = full.reshape(self.n_dp * self.n, D // self.n_dp, -1)
        mine = lax.psum_scatter(full, ("dp", "head"), scatter_dimension=0, tiled=False)
        return mine.astype(f32)


    def add_pair(self, keep, pair):
        add = lambda i: (keep[i].astype(f32) + pair[i].astype(f32)).astype(bf16)
        return add(0), add(1)

    def add_last(self, mine, last):
        return (mine.astype(f32) + last.astype(f32)).astype(bf16)

    def turn(self, k):
        n = self.n
        pairs = []
        for hi in range(self.n_dp // n):
            for lo in range(n):
                for z in range(n):
                    pairs.append(((hi * n + lo) * n + z, (hi * n + (z + k) % n) * n + lo))
        return pairs

    def rows_in(self, array):
        n = self.n
        tokens = array.shape[0] // n
        low = array.astype(bf16).reshape(n, tokens, array.shape[1])
        got = []
        for k in range(n):
            piece = lax.dynamic_index_in_dim(low, (self.z + k) % n, 0, False)
            got.append(lax.ppermute(piece, ("dp", "head"), self.turn(k)))
        return got

    def rows_in_end(self, got):
        stacked = jnp.take(jnp.stack(got), (self.lo - jnp.arange(self.n)) % self.n, axis=0)
        return stacked.transpose(1, 0, 2).reshape(got[0].shape[0], D)

    def rows_out(self, array):
        n = self.n
        width = D // n
        low = array.astype(bf16)
        got = []
        for k in range(n):
            piece = lax.dynamic_slice_in_dim(low, ((self.lo - k) % n) * width, width, 1)
            got.append(lax.ppermute(piece, ("dp", "head"), [(b, a) for a, b in self.turn(k)]))
        return got

    def rows_out_end(self, got):
        stacked = jnp.take(jnp.stack(got), (jnp.arange(self.n) - self.z) % self.n, axis=0)
        return stacked.reshape(-1, got[0].shape[1]).astype(f32)


def local(
    n_dp,
    n_head,
    stream_in,
    qkv_weight,
    out_weight,
    up_weight,
    down_weight,
    norm_gains,
    norm_shifts,
    hidden_gains,
    hidden_shifts,
    buckets,
    valid_mask,
    cotangent,
):
    net = Net(n_dp, n_head)
    n = n_head
    layers = qkv_weight.shape[0]
    tokens = LONG // n
    order = Order()

    flags = jnp.concatenate([valid_mask, buckets])
    flags = jnp.pad(flags, (0, -flags.shape[0] % 1024))
    vectors = [
        v.reshape(layers, -1) for v in (norm_gains, norm_shifts, hidden_gains, hidden_shifts)
    ]
    packed = jnp.concatenate(vectors, axis=1)
    narrow, broad = [None] * layers, [None] * layers
    if net.fast:
        small, large = pack_call(qkv_weight, out_weight, up_weight, down_weight)
        rows = stream_in.astype(bf16).reshape(n, tokens, D // n)
        flags = flags.reshape(-1, LANES)
        vector = packed.reshape(-1, LANES)
        started = order(start_call, [small[0], large[0]], rows, vector, flags, first=1)
        (narrow[0], broad[0]), stream, _, packed, flags, first_parts = started
        narrow[1:] = [net.gather(order.hold(v)) for v in small[1:]]
    else:
        for l in range(layers):
            narrow[l], broad[l] = net.gather_any(
                qkv_weight[l], out_weight[l], up_weight[l], down_weight[l]
            )
        stream = net.rows_in_end(net.rows_in(stream_in))
        flags = lax.ppermute(flags, ("dp", "head"), net.turn(0))
        packed = lax.all_gather(packed.reshape(-1, LANES), "head")
    aux, one, valid, need = masks_call(n, net.lo[None], flags.reshape(-1, LANES))

    low = stream
    cot = cotangent.astype(bf16).reshape(n, tokens, D // n)
    kept = []
    usage = []
    idents = iter(range(10, 64))
    for l in range(layers):
        ahead = net.fast and l + 1 < layers
        if net.fast and l == 0:
            parts = first_parts
        else:
            parts, _ = order(qkv_call, n, next(idents), [], l, low, packed, narrow[l], first=4)
        if ahead:
            broad[l + 1] = net.gather(order.hold(large[l + 1]))
        parts = [parts[0]] + [[net.shift(v, k) for k, v in enumerate(p)] for p in parts[1:]]
        att, lse = [], []
        for p in parts:
            outs = order(attn_call, n, need, aux, one, p, first=2)
            att.append(outs[0])
            lse.append(outs[1])
        last = net.fast and l + 1 == layers
        jobs = [Turn(cot, False, 0)] if last else []
        mid, rows, use_branch, *extra = order(
            proj_call, n, next(idents), jobs, l, valid, stream, packed, narrow[l], att, first=5
        )
        jobs = [Turn(cot, False, 1, extra[0])] if last else []
        slope, hat, normed, low_mid, rstd, stream, next_low, use_rest, *extra = order(
            ffn_call, n, next(idents), jobs, l, valid, mid, packed, broad[l], first=5
        )
        if last:
            grad = extra[0]
        usage += [use_branch, use_rest]
        kept.append((low, parts, att, lse, rows, slope, hat, normed, low_mid, rstd))
        low = next_low

    if not net.fast:
        grad = net.rows_in_end(net.rows_in(cotangent)).astype(f32)
    if not net.fast:
        grad = net.rows_in_end(net.rows_in(cotangent)).astype(f32)
    low_out = low
    units = BLOCKS // n
    ffn_grads, head_grads = [None] * layers, [None] * layers
    vectors, tops = [None] * layers, []

    for l in reversed(range(layers)):
        low, parts, att, lse, rows, slope, hat, normed, low_mid, rstd = kept[l]
        more = net.fast and l + 1 < layers
        last = net.fast and l + 1 == layers
        jobs = []
        if last:
            jobs = [Turn(low_out, True, 0)]
        if more:
            jobs = [Hop(head_odd, "mate")]
        dhid, grad_turned, ffn_turned, grad, hgrads, grads2, *extra = order(
            ffn_back_call, n, next(idents), jobs, l, grad, hat, slope, rstd,
            low_mid, packed, broad[l], first=4,
        )
        ffn_args = (ffn_turned, grad_turned, dhid, normed)
        if net.fast:
            moved = extra
            if more:
                head_keep, send = order(
                    head_grad_call, n, 0, 4, net.table, *head_args, extra[0], first=4
                )
                head_pair = lax.ppermute(order.hold(send), "dp", net.other_way)
            ups = BLOCKS + 2 if l else 0
            (odd,) = order(ffn_grad_call, ups, 4, 4, net.table, *ffn_args, first=4)
            jobs = [Hop(odd, "mate")]
            if more:
                wide_sums = [
                    net.add_last(order.hold(ups_mine), ups_last),
                    net.add_last(order.hold(downs_mine), downs_last),
                ]
                wide_near = [net.across(order.want(v)[2:], 1) for v in wide_sums]
            if last:
                jobs.append(Turn(low_out, True, 1, moved[0]))
        else:
            (full,) = order(ffn_grad_call, 0, 0, BLOCKS, net.table, *ffn_args, first=4)
            ffn_grads[l] = net.scatter(full, (WIDE, WIDE))
        res = order(
            proj_back_call, n, next(idents), jobs, l, grad, packed, narrow[l], rows, first=4
        )
        datt, (out_turned, normed_mid, grads1, *extra) = res[:units], res[units:]
        if net.fast:
            if last:
                turned = extra[1]
            if more:
                head_mine, sent = net.add_pair(order.hold(head_keep), head_pair)
                head_last = lax.ppermute(sent, "dp", net.one_way)
                order.want(sent)
            sums = order(ffn_grad_call, ups, 0, 4, net.table, *ffn_args, extra[0], first=4)
            if l:
                up_pair = lax.ppermute(order.hold(sums[1]), "dp", net.by_y)
                down_pair = lax.ppermute(order.hold(sums[3]), "dp", net.other_way)
            if more:
                wide_own = [
                    order.want(net.add_last(order.hold(v[:2]), other))
                    for v, other in zip(wide_sums, wide_near)
                ]
            if l == 0:
                ffn_pair = lax.ppermute(order.hold(sums[1]), "dp", net.other_way)
        dparts, ready = [], []
        for u in range(units):
            ready += [net.shift(v, -k) for k, v in enumerate(dparts)]
            dparts = order(
                attn_back_call, n, need, aux, one, parts[u], att[u], datt[u], lse[u], first=2
            )
            if more and u == 0:
                head_sum = order.want(net.add_last(order.hold(head_mine), head_last))
                wide_other = [net.across(order.hold(v[1]), 2) for v in wide_own]
            if net.fast and l and u == 0:
                order.want(down_pair)
        jobs = []
        if net.fast and l == 0:
            ffn_mine, sent = net.add_pair(order.hold(sums[0]), ffn_pair)
            ffn_last = lax.ppermute(order.want(sent), "dp", net.one_way)
        if more:
            head_near = net.across(order.hold(head_sum)[2:], 1)
        dlast, grad, in_turned, grads0, grad_low, *extra = order(
            qkv_back_call, n, next(idents), jobs, l, grad, low, packed, narrow[l], ready, dparts,
            first=4,
        )
        head_args = (in_turned, out_turned, ready + dlast, normed_mid)
        vectors[l] = [grads0, grads1, grads2, hgrads]
        if net.fast:
            if more:
                head_own = order.want(net.add_last(order.hold(head_sum[:2]), head_near))
                pairs = [v for pair in zip(wide_own, wide_other) for v in pair]
                tops = [head_own, net.across(head_own[1], 2), *pairs] + tops
            if l:
                (head_odd,) = order(head_grad_call, n, 4, 4, net.table, *head_args, first=4)
                ups_mine, ups_sent = net.add_pair(order.hold(sums[0]), up_pair)
                downs_mine, downs_sent = net.add_pair(order.hold(sums[2]), down_pair)
                order.want(ups_sent)
                order.want(downs_sent)
                ups_last = lax.ppermute(ups_sent, "dp", net.by_x)
                downs_last = lax.ppermute(downs_sent, "dp", net.one_way)
            else:
                (full,) = order(head_grad_call, n, 0, BLOCKS, net.table, *head_args, first=4)
        else:
            (full,) = order(head_grad_call, n, 0, BLOCKS, net.table, *head_args, first=4)
            head_grads[l] = net.scatter(full, (HEADS,) * 4)
    vectors = [v for part in vectors for v in part]
    if net.fast:
        ffn_sum = net.add_last(order.hold(ffn_mine), ffn_last)
        (
            moved, qkv_grad, out_grad, up_grad, down_grad,
            gains_grad, shifts_grad, hidden_gains_grad, hidden_shifts_grad, usage_rms,
        ) = order(
            end_call, grad_low, full, ffn_sum, valid, tops, vectors, usage
        )
        stream_out = turned.reshape(LONG, D // n).astype(f32)
        stream_grad = moved.reshape(LONG, D // n).astype(f32)
        stacked = [qkv_grad, out_grad, up_grad, down_grad]
        usage_rms = usage_rms[: 3 * layers, 0].reshape(layers, 3)
    else:
        stream_out = net.rows_out_end(net.rows_out(stream))
        stream_grad = net.rows_out_end(net.rows_out(grad))
        norms = [jnp.sum(jnp.stack(vectors[4 * l : 4 * l + 3], 1), axis=2) for l in range(layers)]
        norms = lax.psum(jnp.stack(norms), ("dp", "head"))
        hids = [jnp.sum(vectors[4 * l + 3], axis=2).reshape(2, FF) for l in range(layers)]
        hids = lax.psum(jnp.stack(hids), ("dp", "head"))
        share = lambda v: lax.dynamic_slice_in_dim(
            v, net.z * (v.shape[-1] // n), v.shape[-1] // n, v.ndim - 1
        )
        norms, hids = share(norms), share(hids)
        totals = []
        for l in range(layers):
            branch, rest = usage[2 * l : 2 * l + 2]
            totals += [jnp.sum(branch), jnp.sum(rest[0]), jnp.sum(rest[1])]
        totals = lax.psum(jnp.stack(totals + [jnp.sum(valid) * D]), ("dp", "head"))
        usage_rms = jnp.sqrt(totals[:-1] / totals[-1]).reshape(layers, 3)
        weight_grads = []
        for l in range(layers):
            heads = head_grads[l]
            width = heads.shape[1] // 4
            qkv = heads[:, : 3 * width].reshape(-1, 3, width).transpose(1, 0, 2)
            half = ffn_grads[l].shape[1] // 2
            weight_grads.append(
                (qkv, heads[:, 3 * width :].T, ffn_grads[l][:, :half], ffn_grads[l][:, half:].T)
            )
        stacked = [jnp.stack([weight_grads[l][k] for l in range(layers)]) for k in range(4)]
        gains_grad, shifts_grad = norms[:, 0], norms[:, 1]
        hidden_gains_grad, hidden_shifts_grad = hids[:, 0], hids[:, 1]
    return (
        stream_out,
        stream_grad,
        stacked[0],
        stacked[1],
        stacked[2],
        stacked[3],
        gains_grad,
        shifts_grad,
        hidden_gains_grad,
        hidden_shifts_grad,
        usage_rms,
    )


def solution(mesh):
    n_dp, n_head = mesh.shape["dp"], mesh.shape["head"]

    def run(*args):
        return local(n_dp, n_head, *args)

    return jax.shard_map(
        run,
        mesh=mesh,
        in_specs=(
            P("dp", "head"),
            P(None, None, "dp", "head"),
            P(None, "head", "dp"),
            P(None, "dp", "head"),
            P(None, "head", "dp"),
            P(None, None, "head"),
            P(None, None, "head"),
            P(None, "head"),
            P(None, "head"),
            P("dp"),
            P("dp"),
            P("dp", "head"),
        ),
        out_specs=(
            P("dp", "head"),
            P("dp", "head"),
            P(None, None, "dp", "head"),
            P(None, "head", "dp"),
            P(None, "dp", "head"),
            P(None, "head", "dp"),
            P(None, None, "head"),
            P(None, None, "head"),
            P(None, "head"),
            P(None, "head"),
            P(),
        ),
        check_vma=False,
    )
```
